32 devices in a mesh: blk: 8 (over z, y), tp: 4 (over x, core).
Axes of the slice: x: 2, y: 2, z: 4, core: 2. Of those that a mesh axis runs over, the one named last changes fastest.
Arguments:
- latents: bfloat16 [1024, 1536], P('blk'), may hold values from -6 to 6
- media: bfloat16 [4096, 1536], P('blk'), may hold values from -6 to 6
- query_weight: bfloat16 [1536, 1536], P(None, 'tp'), may hold values from -0.15625 to 0.15625
- key_weight: bfloat16 [1536, 1536], P(None, 'tp'), may hold values from -0.15625 to 0.15625
- value_weight: bfloat16 [1536, 1536], P(None, 'tp'), may hold values from -0.15625 to 0.15625
- out_weight: bfloat16 [1536, 1536], P('tp'), may hold values from -0.625 to 0.625
- up_weight: bfloat16 [1536, 6144], P(None, 'tp'), may hold values from -0.15625 to 0.15625
- down_weight: bfloat16 [6144, 1536], P('tp'), may hold values from -0.078125 to 0.078125
- media_gain: float32 [1536], replicated, may hold values from 0.1 to 1.9
- media_shift: float32 [1536], replicated, may hold values from -2.5 to 2.5
- latent_gain: float32 [1536], replicated, may hold values from 0.1 to 1.9
- latent_shift: float32 [1536], replicated, may hold values from -2.5 to 2.5
- feed_gain: float32 [1536], replicated, may hold values from 0.1 to 1.9
- feed_shift: float32 [1536], replicated, may hold values from -2.5 to 2.5
- cotangent: bfloat16 [1024, 1536], P('blk'), may hold values from -6 to 6
- media_image: int32 [4096], P('blk'), may hold values from 0 to 15, as said below
Outputs:
- resampled: bfloat16 [1024, 1536], P('blk')
- media_grad: float32 [4096, 1536], P('blk')
- latent_grad: float32 [1024, 1536], P('blk')
- query_grad: float32 [1536, 1536], P('blk', 'tp')
- key_grad: float32 [1536, 1536], P('blk', 'tp')
- value_grad: float32 [1536, 1536], P('blk', 'tp')
- out_grad: float32 [1536, 1536], P('tp', 'blk')
- up_grad: float32 [1536, 6144], P('blk', 'tp')
- down_grad: float32 [6144, 1536], P('tp', 'blk')
- media_gain_grad: float32 [1536], P('blk')
- media_shift_grad: float32 [1536], P('blk')
- latent_gain_grad: float32 [1536], P('blk')
- latent_shift_grad: float32 [1536], P('blk')
- feed_gain_grad: float32 [1536], P('blk')
- feed_shift_grad: float32 [1536], P('blk')
The draws below stay inside these ranges and needn't reach their ends.
Inputs may be any that keep to these rules, and one draw needn't show every extreme that they name: `media_image`: media rows come in aligned segments of 64 rows; each image owns four segments, placed at random over all 4096 rows, with one exception: one image, drawn from the seed, also takes one row in every aligned block of 512 rows.
All inputs are finite; a program needn't handle non-finite values.
Results may differ from the reference program's by a relative error of at most 0.033.
Values may be sent and summed in bfloat16 or wider, within the bound.
A program may use at most 192 MiB of HBM per device.

```python
import math
import jax
import jax.numpy as jnp
from jax import lax

D = 1536
HEADS = 16
HEAD_DIM = 96
FF = 6144
LATENTS = 64
PATCH = 256
INNER = 1536
MED_DEV = 512
IMAGES = 16
MEDIA = 4096
LAT_ROWS = 1024


def draw_media_image(key, part):
    key = jax.random.fold_in(key, 7)
    order_key, wide_key, place_key = jax.random.split(key, 3)
    segment_rows = PATCH // 4
    segment_count = MEDIA // segment_rows
    order = jax.random.permutation(order_key, segment_count).astype(jnp.int32)
    segment_image = order // 4
    row_index = jnp.arange(MEDIA, dtype=jnp.int32)
    owners = segment_image[row_index // segment_rows]
    wide_image = jax.random.randint(wide_key, (), 0, IMAGES)
    places = jax.random.randint(place_key, (MEDIA // MED_DEV,), 0, MED_DEV)
    chosen = row_index % MED_DEV == places[row_index // MED_DEV]
    return jnp.where(chosen, wide_image, owners).astype(jnp.int32)


def raised(array, key, source, target, blocks, factor):
    def block_of(position):
        return (jnp.arange(array.shape[position]) // (array.shape[position] // blocks)).reshape((-1,) + (1,) * (array.ndim - 1 - position))

    first = jax.random.permutation(key, blocks)[block_of(target)]
    second = (block_of(target) + blocks // 2) % blocks
    return jnp.where((block_of(source) == first) | (block_of(source) == second), factor * array, array)


def levels(own_key, shape, cuts, least, high):
    loudness = 1.0
    for dim, blocks in cuts:
        heights = jax.random.uniform(jax.random.fold_in(jax.random.fold_in(own_key, 6), dim), (blocks,), jnp.float32, least / len(cuts), high / len(cuts))
        loudness = loudness * jnp.repeat(jnp.exp(heights), shape[dim] // blocks).reshape((-1,) + (1,) * (len(shape) - 1 - dim))
    return loudness


def scatter_about(key, extent, deviation, limit, cuts=(), kind=jnp.bfloat16):
    level = levels(key, extent, cuts, -0.22, 0.18) if cuts else 1.0
    drawn = jax.random.normal(key, extent, jnp.float32) * deviation * level
    return jnp.minimum(jnp.maximum(drawn, -limit), limit).astype(kind)


def noise_with(key, extent, deviation, limit, pieces, heavy, kind=jnp.bfloat16):
    array = deviation * jax.random.normal(key, extent, jnp.float32)
    if pieces:
        array = array * levels(key, extent, pieces, -0.22, 0.18)
    return jnp.clip(raised(array, jax.random.fold_in(key, 3), *heavy), -limit, limit).astype(kind)


def setup_inputs(seed: int = 0) -> dict:
    arg_keys = jax.random.split(jax.random.key(seed), 17)
    latents = scatter_about(arg_keys[0], (LAT_ROWS, D), 1.0, 6.0, ((0, 8),))
    media = noise_with(arg_keys[1], (MEDIA, D), 1.0, 6.0, ((0, 8),), (0, 1, 8, 2.0))
    query_weight = scatter_about(arg_keys[2], (D, INNER), D ** -0.5, 0.15625, ((1, 4),))
    key_weight = scatter_about(arg_keys[3], (D, INNER), D ** -0.5, 0.15625, ((1, 4),))
    value_weight = scatter_about(arg_keys[4], (D, INNER), D ** -0.5, 0.15625, ((1, 4),))
    out_weight = scatter_about(arg_keys[5], (INNER, D), (INNER // 16) ** -0.5, 0.625, ((0, 4),))
    up_weight = scatter_about(arg_keys[6], (D, FF), D ** -0.5, 0.15625, ((1, 4),))
    down_weight = scatter_about(arg_keys[7], (FF, D), FF ** -0.5, 0.078125, ((0, 4),))
    media_gain = jnp.clip(1.0 + 0.18 * jax.random.normal(arg_keys[8], (D,), jnp.float32), 0.1, 1.9)
    media_shift = scatter_about(arg_keys[9], (D,), 0.5, 2.5, (), jnp.float32)
    latent_gain = jnp.clip(1.0 + 0.18 * jax.random.normal(arg_keys[10], (D,), jnp.float32), 0.1, 1.9)
    latent_shift = scatter_about(arg_keys[11], (D,), 0.5, 2.5, (), jnp.float32)
    feed_gain = jnp.clip(1.0 + 0.18 * jax.random.normal(arg_keys[12], (D,), jnp.float32), 0.1, 1.9)
    feed_shift = scatter_about(arg_keys[13], (D,), 0.5, 2.5, (), jnp.float32)
    cotangent = noise_with(arg_keys[14], (LAT_ROWS, D), 1.0, 6.0, ((0, 8),), (0, 1, 8, 2.0))
    media_image = draw_media_image(jax.random.fold_in(arg_keys[16], 71), 0)
    return dict(latents=latents, media=media, query_weight=query_weight, key_weight=key_weight, value_weight=value_weight, out_weight=out_weight, up_weight=up_weight, down_weight=down_weight, media_gain=media_gain, media_shift=media_shift, latent_gain=latent_gain, latent_shift=latent_shift, feed_gain=feed_gain, feed_shift=feed_shift, cotangent=cotangent, media_image=media_image)


@jax.custom_vjp
def low(v):
    return lax.optimization_barrier(v.astype(jnp.bfloat16)).astype(jnp.float32)

@jax.custom_vjp
def reduced_backward(v):
    return v

def low_keep(v):
    return (low(v), None)

def low_pass(kept, grad):
    return (grad,)

def back_keep(v):
    return (v, None)

def back_low(kept, grad):
    return (low(grad),)
low.defvjp(low_keep, low_pass)
reduced_backward.defvjp(back_keep, back_low)

def both_ways(values):
    return low(reduced_backward(values))

def layer_norm(values, norm_gain, norm_shift):
    row_mean = lax.optimization_barrier(jnp.mean(values, axis=-1, keepdims=True))
    centred = values - row_mean
    row_var = lax.optimization_barrier(jnp.mean(centred * centred, axis=-1, keepdims=True))
    return centred * lax.rsqrt(row_var + 1e-05) * norm_gain + norm_shift

def forward(latents, media, query_weight, key_weight, value_weight, out_weight, up_weight, down_weight, media_gain, media_shift, latent_gain, latent_shift, feed_gain, feed_shift, media_image):
    precision_highest = lax.Precision.HIGHEST
    score_scale = 1.0 / math.sqrt(HEAD_DIM)
    media_normed = low(layer_norm(media, media_gain, media_shift))
    media_key_rows = both_ways(jnp.dot(media_normed, key_weight, precision=precision_highest)).reshape(MEDIA, HEADS, HEAD_DIM)
    media_value_rows = both_ways(jnp.dot(media_normed, value_weight, precision=precision_highest)).reshape(MEDIA, HEADS, HEAD_DIM)
    latent_normed = low(layer_norm(latents, latent_gain, latent_shift))
    queries = both_ways(jnp.dot(latent_normed, query_weight, precision=precision_highest) * score_scale)
    latent_keys = both_ways(jnp.dot(latent_normed, key_weight, precision=precision_highest))
    latent_values = both_ways(jnp.dot(latent_normed, value_weight, precision=precision_highest))
    queries = queries.reshape(IMAGES, LATENTS, HEADS, HEAD_DIM)
    latent_keys = latent_keys.reshape(IMAGES, LATENTS, HEADS, HEAD_DIM)
    latent_values = latent_values.reshape(IMAGES, LATENTS, HEADS, HEAD_DIM)

    def one_image(inputs):
        picture_queries, image_keys, picture_values, image_index = inputs
        remote_scores = reduced_backward(jnp.einsum('ufq,afq->fua', picture_queries, media_key_rows, precision=precision_highest))
        own_scores = reduced_backward(jnp.einsum('lhd,khd->hlk', picture_queries, image_keys, precision=precision_highest))
        allowed = (media_image == image_index)[None, None, :]
        remote_scores = jnp.where(allowed, remote_scores, -1e+30)
        row_top = jnp.maximum(lax.optimization_barrier(jnp.max(remote_scores, axis=-1, keepdims=True)), lax.optimization_barrier(jnp.max(own_scores, axis=-1, keepdims=True)))
        far_exp = jnp.exp(remote_scores - row_top)
        own_exp = jnp.exp(own_scores - row_top)
        row_total = lax.optimization_barrier(jnp.sum(far_exp, axis=-1, keepdims=True)) + lax.optimization_barrier(jnp.sum(own_exp, axis=-1, keepdims=True))
        remote_probs = low(far_exp / row_total)
        local_probs = low(own_exp / row_total)
        return jnp.einsum('vtu,uvp->tvp', remote_probs, media_value_rows, precision=precision_highest) + jnp.einsum('fba,afg->bfg', local_probs, picture_values, precision=precision_highest)
    image_ids = jnp.arange(IMAGES, dtype=jnp.int32)
    attention = lax.map(jax.checkpoint(one_image), (queries, latent_keys, latent_values, image_ids))
    attention = both_ways(attention.reshape(IMAGES * LATENTS, HEADS * HEAD_DIM))
    middle = latents + reduced_backward(jnp.dot(attention, out_weight, precision=precision_highest))
    feed_normed = low(layer_norm(middle, feed_gain, feed_shift))
    hidden = low(jax.nn.gelu(reduced_backward(jnp.dot(feed_normed, up_weight, precision=precision_highest)), approximate=False))
    return middle + reduced_backward(jnp.dot(hidden, down_weight, precision=precision_highest))

def reference(latents, media, query_weight, key_weight, value_weight, out_weight, up_weight, down_weight, media_gain, media_shift, latent_gain, latent_shift, feed_gain, feed_shift, cotangent, media_image):
    primals = (latents.astype(jnp.float32), media.astype(jnp.float32), query_weight.astype(jnp.float32), key_weight.astype(jnp.float32), value_weight.astype(jnp.float32), out_weight.astype(jnp.float32), up_weight.astype(jnp.float32), down_weight.astype(jnp.float32), media_gain.astype(jnp.float32), media_shift.astype(jnp.float32), latent_gain.astype(jnp.float32), latent_shift.astype(jnp.float32), feed_gain.astype(jnp.float32), feed_shift.astype(jnp.float32))

    def layer_fn(*params):
        return forward(*params, media_image)
    result, pull_back = jax.vjp(layer_fn, *primals)
    grads = pull_back(cotangent.astype(jnp.float32))
    return (result.astype(jnp.bfloat16), grads[1], grads[0], grads[2], grads[3], grads[4], grads[5], grads[6], grads[7], grads[8], grads[9], grads[10], grads[11], grads[12], grads[13])
```

```python
import functools
import math

import jax
import jax.numpy as jnp
from jax import lax
from jax.experimental import pallas as pl
from jax.experimental.pallas import tpu as pltpu
from jax.sharding import PartitionSpec as P

HEAD_DIM = 96
LATENTS = 64
NEG_FILL = -1e30
NORM_EPS = 1e-05
BF = jnp.bfloat16
F32 = jnp.float32
MESH = pl.DeviceIdType.MESH
VMEM_LIMIT = 60 * 1024 * 1024
SCALE = 1.0 / math.sqrt(HEAD_DIM)


def dot_nn(a, b):
    return jnp.dot(a, b, preferred_element_type=F32)


def dot_nt(a, b):
    return lax.dot_general(a, b, (((1,), (1,)), ((), ())), preferred_element_type=F32)


def dot_tn(a, b):
    return lax.dot_general(a, b, (((0,), (0,)), ((), ())), preferred_element_type=F32)


def normalised(x):
    centred = x - jnp.mean(x, axis=-1, keepdims=True)
    rstd = lax.rsqrt(jnp.mean(centred * centred, axis=-1, keepdims=True) + NORM_EPS)
    return centred * rstd, rstd


def norm_back(q, gain, xhat, rstd):
    qg = q * gain
    inner = jnp.mean(qg * xhat, axis=-1, keepdims=True)
    return (qg - jnp.mean(qg, axis=-1, keepdims=True) - xhat * inner) * rstd


def greet(devices):
    barrier = pltpu.get_barrier_semaphore()
    for device in devices:
        pl.semaphore_signal(barrier, inc=1, device_id=device, device_id_type=MESH)
    pl.semaphore_wait(barrier, len(devices))


def remote(src, dst, send_sem, recv_sem, device):
    return pltpu.make_async_remote_copy(
        src_ref=src,
        dst_ref=dst,
        send_sem=send_sem,
        recv_sem=recv_sem,
        device_id=device,
        device_id_type=MESH,
    )


class Place:
    def __init__(self, nb):
        self.nb = nb
        self.no = nb // 2
        self.me = lax.axis_index("blk")
        self.outer = self.me // 2
        self.inner = self.me % 2
        self.partner = 2 * self.outer + 1 - self.inner

    def far(self, d):
        return (self.me + d) % self.nb

    def near(self, d):
        return (self.me - d + self.nb) % self.nb

    def outer_to(self, d):
        return (self.outer + d) % self.no

    def outer_from(self, d):
        return (self.outer - d + self.no) % self.no

    def greeting(self):
        return [{"blk": self.far(d)} for d in range(1, self.nb)]


class Gather:
    def __init__(self, place, slots, sems):
        self.place, self.slots, self.sems = place, slots, sems

    def copy_z(self, d):
        pc = self.place
        slot = self.slots.at[pc.me]
        return remote(
            slot, slot, self.sems.at[0, 0, d], self.sems.at[0, 1, d],
            {"blk": 2 * pc.outer_to(d) + pc.inner},
        )

    def copy_y(self, d):
        pc = self.place
        slot = self.slots.at[2 * pc.outer_from(d) + pc.inner]
        return remote(
            slot, slot, self.sems.at[1, 0, d], self.sems.at[1, 1, d], {"blk": pc.partner}
        )

    def start(self):
        for d in range(1, self.place.no):
            self.copy_z(d).start()
        self.copy_y(0).start()

    def relay(self):
        pc = self.place
        for d in range(1, pc.no):
            arrived = self.slots.at[2 * pc.outer_from(d) + pc.inner]
            remote(
                arrived, arrived, self.sems.at[0, 0, d], self.sems.at[0, 1, d], {"blk": pc.partner}
            ).wait_recv()
            self.copy_y(d).start()

    def finish(self):
        pc = self.place
        for d in range(pc.no):
            slot = self.slots.at[2 * pc.outer_from(d) + 1 - pc.inner]
            remote(
                slot, slot, self.sems.at[1, 0, d], self.sems.at[1, 1, d], {"blk": pc.partner}
            ).wait_recv()
        for d in range(1, pc.no):
            self.copy_z(d).wait_send()
        for d in range(pc.no):
            self.copy_y(d).wait_send()


class Exchange:
    def __init__(self, place, out, into, sems, slot=lambda d: d):
        self.place, self.out, self.into, self.sems, self.slot = place, out, into, sems, slot

    def copy(self, d):
        return remote(
            self.out.at[self.slot(d)], self.into.at[d], self.sems.at[0, d], self.sems.at[1, d],
            {"blk": self.place.far(d)},
        )

    def start(self, d):
        self.copy(d).start()

    def wait_recv(self, d):
        self.copy(d).wait_recv()

    def finish_sends(self):
        for d in range(1, self.place.nb):
            self.copy(d).wait_send()


def lane_image(source, images_here, width):
    lane = lax.broadcasted_iota(jnp.int32, (1, width), 1)
    return source * images_here + lane // LATENTS


def attend_kernel(
    nb,
    lat_ref, med_ref, wq_ref, wk_ref, wv_ref, lg_ref, ls_ref, mg_ref, ms_ref, image_ref,
    ln_ref, mn_ref, q_all, kh_ref, kt_ref, vh_ref, lkh_ref, lkt_ref, lvh_ref, att_ref, lse_ref,
    vt, lvt, acc_out, acc_in, stat_out, stat_in, g_sems, a_sems, s_sems,
):
    place = Place(nb)
    lat_rows = lat_ref.shape[0]
    med_rows = med_ref.shape[0]
    heads = kh_ref.shape[0]
    images_here = lat_rows // LATENTS
    greet(place.greeting())

    xhat, _ = normalised(lat_ref[...].astype(F32))
    ln_ref[...] = (xhat * lg_ref[...] + ls_ref[...]).astype(BF)
    ln = ln_ref[...]

    def heads_t(rows, ref):
        turned = rows.T
        for h in range(heads):
            ref[h] = turned[h * HEAD_DIM : (h + 1) * HEAD_DIM].astype(BF)

    def heads_n(rows, ref):
        for h in range(heads):
            ref[h] = rows[:, h * HEAD_DIM : (h + 1) * HEAD_DIM].astype(BF)

    heads_t(dot_nn(ln, wq_ref[...]) * SCALE, q_all.at[place.me])
    gather = Gather(place, q_all, g_sems)
    gather.start()
    lk = dot_nn(ln, wk_ref[...])
    heads_n(lk, lkh_ref)
    heads_t(lk, lkt_ref)
    lv = dot_nn(ln, wv_ref[...])
    heads_n(lv, lvh_ref)
    heads_t(lv, lvt)

    def norm_rows(i, carry):
        rows = pl.ds(pl.multiple_of(i * 128, 128), 128)
        hat, _ = normalised(med_ref[rows, :].astype(F32))
        mn_ref[rows, :] = (hat * mg_ref[...] + ms_ref[...]).astype(BF)
        return carry

    lax.fori_loop(0, med_rows // 128, norm_rows, 0)
    mk = dot_nn(mn_ref[...], wk_ref[...])
    heads_n(mk, kh_ref)
    heads_t(mk, kt_ref)
    gather.relay()
    mv = dot_nn(mn_ref[...], wv_ref[...])
    heads_n(mv, vh_ref)
    heads_t(mv, vt)
    gather.finish()

    exchange = Exchange(place, acc_out, acc_in, a_sems)
    stats = Exchange(place, stat_out, stat_in, s_sems)
    image = image_ref[...]
    order = list(range(1, nb)) + [0]
    for g in range(nb // 2):
        pair = order[2 * g : 2 * g + 2]
        sources = [place.far(d) for d in pair]
        lanes = jnp.concatenate([lane_image(s, images_here, lat_rows) for s in sources], axis=1)
        allowed = image == lanes
        for h in range(heads):
            queries = jnp.concatenate([q_all[s, h] for s in sources], axis=1)
            scores = jnp.where(allowed, dot_nn(kh_ref[h], queries), NEG_FILL)
            top = jnp.max(scores, axis=0, keepdims=True)
            weights = jnp.exp(scores - top)
            total = jnp.sum(weights, axis=0, keepdims=True)
            acc = dot_nn(vt[h], weights.astype(BF)).astype(BF)
            for n, d in enumerate(pair):
                part = slice(n * lat_rows, (n + 1) * lat_rows)
                acc_out[d, h] = acc[:, part]
                stat_out[d, h : h + 1, :] = top[:, part]
                stat_out[d, heads + h : heads + h + 1, :] = total[:, part]
        for d in pair:
            if d:
                exchange.start(d)
                stats.start(d)

    row_image = lax.broadcasted_iota(jnp.int32, (lat_rows, lat_rows), 0) // LATENTS
    col_image = lax.broadcasted_iota(jnp.int32, (lat_rows, lat_rows), 1) // LATENTS
    same = row_image == col_image
    own = []
    for h in range(heads):
        scores = jnp.where(same, dot_nn(lkh_ref[h], q_all[place.me, h]), NEG_FILL)
        top = jnp.max(scores, axis=0, keepdims=True)
        weights = jnp.exp(scores - top)
        total = jnp.sum(weights, axis=0, keepdims=True)
        own.append((top, total, dot_nn(lvt[h], weights.astype(BF))))
    for d in range(1, nb):
        stats.wait_recv(d)
        exchange.wait_recv(d)
    lse_ref[...] = jnp.zeros_like(lse_ref)
    for h in range(heads):
        own_top, own_total, own_acc = own[h]
        tops = [
            (stat_out if d == 0 else stat_in)[d, h : h + 1, :] for d in range(nb)
        ]
        best = functools.reduce(jnp.maximum, tops, own_top)
        factor = jnp.exp(own_top - best)
        total = own_total * factor
        acc = own_acc * factor
        for d in range(nb):
            factor = jnp.exp(tops[d] - best)
            stat = stat_out if d == 0 else stat_in
            piece = acc_out if d == 0 else acc_in
            total = total + stat[d, heads + h : heads + h + 1, :] * factor
            acc = acc + piece[d, h].astype(F32) * factor
        att_ref[h] = acc / total
        lse_ref[h : h + 1, :] = best + jnp.log(total)
    exchange.finish_sends()
    stats.finish_sends()


class TensorSum:
    def __init__(self, bufs, sems, tile_of):
        self.bufs, self.sems, self.tile_of = bufs, sems, tile_of
        self.tiles, self.rows, self.tile = bufs.shape[1:]
        t = lax.axis_index("tp")
        self.core = t % 2
        self.chip = t // 2
        self.sibling = {"tp": 2 * self.chip + 1 - self.core}
        self.across = {"tp": 2 * (1 - self.chip) + self.core}

    @staticmethod
    def greeting():
        t = lax.axis_index("tp")
        core, chip = t % 2, t // 2
        return [{"tp": 2 * chip + 1 - core}, {"tp": 2 * (1 - chip) + core}]

    def column(self, half, j):
        return pl.multiple_of((half * self.tiles + j) * self.tile, 128)

    def copy(self, stage, j):
        return remote(
            self.bufs.at[2 * stage, j], self.bufs.at[2 * stage + 1, j],
            self.sems.at[stage, 0, j], self.sems.at[stage, 1, j],
            self.across if stage == 1 else self.sibling,
        )

    def give(self):
        for j in range(self.tiles):
            self.bufs[0, j] = self.tile_of(self.column(1 - self.core, j)).astype(BF)
            self.copy(0, j).start()

    def cross(self):
        for j in range(self.tiles):
            mine = self.tile_of(self.column(self.core, j))
            self.copy(0, j).wait_recv()
            self.bufs[2, j] = (mine + self.bufs[1, j].astype(F32)).astype(BF)
            self.copy(1, j).start()

    def back(self):
        for j in range(self.tiles):
            self.copy(1, j).wait_recv()
            self.bufs[4, j] = (self.bufs[2, j].astype(F32) + self.bufs[3, j].astype(F32)).astype(BF)
            self.copy(2, j).start()

    def finish(self, put):
        for j in range(self.tiles):
            put(self.column(self.core, j), self.bufs[4, j])
        for j in range(self.tiles):
            self.copy(2, j).wait_recv()
            put(self.column(1 - self.core, j), self.bufs[5, j])
        for stage in range(3):
            for j in range(self.tiles):
                self.copy(stage, j).wait_send()


def feed_kernel(
    att_ref, lse_ref, lat_ref, cot_ref, wo_ref, fg_ref, fs_ref, up_hbm, down_hbm,
    out_ref, mid_grad_ref, branch_ref, dot_ref, ld_ref, fn_ref, low_ref, gain_ref,
    up, down, hg, mid, hidden, pre_grad, low_t, sum_buf, bufs, sems, w_sems,
):
    loads = [
        pltpu.make_async_copy(up_hbm, up, w_sems.at[0]),
        pltpu.make_async_copy(down_hbm, down, w_sems.at[1]),
    ]
    for load in loads:
        load.start()
    heads = att_ref.shape[0]
    ff_here = up.shape[1]
    ff_tile = math.gcd(ff_here, 512)
    greet(TensorSum.greeting())
    for h in range(heads):
        low_t[h * HEAD_DIM : (h + 1) * HEAD_DIM, :] = att_ref[h]
    low_ref[...] = low_t[...].T.astype(BF)
    low = low_ref[...]

    def put(column, tile):
        sum_buf[:, pl.ds(column, tile.shape[1])] = tile.astype(F32)

    def tile_sum(n, tile_of):
        return TensorSum(bufs.at[n], sems.at[n], tile_of)

    width = bufs.shape[-1]
    branch = tile_sum(0, lambda c: dot_nn(low, wo_ref[:, pl.ds(c, width)]))
    branch.give()
    branch.cross()
    loads[1].wait()
    cot = cot_ref[...]

    def back_hidden(i, carry):
        cols = pl.ds(pl.multiple_of(i * ff_tile, ff_tile), ff_tile)
        hg[:, cols] = dot_nt(cot, down[cols, :])
        return carry

    lax.fori_loop(0, ff_here // ff_tile, back_hidden, 0)
    branch.back()
    branch.finish(put)
    mid[...] = lat_ref[...].astype(F32) + sum_buf[...]
    xhat, rstd = normalised(mid[...])
    fn_ref[...] = (xhat * fg_ref[...] + fs_ref[...]).astype(BF)
    fn = fn_ref[...]
    loads[0].wait()

    def inner(i, carry):
        cols = pl.ds(pl.multiple_of(i * ff_tile, ff_tile), ff_tile)
        pre = dot_nn(fn, up[:, cols])
        bell = 0.5 * (1.0 + lax.erf(pre * math.sqrt(0.5)))
        hidden[:, cols] = (pre * bell).astype(BF)
        slope = bell + pre * jnp.exp(-0.5 * pre * pre) * (1.0 / math.sqrt(2.0 * math.pi))
        pre_grad[:, cols] = (hg[:, cols] * slope).astype(BF)
        return carry

    lax.fori_loop(0, ff_here // ff_tile, inner, 0)
    grads = tile_sum(1, lambda c: dot_nt(pre_grad[...], up[pl.ds(c, width), :]))
    feed = tile_sum(2, lambda c: dot_nn(hidden[...], down[:, pl.ds(c, width)]))
    grads.give()
    grads.cross()
    feed.give()
    feed.cross()
    grads.back()
    feed.back()
    grads.finish(put)
    fng = sum_buf[...]
    xhat, rstd = normalised(mid[...])
    mid_grad = cot_ref[...].astype(F32) + norm_back(fng, fg_ref[...], xhat, rstd)
    mid_grad_ref[...] = mid_grad
    branch_ref[...] = mid_grad.astype(BF)
    gain_ref[...] = jnp.zeros_like(gain_ref)
    gain_ref[0:1, :] = jnp.sum(fng * xhat, axis=0, keepdims=True)
    gain_ref[1:2, :] = jnp.sum(fng, axis=0, keepdims=True)
    back = dot_nt(wo_ref[...], branch_ref[...])
    ld_ref[...] = lse_ref[...]
    for h in range(heads):
        piece = back[h * HEAD_DIM : (h + 1) * HEAD_DIM, :].astype(BF)
        dot_ref[h] = piece
        ld_ref[heads + h : heads + h + 1, :] = jnp.sum(
            piece.astype(F32) * att_ref[h], axis=0, keepdims=True
        )
    feed.finish(put)
    out_ref[...] = (mid[...] + sum_buf[...]).astype(BF)


def back_kernel(
    nb,
    q_all, dot_in, ld_in, kh_ref, kt_ref, vh_ref, lkh_ref, lkt_ref, lvh_ref, ln_ref, mn_ref,
    wq_ref, wk_ref, wv_ref, mid_grad_ref, lat_ref, med_ref, lg_ref, mg_ref, fgain_ref, image_ref,
    mgrad_ref, lgrad_ref, qg_ref, kg_ref, vg_ref, gains_ref,
    dot_all, ld_all, dk, dv, dq_own, dq_in, turn, xall, yall, dq_low, part, pair_in, far_in,
    gain_out, gain_in, med_bufs, lat_bufs,
    g_sems, l_sems, x_sems, y_sems, z_sems, n_sems, t_sems,
):
    place = Place(nb)
    lat_rows = lat_ref.shape[0]
    med_rows, model = med_ref.shape
    heads = kh_ref.shape[0]
    inner = heads * HEAD_DIM
    images_here = lat_rows // LATENTS
    dot_all[place.me] = dot_in[...]
    ld_all[place.me] = ld_in[...]
    greet(place.greeting() + TensorSum.greeting())
    gather = Gather(place, dot_all, g_sems)
    gather_ld = Gather(place, ld_all, l_sems)
    gather_ld.start()
    gather.start()

    row_image = lax.broadcasted_iota(jnp.int32, (lat_rows, lat_rows), 0) // LATENTS
    col_image = lax.broadcasted_iota(jnp.int32, (lat_rows, lat_rows), 1) // LATENTS
    same = row_image == col_image

    def turned(h, value, rows):
        turn[h * HEAD_DIM : (h + 1) * HEAD_DIM, 0:rows] = value

    def grads_of(h, keys, values, queries, grads, lse, delta, allowed):
        scores = jnp.where(allowed, dot_nn(keys, queries), NEG_FILL)
        probs = jnp.exp(scores - lse)
        score_grad = (probs * (dot_nn(values, grads) - delta)).astype(BF)
        return probs.astype(BF), score_grad

    for h in range(heads):
        queries, grads = q_all[place.me, h], dot_in[h]
        probs, score_grad = grads_of(
            h, lkh_ref[h], lvh_ref[h], queries, grads,
            ld_in[h : h + 1, :], ld_in[heads + h : heads + h + 1, :], same,
        )
        dk[h, :, 0:lat_rows] = dot_nt(queries, score_grad)
        dv[h, :, 0:lat_rows] = dot_nt(grads, probs)
        dq_own[h] = dot_nn(lkt_ref[h], score_grad)

    def put_rows(first, rows):
        for acc, column in ((dk, 0), (dv, inner)):
            for h in range(heads):
                turned(h, acc[h, :, 0:rows], rows)
            yall[first : first + rows, column : column + inner] = turn[:, 0:rows].T.astype(BF)

    put_rows(med_rows, lat_rows)
    xall[0:med_rows, :] = mn_ref[...]
    xall[med_rows:, :] = ln_ref[...]
    gather_ld.relay()
    gather.relay()
    gather_ld.finish()
    gather.finish()

    exchange = Exchange(place, dot_all, dq_in, x_sems, place.far)
    image = image_ref[...]
    order = list(range(1, nb)) + [0]
    for g in range(nb // 2):
        pair = order[2 * g : 2 * g + 2]
        sources = [place.far(d) for d in pair]
        lanes = jnp.concatenate([lane_image(s, images_here, lat_rows) for s in sources], axis=1)
        allowed = image == lanes
        for h in range(heads):
            queries = jnp.concatenate([q_all[s, h] for s in sources], axis=1)
            grads = jnp.concatenate([dot_all[s, h] for s in sources], axis=1)
            lse = jnp.concatenate([ld_all[s, h : h + 1, :] for s in sources], axis=1)
            delta = jnp.concatenate(
                [ld_all[s, heads + h : heads + h + 1, :] for s in sources], axis=1
            )
            probs, score_grad = grads_of(
                h, kh_ref[h], vh_ref[h], queries, grads, lse, delta, allowed
            )
            key_part = dot_nt(queries, score_grad)
            value_part = dot_nt(grads, probs)
            dk[h] = key_part if g == 0 else dk[h] + key_part
            dv[h] = value_part if g == 0 else dv[h] + value_part
            dq = dot_nn(kt_ref[h], score_grad)
            for n, d in enumerate(pair):
                piece = dq[:, n * lat_rows : (n + 1) * lat_rows]
                if d:
                    dot_all[place.far(d), h] = piece.astype(BF)
                else:
                    dq_own[h] = dq_own[h] + piece
        for d in pair:
            if d:
                exchange.start(d)
    put_rows(0, med_rows)

    med_tile, lat_tile = med_bufs.shape[-1], lat_bufs.shape[-1]

    def back_rows(first, rows, tile):
        def tile_of(column):
            cols = pl.ds(column, tile)
            values = yall[first : first + rows, :]
            return dot_nt(values[:, 0:inner], wk_ref[cols, :]) + dot_nt(
                values[:, inner:], wv_ref[cols, :]
            )

        return tile_of

    med_sum = TensorSum(med_bufs, t_sems.at[0], back_rows(0, med_rows, med_tile))
    med_sum.give()
    med_sum.cross()

    for d in range(1, nb):
        exchange.wait_recv(d)
    for h in range(heads):
        value = dq_own[h]
        for d in range(1, nb):
            value = value + dq_in[d, h].astype(F32)
        turned(h, value, lat_rows)
    dq_low[...] = turn[:, 0:lat_rows].T.astype(BF)

    own_rows = model // nb
    chunk = 2 * own_rows * max(1, 128 // math.gcd(128, 2 * own_rows))
    per_chunk = chunk // own_rows

    def pair_copy(o):
        return remote(
            part.at[2 * o + 1 - place.inner], pair_in.at[o], y_sems.at[0, o], y_sems.at[1, o],
            {"blk": place.partner},
        )

    def far_copy(o, d):
        return remote(
            part.at[2 * o + place.inner], far_in.at[d], z_sems.at[0, d], z_sems.at[1, d],
            {"blk": 2 * o + place.inner},
        )

    for c in range(model // chunk):
        cols = slice(c * chunk, (c + 1) * chunk)
        lnx = xall[med_rows:, cols]
        query_part = dot_tn(lnx, dq_low[...]) * SCALE
        other_part = dot_tn(xall[:, cols], yall[...])
        for n in range(per_chunk):
            owner = c * per_chunk + n
            rows = slice(n * own_rows, (n + 1) * own_rows)
            part[owner, 0:own_rows, 0:inner] = query_part[rows].astype(BF)
            part[owner, 0:own_rows, inner:] = other_part[rows].astype(BF)
        for o in range(c * per_chunk // 2, (c + 1) * per_chunk // 2):
            pair_copy(o).start()

    def lat_tile_of(column):
        cols = pl.ds(column, lat_tile)
        return (
            back_rows(med_rows, lat_rows, lat_tile)(column)
            + dot_nt(dq_low[...], wq_ref[cols, :]) * SCALE
        )

    lat_sum = TensorSum(lat_bufs, t_sems.at[1], lat_tile_of)
    lat_sum.give()
    lat_sum.cross()

    def own_part(o):
        return part[2 * o + place.inner].astype(F32) + pair_in[o].astype(F32)

    for d in range(1, place.no):
        o = place.outer_to(d)
        pair_copy(o).wait_recv()
        part[2 * o + place.inner] = own_part(o).astype(BF)
        far_copy(o, d).start()
    med_sum.back()

    def put(column, tile):
        xall[0 : tile.shape[0], pl.ds(column, tile.shape[1])] = tile

    med_sum.finish(put)
    gain_rows = [fgain_ref[0:1, :], fgain_ref[1:2, :]]

    def norm_rows(i, carry):
        rows = pl.ds(pl.multiple_of(i * 128, 128), 128)
        xhat, rstd = normalised(med_ref[rows, :].astype(F32))
        q = xall[rows, :].astype(F32)
        mgrad_ref[rows, :] = norm_back(q, mg_ref[...], xhat, rstd)
        return (
            carry[0] + jnp.sum(q * xhat, axis=0, keepdims=True),
            carry[1] + jnp.sum(q, axis=0, keepdims=True),
        )

    zero = jnp.zeros((1, model), F32)
    med_gain = lax.fori_loop(0, med_rows // 128, norm_rows, (zero, zero))
    lat_sum.back()
    lat_sum.finish(put)
    xhat, rstd = normalised(lat_ref[...].astype(F32))
    q = xall[0:lat_rows, :].astype(F32)
    lgrad_ref[...] = mid_grad_ref[...] + norm_back(q, lg_ref[...], xhat, rstd)
    all_rows = [
        *med_gain,
        jnp.sum(q * xhat, axis=0, keepdims=True),
        jnp.sum(q, axis=0, keepdims=True),
        *gain_rows,
    ]
    for o in range(nb):
        for n, row in enumerate(all_rows):
            gain_out[o, n : n + 1, :] = row[:, o * own_rows : (o + 1) * own_rows]

    def gain_copy(d):
        return remote(
            gain_out.at[place.far(d)], gain_in.at[d], n_sems.at[0, d], n_sems.at[1, d],
            {"blk": place.far(d)},
        )

    for d in range(1, nb):
        gain_copy(d).start()
    pair_copy(place.outer).wait_recv()
    total = own_part(place.outer)
    for d in range(1, place.no):
        far_copy(place.outer_to(d), d).wait_recv()
        total = total + far_in[d].astype(F32)
    qg_ref[...] = total[0:own_rows, 0:inner]
    kg_ref[...] = total[0:own_rows, inner : 2 * inner]
    vg_ref[...] = total[0:own_rows, 2 * inner :]
    gains = gain_out[place.me]
    for d in range(1, nb):
        gain_copy(d).wait_recv()
        gains = gains + gain_in[d]
    gains_ref[...] = gains
    exchange.finish_sends()
    for d in range(1, nb):
        gain_copy(d).wait_send()
    for o in range(place.no):
        pair_copy(o).wait_send()
    for d in range(1, place.no):
        far_copy(place.outer_to(d), d).wait_send()


def call(kernel, out_shapes, scratch, collective_id, any_args=(), args=()):
    vmem = pl.BlockSpec(memory_space=pltpu.VMEM)
    return pl.pallas_call(
        kernel,
        out_shape=[jax.ShapeDtypeStruct(s, d) for s, d in out_shapes],
        in_specs=[vmem] * len(args) + [pl.BlockSpec(memory_space=pl.ANY)] * len(any_args),
        out_specs=[vmem] * len(out_shapes),
        scratch_shapes=scratch,
        compiler_params=pltpu.CompilerParams(
            collective_id=collective_id, has_side_effects=True, vmem_limit_bytes=VMEM_LIMIT
        ),
    )(*args, *any_args)


def gelu_pair(pre):
    bell = 0.5 * (1.0 + lax.erf(pre * math.sqrt(0.5)))
    slope = bell + pre * jnp.exp(-0.5 * pre * pre) * (1.0 / math.sqrt(2.0 * math.pi))
    return pre * bell, slope


def per_device(
    latents, media, query_weight, key_weight, value_weight, out_weight, up_weight, down_weight,
    media_gain, media_shift, latent_gain, latent_shift, feed_gain, feed_shift, cotangent, media_image,
):
    nb = lax.axis_size("blk")
    me = lax.axis_index("blk")
    lat_rows, model = latents.shape
    med_rows = media.shape[0]
    inner = query_weight.shape[1]
    heads = inner // HEAD_DIM
    ff_here = up_weight.shape[1]
    no = nb // 2
    own_rows = model // nb
    own_pad = -(-own_rows // 16) * 16
    dma = pltpu.SemaphoreType.DMA
    vm = pltpu.VMEM
    row = lambda v: v.reshape(1, -1)
    image = media_image.reshape(-1, 1)
    hd = HEAD_DIM
    cot_all = lax.all_gather(cotangent, "blk", axis=0, tiled=True)

    (ln, mn, q_all, kh, kt, vh, lkh, lkt, lvh, att, lse) = call(
        functools.partial(attend_kernel, nb),
        [
            ((lat_rows, model), BF), ((med_rows, model), BF), ((nb, heads, hd, lat_rows), BF),
            ((heads, med_rows, hd), BF), ((heads, hd, med_rows), BF), ((heads, med_rows, hd), BF),
            ((heads, lat_rows, hd), BF), ((heads, hd, lat_rows), BF), ((heads, lat_rows, hd), BF),
            ((heads, hd, lat_rows), F32), ((2 * heads, lat_rows), F32),
        ],
        [
            vm((heads, hd, med_rows), BF), vm((heads, hd, lat_rows), BF),
            vm((nb, heads, hd, lat_rows), BF), vm((nb, heads, hd, lat_rows), BF),
            vm((nb, 2 * heads, lat_rows), F32), vm((nb, 2 * heads, lat_rows), F32),
            dma((2, 2, no)), dma((2, nb)), dma((2, nb)),
        ],
        0,
        args=(
            latents, media, query_weight, key_weight, value_weight, row(latent_gain),
            row(latent_shift), row(media_gain), row(media_shift), image,
        ),
    )

    tile = 256
    tiles = model // 2 // tile
    (resampled, mid_grad, branch, dot, ld, fn, low, feed_gains) = call(
        feed_kernel,
        [
            ((lat_rows, model), BF), ((lat_rows, model), F32), ((lat_rows, model), BF),
            ((heads, hd, lat_rows), BF), ((2 * heads, lat_rows), F32), ((lat_rows, model), BF),
            ((lat_rows, inner), BF), ((8, model), F32),
        ],
        [
            vm((model, ff_here), BF), vm((ff_here, model), BF), vm((lat_rows, ff_here), F32),
            vm((lat_rows, model), F32), vm((lat_rows, ff_here), BF), vm((lat_rows, ff_here), BF),
            vm((inner, lat_rows), F32), vm((lat_rows, model), F32),
            vm((3, 6, tiles, lat_rows, tile), BF), dma((3, 3, 2, tiles)), dma((2,)),
        ],
        1,
        any_args=(up_weight, down_weight),
        args=(att, lse, latents, cotangent, out_weight, row(feed_gain), row(feed_shift)),
    )
    fn_all = lax.all_gather(fn, "blk", axis=0, tiled=True)
    low_all = lax.all_gather(low, "blk", axis=0, tiled=True)
    branch_all = lax.all_gather(branch, "blk", axis=0, tiled=True)

    (media_grad, latent_grad, query_grad, key_grad, value_grad, gains) = call(
        functools.partial(back_kernel, nb),
        [
            ((med_rows, model), F32), ((lat_rows, model), F32), ((own_rows, inner), F32),
            ((own_rows, inner), F32), ((own_rows, inner), F32), ((8, own_rows), F32),
        ],
        [
            vm((nb, heads, hd, lat_rows), BF), vm((nb, 2 * heads, lat_rows), F32),
            vm((heads, hd, med_rows), F32), vm((heads, hd, med_rows), F32),
            vm((heads, hd, lat_rows), F32),
            vm((nb, heads, hd, lat_rows), BF),
            vm((inner, med_rows), F32), vm((med_rows + lat_rows, model), BF),
            vm((med_rows + lat_rows, 2 * inner), BF), vm((lat_rows, inner), BF),
            vm((nb, own_pad, 3 * inner), BF), vm((no, own_pad, 3 * inner), BF),
            vm((no, own_pad, 3 * inner), BF),
            vm((nb, 8, own_rows), F32), vm((nb, 8, own_rows), F32),
            vm((6, tiles, med_rows, tile), BF), vm((6, tiles, lat_rows, tile), BF),
            dma((2, 2, no)), dma((2, 2, no)), dma((2, nb)), dma((2, no)), dma((2, no)),
            dma((2, nb)), dma((2, 3, 2, tiles)),
        ],
        2,
        args=(
            q_all, dot, ld, kh, kt, vh, lkh, lkt, lvh, ln, mn, query_weight, key_weight,
            value_weight, mid_grad, latents, media, row(latent_gain), row(media_gain), feed_gains,
            image,
        ),
    )

    def own_columns(rows):
        return lax.dynamic_slice_in_dim(rows, me * own_rows, own_rows, axis=1)

    group = math.gcd(nb, 8)
    group_rows = group * lat_rows

    def feed_step(carry, rows):
        up_acc, down_acc, out_acc = carry
        fn_rows, cot_rows, low_rows, branch_rows = rows
        hidden, slope = gelu_pair(dot_nn(fn_rows, up_weight))
        grad = (dot_nt(cot_rows, down_weight) * slope).astype(BF)
        return (
            up_acc + dot_tn(own_columns(fn_rows), grad),
            down_acc + dot_tn(hidden.astype(BF), own_columns(cot_rows)),
            out_acc + dot_tn(low_rows, own_columns(branch_rows)),
        ), None

    whole = (fn_all, cot_all, low_all, branch_all)
    start = (
        jnp.zeros((own_rows, ff_here), F32),
        jnp.zeros((ff_here, own_rows), F32),
        jnp.zeros((inner, own_rows), F32),
    )
    if group == nb:
        (up_grad, down_grad, out_grad), _ = feed_step(start, whole)
    else:
        (up_grad, down_grad, out_grad), _ = lax.scan(
            feed_step, start, tuple(v.reshape(nb // group, group_rows, -1) for v in whole)
        )
    return (
        resampled, media_grad, latent_grad, query_grad, key_grad, value_grad, out_grad, up_grad,
        down_grad, gains[0], gains[1], gains[2], gains[3], gains[4], gains[5],
    )


def solution(mesh):
    in_specs = (
        P("blk", None), P("blk", None), P(None, "tp"), P(None, "tp"), P(None, "tp"), P("tp", None),
        P(None, "tp"), P("tp", None), P(), P(), P(), P(), P(), P(), P("blk", None), P("blk"),
    )
    out_specs = (
        P("blk", None), P("blk", None), P("blk", None), P("blk", "tp"), P("blk", "tp"),
        P("blk", "tp"), P("tp", "blk"), P("blk", "tp"), P("tp", "blk"), P("blk"), P("blk"),
        P("blk"), P("blk"), P("blk"), P("blk"),
    )
    return jax.shard_map(
        per_device, mesh=mesh, in_specs=in_specs, out_specs=out_specs, check_vma=False
    )
```

```python
import functools
import math

import jax
import jax.numpy as jnp
from jax import lax
from jax.experimental import pallas as pl
from jax.experimental.pallas import tpu as pltpu
from jax.sharding import PartitionSpec as P

HEAD_DIM = 96
LATENTS = 64
NEG_FILL = -1e30
NORM_EPS = 1e-05
BF = jnp.bfloat16
F32 = jnp.float32
MESH = pl.DeviceIdType.MESH
VMEM_LIMIT = 60 * 1024 * 1024
SCALE = 1.0 / math.sqrt(HEAD_DIM)


def dot_nn(a, b):
    return jnp.dot(a, b, preferred_element_type=F32)


def dot_nt(a, b):
    return lax.dot_general(a, b, (((1,), (1,)), ((), ())), preferred_element_type=F32)


def dot_tn(a, b):
    return lax.dot_general(a, b, (((0,), (0,)), ((), ())), preferred_element_type=F32)


def normalised(x):
    centred = x - jnp.mean(x, axis=-1, keepdims=True)
    rstd = lax.rsqrt(jnp.mean(centred * centred, axis=-1, keepdims=True) + NORM_EPS)
    return centred * rstd, rstd


def norm_back(q, gain, xhat, rstd):
    qg = q * gain
    inner = jnp.mean(qg * xhat, axis=-1, keepdims=True)
    return (qg - jnp.mean(qg, axis=-1, keepdims=True) - xhat * inner) * rstd


def greet(devices):
    barrier = pltpu.get_barrier_semaphore()
    for device in devices:
        pl.semaphore_signal(barrier, inc=1, device_id=device, device_id_type=MESH)
    pl.semaphore_wait(barrier, len(devices))


def remote(src, dst, send_sem, recv_sem, device):
    return pltpu.make_async_remote_copy(
        src_ref=src,
        dst_ref=dst,
        send_sem=send_sem,
        recv_sem=recv_sem,
        device_id=device,
        device_id_type=MESH,
    )


class Place:
    def __init__(self, nb):
        self.nb = nb
        self.no = nb // 2
        self.me = lax.axis_index("blk")
        self.outer = self.me // 2
        self.inner = self.me % 2
        self.partner = 2 * self.outer + 1 - self.inner

    def far(self, d):
        return (self.me + d) % self.nb

    def near(self, d):
        return (self.me - d + self.nb) % self.nb

    def outer_to(self, d):
        return (self.outer + d) % self.no

    def outer_from(self, d):
        return (self.outer - d + self.no) % self.no

    def greeting(self):
        return [{"blk": self.far(d)} for d in range(1, self.nb)]


class Gather:
    def __init__(self, place, slots, sems):
        self.place, self.slots, self.sems = place, slots, sems

    def copy_z(self, d):
        pc = self.place
        slot = self.slots.at[pc.me]
        return remote(
            slot, slot, self.sems.at[0, 0, d], self.sems.at[0, 1, d],
            {"blk": 2 * pc.outer_to(d) + pc.inner},
        )

    def copy_y(self, d):
        pc = self.place
        slot = self.slots.at[2 * pc.outer_from(d) + pc.inner]
        return remote(
            slot, slot, self.sems.at[1, 0, d], self.sems.at[1, 1, d], {"blk": pc.partner}
        )

    def start(self):
        for d in range(1, self.place.no):
            self.copy_z(d).start()
        self.copy_y(0).start()

    def relay(self):
        pc = self.place
        for d in range(1, pc.no):
            arrived = self.slots.at[2 * pc.outer_from(d) + pc.inner]
            remote(
                arrived, arrived, self.sems.at[0, 0, d], self.sems.at[0, 1, d], {"blk": pc.partner}
            ).wait_recv()
            self.copy_y(d).start()

    def finish(self):
        pc = self.place
        for d in range(pc.no):
            slot = self.slots.at[2 * pc.outer_from(d) + 1 - pc.inner]
            remote(
                slot, slot, self.sems.at[1, 0, d], self.sems.at[1, 1, d], {"blk": pc.partner}
            ).wait_recv()
        for d in range(1, pc.no):
            self.copy_z(d).wait_send()
        for d in range(pc.no):
            self.copy_y(d).wait_send()


class Exchange:
    def __init__(self, place, out, into, sems, slot=lambda d: d):
        self.place, self.out, self.into, self.sems, self.slot = place, out, into, sems, slot

    def copy(self, d):
        return remote(
            self.out.at[self.slot(d)], self.into.at[d], self.sems.at[0, d], self.sems.at[1, d],
            {"blk": self.place.far(d)},
        )

    def start(self, d):
        self.copy(d).start()

    def wait_recv(self, d):
        self.copy(d).wait_recv()

    def finish_sends(self):
        for d in range(1, self.place.nb):
            self.copy(d).wait_send()


def lane_image(source, images_here, width):
    lane = lax.broadcasted_iota(jnp.int32, (1, width), 1)
    return source * images_here + lane // LATENTS


def attend_kernel(
    nb,
    lat_ref, med_ref, wq_ref, wk_ref, wv_ref, lg_ref, ls_ref, mg_ref, ms_ref, image_ref,
    ln_ref, mn_ref, q_all, kh_ref, kt_ref, vh_ref, lkh_ref, lkt_ref, lvh_ref, att_ref, lse_ref,
    vt, lvt, acc_out, acc_in, stat_out, stat_in, g_sems, a_sems, s_sems,
):
    place = Place(nb)
    lat_rows = lat_ref.shape[0]
    med_rows = med_ref.shape[0]
    heads = kh_ref.shape[0]
    images_here = lat_rows // LATENTS
    greet(place.greeting())

    xhat, _ = normalised(lat_ref[...].astype(F32))
    ln_ref[...] = (xhat * lg_ref[...] + ls_ref[...]).astype(BF)
    ln = ln_ref[...]

    def heads_t(rows, ref):
        turned = rows.T
        for h in range(heads):
            ref[h] = turned[h * HEAD_DIM : (h + 1) * HEAD_DIM].astype(BF)

    def heads_n(rows, ref):
        for h in range(heads):
            ref[h] = rows[:, h * HEAD_DIM : (h + 1) * HEAD_DIM].astype(BF)

    heads_t(dot_nn(ln, wq_ref[...]) * SCALE, q_all.at[place.me])
    gather = Gather(place, q_all, g_sems)
    gather.start()
    lk = dot_nn(ln, wk_ref[...])
    heads_n(lk, lkh_ref)
    heads_t(lk, lkt_ref)
    lv = dot_nn(ln, wv_ref[...])
    heads_n(lv, lvh_ref)
    heads_t(lv, lvt)

    def norm_rows(i, carry):
        rows = pl.ds(pl.multiple_of(i * 128, 128), 128)
        hat, _ = normalised(med_ref[rows, :].astype(F32))
        mn_ref[rows, :] = (hat * mg_ref[...] + ms_ref[...]).astype(BF)
        return carry

    lax.fori_loop(0, med_rows // 128, norm_rows, 0)
    mk = dot_nn(mn_ref[...], wk_ref[...])
    heads_n(mk, kh_ref)
    heads_t(mk, kt_ref)
    gather.relay()
    mv = dot_nn(mn_ref[...], wv_ref[...])
    heads_n(mv, vh_ref)
    heads_t(mv, vt)
    gather.finish()

    exchange = Exchange(place, acc_out, acc_in, a_sems)
    stats = Exchange(place, stat_out, stat_in, s_sems)
    image = image_ref[...]
    order = list(range(1, nb)) + [0]
    for g in range(nb // 2):
        pair = order[2 * g : 2 * g + 2]
        sources = [place.far(d) for d in pair]
        lanes = jnp.concatenate([lane_image(s, images_here, lat_rows) for s in sources], axis=1)
        allowed = image == lanes
        for h in range(heads):
            queries = jnp.concatenate([q_all[s, h] for s in sources], axis=1)
            scores = jnp.where(allowed, dot_nn(kh_ref[h], queries), NEG_FILL)
            top = jnp.max(scores, axis=0, keepdims=True)
            weights = jnp.exp(scores - top)
            total = jnp.sum(weights, axis=0, keepdims=True)
            acc = dot_nn(vt[h], weights.astype(BF)).astype(BF)
            for n, d in enumerate(pair):
                part = slice(n * lat_rows, (n + 1) * lat_rows)
                acc_out[d, h] = acc[:, part]
                stat_out[d, h : h + 1, :] = top[:, part]
                stat_out[d, heads + h : heads + h + 1, :] = total[:, part]
        for d in pair:
            if d:
                exchange.start(d)
                stats.start(d)

    row_image = lax.broadcasted_iota(jnp.int32, (lat_rows, lat_rows), 0) // LATENTS
    col_image = lax.broadcasted_iota(jnp.int32, (lat_rows, lat_rows), 1) // LATENTS
    same = row_image == col_image
    own = []
    for h in range(heads):
        scores = jnp.where(same, dot_nn(lkh_ref[h], q_all[place.me, h]), NEG_FILL)
        top = jnp.max(scores, axis=0, keepdims=True)
        weights = jnp.exp(scores - top)
        total = jnp.sum(weights, axis=0, keepdims=True)
        own.append((top, total, dot_nn(lvt[h], weights.astype(BF))))
    for d in range(1, nb):
        stats.wait_recv(d)
        exchange.wait_recv(d)
    lse_ref[...] = jnp.zeros_like(lse_ref)
    for h in range(heads):
        own_top, own_total, own_acc = own[h]
        tops = [
            (stat_out if d == 0 else stat_in)[d, h : h + 1, :] for d in range(nb)
        ]
        best = functools.reduce(jnp.maximum, tops, own_top)
        factor = jnp.exp(own_top - best)
        total = own_total * factor
        acc = own_acc * factor
        for d in range(nb):
            factor = jnp.exp(tops[d] - best)
            stat = stat_out if d == 0 else stat_in
            piece = acc_out if d == 0 else acc_in
            total = total + stat[d, heads + h : heads + h + 1, :] * factor
            acc = acc + piece[d, h].astype(F32) * factor
        att_ref[h] = acc / total
        lse_ref[h : h + 1, :] = best + jnp.log(total)
    exchange.finish_sends()
    stats.finish_sends()


class TensorSum:
    def __init__(self, bufs, sems, tile_of):
        self.bufs, self.sems, self.tile_of = bufs, sems, tile_of
        self.tiles, self.rows, self.tile = bufs.shape[1:]
        t = lax.axis_index("tp")
        self.core = t % 2
        self.chip = t // 2
        self.sibling = {"tp": 2 * self.chip + 1 - self.core}
        self.across = {"tp": 2 * (1 - self.chip) + self.core}

    @staticmethod
    def greeting():
        t = lax.axis_index("tp")
        core, chip = t % 2, t // 2
        return [{"tp": 2 * chip + 1 - core}, {"tp": 2 * (1 - chip) + core}]

    def column(self, half, j):
        return pl.multiple_of((half * self.tiles + j) * self.tile, 128)

    def copy(self, stage, j):
        return remote(
            self.bufs.at[2 * stage, j], self.bufs.at[2 * stage + 1, j],
            self.sems.at[stage, 0, j], self.sems.at[stage, 1, j],
            self.across if stage == 1 else self.sibling,
        )

    def give(self):
        for j in range(self.tiles):
            self.bufs[0, j] = self.tile_of(self.column(1 - self.core, j)).astype(BF)
            self.copy(0, j).start()

    def cross(self):
        for j in range(self.tiles):
            mine = self.tile_of(self.column(self.core, j))
            self.copy(0, j).wait_recv()
            self.bufs[2, j] = (mine + self.bufs[1, j].astype(F32)).astype(BF)
            self.copy(1, j).start()

    def back(self):
        for j in range(self.tiles):
            self.copy(1, j).wait_recv()
            self.bufs[4, j] = (self.bufs[2, j].astype(F32) + self.bufs[3, j].astype(F32)).astype(BF)
            self.copy(2, j).start()

    def finish(self, put):
        for j in range(self.tiles):
            put(self.column(self.core, j), self.bufs[4, j])
        for j in range(self.tiles):
            self.copy(2, j).wait_recv()
            put(self.column(1 - self.core, j), self.bufs[5, j])
        for stage in range(3):
            for j in range(self.tiles):
                self.copy(stage, j).wait_send()


def feed_kernel(
    att_ref, lse_ref, lat_ref, cot_ref, wo_ref, fg_ref, fs_ref, up_hbm, down_hbm,
    out_ref, mid_grad_ref, branch_ref, dot_ref, ld_ref, fn_ref, low_ref, gain_ref,
    up, down, hg, mid, hidden, pre_grad, low_t, sum_buf, bufs, sems, w_sems,
):
    loads = [
        pltpu.make_async_copy(up_hbm, up, w_sems.at[0]),
        pltpu.make_async_copy(down_hbm, down, w_sems.at[1]),
    ]
    for load in loads:
        load.start()
    heads = att_ref.shape[0]
    ff_here = up.shape[1]
    ff_tile = math.gcd(ff_here, 512)
    greet(TensorSum.greeting())
    for h in range(heads):
        low_t[h * HEAD_DIM : (h + 1) * HEAD_DIM, :] = att_ref[h]
    low_ref[...] = low_t[...].T.astype(BF)
    low = low_ref[...]

    def put(column, tile):
        sum_buf[:, pl.ds(column, tile.shape[1])] = tile.astype(F32)

    def tile_sum(n, tile_of):
        return TensorSum(bufs.at[n], sems.at[n], tile_of)

    width = bufs.shape[-1]
    branch = tile_sum(0, lambda c: dot_nn(low, wo_ref[:, pl.ds(c, width)]))
    branch.give()
    branch.cross()
    loads[1].wait()
    cot = cot_ref[...]

    def back_hidden(i, carry):
        cols = pl.ds(pl.multiple_of(i * ff_tile, ff_tile), ff_tile)
        hg[:, cols] = dot_nt(cot, down[cols, :])
        return carry

    lax.fori_loop(0, ff_here // ff_tile, back_hidden, 0)
    branch.back()
    branch.finish(put)
    mid[...] = lat_ref[...].astype(F32) + sum_buf[...]
    xhat, rstd = normalised(mid[...])
    fn_ref[...] = (xhat * fg_ref[...] + fs_ref[...]).astype(BF)
    fn = fn_ref[...]
    loads[0].wait()

    def inner(i, carry):
        cols = pl.ds(pl.multiple_of(i * ff_tile, ff_tile), ff_tile)
        pre = dot_nn(fn, up[:, cols])
        bell = 0.5 * (1.0 + lax.erf(pre * math.sqrt(0.5)))
        hidden[:, cols] = (pre * bell).astype(BF)
        slope = bell + pre * jnp.exp(-0.5 * pre * pre) * (1.0 / math.sqrt(2.0 * math.pi))
        pre_grad[:, cols] = (hg[:, cols] * slope).astype(BF)
        return carry

    lax.fori_loop(0, ff_here // ff_tile, inner, 0)
    grads = tile_sum(1, lambda c: dot_nt(pre_grad[...], up[pl.ds(c, width), :]))
    feed = tile_sum(2, lambda c: dot_nn(hidden[...], down[:, pl.ds(c, width)]))
    grads.give()
    grads.cross()
    feed.give()
    feed.cross()
    grads.back()
    feed.back()
    grads.finish(put)
    fng = sum_buf[...]
    xhat, rstd = normalised(mid[...])
    mid_grad = cot_ref[...].astype(F32) + norm_back(fng, fg_ref[...], xhat, rstd)
    mid_grad_ref[...] = mid_grad
    branch_ref[...] = mid_grad.astype(BF)
    gain_ref[...] = jnp.zeros_like(gain_ref)
    gain_ref[0:1, :] = jnp.sum(fng * xhat, axis=0, keepdims=True)
    gain_ref[1:2, :] = jnp.sum(fng, axis=0, keepdims=True)
    back = dot_nt(wo_ref[...], branch_ref[...])
    ld_ref[...] = lse_ref[...]
    for h in range(heads):
        piece = back[h * HEAD_DIM : (h + 1) * HEAD_DIM, :].astype(BF)
        dot_ref[h] = piece
        ld_ref[heads + h : heads + h + 1, :] = jnp.sum(
            piece.astype(F32) * att_ref[h], axis=0, keepdims=True
        )
    feed.finish(put)
    out_ref[...] = (mid[...] + sum_buf[...]).astype(BF)


def back_kernel(
    nb,
    q_all, dot_in, ld_in, kh_ref, kt_ref, vh_ref, lkh_ref, lkt_ref, lvh_ref, ln_ref, mn_ref,
    wq_ref, wk_ref, wv_ref, mid_grad_ref, lat_ref, med_ref, lg_ref, mg_ref, fgain_ref, image_ref,
    mgrad_ref, lgrad_ref, qg_ref, kg_ref, vg_ref, gains_ref,
    dot_all, ld_all, dk, dv, dq_own, dq_in, turn, xall, yall, dq_low, part, pair_in, far_in,
    gain_out, gain_in, med_bufs, lat_bufs,
    g_sems, l_sems, x_sems, y_sems, z_sems, n_sems, t_sems,
):
    place = Place(nb)
    lat_rows = lat_ref.shape[0]
    med_rows, model = med_ref.shape
    heads = kh_ref.shape[0]
    inner = heads * HEAD_DIM
    images_here = lat_rows // LATENTS
    dot_all[place.me] = dot_in[...]
    ld_all[place.me] = ld_in[...]
    greet(place.greeting() + TensorSum.greeting())
    gather = Gather(place, dot_all, g_sems)
    gather_ld = Gather(place, ld_all, l_sems)
    gather_ld.start()
    gather.start()

    row_image = lax.broadcasted_iota(jnp.int32, (lat_rows, lat_rows), 0) // LATENTS
    col_image = lax.broadcasted_iota(jnp.int32, (lat_rows, lat_rows), 1) // LATENTS
    same = row_image == col_image

    def turned(h, value, rows):
        turn[h * HEAD_DIM : (h + 1) * HEAD_DIM, 0:rows] = value

    def grads_of(h, keys, values, queries, grads, lse, delta, allowed):
        scores = jnp.where(allowed, dot_nn(keys, queries), NEG_FILL)
        probs = jnp.exp(scores - lse)
        score_grad = (probs * (dot_nn(values, grads) - delta)).astype(BF)
        return probs.astype(BF), score_grad

    for h in range(heads):
        queries, grads = q_all[place.me, h], dot_in[h]
        probs, score_grad = grads_of(
            h, lkh_ref[h], lvh_ref[h], queries, grads,
            ld_in[h : h + 1, :], ld_in[heads + h : heads + h + 1, :], same,
        )
        dk[h, :, 0:lat_rows] = dot_nt(queries, score_grad)
        dv[h, :, 0:lat_rows] = dot_nt(grads, probs)
        dq_own[h] = dot_nn(lkt_ref[h], score_grad)

    def put_rows(first, rows):
        for acc, column in ((dk, 0), (dv, inner)):
            for h in range(heads):
                turned(h, acc[h, :, 0:rows], rows)
            yall[first : first + rows, column : column + inner] = turn[:, 0:rows].T.astype(BF)

    put_rows(med_rows, lat_rows)
    xall[0:med_rows, :] = mn_ref[...]
    xall[med_rows:, :] = ln_ref[...]
    gather_ld.relay()
    gather.relay()
    gather_ld.finish()
    gather.finish()

    exchange = Exchange(place, dot_all, dq_in, x_sems, place.far)
    image = image_ref[...]
    order = list(range(1, nb)) + [0]
    for g in range(nb // 2):
        pair = order[2 * g : 2 * g + 2]
        sources = [place.far(d) for d in pair]
        lanes = jnp.concatenate([lane_image(s, images_here, lat_rows) for s in sources], axis=1)
        allowed = image == lanes
        for h in range(heads):
            queries = jnp.concatenate([q_all[s, h] for s in sources], axis=1)
            grads = jnp.concatenate([dot_all[s, h] for s in sources], axis=1)
            lse = jnp.concatenate([ld_all[s, h : h + 1, :] for s in sources], axis=1)
            delta = jnp.concatenate(
                [ld_all[s, heads + h : heads + h + 1, :] for s in sources], axis=1
            )
            probs, score_grad = grads_of(
                h, kh_ref[h], vh_ref[h], queries, grads, lse, delta, allowed
            )
            key_part = dot_nt(queries, score_grad)
            value_part = dot_nt(grads, probs)
            dk[h] = key_part if g == 0 else dk[h] + key_part
            dv[h] = value_part if g == 0 else dv[h] + value_part
            dq = dot_nn(kt_ref[h], score_grad)
            for n, d in enumerate(pair):
                piece = dq[:, n * lat_rows : (n + 1) * lat_rows]
                if d:
                    dot_all[place.far(d), h] = piece.astype(BF)
                else:
                    dq_own[h] = dq_own[h] + piece
        for d in pair:
            if d:
                exchange.start(d)
    put_rows(0, med_rows)

    med_tile, lat_tile = med_bufs.shape[-1], lat_bufs.shape[-1]

    def back_rows(first, rows, tile):
        def tile_of(column):
            cols = pl.ds(column, tile)
            values = yall[first : first + rows, :]
            return dot_nt(values[:, 0:inner], wk_ref[cols, :]) + dot_nt(
                values[:, inner:], wv_ref[cols, :]
            )

        return tile_of

    med_sum = TensorSum(med_bufs, t_sems.at[0], back_rows(0, med_rows, med_tile))
    med_sum.give()
    med_sum.cross()

    for d in range(1, nb):
        exchange.wait_recv(d)
    for h in range(heads):
        value = dq_own[h]
        for d in range(1, nb):
            value = value + dq_in[d, h].astype(F32)
        turned(h, value, lat_rows)
    dq_low[...] = turn[:, 0:lat_rows].T.astype(BF)

    own_rows = model // nb
    chunk = 2 * own_rows * max(1, 128 // math.gcd(128, 2 * own_rows))
    per_chunk = chunk // own_rows

    def pair_copy(o):
        return remote(
            part.at[2 * o + 1 - place.inner], pair_in.at[o], y_sems.at[0, o], y_sems.at[1, o],
            {"blk": place.partner},
        )

    def far_copy(o, d):
        return remote(
            part.at[2 * o + place.inner], far_in.at[d], z_sems.at[0, d], z_sems.at[1, d],
            {"blk": 2 * o + place.inner},
        )

    for c in range(model // chunk):
        cols = slice(c * chunk, (c + 1) * chunk)
        lnx = xall[med_rows:, cols]
        query_part = dot_tn(lnx, dq_low[...]) * SCALE
        other_part = dot_tn(xall[:, cols], yall[...])
        for n in range(per_chunk):
            owner = c * per_chunk + n
            rows = slice(n * own_rows, (n + 1) * own_rows)
            part[owner, 0:own_rows, 0:inner] = query_part[rows].astype(BF)
            part[owner, 0:own_rows, inner:] = other_part[rows].astype(BF)
        for o in range(c * per_chunk // 2, (c + 1) * per_chunk // 2):
            pair_copy(o).start()

    def lat_tile_of(column):
        cols = pl.ds(column, lat_tile)
        return (
            back_rows(med_rows, lat_rows, lat_tile)(column)
            + dot_nt(dq_low[...], wq_ref[cols, :]) * SCALE
        )

    lat_sum = TensorSum(lat_bufs, t_sems.at[1], lat_tile_of)
    lat_sum.give()
    lat_sum.cross()

    def own_part(o):
        return part[2 * o + place.inner].astype(F32) + pair_in[o].astype(F32)

    for d in range(1, place.no):
        o = place.outer_to(d)
        pair_copy(o).wait_recv()
        part[2 * o + place.inner] = own_part(o).astype(BF)
        far_copy(o, d).start()
    med_sum.back()

    def put(column, tile):
        xall[0 : tile.shape[0], pl.ds(column, tile.shape[1])] = tile

    med_sum.finish(put)
    gain_rows = [fgain_ref[0:1, :], fgain_ref[1:2, :]]

    def norm_rows(i, carry):
        rows = pl.ds(pl.multiple_of(i * 128, 128), 128)
        xhat, rstd = normalised(med_ref[rows, :].astype(F32))
        q = xall[rows, :].astype(F32)
        mgrad_ref[rows, :] = norm_back(q, mg_ref[...], xhat, rstd)
        return (
            carry[0] + jnp.sum(q * xhat, axis=0, keepdims=True),
            carry[1] + jnp.sum(q, axis=0, keepdims=True),
        )

    zero = jnp.zeros((1, model), F32)
    med_gain = lax.fori_loop(0, med_rows // 128, norm_rows, (zero, zero))
    lat_sum.back()
    lat_sum.finish(put)
    xhat, rstd = normalised(lat_ref[...].astype(F32))
    q = xall[0:lat_rows, :].astype(F32)
    lgrad_ref[...] = mid_grad_ref[...] + norm_back(q, lg_ref[...], xhat, rstd)
    all_rows = [
        *med_gain,
        jnp.sum(q * xhat, axis=0, keepdims=True),
        jnp.sum(q, axis=0, keepdims=True),
        *gain_rows,
    ]
    for o in range(nb):
        for n, row in enumerate(all_rows):
            gain_out[o, n : n + 1, :] = row[:, o * own_rows : (o + 1) * own_rows]

    def gain_copy(d):
        return remote(
            gain_out.at[place.far(d)], gain_in.at[d], n_sems.at[0, d], n_sems.at[1, d],
            {"blk": place.far(d)},
        )

    for d in range(1, nb):
        gain_copy(d).start()
    pair_copy(place.outer).wait_recv()
    total = own_part(place.outer)
    for d in range(1, place.no):
        far_copy(place.outer_to(d), d).wait_recv()
        total = total + far_in[d].astype(F32)
    qg_ref[...] = total[0:own_rows, 0:inner]
    kg_ref[...] = total[0:own_rows, inner : 2 * inner]
    vg_ref[...] = total[0:own_rows, 2 * inner :]
    gains = gain_out[place.me]
    for d in range(1, nb):
        gain_copy(d).wait_recv()
        gains = gains + gain_in[d]
    gains_ref[...] = gains
    exchange.finish_sends()
    for d in range(1, nb):
        gain_copy(d).wait_send()
    for o in range(place.no):
        pair_copy(o).wait_send()
    for d in range(1, place.no):
        far_copy(place.outer_to(d), d).wait_send()


def call(kernel, out_shapes, scratch, collective_id, any_args=(), args=()):
    vmem = pl.BlockSpec(memory_space=pltpu.VMEM)
    return pl.pallas_call(
        kernel,
        out_shape=[jax.ShapeDtypeStruct(s, d) for s, d in out_shapes],
        in_specs=[vmem] * len(args) + [pl.BlockSpec(memory_space=pl.ANY)] * len(any_args),
        out_specs=[vmem] * len(out_shapes),
        scratch_shapes=scratch,
        compiler_params=pltpu.CompilerParams(
            collective_id=collective_id, has_side_effects=True, vmem_limit_bytes=VMEM_LIMIT
        ),
    )(*args, *any_args)


def gelu_pair(pre):
    bell = 0.5 * (1.0 + lax.erf(pre * math.sqrt(0.5)))
    slope = bell + pre * jnp.exp(-0.5 * pre * pre) * (1.0 / math.sqrt(2.0 * math.pi))
    return pre * bell, slope


def per_device_many(
    latents, media, query_weight, key_weight, value_weight, out_weight, up_weight, down_weight,
    media_gain, media_shift, latent_gain, latent_shift, feed_gain, feed_shift, cotangent, media_image,
):
    nb = lax.axis_size("blk")
    me = lax.axis_index("blk")
    lat_rows, model = latents.shape
    med_rows = media.shape[0]
    inner = query_weight.shape[1]
    heads = inner // HEAD_DIM
    ff_here = up_weight.shape[1]
    no = nb // 2
    own_rows = model // nb
    own_pad = -(-own_rows // 16) * 16
    dma = pltpu.SemaphoreType.DMA
    vm = pltpu.VMEM
    row = lambda v: v.reshape(1, -1)
    image = media_image.reshape(-1, 1)
    hd = HEAD_DIM
    cot_all = lax.all_gather(cotangent, "blk", axis=0, tiled=True)

    (ln, mn, q_all, kh, kt, vh, lkh, lkt, lvh, att, lse) = call(
        functools.partial(attend_kernel, nb),
        [
            ((lat_rows, model), BF), ((med_rows, model), BF), ((nb, heads, hd, lat_rows), BF),
            ((heads, med_rows, hd), BF), ((heads, hd, med_rows), BF), ((heads, med_rows, hd), BF),
            ((heads, lat_rows, hd), BF), ((heads, hd, lat_rows), BF), ((heads, lat_rows, hd), BF),
            ((heads, hd, lat_rows), F32), ((2 * heads, lat_rows), F32),
        ],
        [
            vm((heads, hd, med_rows), BF), vm((heads, hd, lat_rows), BF),
            vm((nb, heads, hd, lat_rows), BF), vm((nb, heads, hd, lat_rows), BF),
            vm((nb, 2 * heads, lat_rows), F32), vm((nb, 2 * heads, lat_rows), F32),
            dma((2, 2, no)), dma((2, nb)), dma((2, nb)),
        ],
        0,
        args=(
            latents, media, query_weight, key_weight, value_weight, row(latent_gain),
            row(latent_shift), row(media_gain), row(media_shift), image,
        ),
    )

    tile = 256
    tiles = model // 2 // tile
    (resampled, mid_grad, branch, dot, ld, fn, low, feed_gains) = call(
        feed_kernel,
        [
            ((lat_rows, model), BF), ((lat_rows, model), F32), ((lat_rows, model), BF),
            ((heads, hd, lat_rows), BF), ((2 * heads, lat_rows), F32), ((lat_rows, model), BF),
            ((lat_rows, inner), BF), ((8, model), F32),
        ],
        [
            vm((model, ff_here), BF), vm((ff_here, model), BF), vm((lat_rows, ff_here), F32),
            vm((lat_rows, model), F32), vm((lat_rows, ff_here), BF), vm((lat_rows, ff_here), BF),
            vm((inner, lat_rows), F32), vm((lat_rows, model), F32),
            vm((3, 6, tiles, lat_rows, tile), BF), dma((3, 3, 2, tiles)), dma((2,)),
        ],
        1,
        any_args=(up_weight, down_weight),
        args=(att, lse, latents, cotangent, out_weight, row(feed_gain), row(feed_shift)),
    )
    fn_all = lax.all_gather(fn, "blk", axis=0, tiled=True)
    low_all = lax.all_gather(low, "blk", axis=0, tiled=True)
    branch_all = lax.all_gather(branch, "blk", axis=0, tiled=True)

    (media_grad, latent_grad, query_grad, key_grad, value_grad, gains) = call(
        functools.partial(back_kernel, nb),
        [
            ((med_rows, model), F32), ((lat_rows, model), F32), ((own_rows, inner), F32),
            ((own_rows, inner), F32), ((own_rows, inner), F32), ((8, own_rows), F32),
        ],
        [
            vm((nb, heads, hd, lat_rows), BF), vm((nb, 2 * heads, lat_rows), F32),
            vm((heads, hd, med_rows), F32), vm((heads, hd, med_rows), F32),
            vm((heads, hd, lat_rows), F32),
            vm((nb, heads, hd, lat_rows), BF),
            vm((inner, med_rows), F32), vm((med_rows + lat_rows, model), BF),
            vm((med_rows + lat_rows, 2 * inner), BF), vm((lat_rows, inner), BF),
            vm((nb, own_pad, 3 * inner), BF), vm((no, own_pad, 3 * inner), BF),
            vm((no, own_pad, 3 * inner), BF),
            vm((nb, 8, own_rows), F32), vm((nb, 8, own_rows), F32),
            vm((6, tiles, med_rows, tile), BF), vm((6, tiles, lat_rows, tile), BF),
            dma((2, 2, no)), dma((2, 2, no)), dma((2, nb)), dma((2, no)), dma((2, no)),
            dma((2, nb)), dma((2, 3, 2, tiles)),
        ],
        2,
        args=(
            q_all, dot, ld, kh, kt, vh, lkh, lkt, lvh, ln, mn, query_weight, key_weight,
            value_weight, mid_grad, latents, media, row(latent_gain), row(media_gain), feed_gains,
            image,
        ),
    )

    def own_columns(rows):
        return lax.dynamic_slice_in_dim(rows, me * own_rows, own_rows, axis=1)

    group = math.gcd(nb, 8)
    group_rows = group * lat_rows

    def feed_step(carry, rows):
        up_acc, down_acc, out_acc = carry
        fn_rows, cot_rows, low_rows, branch_rows = rows
        hidden, slope = gelu_pair(dot_nn(fn_rows, up_weight))
        grad = (dot_nt(cot_rows, down_weight) * slope).astype(BF)
        return (
            up_acc + dot_tn(own_columns(fn_rows), grad),
            down_acc + dot_tn(hidden.astype(BF), own_columns(cot_rows)),
            out_acc + dot_tn(low_rows, own_columns(branch_rows)),
        ), None

    whole = (fn_all, cot_all, low_all, branch_all)
    start = (
        jnp.zeros((own_rows, ff_here), F32),
        jnp.zeros((ff_here, own_rows), F32),
        jnp.zeros((inner, own_rows), F32),
    )
    if group == nb:
        (up_grad, down_grad, out_grad), _ = feed_step(start, whole)
    else:
        (up_grad, down_grad, out_grad), _ = lax.scan(
            feed_step, start, tuple(v.reshape(nb // group, group_rows, -1) for v in whole)
        )
    return (
        resampled, media_grad, latent_grad, query_grad, key_grad, value_grad, out_grad, up_grad,
        down_grad, gains[0], gains[1], gains[2], gains[3], gains[4], gains[5],
    )


class Spread:
    def __init__(self, place, own, slots, sems, own_sem):
        self.place, self.own, self.slots, self.sems, self.own_sem = place, own, slots, sems, own_sem
        t = lax.axis_index("tp")
        self.t = t
        core, chip = t % 2, t // 2
        self.sibling_t = 2 * chip + 1 - core
        self.across_t = 2 * (1 - chip) + core
        self.diagonal_t = 2 * (1 - chip) + 1 - core
        self.rows = slots.shape[2]

    def source(self, kind, d):
        pc = self.place
        side = pc.inner if kind == 0 else 1 - pc.inner
        return 2 * pc.outer_from(d) + side

    def arrivals(self):
        no = self.place.no
        return [(0, d) for d in range(1, no)] + [(1, d) for d in range(no)]

    def own_rows(self):
        return self.own.at[pl.ds(pl.multiple_of(self.t * self.rows, self.rows), self.rows)]

    def copy_z(self, d):
        pc = self.place
        return remote(
            self.own_rows(), self.slots.at[pc.me, self.t], self.sems.at[0, 0, d], self.sems.at[0, 1, d],
            {"blk": 2 * pc.outer_to(d) + pc.inner},
        )

    def copy_y(self, d):
        pc = self.place
        there = self.slots.at[self.source(0, d), self.t]
        return remote(
            self.own_rows() if d == 0 else there, there, self.sems.at[1, 0, d],
            self.sems.at[1, 1, d], {"blk": pc.partner},
        )

    def copy_x(self, kind, d):
        slot = self.slots.at[self.source(kind, d), self.t]
        n = kind * self.place.no + d
        return remote(slot, slot, self.sems.at[2, 0, n], self.sems.at[2, 1, n], {"tp": self.across_t})

    def copy_c(self, far, kind, d):
        slot = self.slots.at[self.source(kind, d), self.across_t if far else self.t]
        n = far * 2 * self.place.no + kind * self.place.no + d
        return remote(slot, slot, self.sems.at[3, 0, n], self.sems.at[3, 1, n], {"tp": self.sibling_t})

    def arrived(self, stage, n, kind, d, t):
        slot = self.slots.at[self.source(kind, d), t]
        remote(
            slot, slot, self.sems.at[stage, 0, n], self.sems.at[stage, 1, n], {"tp": self.sibling_t}
        ).wait_recv()

    def own_copy(self):
        rows = self.rows
        return [
            pltpu.make_async_copy(
                self.own.at[pl.ds(q * rows, rows)], self.slots.at[self.place.me, q], self.own_sem.at[q]
            )
            for q in range(4)
        ]

    def start(self):
        for d in range(1, self.place.no):
            self.copy_z(d).start()
        self.copy_y(0).start()
        for copy in self.own_copy():
            copy.start()

    def relay_z(self):
        for d in range(1, self.place.no):
            self.arrived(0, d, 0, d, self.t)
            self.copy_y(d).start()
            self.copy_x(0, d).start()
            self.copy_c(0, 0, d).start()

    def relay_y(self):
        for d in range(self.place.no):
            self.arrived(1, d, 1, d, self.t)
            self.copy_x(1, d).start()
            self.copy_c(0, 1, d).start()

    def relay_x(self):
        for kind, d in self.arrivals():
            self.arrived(2, kind * self.place.no + d, kind, d, self.across_t)
            self.copy_c(1, kind, d).start()

    def finish(self):
        no = self.place.no
        for far in range(2):
            for kind, d in self.arrivals():
                self.arrived(
                    3, far * 2 * no + kind * no + d, kind, d, self.diagonal_t if far else self.sibling_t
                )
        for d in range(1, no):
            self.copy_z(d).wait_send()
        for d in range(no):
            self.copy_y(d).wait_send()
        for kind, d in self.arrivals():
            self.copy_x(kind, d).wait_send()
            self.copy_c(0, kind, d).wait_send()
            self.copy_c(1, kind, d).wait_send()
        for copy in self.own_copy():
            copy.wait()


class Halves:
    def __init__(self, place, own, slots, sems):
        self.place, self.own, self.slots, self.sems = place, own, slots, sems
        t = lax.axis_index("tp")
        self.core = t % 2
        self.sibling = {"tp": 2 * (t // 2) + 1 - self.core}

    def source(self, kind, d):
        pc = self.place
        return 2 * pc.outer_from(d) + (pc.inner if kind == 0 else 1 - pc.inner)

    def copy_z(self, d):
        pc = self.place
        return remote(
            self.own.at[self.core], self.slots.at[pc.me, self.core], self.sems.at[0, 0, d],
            self.sems.at[0, 1, d], {"blk": 2 * pc.outer_to(d) + pc.inner},
        )

    def copy_y(self, d):
        pc = self.place
        there = self.slots.at[self.source(0, d), self.core]
        return remote(
            self.own.at[self.core] if d == 0 else there, there, self.sems.at[1, 0, d],
            self.sems.at[1, 1, d], {"blk": pc.partner},
        )

    def copy_c(self, kind, d):
        slot = self.slots.at[self.source(kind, d), self.core]
        n = kind * self.place.no + d
        return remote(slot, slot, self.sems.at[2, 0, n], self.sems.at[2, 1, n], self.sibling)

    def arrived(self, stage, n, kind, d, core):
        slot = self.slots.at[self.source(kind, d), core]
        remote(
            slot, slot, self.sems.at[stage, 0, n], self.sems.at[stage, 1, n], self.sibling
        ).wait_recv()

    def arrivals(self):
        no = self.place.no
        return [(0, d) for d in range(1, no)] + [(1, d) for d in range(no)]

    def start(self):
        for d in range(1, self.place.no):
            self.copy_z(d).start()
        self.copy_y(0).start()

    def relay_z(self):
        for d in range(1, self.place.no):
            self.arrived(0, d, 0, d, self.core)
            self.copy_y(d).start()
            self.copy_c(0, d).start()

    def relay_y(self):
        for d in range(self.place.no):
            self.arrived(1, d, 1, d, self.core)
            self.copy_c(1, d).start()

    def finish(self):
        no = self.place.no
        for kind, d in self.arrivals():
            self.arrived(2, kind * no + d, kind, d, 1 - self.core)
        for d in range(1, no):
            self.copy_z(d).wait_send()
        for d in range(no):
            self.copy_y(d).wait_send()
        for kind, d in self.arrivals():
            self.copy_c(kind, d).wait_send()


class Slices:
    def __init__(self, place, out, into, sems):
        self.place, self.out, self.into, self.sems = place, out, into, sems
        t = lax.axis_index("tp")
        self.core = t % 2
        self.sibling = {"tp": 2 * (t // 2) + 1 - self.core}

    def copy(self, d):
        pc = self.place
        return remote(
            self.out.at[pc.far(d), self.core], self.into.at[pc.me, self.core],
            self.sems.at[0, 0, d], self.sems.at[0, 1, d], {"blk": pc.far(d)},
        )

    def share(self, d):
        slot = self.into.at[self.place.near(d), self.core]
        return remote(slot, slot, self.sems.at[1, 0, d], self.sems.at[1, 1, d], self.sibling)

    def arrived(self, stage, d, core):
        slot = self.into.at[self.place.near(d), core]
        remote(
            slot, slot, self.sems.at[stage, 0, d], self.sems.at[stage, 1, d], self.sibling
        ).wait_recv()

    def start(self):
        for d in range(1, self.place.nb):
            self.copy(d).start()

    def relay(self):
        for d in range(1, self.place.nb):
            self.arrived(0, d, self.core)
            self.share(d).start()

    def finish(self):
        for d in range(1, self.place.nb):
            self.arrived(1, d, 1 - self.core)
        for d in range(1, self.place.nb):
            self.copy(d).wait_send()
            self.share(d).wait_send()

    def cut(self, rows):
        nb, _, half, width = self.out.shape
        for o in range(nb):
            piece = rows[:, o * width : (o + 1) * width]
            self.out[o, 0] = piece[0:half]
            self.out[o, 1] = piece[half:]
        for c in range(2):
            self.into[self.place.me, c] = self.out[self.place.me, c]


class Fold:
    def __init__(self, place, give, got, send, into, sems):
        self.place, self.give, self.got, self.send, self.into = place, give, got, send, into
        self.sems = sems

    def pair(self, o):
        return remote(
            self.give(o), self.got.at[o], self.sems.at[0, 0, o], self.sems.at[0, 1, o],
            {"blk": self.place.partner},
        )

    def far(self, d):
        o = self.place.outer_to(d)
        return remote(
            self.send(o), self.into.at[d], self.sems.at[1, 0, d], self.sems.at[1, 1, d],
            {"blk": 2 * o + self.place.inner},
        )

    def finish(self):
        for o in range(self.place.no):
            self.pair(o).wait_send()
        for d in range(1, self.place.no):
            self.far(d).wait_send()


def image_columns(image_ref, rows, lanes):
    line = image_ref[...].astype(F32).reshape(1, rows)
    return jnp.broadcast_to(line, (lanes, rows)).T


def pair_lanes(place, sources, images_here, lat_rows):
    return jnp.concatenate(
        [lane_image(s, images_here, lat_rows).astype(F32) for s in sources], axis=1
    )


def whole_greeting(place):
    return place.greeting() + TensorSum.greeting()


def near_attend(
    nb,
    lat_ref, image_ref, norm_ref, med_hbm, wq_hbm, wk_hbm, wv_hbm, cot_hbm,
    x_ref, q_all, kh_ref, kt_ref, vh_ref, lkh_ref, lkt_ref, lvh_ref, att_ref, lse_ref, cot_all,
    med, wq, wk, wv, vt, lvt, mine, give, got, send, into, mstat, gstat, rstat, sstat, istat,
    g_sems, a_sems, s_sems, c_sems, o_sems, w_sems,
):
    place = Place(nb)
    lat_rows = lat_ref.shape[0]
    med_rows = med.shape[0]
    heads = kh_ref.shape[0]
    images_here = lat_rows // LATENTS
    loads = {
        name: pltpu.make_async_copy(source, target, w_sems.at[n])
        for n, (name, source, target) in enumerate(
            (("q", wq_hbm, wq), ("k", wk_hbm, wk), ("m", med_hbm, med), ("v", wv_hbm, wv))
        )
    }
    for load in loads.values():
        load.start()
    greet(whole_greeting(place))
    spread = Spread(place, cot_hbm, cot_all, c_sems, o_sems)
    spread.start()

    xhat, _ = normalised(lat_ref[...].astype(F32))
    ln = (xhat * norm_ref[0:1, :] + norm_ref[1:2, :]).astype(BF)
    x_ref[med_rows:, :] = ln

    def heads_t(rows, ref):
        turned = rows.T
        for h in range(heads):
            ref[h] = turned[h * HEAD_DIM : (h + 1) * HEAD_DIM].astype(BF)

    def heads_n(rows, ref):
        for h in range(heads):
            ref[h] = rows[:, h * HEAD_DIM : (h + 1) * HEAD_DIM].astype(BF)

    loads["q"].wait()
    heads_t(dot_nn(ln, wq[...]) * SCALE, q_all.at[place.me])
    gather = Gather(place, q_all, g_sems)
    gather.start()
    loads["k"].wait()
    lk = dot_nn(ln, wk[...])
    heads_n(lk, lkh_ref)
    heads_t(lk, lkt_ref)
    loads["m"].wait()

    def norm_rows(i, carry):
        rows = pl.ds(pl.multiple_of(i * 128, 128), 128)
        hat, _ = normalised(med[rows, :].astype(F32))
        x_ref[rows, :] = (hat * norm_ref[2:3, :] + norm_ref[3:4, :]).astype(BF)
        return carry

    lax.fori_loop(0, med_rows // 128, norm_rows, 0)
    mk = dot_nn(x_ref[0:med_rows, :], wk[...])
    heads_n(mk, kh_ref)
    heads_t(mk, kt_ref)
    gather.relay()
    loads["v"].wait()
    mv = dot_nn(x_ref[0:med_rows, :], wv[...])
    heads_n(mv, vh_ref)
    heads_t(mv, vt)
    lv = dot_nn(ln, wv[...])
    heads_n(lv, lvh_ref)
    heads_t(lv, lvt)
    row_image = lax.broadcasted_iota(jnp.int32, (lat_rows, lat_rows), 0) // LATENTS
    col_image = lax.broadcasted_iota(jnp.int32, (lat_rows, lat_rows), 1) // LATENTS
    same = row_image == col_image
    own = []
    for h in range(heads):
        scores = jnp.where(same, dot_nn(lkh_ref[h], q_all[place.me, h]), NEG_FILL)
        top = jnp.max(scores, axis=0, keepdims=True)
        weights = jnp.exp(scores - top)
        total = jnp.sum(weights, axis=0, keepdims=True)
        own.append((top, total, dot_nn(lvt[h], weights.astype(BF))))
    spread.relay_z()
    gather.finish()

    fold = Fold(place, lambda o: give.at[o], got, lambda o: send.at[o], into, a_sems)
    stats = Fold(place, lambda o: gstat.at[o], rstat, lambda o: sstat.at[o], istat, s_sems)
    image = image_columns(image_ref, med_rows, lat_rows)
    image = jnp.concatenate([image, image], axis=1)

    def piece(acc_ref, stat_ref, at):
        return [
            (
                stat_ref[at, h : h + 1, :],
                stat_ref[at, heads + h : heads + h + 1, :],
                acc_ref[at, h].astype(F32),
            )
            for h in range(heads)
        ]

    def merged(left, right):
        both = []
        for (lt, ll, la), (rt, rl, ra) in zip(left, right):
            top = jnp.maximum(lt, rt)
            lf, rf = jnp.exp(lt - top), jnp.exp(rt - top)
            both.append((top, ll * lf + rl * rf, la * lf + ra * rf))
        return both

    def pass_on(d):
        o = place.outer_to(d)
        stats.pair(o).wait_recv()
        fold.pair(o).wait_recv()
        both = merged(piece(mine, mstat, o), piece(got, rstat, o))
        if d == 0:
            return both
        for h, (top, total, acc) in enumerate(both):
            sstat[o, h : h + 1, :] = top
            sstat[o, heads + h : heads + h + 1, :] = total
            send[o, h] = acc.astype(BF)
        stats.far(d).start()
        fold.far(d).start()
        return None

    order = [*range(1, place.no), 0]
    for step, d in enumerate(order):
        o = place.outer_to(d)
        sources = [2 * o + place.inner, 2 * o + 1 - place.inner]
        allowed = image == pair_lanes(place, sources, images_here, lat_rows)
        for h in range(heads):
            queries = jnp.concatenate([q_all[s, h] for s in sources], axis=1)
            scores = jnp.where(allowed, dot_nn(kh_ref[h], queries), NEG_FILL)
            top = jnp.max(scores, axis=0, keepdims=True)
            weights = jnp.exp(scores - top)
            total = jnp.sum(weights, axis=0, keepdims=True)
            acc = dot_nn(vt[h], weights.astype(BF))
            mine[o, h] = acc[:, 0:lat_rows]
            give[o, h] = acc[:, lat_rows:].astype(BF)
            for ref, part in ((mstat, slice(0, lat_rows)), (gstat, slice(lat_rows, 2 * lat_rows))):
                ref[o, h : h + 1, :] = top[:, part]
                ref[o, heads + h : heads + h + 1, :] = total[:, part]
        stats.pair(o).start()
        fold.pair(o).start()
        if step:
            pass_on(order[step - 1])
    spread.relay_y()
    result = merged(own, pass_on(0))
    spread.relay_x()
    for d in range(1, place.no):
        stats.far(d).wait_recv()
        fold.far(d).wait_recv()
        result = merged(result, piece(into, istat, d))
    lse_ref[...] = jnp.zeros_like(lse_ref)
    for h, (top, total, acc) in enumerate(result):
        att_ref[h] = acc / total
        lse_ref[h : h + 1, :] = top + jnp.log(total)
    fold.finish()
    stats.finish()
    spread.finish()


def near_feed(
    nb,
    att_ref, lse_ref, lat_ref, cot_ref, wo_ref, norm_ref, x_hbm, up_hbm, down_hbm,
    out_ref, mid_grad_ref, branch_ref, dot_ref, ld_ref, low_all, lns_ref, gain_ref, fn_all,
    up, down, hg, mid, fn, hidden, pre_grad, low_t, sum_buf, bufs, ln, ln_out,
    sems, w_sems, l_sems, f_sems, n_sems, o_sem,
):
    place = Place(nb)
    med_rows = x_hbm.shape[0] - lat_ref.shape[0]
    lat_rows = lat_ref.shape[0]
    half = lat_rows // 2
    loads = [
        pltpu.make_async_copy(x_hbm.at[pl.ds(med_rows, lat_rows)], ln, w_sems.at[0]),
        pltpu.make_async_copy(down_hbm, down, w_sems.at[1]),
        pltpu.make_async_copy(up_hbm, up, w_sems.at[2]),
    ]
    for load in loads:
        load.start()
    heads = att_ref.shape[0]
    ff_here = up.shape[1]
    ff_tile = math.gcd(ff_here, 512)
    greet(whole_greeting(place))
    for h in range(heads):
        low_t[h * HEAD_DIM : (h + 1) * HEAD_DIM, :] = att_ref[h]
    low_all[place.me] = low_t[...].T.astype(BF)
    low_gather = Gather(place, low_all, l_sems)
    low_gather.start()
    low = low_all[place.me]

    def put(column, tile):
        sum_buf[:, pl.ds(column, tile.shape[1])] = tile.astype(F32)

    def tile_sum(n, tile_of):
        return TensorSum(bufs.at[n], sems.at[n], tile_of)

    width = bufs.shape[-1]
    branch = tile_sum(0, lambda c: dot_nn(low, wo_ref[:, pl.ds(c, width)]))
    branch.give()
    branch.cross()
    loads[0].wait()
    slices = Slices(place, ln_out, lns_ref, n_sems)
    slices.cut(ln[...])
    slices.start()
    loads[1].wait()
    cot = cot_ref[...]

    def back_hidden(i, carry):
        cols = pl.ds(pl.multiple_of(i * ff_tile, ff_tile), ff_tile)
        hg[:, cols] = dot_nt(cot, down[cols, :])
        return carry

    branch.back()
    lax.fori_loop(0, ff_here // ff_tile, back_hidden, 0)
    branch.finish(put)
    low_gather.relay()
    mid[...] = lat_ref[...].astype(F32) + sum_buf[...]
    xhat, rstd = normalised(mid[...])
    normed = (xhat * norm_ref[4:5, :] + norm_ref[5:6, :]).astype(BF)
    fn[0] = normed[0:half]
    fn[1] = normed[half:]
    spread = Halves(place, fn, fn_all, f_sems)
    spread.start()
    keep = pltpu.make_async_copy(fn, fn_all.at[place.me], o_sem)
    keep.start()
    loads[2].wait()

    def inner(i, carry):
        cols = pl.ds(pl.multiple_of(i * ff_tile, ff_tile), ff_tile)
        pre = dot_nn(normed, up[:, cols])
        value, slope = gelu_pair(pre)
        hidden[:, cols] = value.astype(BF)
        pre_grad[:, cols] = (hg[:, cols] * slope).astype(BF)
        return carry

    lax.fori_loop(0, ff_here // ff_tile, inner, 0)
    grads = tile_sum(1, lambda c: dot_nt(pre_grad[...], up[pl.ds(c, width), :]))
    feed = tile_sum(2, lambda c: dot_nn(hidden[...], down[:, pl.ds(c, width)]))
    grads.give()
    grads.cross()
    feed.give()
    slices.relay()
    grads.back()
    spread.relay_z()
    feed.cross()
    grads.finish(put)
    fng = sum_buf[...]
    xhat, rstd = normalised(mid[...])
    mid_grad = cot_ref[...].astype(F32) + norm_back(fng, norm_ref[4:5, :], xhat, rstd)
    mid_grad_ref[...] = mid_grad
    branch_ref[...] = mid_grad.astype(BF)
    gain_ref[...] = jnp.zeros_like(gain_ref)
    gain_ref[0:1, :] = jnp.sum(fng * xhat, axis=0, keepdims=True)
    gain_ref[1:2, :] = jnp.sum(fng, axis=0, keepdims=True)
    back = dot_nt(wo_ref[...], branch_ref[...])
    ld_ref[...] = lse_ref[...]
    for h in range(heads):
        piece = back[h * HEAD_DIM : (h + 1) * HEAD_DIM, :].astype(BF)
        dot_ref[h] = piece
        ld_ref[heads + h : heads + h + 1, :] = jnp.sum(
            piece.astype(F32) * att_ref[h], axis=0, keepdims=True
        )
    feed.back()
    feed.finish(put)
    out_ref[...] = (mid[...] + sum_buf[...]).astype(BF)
    low_gather.finish()
    slices.finish()
    spread.relay_y()
    spread.finish()
    keep.wait()


def near_back(
    nb,
    q_all, dot_in, ld_in, kh_ref, kt_ref, vh_ref, lkh_ref, lkt_ref, lvh_ref, x_ref, low_all,
    lns_ref, branch_ref, mid_grad_ref, lat_ref, med_ref, norm_ref, fgain_ref, image_ref,
    wq_hbm, wk_hbm, wv_hbm, up_hbm, down_hbm, fn_all, cot_all,
    mgrad_ref, lgrad_ref, qg_ref, kg_ref, vg_ref, og_ref, ug_ref, dg_ref, gains_ref,
    wq, wk, wv, up, down, rows_buf, down_t, dot_all, ld_all, dk, dv, dq_own, dq_mine, dq_give, dq_got,
    dq_send, dq_into, dq_all, turn, yall, part, pair_in, far_in, msum, br_out, br_in, gain_out, gain_in,
    med_bufs, lat_bufs,
    g_sems, l_sems, x_sems, p_sems, q_sems, n_sems, t_sems, b_sems, w_sems, r_sems,
):
    place = Place(nb)
    lat_rows = lat_ref.shape[0]
    med_rows, model = med_ref.shape
    heads = kh_ref.shape[0]
    half_heads = heads // 2
    inner = heads * HEAD_DIM
    images_here = lat_rows // LATENTS
    own_rows = model // nb
    weights = [
        pltpu.make_async_copy(source, target, w_sems.at[n])
        for n, (source, target) in enumerate(
            ((up_hbm, up), (down_hbm, down), (wk_hbm, wk), (wv_hbm, wv), (wq_hbm, wq))
        )
    ]
    dot_all[place.me] = dot_in[...]
    ld_all[place.me] = ld_in[...]
    greet(whole_greeting(place))
    gather = Gather(place, dot_all, g_sems)
    gather_ld = Gather(place, ld_all, l_sems)
    gather_ld.start()
    gather.start()

    def row_loads(j, slot):
        return [
            pltpu.make_async_copy(
                source.at[2 * j + n], rows_buf.at[slot, k, n], r_sems.at[slot, k, n]
            )
            for k, source in enumerate((fn_all, cot_all))
            for n in range(2)
        ]

    def start_rows(j, slot):
        for load in row_loads(j, slot):
            load.start()

    start_rows(0, 0)
    for load in weights:
        load.start()

    row_image = lax.broadcasted_iota(jnp.int32, (lat_rows, lat_rows), 0) // LATENTS
    col_image = lax.broadcasted_iota(jnp.int32, (lat_rows, lat_rows), 1) // LATENTS
    same = row_image == col_image

    def grads_of(keys, values, queries, grads, lse, delta, allowed):
        scores = jnp.where(allowed, dot_nn(keys, queries), NEG_FILL)
        probs = jnp.exp(scores - lse)
        score_grad = (probs * (dot_nn(values, grads) - delta)).astype(BF)
        return probs.astype(BF), score_grad

    for h in range(heads):
        queries, grads = q_all[place.me, h], dot_in[h]
        probs, score_grad = grads_of(
            lkh_ref[h], lvh_ref[h], queries, grads,
            ld_in[h : h + 1, :], ld_in[heads + h : heads + h + 1, :], same,
        )
        dk[h, :, 0:lat_rows] = dot_nt(queries, score_grad)
        dv[h, :, 0:lat_rows] = dot_nt(grads, probs)
        dq_own[h] = dot_nn(lkt_ref[h], score_grad)

    def put_rows(half, first, rows):
        for k, acc in enumerate((dk, dv)):
            for n in range(half_heads):
                at = (k * half_heads + n) * HEAD_DIM
                turn[at : at + HEAD_DIM, 0:rows] = acc[half * half_heads + n, :, 0:rows]
        yall[half, first : first + rows, :] = turn[:, 0:rows].T.astype(BF)

    for half in range(2):
        put_rows(half, med_rows, lat_rows)
    slices = Slices(place, br_out, br_in, b_sems)
    slices.cut(branch_ref[...])
    slices.start()

    pick = (
        lax.broadcasted_iota(jnp.int32, (own_rows, model), 1)
        == lax.broadcasted_iota(jnp.int32, (own_rows, model), 0) + place.me * own_rows
    )
    pick = jnp.where(pick, 1.0, 0.0).astype(BF)
    ff_here = up.shape[1]
    ff_tile = math.gcd(ff_here, 512)

    def feed_step(j, first=False, last=False):
        slot = j % 2
        for load in row_loads(j, slot):
            load.wait()
        if not last:
            start_rows(j + 1, 1 - slot)
        fn_rows = rows_buf[slot, 0].reshape(2 * lat_rows, model)
        cot_rows = rows_buf[slot, 1].reshape(2 * lat_rows, model)
        fn_own = dot_nt(pick, fn_rows).astype(BF)
        cot_own = dot_nt(pick, cot_rows).astype(BF)

        def tile(i, carry):
            cols = pl.ds(pl.multiple_of(i * ff_tile, ff_tile), ff_tile)
            value, slope = gelu_pair(dot_nn(fn_rows, up[:, cols]))
            grad = (dot_nt(cot_rows, down[cols, :]) * slope).astype(BF)
            up_part = dot_nn(fn_own, grad)
            down_part = dot_nn(cot_own, value.astype(BF))
            if first:
                ug_ref[:, cols] = up_part
                down_t[:, cols] = down_part
            else:
                ug_ref[:, cols] += up_part
                down_t[:, cols] += down_part
            return carry

        lax.fori_loop(0, ff_here // ff_tile, tile, 0)

    steps = place.no
    done = 0
    for load in weights[:2]:
        load.wait()
    feed_step(0, first=True, last=steps == 1)
    gather_ld.relay()
    gather.relay()
    done = 1
    if steps > 2:
        feed_step(1)
        done = 2
    gather_ld.finish()
    gather.finish()

    dq_fold = Fold(place, lambda o: dq_give.at[o], dq_got, lambda o: dq_send.at[o], dq_into, x_sems)
    folds = [
        Fold(
            place, lambda o, f=f: part.at[f, 2 * o + 1 - place.inner], pair_in.at[f],
            lambda o, f=f: part.at[f, 2 * o + place.inner], far_in.at[f], p_sems.at[f],
        )
        for f in range(2)
    ]
    image = image_columns(image_ref, med_rows, lat_rows)
    image = jnp.concatenate([image, image], axis=1)
    order = [*range(1, place.no), 0]

    def attend(half):
        for step, d in enumerate(order):
            o = place.outer_to(d)
            sources = [2 * o + place.inner, 2 * o + 1 - place.inner]
            allowed = image == pair_lanes(place, sources, images_here, lat_rows)
            for h in range(half * half_heads, (half + 1) * half_heads):
                queries = jnp.concatenate([q_all[s, h] for s in sources], axis=1)
                grads = jnp.concatenate([dot_all[s, h] for s in sources], axis=1)
                lse = jnp.concatenate([ld_all[s, h : h + 1, :] for s in sources], axis=1)
                delta = jnp.concatenate(
                    [ld_all[s, heads + h : heads + h + 1, :] for s in sources], axis=1
                )
                probs, score_grad = grads_of(
                    kh_ref[h], vh_ref[h], queries, grads, lse, delta, allowed
                )
                key_part = dot_nt(queries, score_grad)
                value_part = dot_nt(grads, probs)
                dk[h] = key_part if step == 0 else dk[h] + key_part
                dv[h] = value_part if step == 0 else dv[h] + value_part
                dq = dot_nn(kt_ref[h], score_grad)
                dq_mine[o, h] = dq[:, 0:lat_rows]
                dq_give[o, h] = dq[:, lat_rows:].astype(BF)
            if half:
                dq_fold.pair(o).start()

    chunk = 2 * own_rows * max(1, 128 // math.gcd(128, 2 * own_rows))
    per_chunk = chunk // own_rows

    def weight_parts(half):
        put_rows(half, 0, med_rows)
        for c in range(model // chunk):
            value = dot_tn(x_ref[:, c * chunk : (c + 1) * chunk], yall[half])
            for n in range(per_chunk):
                part[half, c * per_chunk + n] = value[n * own_rows : (n + 1) * own_rows].astype(BF)
            for o in range(c * per_chunk // 2, (c + 1) * per_chunk // 2):
                folds[half].pair(o).start()

    def both(half, o):
        return part[half, 2 * o + place.inner].astype(F32) + pair_in[half, o].astype(F32)

    def pass_on(half):
        for d in range(1, place.no):
            o = place.outer_to(d)
            folds[half].pair(o).wait_recv()
            part[half, 2 * o + place.inner] = both(half, o).astype(BF)
            folds[half].far(d).start()

    attend(0)
    weight_parts(0)
    attend(1)
    for load in weights[2:]:
        load.wait()
    weight_parts(1)

    med_tile, lat_tile = med_bufs.shape[-1], lat_bufs.shape[-1]
    width = half_heads * HEAD_DIM

    def back_rows(first, rows, tile):
        def tile_of(column):
            cols = pl.ds(column, tile)
            total = None
            for half in range(2):
                values = yall[half, first : first + rows, :]
                for k, weight in enumerate((wk, wv)):
                    term = dot_nt(
                        values[:, k * width : (k + 1) * width],
                        weight[cols, half * width : (half + 1) * width],
                    )
                    total = term if total is None else total + term
            return total

        return tile_of

    med_sum = TensorSum(med_bufs, t_sems.at[0], back_rows(0, med_rows, med_tile))
    med_sum.give()
    for d in range(1, place.no):
        o = place.outer_to(d)
        dq_fold.pair(o).wait_recv()
        for h in range(heads):
            dq_send[o, h] = (dq_mine[o, h] + dq_got[o, h].astype(F32)).astype(BF)
        dq_fold.far(d).start()
    med_sum.cross()
    pass_on(0)
    o = place.outer
    dq_fold.pair(o).wait_recv()
    for h in range(heads):
        dq_own[h] = dq_own[h] + dq_mine[o, h] + dq_got[o, h].astype(F32)
    for d in range(1, place.no):
        dq_fold.far(d).wait_recv()
        for h in range(heads):
            dq_own[h] = dq_own[h] + dq_into[d, h].astype(F32)
    for h in range(heads):
        turn[h * HEAD_DIM : (h + 1) * HEAD_DIM, 0:lat_rows] = dq_own[h]
    dq_all[place.me] = turn[:, 0:lat_rows].T.astype(BF)
    dq_gather = Gather(place, dq_all, q_sems)
    dq_gather.start()

    def lat_tile_of(column):
        cols = pl.ds(column, lat_tile)
        return (
            back_rows(med_rows, lat_rows, lat_tile)(column)
            + dot_nt(dq_all[place.me], wq[cols, :]) * SCALE
        )

    lat_sum = TensorSum(lat_bufs, t_sems.at[1], lat_tile_of)
    lat_sum.give()
    pass_on(1)
    slices.relay()
    if steps - 1 > done:
        lax.fori_loop(done, steps - 1, lambda j, c: (feed_step(j), c)[1], 0)
        done = steps - 1
    lat_sum.cross()
    med_sum.back()
    dq_gather.relay()
    if done < steps:
        feed_step(steps - 1, last=True)
    dg_ref[...] = down_t[...].T

    def put(column, tile):
        msum[0 : tile.shape[0], pl.ds(column, tile.shape[1])] = tile

    lat_sum.back()
    med_sum.finish(put)

    def norm_rows(i, carry):
        rows = pl.ds(pl.multiple_of(i * 128, 128), 128)
        xhat, rstd = normalised(med_ref[rows, :].astype(F32))
        q = msum[rows, :].astype(F32)
        mgrad_ref[rows, :] = norm_back(q, norm_ref[2:3, :], xhat, rstd)
        return (
            carry[0] + jnp.sum(q * xhat, axis=0, keepdims=True),
            carry[1] + jnp.sum(q, axis=0, keepdims=True),
        )

    zero = jnp.zeros((1, model), F32)
    med_gain = lax.fori_loop(0, med_rows // 128, norm_rows, (zero, zero))
    lat_sum.finish(put)
    xhat, rstd = normalised(lat_ref[...].astype(F32))
    q = msum[0:lat_rows, :].astype(F32)
    lgrad_ref[...] = mid_grad_ref[...] + norm_back(q, norm_ref[0:1, :], xhat, rstd)
    all_rows = [
        *med_gain,
        jnp.sum(q * xhat, axis=0, keepdims=True),
        jnp.sum(q, axis=0, keepdims=True),
        fgain_ref[0:1, :],
        fgain_ref[1:2, :],
    ]
    for o in range(nb):
        for n, line in enumerate(all_rows):
            gain_out[o, n : n + 1, :] = line[:, o * own_rows : (o + 1) * own_rows]

    def gain_copy(d):
        return remote(
            gain_out.at[place.far(d)], gain_in.at[d], n_sems.at[0, d], n_sems.at[1, d],
            {"blk": place.far(d)},
        )

    for d in range(1, nb):
        gain_copy(d).start()
    slices.finish()
    dq_gather.finish()
    all_rows_of = lambda ref: ref[...].reshape(nb * lat_rows, -1)
    og_ref[...] = dot_tn(all_rows_of(low_all), all_rows_of(br_in))
    qg_ref[...] = dot_tn(all_rows_of(lns_ref), all_rows_of(dq_all)) * SCALE
    for half in range(2):
        folds[half].pair(place.outer).wait_recv()
        total = both(half, place.outer)
        for d in range(1, place.no):
            folds[half].far(d).wait_recv()
            total = total + far_in[half, d].astype(F32)
        for n in range(half_heads):
            at = (half * half_heads + n) * HEAD_DIM
            kg_ref[:, at : at + HEAD_DIM] = total[:, n * HEAD_DIM : (n + 1) * HEAD_DIM]
            vg_ref[:, at : at + HEAD_DIM] = total[:, width + n * HEAD_DIM : width + (n + 1) * HEAD_DIM]
    gains = gain_out[place.me]
    for d in range(1, nb):
        gain_copy(d).wait_recv()
        gains = gains + gain_in[d]
    gains_ref[...] = gains
    for d in range(1, nb):
        gain_copy(d).wait_send()
    dq_fold.finish()
    for fold in folds:
        fold.finish()


def near_call(kernel, out_shapes, scratch, collective_id, args, any_args, any_outs=()):
    vmem = pl.BlockSpec(memory_space=pltpu.VMEM)
    anywhere = pl.BlockSpec(memory_space=pl.ANY)
    return pl.pallas_call(
        kernel,
        out_shape=[jax.ShapeDtypeStruct(s, d) for s, d in (*out_shapes, *any_outs)],
        in_specs=[vmem] * len(args) + [anywhere] * len(any_args),
        out_specs=[vmem] * len(out_shapes) + [anywhere] * len(any_outs),
        scratch_shapes=scratch,
        compiler_params=pltpu.CompilerParams(
            collective_id=collective_id, has_side_effects=True, vmem_limit_bytes=VMEM_LIMIT
        ),
    )(*args, *any_args)


def per_device(
    latents, media, query_weight, key_weight, value_weight, out_weight, up_weight, down_weight,
    media_gain, media_shift, latent_gain, latent_shift, feed_gain, feed_shift, cotangent, media_image,
):
    nb = lax.axis_size("blk")
    lat_rows, model = latents.shape
    med_rows = media.shape[0]
    inner = query_weight.shape[1]
    heads = inner // HEAD_DIM
    ff_here = up_weight.shape[1]
    no = nb // 2
    own_rows = model // nb
    dma = pltpu.SemaphoreType.DMA
    vm = pltpu.VMEM
    hd = HEAD_DIM
    half, quarter = lat_rows // 2, lat_rows // 4
    norms = jnp.stack([latent_gain, latent_shift, media_gain, media_shift, feed_gain, feed_shift])

    (x, q_all, kh, kt, vh, lkh, lkt, lvh, att, lse, cot_all) = near_call(
        functools.partial(near_attend, nb),
        [
            ((med_rows + lat_rows, model), BF), ((nb, heads, hd, lat_rows), BF),
            ((heads, med_rows, hd), BF), ((heads, hd, med_rows), BF), ((heads, med_rows, hd), BF),
            ((heads, lat_rows, hd), BF), ((heads, hd, lat_rows), BF), ((heads, lat_rows, hd), BF),
            ((heads, hd, lat_rows), F32), ((2 * heads, lat_rows), F32),
        ],
        [
            vm((med_rows, model), BF), vm((model, inner), BF), vm((model, inner), BF),
            vm((model, inner), BF), vm((heads, hd, med_rows), BF), vm((heads, hd, lat_rows), BF),
            vm((no, heads, hd, lat_rows), F32), *[vm((no, heads, hd, lat_rows), BF)] * 4,
            *[vm((no, 2 * heads, lat_rows), F32)] * 5,
            dma((2, 2, no)), dma((2, 2, no)), dma((2, 2, no)), dma((4, 2, 4 * no)), dma((4,)), dma((4,)),
        ],
        0,
        (latents, media_image, norms),
        (media, query_weight, key_weight, value_weight, cotangent),
        [((nb, 4, quarter, model), BF)],
    )

    tile = 256
    tiles = model // 2 // tile
    (resampled, mid_grad, branch, dot, ld, low_all, lns, feed_gains, fn_all) = near_call(
        functools.partial(near_feed, nb),
        [
            ((lat_rows, model), BF), ((lat_rows, model), F32), ((lat_rows, model), BF),
            ((heads, hd, lat_rows), BF), ((2 * heads, lat_rows), F32), ((nb, lat_rows, inner), BF),
            ((nb, 2, half, own_rows), BF), ((8, model), F32),
        ],
        [
            vm((model, ff_here), BF), vm((ff_here, model), BF), vm((lat_rows, ff_here), F32),
            vm((lat_rows, model), F32), vm((2, half, model), BF), vm((lat_rows, ff_here), BF),
            vm((lat_rows, ff_here), BF), vm((inner, lat_rows), F32), vm((lat_rows, model), F32),
            vm((3, 6, tiles, lat_rows, tile), BF), vm((lat_rows, model), BF),
            vm((nb, 2, half, own_rows), BF),
            dma((3, 3, 2, tiles)), dma((3,)), dma((2, 2, no)), dma((3, 2, 2 * no)), dma((2, 2, nb)), dma,
        ],
        1,
        (att, lse, latents, cotangent, out_weight, norms),
        (x, up_weight, down_weight),
        [((nb, 2, half, model), BF)],
    )

    (media_grad, latent_grad, query_grad, key_grad, value_grad, out_grad, up_grad, down_grad, gains) = near_call(
        functools.partial(near_back, nb),
        [
            ((med_rows, model), F32), ((lat_rows, model), F32), ((own_rows, inner), F32),
            ((own_rows, inner), F32), ((own_rows, inner), F32), ((inner, own_rows), F32),
            ((own_rows, ff_here), F32), ((ff_here, own_rows), F32), ((8, own_rows), F32),
        ],
        [
            vm((model, inner), BF), vm((model, inner), BF), vm((model, inner), BF),
            vm((model, ff_here), BF), vm((ff_here, model), BF), vm((2, 2, 2, lat_rows, model), BF),
            vm((own_rows, ff_here), F32), vm((nb, heads, hd, lat_rows), BF),
            vm((nb, 2 * heads, lat_rows), F32), vm((heads, hd, med_rows), F32),
            vm((heads, hd, med_rows), F32), vm((heads, hd, lat_rows), F32),
            vm((no, heads, hd, lat_rows), F32), *[vm((no, heads, hd, lat_rows), BF)] * 4,
            vm((nb, lat_rows, inner), BF), vm((inner, med_rows), F32),
            vm((2, med_rows + lat_rows, inner), BF), vm((2, nb, own_rows, inner), BF),
            vm((2, no, own_rows, inner), BF), vm((2, no, own_rows, inner), BF),
            vm((med_rows, model), BF), vm((nb, 2, half, own_rows), BF), vm((nb, 2, half, own_rows), BF),
            vm((nb, 8, own_rows), F32), vm((nb, 8, own_rows), F32),
            vm((6, tiles, med_rows, tile), BF), vm((6, tiles, lat_rows, tile), BF),
            dma((2, 2, no)), dma((2, 2, no)), dma((2, 2, no)), dma((2, 2, 2, no)), dma((2, 2, no)),
            dma((2, nb)), dma((2, 3, 2, tiles)), dma((2, 2, nb)), dma((5,)), dma((2, 2, 2)),
        ],
        2,
        (
            q_all, dot, ld, kh, kt, vh, lkh, lkt, lvh, x, low_all, lns, branch, mid_grad, latents,
            media, norms, feed_gains, media_image,
        ),
        (
            query_weight, key_weight, value_weight, up_weight, down_weight,
            fn_all.reshape(nb, lat_rows, model), cot_all.reshape(nb, lat_rows, model),
        ),
    )
    return (
        resampled, media_grad, latent_grad, query_grad, key_grad, value_grad, out_grad, up_grad,
        down_grad, gains[0], gains[1], gains[2], gains[3], gains[4], gains[5],
    )


def solution(mesh):
    in_specs = (
        P("blk", None), P("blk", None), P(None, "tp"), P(None, "tp"), P(None, "tp"), P("tp", None),
        P(None, "tp"), P("tp", None), P(), P(), P(), P(), P(), P(), P("blk", None), P("blk"),
    )
    out_specs = (
        P("blk", None), P("blk", None), P("blk", None), P("blk", "tp"), P("blk", "tp"),
        P("blk", "tp"), P("tp", "blk"), P("blk", "tp"), P("tp", "blk"), P("blk"), P("blk"),
        P("blk"), P("blk"), P("blk"), P("blk"),
    )
    body = per_device if mesh.shape["blk"] <= 16 else per_device_many
    return jax.shard_map(
        body, mesh=mesh, in_specs=in_specs, out_specs=out_specs, check_vma=False
    )
```

```python
import functools
import math

import jax
import jax.numpy as jnp
from jax import lax
from jax.experimental import pallas as pl
from jax.experimental.pallas import tpu as pltpu
from jax.sharding import PartitionSpec as P

HEAD_DIM = 96
LATENTS = 64
NEG_FILL = -1e30
NORM_EPS = 1e-05
BF = jnp.bfloat16
F32 = jnp.float32
MESH = pl.DeviceIdType.MESH
VMEM_LIMIT = 60 * 1024 * 1024
SCALE = 1.0 / math.sqrt(HEAD_DIM)


def dot_nn(a, b):
    return jnp.dot(a, b, preferred_element_type=F32)


def dot_nt(a, b):
    return lax.dot_general(a, b, (((1,), (1,)), ((), ())), preferred_element_type=F32)


def dot_tn(a, b):
    return lax.dot_general(a, b, (((0,), (0,)), ((), ())), preferred_element_type=F32)


def normalised(x):
    centred = x - jnp.mean(x, axis=-1, keepdims=True)
    rstd = lax.rsqrt(jnp.mean(centred * centred, axis=-1, keepdims=True) + NORM_EPS)
    return centred * rstd, rstd


def norm_back(q, gain, xhat, rstd):
    qg = q * gain
    inner = jnp.mean(qg * xhat, axis=-1, keepdims=True)
    return (qg - jnp.mean(qg, axis=-1, keepdims=True) - xhat * inner) * rstd


def greet(devices):
    barrier = pltpu.get_barrier_semaphore()
    for device in devices:
        pl.semaphore_signal(barrier, inc=1, device_id=device, device_id_type=MESH)
    pl.semaphore_wait(barrier, len(devices))


def remote(src, dst, send_sem, recv_sem, device):
    return pltpu.make_async_remote_copy(
        src_ref=src,
        dst_ref=dst,
        send_sem=send_sem,
        recv_sem=recv_sem,
        device_id=device,
        device_id_type=MESH,
    )


class Place:
    def __init__(self, nb):
        self.nb = nb
        self.no = nb // 2
        self.me = lax.axis_index("blk")
        self.outer = self.me // 2
        self.inner = self.me % 2
        self.partner = 2 * self.outer + 1 - self.inner

    def far(self, d):
        return (self.me + d) % self.nb

    def near(self, d):
        return (self.me - d + self.nb) % self.nb

    def outer_to(self, d):
        return (self.outer + d) % self.no

    def outer_from(self, d):
        return (self.outer - d + self.no) % self.no

    def greeting(self):
        return [{"blk": self.far(d)} for d in range(1, self.nb)]


class Gather:
    def __init__(self, place, slots, sems):
        self.place, self.slots, self.sems = place, slots, sems

    def copy_z(self, d):
        pc = self.place
        slot = self.slots.at[pc.me]
        return remote(
            slot, slot, self.sems.at[0, 0, d], self.sems.at[0, 1, d],
            {"blk": 2 * pc.outer_to(d) + pc.inner},
        )

    def copy_y(self, d):
        pc = self.place
        slot = self.slots.at[2 * pc.outer_from(d) + pc.inner]
        return remote(
            slot, slot, self.sems.at[1, 0, d], self.sems.at[1, 1, d], {"blk": pc.partner}
        )

    def start(self):
        for d in range(1, self.place.no):
            self.copy_z(d).start()
        self.copy_y(0).start()

    def relay(self):
        pc = self.place
        for d in range(1, pc.no):
            arrived = self.slots.at[2 * pc.outer_from(d) + pc.inner]
            remote(
                arrived, arrived, self.sems.at[0, 0, d], self.sems.at[0, 1, d], {"blk": pc.partner}
            ).wait_recv()
            self.copy_y(d).start()

    def finish(self):
        pc = self.place
        for d in range(pc.no):
            slot = self.slots.at[2 * pc.outer_from(d) + 1 - pc.inner]
            remote(
                slot, slot, self.sems.at[1, 0, d], self.sems.at[1, 1, d], {"blk": pc.partner}
            ).wait_recv()
        for d in range(1, pc.no):
            self.copy_z(d).wait_send()
        for d in range(pc.no):
            self.copy_y(d).wait_send()


class Exchange:
    def __init__(self, place, out, into, sems, slot=lambda d: d):
        self.place, self.out, self.into, self.sems, self.slot = place, out, into, sems, slot

    def copy(self, d):
        return remote(
            self.out.at[self.slot(d)], self.into.at[d], self.sems.at[0, d], self.sems.at[1, d],
            {"blk": self.place.far(d)},
        )

    def start(self, d):
        self.copy(d).start()

    def wait_recv(self, d):
        self.copy(d).wait_recv()

    def finish_sends(self):
        for d in range(1, self.place.nb):
            self.copy(d).wait_send()


def lane_image(source, images_here, width):
    lane = lax.broadcasted_iota(jnp.int32, (1, width), 1)
    return source * images_here + lane // LATENTS


def attend_kernel(
    nb,
    lat_ref, med_ref, wq_ref, wk_ref, wv_ref, lg_ref, ls_ref, mg_ref, ms_ref, image_ref,
    ln_ref, mn_ref, q_all, kh_ref, kt_ref, vh_ref, lkh_ref, lkt_ref, lvh_ref, att_ref, lse_ref,
    vt, lvt, acc_out, acc_in, stat_out, stat_in, g_sems, a_sems, s_sems,
):
    place = Place(nb)
    lat_rows = lat_ref.shape[0]
    med_rows = med_ref.shape[0]
    heads = kh_ref.shape[0]
    images_here = lat_rows // LATENTS
    greet(place.greeting())

    xhat, _ = normalised(lat_ref[...].astype(F32))
    ln_ref[...] = (xhat * lg_ref[...] + ls_ref[...]).astype(BF)
    ln = ln_ref[...]

    def heads_t(rows, ref):
        turned = rows.T
        for h in range(heads):
            ref[h] = turned[h * HEAD_DIM : (h + 1) * HEAD_DIM].astype(BF)

    def heads_n(rows, ref):
        for h in range(heads):
            ref[h] = rows[:, h * HEAD_DIM : (h + 1) * HEAD_DIM].astype(BF)

    heads_t(dot_nn(ln, wq_ref[...]) * SCALE, q_all.at[place.me])
    gather = Gather(place, q_all, g_sems)
    gather.start()
    lk = dot_nn(ln, wk_ref[...])
    heads_n(lk, lkh_ref)
    heads_t(lk, lkt_ref)
    lv = dot_nn(ln, wv_ref[...])
    heads_n(lv, lvh_ref)
    heads_t(lv, lvt)

    def norm_rows(i, carry):
        rows = pl.ds(pl.multiple_of(i * 128, 128), 128)
        hat, _ = normalised(med_ref[rows, :].astype(F32))
        mn_ref[rows, :] = (hat * mg_ref[...] + ms_ref[...]).astype(BF)
        return carry

    lax.fori_loop(0, med_rows // 128, norm_rows, 0)
    mk = dot_nn(mn_ref[...], wk_ref[...])
    heads_n(mk, kh_ref)
    heads_t(mk, kt_ref)
    gather.relay()
    mv = dot_nn(mn_ref[...], wv_ref[...])
    heads_n(mv, vh_ref)
    heads_t(mv, vt)
    gather.finish()

    exchange = Exchange(place, acc_out, acc_in, a_sems)
    stats = Exchange(place, stat_out, stat_in, s_sems)
    image = image_ref[...]
    order = list(range(1, nb)) + [0]
    for g in range(nb // 2):
        pair = order[2 * g : 2 * g + 2]
        sources = [place.far(d) for d in pair]
        lanes = jnp.concatenate([lane_image(s, images_here, lat_rows) for s in sources], axis=1)
        allowed = image == lanes
        for h in range(heads):
            queries = jnp.concatenate([q_all[s, h] for s in sources], axis=1)
            scores = jnp.where(allowed, dot_nn(kh_ref[h], queries), NEG_FILL)
            top = jnp.max(scores, axis=0, keepdims=True)
            weights = jnp.exp(scores - top)
            total = jnp.sum(weights, axis=0, keepdims=True)
            acc = dot_nn(vt[h], weights.astype(BF)).astype(BF)
            for n, d in enumerate(pair):
                part = slice(n * lat_rows, (n + 1) * lat_rows)
                acc_out[d, h] = acc[:, part]
                stat_out[d, h : h + 1, :] = top[:, part]
                stat_out[d, heads + h : heads + h + 1, :] = total[:, part]
        for d in pair:
            if d:
                exchange.start(d)
                stats.start(d)

    row_image = lax.broadcasted_iota(jnp.int32, (lat_rows, lat_rows), 0) // LATENTS
    col_image = lax.broadcasted_iota(jnp.int32, (lat_rows, lat_rows), 1) // LATENTS
    same = row_image == col_image
    own = []
    for h in range(heads):
        scores = jnp.where(same, dot_nn(lkh_ref[h], q_all[place.me, h]), NEG_FILL)
        top = jnp.max(scores, axis=0, keepdims=True)
        weights = jnp.exp(scores - top)
        total = jnp.sum(weights, axis=0, keepdims=True)
        own.append((top, total, dot_nn(lvt[h], weights.astype(BF))))
    for d in range(1, nb):
        stats.wait_recv(d)
        exchange.wait_recv(d)
    lse_ref[...] = jnp.zeros_like(lse_ref)
    for h in range(heads):
        own_top, own_total, own_acc = own[h]
        tops = [
            (stat_out if d == 0 else stat_in)[d, h : h + 1, :] for d in range(nb)
        ]
        best = functools.reduce(jnp.maximum, tops, own_top)
        factor = jnp.exp(own_top - best)
        total = own_total * factor
        acc = own_acc * factor
        for d in range(nb):
            factor = jnp.exp(tops[d] - best)
            stat = stat_out if d == 0 else stat_in
            piece = acc_out if d == 0 else acc_in
            total = total + stat[d, heads + h : heads + h + 1, :] * factor
            acc = acc + piece[d, h].astype(F32) * factor
        att_ref[h] = acc / total
        lse_ref[h : h + 1, :] = best + jnp.log(total)
    exchange.finish_sends()
    stats.finish_sends()


class TensorSum:
    def __init__(self, bufs, sems, tile_of):
        self.bufs, self.sems, self.tile_of = bufs, sems, tile_of
        self.tiles, self.rows, self.tile = bufs.shape[1:]
        t = lax.axis_index("tp")
        self.core = t % 2
        self.chip = t // 2
        self.sibling = {"tp": 2 * self.chip + 1 - self.core}
        self.across = {"tp": 2 * (1 - self.chip) + self.core}

    @staticmethod
    def greeting():
        t = lax.axis_index("tp")
        core, chip = t % 2, t // 2
        return [{"tp": 2 * chip + 1 - core}, {"tp": 2 * (1 - chip) + core}]

    def column(self, half, j):
        return pl.multiple_of((half * self.tiles + j) * self.tile, 128)

    def copy(self, stage, j):
        return remote(
            self.bufs.at[2 * stage, j], self.bufs.at[2 * stage + 1, j],
            self.sems.at[stage, 0, j], self.sems.at[stage, 1, j],
            self.across if stage == 1 else self.sibling,
        )

    def give(self):
        for j in range(self.tiles):
            self.bufs[0, j] = self.tile_of(self.column(1 - self.core, j)).astype(BF)
            self.copy(0, j).start()

    def cross(self):
        for j in range(self.tiles):
            mine = self.tile_of(self.column(self.core, j))
            self.copy(0, j).wait_recv()
            self.bufs[2, j] = (mine + self.bufs[1, j].astype(F32)).astype(BF)
            self.copy(1, j).start()

    def back(self):
        for j in range(self.tiles):
            self.copy(1, j).wait_recv()
            self.bufs[4, j] = (self.bufs[2, j].astype(F32) + self.bufs[3, j].astype(F32)).astype(BF)
            self.copy(2, j).start()

    def finish(self, put):
        for j in range(self.tiles):
            put(self.column(self.core, j), self.bufs[4, j])
        for j in range(self.tiles):
            self.copy(2, j).wait_recv()
            put(self.column(1 - self.core, j), self.bufs[5, j])
        for stage in range(3):
            for j in range(self.tiles):
                self.copy(stage, j).wait_send()


def feed_kernel(
    att_ref, lse_ref, lat_ref, cot_ref, wo_ref, fg_ref, fs_ref, up_hbm, down_hbm,
    out_ref, mid_grad_ref, branch_ref, dot_ref, ld_ref, fn_ref, low_ref, gain_ref,
    up, down, hg, mid, hidden, pre_grad, low_t, sum_buf, bufs, sems, w_sems,
):
    loads = [
        pltpu.make_async_copy(up_hbm, up, w_sems.at[0]),
        pltpu.make_async_copy(down_hbm, down, w_sems.at[1]),
    ]
    for load in loads:
        load.start()
    heads = att_ref.shape[0]
    ff_here = up.shape[1]
    ff_tile = math.gcd(ff_here, 512)
    greet(TensorSum.greeting())
    for h in range(heads):
        low_t[h * HEAD_DIM : (h + 1) * HEAD_DIM, :] = att_ref[h]
    low_ref[...] = low_t[...].T.astype(BF)
    low = low_ref[...]

    def put(column, tile):
        sum_buf[:, pl.ds(column, tile.shape[1])] = tile.astype(F32)

    def tile_sum(n, tile_of):
        return TensorSum(bufs.at[n], sems.at[n], tile_of)

    width = bufs.shape[-1]
    branch = tile_sum(0, lambda c: dot_nn(low, wo_ref[:, pl.ds(c, width)]))
    branch.give()
    branch.cross()
    loads[1].wait()
    cot = cot_ref[...]

    def back_hidden(i, carry):
        cols = pl.ds(pl.multiple_of(i * ff_tile, ff_tile), ff_tile)
        hg[:, cols] = dot_nt(cot, down[cols, :])
        return carry

    lax.fori_loop(0, ff_here // ff_tile, back_hidden, 0)
    branch.back()
    branch.finish(put)
    mid[...] = lat_ref[...].astype(F32) + sum_buf[...]
    xhat, rstd = normalised(mid[...])
    fn_ref[...] = (xhat * fg_ref[...] + fs_ref[...]).astype(BF)
    fn = fn_ref[...]
    loads[0].wait()

    def inner(i, carry):
        cols = pl.ds(pl.multiple_of(i * ff_tile, ff_tile), ff_tile)
        pre = dot_nn(fn, up[:, cols])
        bell = 0.5 * (1.0 + lax.erf(pre * math.sqrt(0.5)))
        hidden[:, cols] = (pre * bell).astype(BF)
        slope = bell + pre * jnp.exp(-0.5 * pre * pre) * (1.0 / math.sqrt(2.0 * math.pi))
        pre_grad[:, cols] = (hg[:, cols] * slope).astype(BF)
        return carry

    lax.fori_loop(0, ff_here // ff_tile, inner, 0)
    grads = tile_sum(1, lambda c: dot_nt(pre_grad[...], up[pl.ds(c, width), :]))
    feed = tile_sum(2, lambda c: dot_nn(hidden[...], down[:, pl.ds(c, width)]))
    grads.give()
    grads.cross()
    feed.give()
    feed.cross()
    grads.back()
    feed.back()
    grads.finish(put)
    fng = sum_buf[...]
    xhat, rstd = normalised(mid[...])
    mid_grad = cot_ref[...].astype(F32) + norm_back(fng, fg_ref[...], xhat, rstd)
    mid_grad_ref[...] = mid_grad
    branch_ref[...] = mid_grad.astype(BF)
    gain_ref[...] = jnp.zeros_like(gain_ref)
    gain_ref[0:1, :] = jnp.sum(fng * xhat, axis=0, keepdims=True)
    gain_ref[1:2, :] = jnp.sum(fng, axis=0, keepdims=True)
    back = dot_nt(wo_ref[...], branch_ref[...])
    ld_ref[...] = lse_ref[...]
    for h in range(heads):
        piece = back[h * HEAD_DIM : (h + 1) * HEAD_DIM, :].astype(BF)
        dot_ref[h] = piece
        ld_ref[heads + h : heads + h + 1, :] = jnp.sum(
            piece.astype(F32) * att_ref[h], axis=0, keepdims=True
        )
    feed.finish(put)
    out_ref[...] = (mid[...] + sum_buf[...]).astype(BF)


def back_kernel(
    nb,
    q_all, dot_in, ld_in, kh_ref, kt_ref, vh_ref, lkh_ref, lkt_ref, lvh_ref, ln_ref, mn_ref,
    wq_ref, wk_ref, wv_ref, mid_grad_ref, lat_ref, med_ref, lg_ref, mg_ref, fgain_ref, image_ref,
    mgrad_ref, lgrad_ref, qg_ref, kg_ref, vg_ref, gains_ref,
    dot_all, ld_all, dk, dv, dq_own, dq_in, turn, xall, yall, dq_low, part, pair_in, far_in,
    gain_out, gain_in, med_bufs, lat_bufs,
    g_sems, l_sems, x_sems, y_sems, z_sems, n_sems, t_sems,
):
    place = Place(nb)
    lat_rows = lat_ref.shape[0]
    med_rows, model = med_ref.shape
    heads = kh_ref.shape[0]
    inner = heads * HEAD_DIM
    images_here = lat_rows // LATENTS
    dot_all[place.me] = dot_in[...]
    ld_all[place.me] = ld_in[...]
    greet(place.greeting() + TensorSum.greeting())
    gather = Gather(place, dot_all, g_sems)
    gather_ld = Gather(place, ld_all, l_sems)
    gather_ld.start()
    gather.start()

    row_image = lax.broadcasted_iota(jnp.int32, (lat_rows, lat_rows), 0) // LATENTS
    col_image = lax.broadcasted_iota(jnp.int32, (lat_rows, lat_rows), 1) // LATENTS
    same = row_image == col_image

    def turned(h, value, rows):
        turn[h * HEAD_DIM : (h + 1) * HEAD_DIM, 0:rows] = value

    def grads_of(h, keys, values, queries, grads, lse, delta, allowed):
        scores = jnp.where(allowed, dot_nn(keys, queries), NEG_FILL)
        probs = jnp.exp(scores - lse)
        score_grad = (probs * (dot_nn(values, grads) - delta)).astype(BF)
        return probs.astype(BF), score_grad

    for h in range(heads):
        queries, grads = q_all[place.me, h], dot_in[h]
        probs, score_grad = grads_of(
            h, lkh_ref[h], lvh_ref[h], queries, grads,
            ld_in[h : h + 1, :], ld_in[heads + h : heads + h + 1, :], same,
        )
        dk[h, :, 0:lat_rows] = dot_nt(queries, score_grad)
        dv[h, :, 0:lat_rows] = dot_nt(grads, probs)
        dq_own[h] = dot_nn(lkt_ref[h], score_grad)

    def put_rows(first, rows):
        for acc, column in ((dk, 0), (dv, inner)):
            for h in range(heads):
                turned(h, acc[h, :, 0:rows], rows)
            yall[first : first + rows, column : column + inner] = turn[:, 0:rows].T.astype(BF)

    put_rows(med_rows, lat_rows)
    xall[0:med_rows, :] = mn_ref[...]
    xall[med_rows:, :] = ln_ref[...]
    gather_ld.relay()
    gather.relay()
    gather_ld.finish()
    gather.finish()

    exchange = Exchange(place, dot_all, dq_in, x_sems, place.far)
    image = image_ref[...]
    order = list(range(1, nb)) + [0]
    for g in range(nb // 2):
        pair = order[2 * g : 2 * g + 2]
        sources = [place.far(d) for d in pair]
        lanes = jnp.concatenate([lane_image(s, images_here, lat_rows) for s in sources], axis=1)
        allowed = image == lanes
        for h in range(heads):
            queries = jnp.concatenate([q_all[s, h] for s in sources], axis=1)
            grads = jnp.concatenate([dot_all[s, h] for s in sources], axis=1)
            lse = jnp.concatenate([ld_all[s, h : h + 1, :] for s in sources], axis=1)
            delta = jnp.concatenate(
                [ld_all[s, heads + h : heads + h + 1, :] for s in sources], axis=1
            )
            probs, score_grad = grads_of(
                h, kh_ref[h], vh_ref[h], queries, grads, lse, delta, allowed
            )
            key_part = dot_nt(queries, score_grad)
            value_part = dot_nt(grads, probs)
            dk[h] = key_part if g == 0 else dk[h] + key_part
            dv[h] = value_part if g == 0 else dv[h] + value_part
            dq = dot_nn(kt_ref[h], score_grad)
            for n, d in enumerate(pair):
                piece = dq[:, n * lat_rows : (n + 1) * lat_rows]
                if d:
                    dot_all[place.far(d), h] = piece.astype(BF)
                else:
                    dq_own[h] = dq_own[h] + piece
        for d in pair:
            if d:
                exchange.start(d)
    put_rows(0, med_rows)

    med_tile, lat_tile = med_bufs.shape[-1], lat_bufs.shape[-1]

    def back_rows(first, rows, tile):
        def tile_of(column):
            cols = pl.ds(column, tile)
            values = yall[first : first + rows, :]
            return dot_nt(values[:, 0:inner], wk_ref[cols, :]) + dot_nt(
                values[:, inner:], wv_ref[cols, :]
            )

        return tile_of

    med_sum = TensorSum(med_bufs, t_sems.at[0], back_rows(0, med_rows, med_tile))
    med_sum.give()
    med_sum.cross()

    for d in range(1, nb):
        exchange.wait_recv(d)
    for h in range(heads):
        value = dq_own[h]
        for d in range(1, nb):
            value = value + dq_in[d, h].astype(F32)
        turned(h, value, lat_rows)
    dq_low[...] = turn[:, 0:lat_rows].T.astype(BF)

    own_rows = model // nb
    chunk = 2 * own_rows * max(1, 128 // math.gcd(128, 2 * own_rows))
    per_chunk = chunk // own_rows

    def pair_copy(o):
        return remote(
            part.at[2 * o + 1 - place.inner], pair_in.at[o], y_sems.at[0, o], y_sems.at[1, o],
            {"blk": place.partner},
        )

    def far_copy(o, d):
        return remote(
            part.at[2 * o + place.inner], far_in.at[d], z_sems.at[0, d], z_sems.at[1, d],
            {"blk": 2 * o + place.inner},
        )

    for c in range(model // chunk):
        cols = slice(c * chunk, (c + 1) * chunk)
        lnx = xall[med_rows:, cols]
        query_part = dot_tn(lnx, dq_low[...]) * SCALE
        other_part = dot_tn(xall[:, cols], yall[...])
        for n in range(per_chunk):
            owner = c * per_chunk + n
            rows = slice(n * own_rows, (n + 1) * own_rows)
            part[owner, 0:own_rows, 0:inner] = query_part[rows].astype(BF)
            part[owner, 0:own_rows, inner:] = other_part[rows].astype(BF)
        for o in range(c * per_chunk // 2, (c + 1) * per_chunk // 2):
            pair_copy(o).start()

    def lat_tile_of(column):
        cols = pl.ds(column, lat_tile)
        return (
            back_rows(med_rows, lat_rows, lat_tile)(column)
            + dot_nt(dq_low[...], wq_ref[cols, :]) * SCALE
        )

    lat_sum = TensorSum(lat_bufs, t_sems.at[1], lat_tile_of)
    lat_sum.give()
    lat_sum.cross()

    def own_part(o):
        return part[2 * o + place.inner].astype(F32) + pair_in[o].astype(F32)

    for d in range(1, place.no):
        o = place.outer_to(d)
        pair_copy(o).wait_recv()
        part[2 * o + place.inner] = own_part(o).astype(BF)
        far_copy(o, d).start()
    med_sum.back()

    def put(column, tile):
        xall[0 : tile.shape[0], pl.ds(column, tile.shape[1])] = tile

    med_sum.finish(put)
    gain_rows = [fgain_ref[0:1, :], fgain_ref[1:2, :]]

    def norm_rows(i, carry):
        rows = pl.ds(pl.multiple_of(i * 128, 128), 128)
        xhat, rstd = normalised(med_ref[rows, :].astype(F32))
        q = xall[rows, :].astype(F32)
        mgrad_ref[rows, :] = norm_back(q, mg_ref[...], xhat, rstd)
        return (
            carry[0] + jnp.sum(q * xhat, axis=0, keepdims=True),
            carry[1] + jnp.sum(q, axis=0, keepdims=True),
        )

    zero = jnp.zeros((1, model), F32)
    med_gain = lax.fori_loop(0, med_rows // 128, norm_rows, (zero, zero))
    lat_sum.back()
    lat_sum.finish(put)
    xhat, rstd = normalised(lat_ref[...].astype(F32))
    q = xall[0:lat_rows, :].astype(F32)
    lgrad_ref[...] = mid_grad_ref[...] + norm_back(q, lg_ref[...], xhat, rstd)
    all_rows = [
        *med_gain,
        jnp.sum(q * xhat, axis=0, keepdims=True),
        jnp.sum(q, axis=0, keepdims=True),
        *gain_rows,
    ]
    for o in range(nb):
        for n, row in enumerate(all_rows):
            gain_out[o, n : n + 1, :] = row[:, o * own_rows : (o + 1) * own_rows]

    def gain_copy(d):
        return remote(
            gain_out.at[place.far(d)], gain_in.at[d], n_sems.at[0, d], n_sems.at[1, d],
            {"blk": place.far(d)},
        )

    for d in range(1, nb):
        gain_copy(d).start()
    pair_copy(place.outer).wait_recv()
    total = own_part(place.outer)
    for d in range(1, place.no):
        far_copy(place.outer_to(d), d).wait_recv()
        total = total + far_in[d].astype(F32)
    qg_ref[...] = total[0:own_rows, 0:inner]
    kg_ref[...] = total[0:own_rows, inner : 2 * inner]
    vg_ref[...] = total[0:own_rows, 2 * inner :]
    gains = gain_out[place.me]
    for d in range(1, nb):
        gain_copy(d).wait_recv()
        gains = gains + gain_in[d]
    gains_ref[...] = gains
    exchange.finish_sends()
    for d in range(1, nb):
        gain_copy(d).wait_send()
    for o in range(place.no):
        pair_copy(o).wait_send()
    for d in range(1, place.no):
        far_copy(place.outer_to(d), d).wait_send()


def call(kernel, out_shapes, scratch, collective_id, any_args=(), args=()):
    vmem = pl.BlockSpec(memory_space=pltpu.VMEM)
    return pl.pallas_call(
        kernel,
        out_shape=[jax.ShapeDtypeStruct(s, d) for s, d in out_shapes],
        in_specs=[vmem] * len(args) + [pl.BlockSpec(memory_space=pl.ANY)] * len(any_args),
        out_specs=[vmem] * len(out_shapes),
        scratch_shapes=scratch,
        compiler_params=pltpu.CompilerParams(
            collective_id=collective_id, has_side_effects=True, vmem_limit_bytes=VMEM_LIMIT
        ),
    )(*args, *any_args)


def gelu_pair(pre):
    bell = 0.5 * (1.0 + lax.erf(pre * math.sqrt(0.5)))
    slope = bell + pre * jnp.exp(-0.5 * pre * pre) * (1.0 / math.sqrt(2.0 * math.pi))
    return pre * bell, slope


def per_device_many(
    latents, media, query_weight, key_weight, value_weight, out_weight, up_weight, down_weight,
    media_gain, media_shift, latent_gain, latent_shift, feed_gain, feed_shift, cotangent, media_image,
):
    nb = lax.axis_size("blk")
    me = lax.axis_index("blk")
    lat_rows, model = latents.shape
    med_rows = media.shape[0]
    inner = query_weight.shape[1]
    heads = inner // HEAD_DIM
    ff_here = up_weight.shape[1]
    no = nb // 2
    own_rows = model // nb
    own_pad = -(-own_rows // 16) * 16
    dma = pltpu.SemaphoreType.DMA
    vm = pltpu.VMEM
    row = lambda v: v.reshape(1, -1)
    image = media_image.reshape(-1, 1)
    hd = HEAD_DIM
    cot_all = lax.all_gather(cotangent, "blk", axis=0, tiled=True)

    (ln, mn, q_all, kh, kt, vh, lkh, lkt, lvh, att, lse) = call(
        functools.partial(attend_kernel, nb),
        [
            ((lat_rows, model), BF), ((med_rows, model), BF), ((nb, heads, hd, lat_rows), BF),
            ((heads, med_rows, hd), BF), ((heads, hd, med_rows), BF), ((heads, med_rows, hd), BF),
            ((heads, lat_rows, hd), BF), ((heads, hd, lat_rows), BF), ((heads, lat_rows, hd), BF),
            ((heads, hd, lat_rows), F32), ((2 * heads, lat_rows), F32),
        ],
        [
            vm((heads, hd, med_rows), BF), vm((heads, hd, lat_rows), BF),
            vm((nb, heads, hd, lat_rows), BF), vm((nb, heads, hd, lat_rows), BF),
            vm((nb, 2 * heads, lat_rows), F32), vm((nb, 2 * heads, lat_rows), F32),
            dma((2, 2, no)), dma((2, nb)), dma((2, nb)),
        ],
        0,
        args=(
            latents, media, query_weight, key_weight, value_weight, row(latent_gain),
            row(latent_shift), row(media_gain), row(media_shift), image,
        ),
    )

    tile = 256
    tiles = model // 2 // tile
    (resampled, mid_grad, branch, dot, ld, fn, low, feed_gains) = call(
        feed_kernel,
        [
            ((lat_rows, model), BF), ((lat_rows, model), F32), ((lat_rows, model), BF),
            ((heads, hd, lat_rows), BF), ((2 * heads, lat_rows), F32), ((lat_rows, model), BF),
            ((lat_rows, inner), BF), ((8, model), F32),
        ],
        [
            vm((model, ff_here), BF), vm((ff_here, model), BF), vm((lat_rows, ff_here), F32),
            vm((lat_rows, model), F32), vm((lat_rows, ff_here), BF), vm((lat_rows, ff_here), BF),
            vm((inner, lat_rows), F32), vm((lat_rows, model), F32),
            vm((3, 6, tiles, lat_rows, tile), BF), dma((3, 3, 2, tiles)), dma((2,)),
        ],
        1,
        any_args=(up_weight, down_weight),
        args=(att, lse, latents, cotangent, out_weight, row(feed_gain), row(feed_shift)),
    )
    fn_all = lax.all_gather(fn, "blk", axis=0, tiled=True)
    low_all = lax.all_gather(low, "blk", axis=0, tiled=True)
    branch_all = lax.all_gather(branch, "blk", axis=0, tiled=True)

    (media_grad, latent_grad, query_grad, key_grad, value_grad, gains) = call(
        functools.partial(back_kernel, nb),
        [
            ((med_rows, model), F32), ((lat_rows, model), F32), ((own_rows, inner), F32),
            ((own_rows, inner), F32), ((own_rows, inner), F32), ((8, own_rows), F32),
        ],
        [
            vm((nb, heads, hd, lat_rows), BF), vm((nb, 2 * heads, lat_rows), F32),
            vm((heads, hd, med_rows), F32), vm((heads, hd, med_rows), F32),
            vm((heads, hd, lat_rows), F32),
            vm((nb, heads, hd, lat_rows), BF),
            vm((inner, med_rows), F32), vm((med_rows + lat_rows, model), BF),
            vm((med_rows + lat_rows, 2 * inner), BF), vm((lat_rows, inner), BF),
            vm((nb, own_pad, 3 * inner), BF), vm((no, own_pad, 3 * inner), BF),
            vm((no, own_pad, 3 * inner), BF),
            vm((nb, 8, own_rows), F32), vm((nb, 8, own_rows), F32),
            vm((6, tiles, med_rows, tile), BF), vm((6, tiles, lat_rows, tile), BF),
            dma((2, 2, no)), dma((2, 2, no)), dma((2, nb)), dma((2, no)), dma((2, no)),
            dma((2, nb)), dma((2, 3, 2, tiles)),
        ],
        2,
        args=(
            q_all, dot, ld, kh, kt, vh, lkh, lkt, lvh, ln, mn, query_weight, key_weight,
            value_weight, mid_grad, latents, media, row(latent_gain), row(media_gain), feed_gains,
            image,
        ),
    )

    def own_columns(rows):
        return lax.dynamic_slice_in_dim(rows, me * own_rows, own_rows, axis=1)

    group = math.gcd(nb, 8)
    group_rows = group * lat_rows

    def feed_step(carry, rows):
        up_acc, down_acc, out_acc = carry
        fn_rows, cot_rows, low_rows, branch_rows = rows
        hidden, slope = gelu_pair(dot_nn(fn_rows, up_weight))
        grad = (dot_nt(cot_rows, down_weight) * slope).astype(BF)
        return (
            up_acc + dot_tn(own_columns(fn_rows), grad),
            down_acc + dot_tn(hidden.astype(BF), own_columns(cot_rows)),
            out_acc + dot_tn(low_rows, own_columns(branch_rows)),
        ), None

    whole = (fn_all, cot_all, low_all, branch_all)
    start = (
        jnp.zeros((own_rows, ff_here), F32),
        jnp.zeros((ff_here, own_rows), F32),
        jnp.zeros((inner, own_rows), F32),
    )
    if group == nb:
        (up_grad, down_grad, out_grad), _ = feed_step(start, whole)
    else:
        (up_grad, down_grad, out_grad), _ = lax.scan(
            feed_step, start, tuple(v.reshape(nb // group, group_rows, -1) for v in whole)
        )
    return (
        resampled, media_grad, latent_grad, query_grad, key_grad, value_grad, out_grad, up_grad,
        down_grad, gains[0], gains[1], gains[2], gains[3], gains[4], gains[5],
    )


class Spread:
    def __init__(self, place, own, slots, sems, share=True):
        self.place, self.own, self.slots, self.sems = place, own, slots, sems
        self.share = share
        t = lax.axis_index("tp")
        self.t = t
        core, chip = t % 2, t // 2
        self.sibling_t = 2 * chip + 1 - core
        self.across_t = 2 * (1 - chip) + core
        self.diagonal_t = 2 * (1 - chip) + 1 - core
        self.rows = slots.shape[2]

    def source(self, kind, d):
        pc = self.place
        side = pc.inner if kind == 0 else 1 - pc.inner
        return 2 * pc.outer_from(d) + side

    def arrivals(self):
        no = self.place.no
        return [(0, d) for d in range(1, no)] + [(1, d) for d in range(no)]

    def own_rows(self):
        return self.own.at[pl.ds(pl.multiple_of(self.t * self.rows, self.rows), self.rows)]

    def copy_z(self, d):
        pc = self.place
        return remote(
            self.own_rows(), self.slots.at[pc.me, self.t], self.sems.at[0, 0, d], self.sems.at[0, 1, d],
            {"blk": 2 * pc.outer_to(d) + pc.inner},
        )

    def copy_y(self, d):
        pc = self.place
        there = self.slots.at[self.source(0, d), self.t]
        return remote(
            self.own_rows() if d == 0 else there, there, self.sems.at[1, 0, d],
            self.sems.at[1, 1, d], {"blk": pc.partner},
        )

    def copy_x(self, kind, d):
        slot = self.slots.at[self.source(kind, d), self.t]
        n = kind * self.place.no + d
        return remote(slot, slot, self.sems.at[2, 0, n], self.sems.at[2, 1, n], {"tp": self.across_t})

    def copy_c(self, far, kind, d):
        slot = self.slots.at[self.source(kind, d), self.across_t if far else self.t]
        n = far * 2 * self.place.no + kind * self.place.no + d
        return remote(slot, slot, self.sems.at[3, 0, n], self.sems.at[3, 1, n], {"tp": self.sibling_t})

    def arrived(self, stage, n, kind, d, t):
        slot = self.slots.at[self.source(kind, d), t]
        remote(
            slot, slot, self.sems.at[stage, 0, n], self.sems.at[stage, 1, n], {"tp": self.sibling_t}
        ).wait_recv()

    def start(self):
        for d in range(1, self.place.no):
            self.copy_z(d).start()
        self.copy_y(0).start()
        for q in range(4):
            self.slots[self.place.me, q] = self.own[q * self.rows : (q + 1) * self.rows]

    def relay_z(self):
        for d in range(1, self.place.no):
            self.arrived(0, d, 0, d, self.t)
            self.copy_y(d).start()
            if self.share:
                self.copy_x(0, d).start()
                self.copy_c(0, 0, d).start()

    def relay_y(self):
        for d in range(self.place.no):
            self.arrived(1, d, 1, d, self.t)
            if self.share:
                self.copy_x(1, d).start()
                self.copy_c(0, 1, d).start()

    def relay_x(self):
        for kind, d in self.arrivals():
            self.arrived(2, kind * self.place.no + d, kind, d, self.across_t)
            self.copy_c(1, kind, d).start()

    def finish(self):
        no = self.place.no
        for far in range(2 * self.share):
            for kind, d in self.arrivals():
                self.arrived(
                    3, far * 2 * no + kind * no + d, kind, d, self.diagonal_t if far else self.sibling_t
                )
        for d in range(1, no):
            self.copy_z(d).wait_send()
        for d in range(no):
            self.copy_y(d).wait_send()
        for kind, d in self.arrivals() if self.share else ():
            self.copy_x(kind, d).wait_send()
            self.copy_c(0, kind, d).wait_send()
            self.copy_c(1, kind, d).wait_send()


class Share:
    def __init__(self, place, held, full, sems, own_sems):
        self.place, self.held, self.full, self.sems, self.own_sems = place, held, full, sems, own_sems
        t = lax.axis_index("tp")
        self.t = t
        core, chip = t % 2, t // 2
        self.sibling_t = 2 * chip + 1 - core
        self.across_t = 2 * (1 - chip) + core
        self.diagonal_t = 2 * (1 - chip) + 1 - core

    def blocks(self, step):
        pc = self.place
        base = 2 * pc.outer_from(step)
        partner = (pc.no + step, base + 1 - pc.inner)
        return [partner] if step == 0 else [(step, base + pc.inner), partner]

    def copy(self, stage, n, s):
        there = self.full.at[s, self.across_t if stage == 2 else self.t]
        return remote(
            there if stage == 2 else self.held.at[s, self.t], there,
            self.sems.at[stage, 0, n], self.sems.at[stage, 1, n],
            {"tp": self.sibling_t if stage else self.across_t},
        )

    def local(self, n, s):
        return pltpu.make_async_copy(
            self.held.at[s, self.t], self.full.at[s, self.t], self.own_sems.at[n]
        )

    def own_block(self):
        me = self.place.me
        return pltpu.make_async_copy(self.held.at[me], self.full.at[me], self.own_sems.at[0])

    def arrived(self, stage, n, s, t):
        slot = self.full.at[s, t]
        remote(
            slot, slot, self.sems.at[stage, 0, n], self.sems.at[stage, 1, n], {"tp": self.sibling_t}
        ).wait_recv()

    def start(self):
        self.own_block().start()
        for step in range(self.place.no):
            for n, s in self.blocks(step):
                self.copy(0, n, s).start()
                self.copy(1, n, s).start()
                self.local(n, s).start()

    def forward(self, step):
        for n, s in self.blocks(step):
            self.arrived(0, n, s, self.across_t)
            self.copy(2, n, s).start()

    def ready(self, step):
        if step == 0:
            self.own_block().wait()
        for n, s in self.blocks(step):
            self.local(n, s).wait()
            self.arrived(1, n, s, self.sibling_t)
            self.arrived(2, n, s, self.diagonal_t)

    def finish(self):
        for step in range(self.place.no):
            for n, s in self.blocks(step):
                for stage in range(3):
                    self.copy(stage, n, s).wait_send()


class Slices:
    def __init__(self, place, out, into, sems):
        self.place, self.out, self.into, self.sems = place, out, into, sems
        t = lax.axis_index("tp")
        self.core = t % 2
        self.sibling = {"tp": 2 * (t // 2) + 1 - self.core}

    def copy(self, d):
        pc = self.place
        return remote(
            self.out.at[pc.far(d), self.core], self.into.at[pc.me, self.core],
            self.sems.at[0, 0, d], self.sems.at[0, 1, d], {"blk": pc.far(d)},
        )

    def share(self, d):
        slot = self.into.at[self.place.near(d), self.core]
        return remote(slot, slot, self.sems.at[1, 0, d], self.sems.at[1, 1, d], self.sibling)

    def arrived(self, stage, d, core):
        slot = self.into.at[self.place.near(d), core]
        remote(
            slot, slot, self.sems.at[stage, 0, d], self.sems.at[stage, 1, d], self.sibling
        ).wait_recv()

    def start(self):
        for d in range(1, self.place.nb):
            self.copy(d).start()

    def relay(self):
        for d in range(1, self.place.nb):
            self.arrived(0, d, self.core)
            self.share(d).start()

    def finish(self):
        for d in range(1, self.place.nb):
            self.arrived(1, d, 1 - self.core)
        for d in range(1, self.place.nb):
            self.copy(d).wait_send()
            self.share(d).wait_send()

    def cut(self, rows):
        nb, _, half, width = self.out.shape
        for o in range(nb):
            piece = rows[:, o * width : (o + 1) * width]
            self.out[o, 0] = piece[0:half]
            self.out[o, 1] = piece[half:]
        for c in range(2):
            self.into[self.place.me, c] = self.out[self.place.me, c]


class Fold:
    def __init__(self, place, give, got, send, into, sems):
        self.place, self.give, self.got, self.send, self.into = place, give, got, send, into
        self.sems = sems

    def pair(self, o):
        return remote(
            self.give(o), self.got.at[o], self.sems.at[0, 0, o], self.sems.at[0, 1, o],
            {"blk": self.place.partner},
        )

    def far(self, d):
        o = self.place.outer_to(d)
        return remote(
            self.send(o), self.into.at[d], self.sems.at[1, 0, d], self.sems.at[1, 1, d],
            {"blk": 2 * o + self.place.inner},
        )

    def finish(self):
        for o in range(self.place.no):
            self.pair(o).wait_send()
        for d in range(1, self.place.no):
            self.far(d).wait_send()


def image_columns(image_ref, rows, lanes):
    line = image_ref[...].astype(F32).reshape(1, rows)
    return jnp.broadcast_to(line, (lanes, rows)).T


def pair_lanes(place, sources, images_here, lat_rows):
    return jnp.concatenate(
        [lane_image(s, images_here, lat_rows).astype(F32) for s in sources], axis=1
    )


def line_of(ref):
    return ref[...].reshape(1, -1)


def whole_greeting(place):
    return place.greeting() + TensorSum.greeting()


def near_attend(
    nb,
    lat_ref, image_ref, lg_ref, ls_ref, mg_ref, ms_ref, cot_ref, med_hbm, wq_hbm, wk_hbm, wv_hbm,
    x_ref, q_all, kh_ref, kt_ref, vh_ref, lkh_ref, lkt_ref, lvh_ref, att_ref, lse_ref, cot_all,
    med, wq, wk, wv, vt, lvt, mine, give, got, send, into, mstat, gstat, rstat, sstat, istat,
    g_sems, a_sems, s_sems, c_sems, w_sems,
):
    place = Place(nb)
    lat_rows = lat_ref.shape[0]
    med_rows = med.shape[0]
    heads = kh_ref.shape[0]
    images_here = lat_rows // LATENTS
    loads = {
        name: pltpu.make_async_copy(source, target, w_sems.at[n])
        for n, (name, source, target) in enumerate(
            (("q", wq_hbm, wq), ("k", wk_hbm, wk), ("m", med_hbm, med), ("v", wv_hbm, wv))
        )
    }
    for load in loads.values():
        load.start()
    greet(whole_greeting(place))
    spread = Spread(place, cot_ref, cot_all, c_sems)
    spread.start()

    xhat, _ = normalised(lat_ref[...].astype(F32))
    ln = (xhat * line_of(lg_ref) + line_of(ls_ref)).astype(BF)
    x_ref[med_rows:, :] = ln

    def heads_t(rows, ref):
        turned = rows.T
        for h in range(heads):
            ref[h] = turned[h * HEAD_DIM : (h + 1) * HEAD_DIM].astype(BF)

    def heads_n(rows, ref):
        for h in range(heads):
            ref[h] = rows[:, h * HEAD_DIM : (h + 1) * HEAD_DIM].astype(BF)

    loads["q"].wait()
    heads_t(dot_nn(ln, wq[...]) * SCALE, q_all.at[place.me])
    gather = Gather(place, q_all, g_sems)
    gather.start()
    spread.relay_z()
    loads["k"].wait()
    lk = dot_nn(ln, wk[...])
    heads_n(lk, lkh_ref)
    heads_t(lk, lkt_ref)
    loads["m"].wait()

    med_gain, med_shift = line_of(mg_ref), line_of(ms_ref)

    def norm_rows(i, carry):
        rows = pl.ds(pl.multiple_of(i * 128, 128), 128)
        hat, _ = normalised(med[rows, :].astype(F32))
        x_ref[rows, :] = (hat * med_gain + med_shift).astype(BF)
        return carry

    lax.fori_loop(0, med_rows // 128, norm_rows, 0)
    mk = dot_nn(x_ref[0:med_rows, :], wk[...])
    heads_n(mk, kh_ref)
    heads_t(mk, kt_ref)
    gather.relay()
    spread.relay_y()
    loads["v"].wait()
    mv = dot_nn(x_ref[0:med_rows, :], wv[...])
    heads_n(mv, vh_ref)
    heads_t(mv, vt)
    lv = dot_nn(ln, wv[...])
    heads_n(lv, lvh_ref)
    heads_t(lv, lvt)
    row_image = lax.broadcasted_iota(jnp.int32, (lat_rows, lat_rows), 0) // LATENTS
    col_image = lax.broadcasted_iota(jnp.int32, (lat_rows, lat_rows), 1) // LATENTS
    same = row_image == col_image
    own = []
    for h in range(heads):
        scores = jnp.where(same, dot_nn(lkh_ref[h], q_all[place.me, h]), NEG_FILL)
        top = jnp.max(scores, axis=0, keepdims=True)
        weights = jnp.exp(scores - top)
        total = jnp.sum(weights, axis=0, keepdims=True)
        own.append((top, total, dot_nn(lvt[h], weights.astype(BF))))
    gather.finish()

    fold = Fold(place, lambda o: give.at[o], got, lambda o: send.at[o], into, a_sems)
    stats = Fold(place, lambda o: gstat.at[o], rstat, lambda o: sstat.at[o], istat, s_sems)
    image = image_columns(image_ref, med_rows, lat_rows)
    image = jnp.concatenate([image, image], axis=1)

    def piece(acc_ref, stat_ref, at):
        return [
            (
                stat_ref[at, h : h + 1, :],
                stat_ref[at, heads + h : heads + h + 1, :],
                acc_ref[at, h].astype(F32),
            )
            for h in range(heads)
        ]

    def merged(left, right):
        both = []
        for (lt, ll, la), (rt, rl, ra) in zip(left, right):
            top = jnp.maximum(lt, rt)
            lf, rf = jnp.exp(lt - top), jnp.exp(rt - top)
            both.append((top, ll * lf + rl * rf, la * lf + ra * rf))
        return both

    def pass_on(d):
        o = place.outer_to(d)
        stats.pair(o).wait_recv()
        fold.pair(o).wait_recv()
        both = merged(piece(mine, mstat, o), piece(got, rstat, o))
        if d == 0:
            return both
        for h, (top, total, acc) in enumerate(both):
            sstat[o, h : h + 1, :] = top
            sstat[o, heads + h : heads + h + 1, :] = total
            send[o, h] = acc.astype(BF)
        stats.far(d).start()
        fold.far(d).start()
        return None

    order = [*range(1, place.no), 0]
    for step, d in enumerate(order):
        o = place.outer_to(d)
        sources = [2 * o + place.inner, 2 * o + 1 - place.inner]
        allowed = image == pair_lanes(place, sources, images_here, lat_rows)
        for h in range(heads):
            queries = jnp.concatenate([q_all[s, h] for s in sources], axis=1)
            scores = jnp.where(allowed, dot_nn(kh_ref[h], queries), NEG_FILL)
            top = jnp.max(scores, axis=0, keepdims=True)
            weights = jnp.exp(scores - top)
            total = jnp.sum(weights, axis=0, keepdims=True)
            acc = dot_nn(vt[h], weights.astype(BF))
            mine[o, h] = acc[:, 0:lat_rows]
            give[o, h] = acc[:, lat_rows:].astype(BF)
            for ref, part in ((mstat, slice(0, lat_rows)), (gstat, slice(lat_rows, 2 * lat_rows))):
                ref[o, h : h + 1, :] = top[:, part]
                ref[o, heads + h : heads + h + 1, :] = total[:, part]
        stats.pair(o).start()
        fold.pair(o).start()
        if step == 0:
            spread.relay_x()
        else:
            pass_on(order[step - 1])
    result = merged(own, pass_on(0))
    for d in range(1, place.no):
        stats.far(d).wait_recv()
        fold.far(d).wait_recv()
        result = merged(result, piece(into, istat, d))
    lse_ref[...] = jnp.zeros_like(lse_ref)
    for h, (top, total, acc) in enumerate(result):
        att_ref[h] = acc / total
        lse_ref[h : h + 1, :] = top + jnp.log(total)
    fold.finish()
    stats.finish()
    spread.finish()


def near_feed(
    nb,
    att_ref, lse_ref, lat_ref, cot_ref, wo_ref, fg_ref, fs_ref, x_hbm, up_hbm, down_hbm,
    out_ref, mid_grad_ref, branch_ref, dot_ref, ld_ref, low_all, lns_ref, gain_ref, fn_all,
    up, down, hg, mid, fn, hidden, pre_grad, low_t, sum_buf, bufs, ln, ln_out,
    sems, w_sems, l_sems, f_sems, n_sems,
):
    place = Place(nb)
    med_rows = x_hbm.shape[0] - lat_ref.shape[0]
    lat_rows = lat_ref.shape[0]
    loads = [
        pltpu.make_async_copy(x_hbm.at[pl.ds(med_rows, lat_rows)], ln, w_sems.at[0]),
        pltpu.make_async_copy(down_hbm, down, w_sems.at[1]),
        pltpu.make_async_copy(up_hbm, up, w_sems.at[2]),
    ]
    for load in loads:
        load.start()
    heads = att_ref.shape[0]
    ff_here = up.shape[1]
    ff_tile = math.gcd(ff_here, 512)
    greet(whole_greeting(place))
    for h in range(heads):
        low_t[h * HEAD_DIM : (h + 1) * HEAD_DIM, :] = att_ref[h]
    low_all[place.me] = low_t[...].T.astype(BF)
    low_gather = Gather(place, low_all, l_sems)
    low_gather.start()
    low = low_all[place.me]

    def put(column, tile):
        sum_buf[:, pl.ds(column, tile.shape[1])] = tile.astype(F32)

    def tile_sum(n, tile_of):
        return TensorSum(bufs.at[n], sems.at[n], tile_of)

    width = bufs.shape[-1]
    branch = tile_sum(0, lambda c: dot_nn(low, wo_ref[:, pl.ds(c, width)]))
    branch.give()
    branch.cross()
    loads[0].wait()
    slices = Slices(place, ln_out, lns_ref, n_sems)
    slices.cut(ln[...])
    slices.start()
    loads[1].wait()
    cot = cot_ref[...]

    def back_hidden(i, carry):
        cols = pl.ds(pl.multiple_of(i * ff_tile, ff_tile), ff_tile)
        hg[:, cols] = dot_nt(cot, down[cols, :])
        return carry

    branch.back()
    lax.fori_loop(0, ff_here // ff_tile, back_hidden, 0)
    branch.finish(put)
    low_gather.relay()
    mid[...] = lat_ref[...].astype(F32) + sum_buf[...]
    xhat, rstd = normalised(mid[...])
    normed = (xhat * line_of(fg_ref) + line_of(fs_ref)).astype(BF)
    fn[...] = normed
    spread = Spread(place, fn, fn_all, f_sems, share=False)
    spread.start()
    loads[2].wait()

    def inner(i, carry):
        cols = pl.ds(pl.multiple_of(i * ff_tile, ff_tile), ff_tile)
        pre = dot_nn(normed, up[:, cols])
        value, slope = gelu_pair(pre)
        hidden[:, cols] = value.astype(BF)
        pre_grad[:, cols] = (hg[:, cols] * slope).astype(BF)
        return carry

    lax.fori_loop(0, ff_here // ff_tile, inner, 0)
    grads = tile_sum(1, lambda c: dot_nt(pre_grad[...], up[pl.ds(c, width), :]))
    feed = tile_sum(2, lambda c: dot_nn(hidden[...], down[:, pl.ds(c, width)]))
    grads.give()
    grads.cross()
    feed.give()
    slices.relay()
    grads.back()
    spread.relay_z()
    feed.cross()
    grads.finish(put)
    fng = sum_buf[...]
    xhat, rstd = normalised(mid[...])
    mid_grad = cot_ref[...].astype(F32) + norm_back(fng, line_of(fg_ref), xhat, rstd)
    mid_grad_ref[...] = mid_grad
    branch_ref[...] = mid_grad.astype(BF)
    gain_ref[...] = jnp.zeros_like(gain_ref)
    gain_ref[0:1, :] = jnp.sum(fng * xhat, axis=0, keepdims=True)
    gain_ref[1:2, :] = jnp.sum(fng, axis=0, keepdims=True)
    back = dot_nt(wo_ref[...], branch_ref[...])
    ld_ref[...] = lse_ref[...]
    for h in range(heads):
        piece = back[h * HEAD_DIM : (h + 1) * HEAD_DIM, :].astype(BF)
        dot_ref[h] = piece
        ld_ref[heads + h : heads + h + 1, :] = jnp.sum(
            piece.astype(F32) * att_ref[h], axis=0, keepdims=True
        )
    feed.back()
    feed.finish(put)
    out_ref[...] = (mid[...] + sum_buf[...]).astype(BF)
    low_gather.finish()
    slices.finish()
    spread.relay_y()
    spread.finish()


def near_back(
    nb,
    dot_in, ld_in, lkh_ref, lkt_ref, lvh_ref, q_all, kh_ref, kt_ref, vh_ref, branch_ref, lg_ref,
    fgain_ref, image_ref,
    wq_hbm, wk_hbm, wv_hbm, up_hbm, down_hbm, x_hbm, low_hbm, lns_hbm, mid_grad_hbm, lat_hbm, med_hbm,
    fn_part, cot_all,
    msum, lgrad_ref, qg_ref, kg_ref, vg_ref, og_ref, ug_ref, down_t, gains_ref,
    wq, wk, wv, up, down, x_ref, low_all, lns_ref, mid_grad_ref, lat_ref, med_ref, fn_all, rows_buf,
    dot_all, ld_all, dk, dv, dq_own, dq_mine, dq_give, dq_got,
    dq_send, dq_into, dq_all, turn, yall, part, pair_in, far_in, br_out, br_in, gain_out, gain_in,
    branch_sum, med_bufs, lat_bufs,
    g_sems, l_sems, x_sems, p_sems, q_sems, n_sems, t_sems, b_sems, w_sems, r_sems, h_sems, e_sems,
):
    place = Place(nb)
    lat_rows = lat_ref.shape[0]
    med_rows, model = med_ref.shape
    heads = kh_ref.shape[0]
    half_heads = heads // 2
    inner = heads * HEAD_DIM
    images_here = lat_rows // LATENTS
    own_rows = model // nb
    weights = [
        pltpu.make_async_copy(source, target, w_sems.at[n])
        for n, (source, target) in enumerate(
            (
                (up_hbm, up), (down_hbm, down), (x_hbm, x_ref), (wk_hbm, wk), (wv_hbm, wv),
                (wq_hbm, wq), (med_hbm, med_ref), (lat_hbm, lat_ref), (mid_grad_hbm, mid_grad_ref),
                (low_hbm, low_all), (lns_hbm, lns_ref),
            )
        )
    ]
    dot_all[place.me] = dot_in[...]
    ld_all[place.me] = ld_in[...]
    greet(whole_greeting(place))
    gather = Gather(place, dot_all, g_sems)
    gather_ld = Gather(place, ld_all, l_sems)
    gather_ld.start()
    gather.start()

    share = Share(place, fn_part, fn_all, h_sems, e_sems)
    share.start()

    def step_blocks(j):
        base = 2 * place.outer_from(j)
        return base + place.inner, base + 1 - place.inner

    def row_loads(j):
        slot = j % 2
        return [
            pltpu.make_async_copy(cot_all.at[s], rows_buf.at[slot, n], r_sems.at[slot, n])
            for n, s in enumerate(step_blocks(j))
        ]

    for load in row_loads(0):
        load.start()
    for load in weights:
        load.start()

    row_image = lax.broadcasted_iota(jnp.int32, (lat_rows, lat_rows), 0) // LATENTS
    col_image = lax.broadcasted_iota(jnp.int32, (lat_rows, lat_rows), 1) // LATENTS
    same = row_image == col_image

    def grads_of(keys, values, queries, grads, lse, delta, allowed):
        scores = jnp.where(allowed, dot_nn(keys, queries), NEG_FILL)
        probs = jnp.exp(scores - lse)
        score_grad = (probs * (dot_nn(values, grads) - delta)).astype(BF)
        return probs.astype(BF), score_grad

    for h in range(heads):
        queries, grads = q_all[place.me, h], dot_in[h]
        probs, score_grad = grads_of(
            lkh_ref[h], lvh_ref[h], queries, grads,
            ld_in[h : h + 1, :], ld_in[heads + h : heads + h + 1, :], same,
        )
        dk[h, :, 0:lat_rows] = dot_nt(queries, score_grad)
        dv[h, :, 0:lat_rows] = dot_nt(grads, probs)
        dq_own[h] = dot_nn(lkt_ref[h], score_grad)

    def put_rows(half, first, rows):
        for k, acc in enumerate((dk, dv)):
            for n in range(half_heads):
                at = (k * half_heads + n) * HEAD_DIM
                turn[at : at + HEAD_DIM, 0:rows] = acc[half * half_heads + n, :, 0:rows]
        yall[half, first : first + rows, :] = turn[:, 0:rows].T.astype(BF)

    for half in range(2):
        put_rows(half, med_rows, lat_rows)
    slices = Slices(place, br_out, br_in, b_sems)
    slices.cut(branch_ref[...])
    slices.start()

    pick = (
        lax.broadcasted_iota(jnp.int32, (own_rows, model), 1)
        == lax.broadcasted_iota(jnp.int32, (own_rows, model), 0) + place.me * own_rows
    )
    pick = jnp.where(pick, 1.0, 0.0).astype(BF)
    ff_here = up.shape[1]
    ff_tile = math.gcd(ff_here, 512)

    def feed_step(j):
        for load in row_loads(j):
            load.wait()
        if j + 1 < place.no:
            for load in row_loads(j + 1):
                load.start()
        share.ready(j)
        fn_rows = jnp.concatenate([fn_all[b].reshape(lat_rows, model) for b in step_blocks(j)], axis=0)
        cot_rows = rows_buf[j % 2].reshape(2 * lat_rows, model)
        fn_own = dot_nt(pick, fn_rows).astype(BF)
        cot_own = dot_nt(pick, cot_rows).astype(BF)

        def tile(i, carry):
            cols = pl.ds(pl.multiple_of(i * ff_tile, ff_tile), ff_tile)
            value, slope = gelu_pair(dot_nn(fn_rows, up[:, cols]))
            grad = (dot_nt(cot_rows, down[cols, :]) * slope).astype(BF)
            up_part = dot_nn(fn_own, grad)
            down_part = dot_nn(cot_own, value.astype(BF))
            if j == 0:
                ug_ref[:, cols] = up_part
                down_t[:, cols] = down_part
            else:
                ug_ref[:, cols] += up_part
                down_t[:, cols] += down_part
            return carry

        lax.fori_loop(0, ff_here // ff_tile, tile, 0)

    steps = place.no
    share.forward(0)
    for load in weights[:2]:
        load.wait()
    if steps > 1:
        share.forward(1)
    feed_step(0)
    gather_ld.relay()
    gather.relay()
    for step in range(2, steps):
        share.forward(step)
    done = 1
    if steps > 2:
        feed_step(1)
        done = 2
    gather_ld.finish()
    gather.finish()

    dq_fold = Fold(place, lambda o: dq_give.at[o], dq_got, lambda o: dq_send.at[o], dq_into, x_sems)
    folds = [
        Fold(
            place, lambda o, f=f: part.at[f, 2 * o + 1 - place.inner], pair_in.at[f],
            lambda o, f=f: part.at[f, 2 * o + place.inner], far_in.at[f], p_sems.at[f],
        )
        for f in range(2)
    ]
    image = image_columns(image_ref, med_rows, lat_rows)
    image = jnp.concatenate([image, image], axis=1)
    order = [*range(1, place.no), 0]

    def pass_queries(d):
        o = place.outer_to(d)
        dq_fold.pair(o).wait_recv()
        for h in range(heads):
            dq_send[o, h] = (dq_mine[o, h] + dq_got[o, h].astype(F32)).astype(BF)
        dq_fold.far(d).start()

    for step, d in enumerate(order):
        o = place.outer_to(d)
        sources = [2 * o + place.inner, 2 * o + 1 - place.inner]
        allowed = image == pair_lanes(place, sources, images_here, lat_rows)
        for h in range(heads):
            queries = jnp.concatenate([q_all[s, h] for s in sources], axis=1)
            grads = jnp.concatenate([dot_all[s, h] for s in sources], axis=1)
            lse = jnp.concatenate([ld_all[s, h : h + 1, :] for s in sources], axis=1)
            delta = jnp.concatenate(
                [ld_all[s, heads + h : heads + h + 1, :] for s in sources], axis=1
            )
            probs, score_grad = grads_of(kh_ref[h], vh_ref[h], queries, grads, lse, delta, allowed)
            key_part = dot_nt(queries, score_grad)
            value_part = dot_nt(grads, probs)
            dk[h] = key_part if step == 0 else dk[h] + key_part
            dv[h] = value_part if step == 0 else dv[h] + value_part
            dq = dot_nn(kt_ref[h], score_grad)
            dq_mine[o, h] = dq[:, 0:lat_rows]
            dq_give[o, h] = dq[:, lat_rows:].astype(BF)
        dq_fold.pair(o).start()
        if step:
            pass_queries(order[step - 1])

    chunk = 2 * own_rows * max(1, 128 // math.gcd(128, 2 * own_rows))
    per_chunk = chunk // own_rows

    def weight_parts(half):
        put_rows(half, 0, med_rows)
        for c in range(model // chunk):
            value = dot_tn(x_ref[:, c * chunk : (c + 1) * chunk], yall[half])
            for n in range(per_chunk):
                part[half, c * per_chunk + n] = value[n * own_rows : (n + 1) * own_rows].astype(BF)
            for o in range(c * per_chunk // 2, (c + 1) * per_chunk // 2):
                folds[half].pair(o).start()

    def both(half, o):
        return part[half, 2 * o + place.inner].astype(F32) + pair_in[half, o].astype(F32)

    def pass_on(half):
        for d in range(1, place.no):
            o = place.outer_to(d)
            folds[half].pair(o).wait_recv()
            part[half, 2 * o + place.inner] = both(half, o).astype(BF)
            folds[half].far(d).start()

    for load in weights[2:]:
        load.wait()
    weight_parts(0)
    weight_parts(1)

    med_tile, lat_tile = med_bufs.shape[-1], lat_bufs.shape[-1]
    width = half_heads * HEAD_DIM

    def back_rows(first, rows, tile):
        def tile_of(column):
            cols = pl.ds(column, tile)
            total = None
            for half in range(2):
                values = yall[half, first : first + rows, :]
                for k, weight in enumerate((wk, wv)):
                    term = dot_nt(
                        values[:, k * width : (k + 1) * width],
                        weight[cols, half * width : (half + 1) * width],
                    )
                    total = term if total is None else total + term
            return total

        return tile_of

    med_sum = TensorSum(med_bufs, t_sems.at[0], back_rows(0, med_rows, med_tile))
    med_sum.give()
    med_sum.cross()
    o = place.outer
    dq_fold.pair(o).wait_recv()
    for h in range(heads):
        dq_own[h] = dq_own[h] + dq_mine[o, h] + dq_got[o, h].astype(F32)
    for d in range(1, place.no):
        dq_fold.far(d).wait_recv()
        for h in range(heads):
            dq_own[h] = dq_own[h] + dq_into[d, h].astype(F32)
    for h in range(heads):
        turn[h * HEAD_DIM : (h + 1) * HEAD_DIM, 0:lat_rows] = dq_own[h]
    dq_all[place.me] = turn[:, 0:lat_rows].T.astype(BF)
    dq_gather = Gather(place, dq_all, q_sems)
    dq_gather.start()

    def lat_tile_of(column):
        cols = pl.ds(column, lat_tile)
        return (
            back_rows(med_rows, lat_rows, lat_tile)(column)
            + dot_nt(dq_all[place.me], wq[cols, :]) * SCALE
        )

    lat_sum = TensorSum(lat_bufs, t_sems.at[1], lat_tile_of)
    lat_sum.give()
    pass_on(0)
    slices.relay()
    lat_sum.cross()
    med_sum.back()
    dq_gather.relay()
    for step in range(done, steps):
        feed_step(step)
        if step == done:
            pass_on(1)
    if done == steps:
        pass_on(1)
    share.finish()

    def put(column, tile):
        msum[:, pl.ds(column, tile.shape[1])] = tile

    def put_lat(column, tile):
        branch_sum[:, pl.ds(column, tile.shape[1])] = tile

    lat_sum.back()
    med_sum.finish(put)

    def norm_rows(i, carry):
        rows = pl.ds(pl.multiple_of(i * 128, 128), 128)
        xhat, _ = normalised(med_ref[rows, :].astype(F32))
        q = msum[rows, :].astype(F32)
        return (
            carry[0] + jnp.sum(q * xhat, axis=0, keepdims=True),
            carry[1] + jnp.sum(q, axis=0, keepdims=True),
        )

    zero = jnp.zeros((1, model), F32)
    med_gain = lax.fori_loop(0, med_rows // 128, norm_rows, (zero, zero))
    lat_sum.finish(put_lat)
    xhat, rstd = normalised(lat_ref[...].astype(F32))
    q = branch_sum[...].astype(F32)
    lgrad_ref[...] = mid_grad_ref[...] + norm_back(q, line_of(lg_ref), xhat, rstd)
    all_rows = [
        *med_gain,
        jnp.sum(q * xhat, axis=0, keepdims=True),
        jnp.sum(q, axis=0, keepdims=True),
        fgain_ref[0:1, :],
        fgain_ref[1:2, :],
    ]
    for o in range(nb):
        for n, line in enumerate(all_rows):
            gain_out[o, n : n + 1, :] = line[:, o * own_rows : (o + 1) * own_rows]

    def gain_copy(d):
        return remote(
            gain_out.at[place.far(d)], gain_in.at[d], n_sems.at[0, d], n_sems.at[1, d],
            {"blk": place.far(d)},
        )

    for d in range(1, nb):
        gain_copy(d).start()
    slices.finish()
    dq_gather.finish()
    all_rows_of = lambda ref: ref[...].reshape(nb * lat_rows, -1)
    og_ref[...] = dot_tn(all_rows_of(br_in), all_rows_of(low_all))
    qg_ref[...] = dot_tn(all_rows_of(lns_ref), all_rows_of(dq_all)) * SCALE
    for half in range(2):
        folds[half].pair(place.outer).wait_recv()
        total = both(half, place.outer)
        for d in range(1, place.no):
            folds[half].far(d).wait_recv()
            total = total + far_in[half, d].astype(F32)
        for n in range(half_heads):
            at = (half * half_heads + n) * HEAD_DIM
            kg_ref[:, at : at + HEAD_DIM] = total[:, n * HEAD_DIM : (n + 1) * HEAD_DIM]
            vg_ref[:, at : at + HEAD_DIM] = total[:, width + n * HEAD_DIM : width + (n + 1) * HEAD_DIM]
    gains = gain_out[place.me]
    for d in range(1, nb):
        gain_copy(d).wait_recv()
        gains = gains + gain_in[d]
    gains_ref[...] = gains
    for d in range(1, nb):
        gain_copy(d).wait_send()
    dq_fold.finish()
    for fold in folds:
        fold.finish()


def near_call(kernel, out_shapes, scratch, collective_id, args, any_args, any_outs=()):
    vmem = pl.BlockSpec(memory_space=pltpu.VMEM)
    anywhere = pl.BlockSpec(memory_space=pl.ANY)
    return pl.pallas_call(
        kernel,
        out_shape=[jax.ShapeDtypeStruct(s, d) for s, d in (*out_shapes, *any_outs)],
        in_specs=[vmem] * len(args) + [anywhere] * len(any_args),
        out_specs=[vmem] * len(out_shapes) + [anywhere] * len(any_outs),
        scratch_shapes=scratch,
        compiler_params=pltpu.CompilerParams(
            collective_id=collective_id, has_side_effects=True, vmem_limit_bytes=VMEM_LIMIT
        ),
    )(*args, *any_args)


def per_device(
    latents, media, query_weight, key_weight, value_weight, out_weight, up_weight, down_weight,
    media_gain, media_shift, latent_gain, latent_shift, feed_gain, feed_shift, cotangent, media_image,
):
    nb = lax.axis_size("blk")
    lat_rows, model = latents.shape
    med_rows = media.shape[0]
    inner = query_weight.shape[1]
    heads = inner // HEAD_DIM
    ff_here = up_weight.shape[1]
    no = nb // 2
    own_rows = model // nb
    dma = pltpu.SemaphoreType.DMA
    vm = pltpu.VMEM
    hd = HEAD_DIM
    half, quarter = lat_rows // 2, lat_rows // 4

    (x, q_all, kh, kt, vh, lkh, lkt, lvh, att, lse, cot_all) = near_call(
        functools.partial(near_attend, nb),
        [
            ((med_rows + lat_rows, model), BF), ((nb, heads, hd, lat_rows), BF),
            ((heads, med_rows, hd), BF), ((heads, hd, med_rows), BF), ((heads, med_rows, hd), BF),
            ((heads, lat_rows, hd), BF), ((heads, hd, lat_rows), BF), ((heads, lat_rows, hd), BF),
            ((heads, hd, lat_rows), F32), ((2 * heads, lat_rows), F32), ((nb, 4, quarter, model), BF),
        ],
        [
            vm((med_rows, model), BF), vm((model, inner), BF), vm((model, inner), BF),
            vm((model, inner), BF), vm((heads, hd, med_rows), BF), vm((heads, hd, lat_rows), BF),
            vm((no, heads, hd, lat_rows), F32), *[vm((no, heads, hd, lat_rows), BF)] * 4,
            *[vm((no, 2 * heads, lat_rows), F32)] * 5,
            dma((2, 2, no)), dma((2, 2, no)), dma((2, 2, no)), dma((4, 2, 4 * no)), dma((4,)),
        ],
        0,
        (latents, media_image, latent_gain, latent_shift, media_gain, media_shift, cotangent),
        (media, query_weight, key_weight, value_weight),
    )

    tile = 256
    tiles = model // 2 // tile
    (resampled, mid_grad, branch, dot, ld, low_all, lns, feed_gains, fn_part) = near_call(
        functools.partial(near_feed, nb),
        [
            ((lat_rows, model), BF), ((lat_rows, model), F32), ((lat_rows, model), BF),
            ((heads, hd, lat_rows), BF), ((2 * heads, lat_rows), F32), ((nb, lat_rows, inner), BF),
            ((nb, 2, half, own_rows), BF), ((8, model), F32), ((nb, 4, quarter, model), BF),
        ],
        [
            vm((model, ff_here), BF), vm((ff_here, model), BF), vm((lat_rows, ff_here), F32),
            vm((lat_rows, model), F32), vm((lat_rows, model), BF), vm((lat_rows, ff_here), BF),
            vm((lat_rows, ff_here), BF), vm((inner, lat_rows), F32), vm((lat_rows, model), F32),
            vm((3, 6, tiles, lat_rows, tile), BF), vm((lat_rows, model), BF),
            vm((nb, 2, half, own_rows), BF),
            dma((3, 3, 2, tiles)), dma((3,)), dma((2, 2, no)), dma((2, 2, no)), dma((2, 2, nb)),
        ],
        1,
        (att, lse, latents, cotangent, out_weight, feed_gain, feed_shift),
        (x, up_weight, down_weight),
    )

    results = near_call(
        functools.partial(near_back, nb),
        [
            ((med_rows, model), BF), ((lat_rows, model), F32), ((own_rows, inner), F32),
            ((own_rows, inner), F32), ((own_rows, inner), F32), ((own_rows, inner), F32),
            ((own_rows, ff_here), F32), ((own_rows, ff_here), F32), ((8, own_rows), F32),
        ],
        [
            vm((model, inner), BF), vm((model, inner), BF), vm((model, inner), BF),
            vm((model, ff_here), BF), vm((ff_here, model), BF), vm((med_rows + lat_rows, model), BF),
            vm((nb, lat_rows, inner), BF), vm((nb, 2, half, own_rows), BF), vm((lat_rows, model), F32),
            vm((lat_rows, model), BF), vm((med_rows, model), BF), vm((nb, 4, quarter, model), BF),
            vm((2, 2, lat_rows, model), BF),
            vm((nb, heads, hd, lat_rows), BF),
            vm((nb, 2 * heads, lat_rows), F32), vm((heads, hd, med_rows), F32),
            vm((heads, hd, med_rows), F32), vm((heads, hd, lat_rows), F32),
            vm((no, heads, hd, lat_rows), F32), *[vm((no, heads, hd, lat_rows), BF)] * 4,
            vm((nb, lat_rows, inner), BF), vm((inner, med_rows), F32),
            vm((2, med_rows + lat_rows, inner), BF), vm((2, nb, own_rows, inner), BF),
            vm((2, no, own_rows, inner), BF), vm((2, no, own_rows, inner), BF),
            vm((nb, 2, half, own_rows), BF), vm((nb, 2, half, own_rows), BF),
            vm((nb, 8, own_rows), F32), vm((nb, 8, own_rows), F32), vm((lat_rows, model), BF),
            vm((6, tiles, med_rows, tile), BF), vm((6, tiles, lat_rows, tile), BF),
            dma((2, 2, no)), dma((2, 2, no)), dma((2, 2, no)), dma((2, 2, 2, no)), dma((2, 2, no)),
            dma((2, nb)), dma((2, 3, 2, tiles)), dma((2, 2, nb)), dma((11,)), dma((2, 2)),
            dma((3, 2, 2 * no)), dma((2 * no,)),
        ],
        2,
        (dot, ld, lkh, lkt, lvh, q_all, kh, kt, vh, branch, latent_gain, feed_gains, media_image),
        (
            query_weight, key_weight, value_weight, up_weight, down_weight, x, low_all, lns,
            mid_grad, latents, media, fn_part, cot_all.reshape(nb, lat_rows, model),
        ),
    )
    return last_step(media, media_gain, resampled, *results)


def last_kernel(media_ref, sum_ref, gain_ref, gains_ref, *refs):
    count = (len(refs) - 7) // 2
    moved, grad_ref = refs[0:count], refs[count]
    placed, gain_refs = refs[count + 1 : 2 * count + 1], refs[2 * count + 1 :]
    for source, target in zip(moved, placed, strict=True):
        target[...] = source[...]

    @pl.when(pl.program_id(0) == 0)
    def _():
        for n, ref in enumerate(gain_refs):
            ref[...] = gains_ref[n, :]

    xhat, rstd = normalised(media_ref[...].astype(F32))
    grad_ref[...] = norm_back(sum_ref[...].astype(F32), line_of(gain_ref), xhat, rstd)


def last_step(media, media_gain, resampled, media_sum, *rest):
    *moved, gains = (resampled, *rest)
    own_rows = gains.shape[1]
    steps = 4
    blocked = lambda v: pl.BlockSpec((v.shape[0] // steps, v.shape[1]), lambda i: (i, 0))
    gain_spec = pl.BlockSpec((own_rows,), lambda i: (0,))
    outs = pl.pallas_call(
        last_kernel,
        grid=(steps,),
        out_shape=[
            jax.ShapeDtypeStruct(media.shape, F32),
            *[jax.ShapeDtypeStruct(v.shape, v.dtype) for v in moved],
            *[jax.ShapeDtypeStruct((own_rows,), F32)] * 6,
        ],
        in_specs=[
            blocked(media), blocked(media_sum), pl.BlockSpec(media_gain.shape, lambda i: (0,)),
            pl.BlockSpec(gains.shape, lambda i: (0, 0)), *[blocked(v) for v in moved],
        ],
        out_specs=[blocked(media), *[blocked(v) for v in moved], *[gain_spec] * 6],
        compiler_params=pltpu.CompilerParams(vmem_limit_bytes=VMEM_LIMIT),
    )(media, media_sum, media_gain, gains, *moved)
    (
        media_grad, resampled, latent_grad, query_grad, key_grad, value_grad, out_turned, up_grad,
        down_turned, *gain_grads,
    ) = outs
    return (
        resampled, media_grad, latent_grad, query_grad, key_grad, value_grad, out_turned.T, up_grad,
        down_turned.T, *gain_grads,
    )


def solution(mesh):
    in_specs = (
        P("blk", None), P("blk", None), P(None, "tp"), P(None, "tp"), P(None, "tp"), P("tp", None),
        P(None, "tp"), P("tp", None), P(), P(), P(), P(), P(), P(), P("blk", None), P("blk"),
    )
    out_specs = (
        P("blk", None), P("blk", None), P("blk", None), P("blk", "tp"), P("blk", "tp"),
        P("blk", "tp"), P("tp", "blk"), P("blk", "tp"), P("tp", "blk"), P("blk"), P("blk"),
        P("blk"), P("blk"), P("blk"), P("blk"),
    )
    body = per_device if mesh.shape["blk"] <= 16 else per_device_many
    return jax.shard_map(
        body, mesh=mesh, in_specs=in_specs, out_specs=out_specs, check_vma=False
    )
```

```python
import functools
import math

import jax
import jax.numpy as jnp
from jax import lax
from jax.experimental import pallas as pl
from jax.experimental.pallas import tpu as pltpu
from jax.sharding import PartitionSpec as P

HEAD_DIM = 96
LATENTS = 64
NEG_FILL = -1e30
NORM_EPS = 1e-05
BF = jnp.bfloat16
F32 = jnp.float32
MESH = pl.DeviceIdType.MESH
VMEM_LIMIT = 60 * 1024 * 1024
SCALE = 1.0 / math.sqrt(HEAD_DIM)


def dot_nn(a, b):
    return jnp.dot(a, b, preferred_element_type=F32)


def dot_nt(a, b):
    return lax.dot_general(a, b, (((1,), (1,)), ((), ())), preferred_element_type=F32)


def dot_tn(a, b):
    return lax.dot_general(a, b, (((0,), (0,)), ((), ())), preferred_element_type=F32)


def normalised(x):
    centred = x - jnp.mean(x, axis=-1, keepdims=True)
    rstd = lax.rsqrt(jnp.mean(centred * centred, axis=-1, keepdims=True) + NORM_EPS)
    return centred * rstd, rstd


def norm_back(q, gain, xhat, rstd):
    qg = q * gain
    inner = jnp.mean(qg * xhat, axis=-1, keepdims=True)
    return (qg - jnp.mean(qg, axis=-1, keepdims=True) - xhat * inner) * rstd


def greet(devices):
    barrier = pltpu.get_barrier_semaphore()
    for device in devices:
        pl.semaphore_signal(barrier, inc=1, device_id=device, device_id_type=MESH)
    pl.semaphore_wait(barrier, len(devices))


def remote(src, dst, send_sem, recv_sem, device):
    return pltpu.make_async_remote_copy(
        src_ref=src,
        dst_ref=dst,
        send_sem=send_sem,
        recv_sem=recv_sem,
        device_id=device,
        device_id_type=MESH,
    )


class Place:
    def __init__(self, nb):
        self.nb = nb
        self.no = nb // 2
        self.me = lax.axis_index("blk")
        self.outer = self.me // 2
        self.inner = self.me % 2
        self.partner = 2 * self.outer + 1 - self.inner

    def far(self, d):
        return (self.me + d) % self.nb

    def near(self, d):
        return (self.me - d + self.nb) % self.nb

    def outer_to(self, d):
        return (self.outer + d) % self.no

    def outer_from(self, d):
        return (self.outer - d + self.no) % self.no

    def greeting(self):
        return [{"blk": self.far(d)} for d in range(1, self.nb)]


class Gather:
    def __init__(self, place, slots, sems):
        self.place, self.slots, self.sems = place, slots, sems

    def copy_z(self, d):
        pc = self.place
        slot = self.slots.at[pc.me]
        return remote(
            slot, slot, self.sems.at[0, 0, d], self.sems.at[0, 1, d],
            {"blk": 2 * pc.outer_to(d) + pc.inner},
        )

    def copy_y(self, d):
        pc = self.place
        slot = self.slots.at[2 * pc.outer_from(d) + pc.inner]
        return remote(
            slot, slot, self.sems.at[1, 0, d], self.sems.at[1, 1, d], {"blk": pc.partner}
        )

    def start(self):
        for d in range(1, self.place.no):
            self.copy_z(d).start()
        self.copy_y(0).start()

    def relay(self):
        pc = self.place
        for d in range(1, pc.no):
            arrived = self.slots.at[2 * pc.outer_from(d) + pc.inner]
            remote(
                arrived, arrived, self.sems.at[0, 0, d], self.sems.at[0, 1, d], {"blk": pc.partner}
            ).wait_recv()
            self.copy_y(d).start()

    def finish(self):
        pc = self.place
        for d in range(pc.no):
            slot = self.slots.at[2 * pc.outer_from(d) + 1 - pc.inner]
            remote(
                slot, slot, self.sems.at[1, 0, d], self.sems.at[1, 1, d], {"blk": pc.partner}
            ).wait_recv()
        for d in range(1, pc.no):
            self.copy_z(d).wait_send()
        for d in range(pc.no):
            self.copy_y(d).wait_send()


class Exchange:
    def __init__(self, place, out, into, sems, slot=lambda d: d):
        self.place, self.out, self.into, self.sems, self.slot = place, out, into, sems, slot

    def copy(self, d):
        return remote(
            self.out.at[self.slot(d)], self.into.at[d], self.sems.at[0, d], self.sems.at[1, d],
            {"blk": self.place.far(d)},
        )

    def start(self, d):
        self.copy(d).start()

    def wait_recv(self, d):
        self.copy(d).wait_recv()

    def finish_sends(self):
        for d in range(1, self.place.nb):
            self.copy(d).wait_send()


def lane_image(source, images_here, width):
    lane = lax.broadcasted_iota(jnp.int32, (1, width), 1)
    return source * images_here + lane // LATENTS


def attend_kernel(
    nb,
    lat_ref, med_ref, wq_ref, wk_ref, wv_ref, lg_ref, ls_ref, mg_ref, ms_ref, image_ref,
    ln_ref, mn_ref, q_all, kh_ref, kt_ref, vh_ref, lkh_ref, lkt_ref, lvh_ref, att_ref, lse_ref,
    vt, lvt, acc_out, acc_in, stat_out, stat_in, g_sems, a_sems, s_sems,
):
    place = Place(nb)
    lat_rows = lat_ref.shape[0]
    med_rows = med_ref.shape[0]
    heads = kh_ref.shape[0]
    images_here = lat_rows // LATENTS
    greet(place.greeting())

    xhat, _ = normalised(lat_ref[...].astype(F32))
    ln_ref[...] = (xhat * lg_ref[...] + ls_ref[...]).astype(BF)
    ln = ln_ref[...]

    def heads_t(rows, ref):
        turned = rows.T
        for h in range(heads):
            ref[h] = turned[h * HEAD_DIM : (h + 1) * HEAD_DIM].astype(BF)

    def heads_n(rows, ref):
        for h in range(heads):
            ref[h] = rows[:, h * HEAD_DIM : (h + 1) * HEAD_DIM].astype(BF)

    heads_t(dot_nn(ln, wq_ref[...]) * SCALE, q_all.at[place.me])
    gather = Gather(place, q_all, g_sems)
    gather.start()
    lk = dot_nn(ln, wk_ref[...])
    heads_n(lk, lkh_ref)
    heads_t(lk, lkt_ref)
    lv = dot_nn(ln, wv_ref[...])
    heads_n(lv, lvh_ref)
    heads_t(lv, lvt)

    def norm_rows(i, carry):
        rows = pl.ds(pl.multiple_of(i * 128, 128), 128)
        hat, _ = normalised(med_ref[rows, :].astype(F32))
        mn_ref[rows, :] = (hat * mg_ref[...] + ms_ref[...]).astype(BF)
        return carry

    lax.fori_loop(0, med_rows // 128, norm_rows, 0)
    mk = dot_nn(mn_ref[...], wk_ref[...])
    heads_n(mk, kh_ref)
    heads_t(mk, kt_ref)
    gather.relay()
    mv = dot_nn(mn_ref[...], wv_ref[...])
    heads_n(mv, vh_ref)
    heads_t(mv, vt)
    gather.finish()

    exchange = Exchange(place, acc_out, acc_in, a_sems)
    stats = Exchange(place, stat_out, stat_in, s_sems)
    image = image_ref[...]
    order = list(range(1, nb)) + [0]
    for g in range(nb // 2):
        pair = order[2 * g : 2 * g + 2]
        sources = [place.far(d) for d in pair]
        lanes = jnp.concatenate([lane_image(s, images_here, lat_rows) for s in sources], axis=1)
        allowed = image == lanes
        for h in range(heads):
            queries = jnp.concatenate([q_all[s, h] for s in sources], axis=1)
            scores = jnp.where(allowed, dot_nn(kh_ref[h], queries), NEG_FILL)
            top = jnp.max(scores, axis=0, keepdims=True)
            weights = jnp.exp(scores - top)
            total = jnp.sum(weights, axis=0, keepdims=True)
            acc = dot_nn(vt[h], weights.astype(BF)).astype(BF)
            for n, d in enumerate(pair):
                part = slice(n * lat_rows, (n + 1) * lat_rows)
                acc_out[d, h] = acc[:, part]
                stat_out[d, h : h + 1, :] = top[:, part]
                stat_out[d, heads + h : heads + h + 1, :] = total[:, part]
        for d in pair:
            if d:
                exchange.start(d)
                stats.start(d)

    row_image = lax.broadcasted_iota(jnp.int32, (lat_rows, lat_rows), 0) // LATENTS
    col_image = lax.broadcasted_iota(jnp.int32, (lat_rows, lat_rows), 1) // LATENTS
    same = row_image == col_image
    own = []
    for h in range(heads):
        scores = jnp.where(same, dot_nn(lkh_ref[h], q_all[place.me, h]), NEG_FILL)
        top = jnp.max(scores, axis=0, keepdims=True)
        weights = jnp.exp(scores - top)
        total = jnp.sum(weights, axis=0, keepdims=True)
        own.append((top, total, dot_nn(lvt[h], weights.astype(BF))))
    for d in range(1, nb):
        stats.wait_recv(d)
        exchange.wait_recv(d)
    lse_ref[...] = jnp.zeros_like(lse_ref)
    for h in range(heads):
        own_top, own_total, own_acc = own[h]
        tops = [
            (stat_out if d == 0 else stat_in)[d, h : h + 1, :] for d in range(nb)
        ]
        best = functools.reduce(jnp.maximum, tops, own_top)
        factor = jnp.exp(own_top - best)
        total = own_total * factor
        acc = own_acc * factor
        for d in range(nb):
            factor = jnp.exp(tops[d] - best)
            stat = stat_out if d == 0 else stat_in
            piece = acc_out if d == 0 else acc_in
            total = total + stat[d, heads + h : heads + h + 1, :] * factor
            acc = acc + piece[d, h].astype(F32) * factor
        att_ref[h] = acc / total
        lse_ref[h : h + 1, :] = best + jnp.log(total)
    exchange.finish_sends()
    stats.finish_sends()


class TensorSum:
    def __init__(self, bufs, sems, tile_of):
        self.bufs, self.sems, self.tile_of = bufs, sems, tile_of
        self.tiles, self.rows, self.tile = bufs.shape[1:]
        t = lax.axis_index("tp")
        self.core = t % 2
        self.chip = t // 2
        self.sibling = {"tp": 2 * self.chip + 1 - self.core}
        self.across = {"tp": 2 * (1 - self.chip) + self.core}

    @staticmethod
    def greeting():
        t = lax.axis_index("tp")
        core, chip = t % 2, t // 2
        return [{"tp": 2 * chip + 1 - core}, {"tp": 2 * (1 - chip) + core}]

    def column(self, half, j):
        return pl.multiple_of((half * self.tiles + j) * self.tile, 128)

    def copy(self, stage, j):
        return remote(
            self.bufs.at[2 * stage, j], self.bufs.at[2 * stage + 1, j],
            self.sems.at[stage, 0, j], self.sems.at[stage, 1, j],
            self.across if stage == 1 else self.sibling,
        )

    def give(self):
        for j in range(self.tiles):
            self.bufs[0, j] = self.tile_of(self.column(1 - self.core, j)).astype(BF)
            self.copy(0, j).start()

    def cross(self):
        for j in range(self.tiles):
            mine = self.tile_of(self.column(self.core, j))
            self.copy(0, j).wait_recv()
            self.bufs[2, j] = (mine + self.bufs[1, j].astype(F32)).astype(BF)
            self.copy(1, j).start()

    def back(self):
        for j in range(self.tiles):
            self.copy(1, j).wait_recv()
            self.bufs[4, j] = (self.bufs[2, j].astype(F32) + self.bufs[3, j].astype(F32)).astype(BF)
            self.copy(2, j).start()

    def finish(self, put):
        for j in range(self.tiles):
            put(self.column(self.core, j), self.bufs[4, j])
        for j in range(self.tiles):
            self.copy(2, j).wait_recv()
            put(self.column(1 - self.core, j), self.bufs[5, j])
        for stage in range(3):
            for j in range(self.tiles):
                self.copy(stage, j).wait_send()


def feed_kernel(
    att_ref, lse_ref, lat_ref, cot_ref, wo_ref, fg_ref, fs_ref, up_hbm, down_hbm,
    out_ref, mid_grad_ref, branch_ref, dot_ref, ld_ref, fn_ref, low_ref, gain_ref,
    up, down, hg, mid, hidden, pre_grad, low_t, sum_buf, bufs, sems, w_sems,
):
    loads = [
        pltpu.make_async_copy(up_hbm, up, w_sems.at[0]),
        pltpu.make_async_copy(down_hbm, down, w_sems.at[1]),
    ]
    for load in loads:
        load.start()
    heads = att_ref.shape[0]
    ff_here = up.shape[1]
    ff_tile = math.gcd(ff_here, 512)
    greet(TensorSum.greeting())
    for h in range(heads):
        low_t[h * HEAD_DIM : (h + 1) * HEAD_DIM, :] = att_ref[h]
    low_ref[...] = low_t[...].T.astype(BF)
    low = low_ref[...]

    def put(column, tile):
        sum_buf[:, pl.ds(column, tile.shape[1])] = tile.astype(F32)

    def tile_sum(n, tile_of):
        return TensorSum(bufs.at[n], sems.at[n], tile_of)

    width = bufs.shape[-1]
    branch = tile_sum(0, lambda c: dot_nn(low, wo_ref[:, pl.ds(c, width)]))
    branch.give()
    branch.cross()
    loads[1].wait()
    cot = cot_ref[...]

    def back_hidden(i, carry):
        cols = pl.ds(pl.multiple_of(i * ff_tile, ff_tile), ff_tile)
        hg[:, cols] = dot_nt(cot, down[cols, :])
        return carry

    lax.fori_loop(0, ff_here // ff_tile, back_hidden, 0)
    branch.back()
    branch.finish(put)
    mid[...] = lat_ref[...].astype(F32) + sum_buf[...]
    xhat, rstd = normalised(mid[...])
    fn_ref[...] = (xhat * fg_ref[...] + fs_ref[...]).astype(BF)
    fn = fn_ref[...]
    loads[0].wait()

    def inner(i, carry):
        cols = pl.ds(pl.multiple_of(i * ff_tile, ff_tile), ff_tile)
        pre = dot_nn(fn, up[:, cols])
        bell = 0.5 * (1.0 + lax.erf(pre * math.sqrt(0.5)))
        hidden[:, cols] = (pre * bell).astype(BF)
        slope = bell + pre * jnp.exp(-0.5 * pre * pre) * (1.0 / math.sqrt(2.0 * math.pi))
        pre_grad[:, cols] = (hg[:, cols] * slope).astype(BF)
        return carry

    lax.fori_loop(0, ff_here // ff_tile, inner, 0)
    grads = tile_sum(1, lambda c: dot_nt(pre_grad[...], up[pl.ds(c, width), :]))
    feed = tile_sum(2, lambda c: dot_nn(hidden[...], down[:, pl.ds(c, width)]))
    grads.give()
    grads.cross()
    feed.give()
    feed.cross()
    grads.back()
    feed.back()
    grads.finish(put)
    fng = sum_buf[...]
    xhat, rstd = normalised(mid[...])
    mid_grad = cot_ref[...].astype(F32) + norm_back(fng, fg_ref[...], xhat, rstd)
    mid_grad_ref[...] = mid_grad
    branch_ref[...] = mid_grad.astype(BF)
    gain_ref[...] = jnp.zeros_like(gain_ref)
    gain_ref[0:1, :] = jnp.sum(fng * xhat, axis=0, keepdims=True)
    gain_ref[1:2, :] = jnp.sum(fng, axis=0, keepdims=True)
    back = dot_nt(wo_ref[...], branch_ref[...])
    ld_ref[...] = lse_ref[...]
    for h in range(heads):
        piece = back[h * HEAD_DIM : (h + 1) * HEAD_DIM, :].astype(BF)
        dot_ref[h] = piece
        ld_ref[heads + h : heads + h + 1, :] = jnp.sum(
            piece.astype(F32) * att_ref[h], axis=0, keepdims=True
        )
    feed.finish(put)
    out_ref[...] = (mid[...] + sum_buf[...]).astype(BF)


def back_kernel(
    nb,
    q_all, dot_in, ld_in, kh_ref, kt_ref, vh_ref, lkh_ref, lkt_ref, lvh_ref, ln_ref, mn_ref,
    wq_ref, wk_ref, wv_ref, mid_grad_ref, lat_ref, med_ref, lg_ref, mg_ref, fgain_ref, image_ref,
    mgrad_ref, lgrad_ref, qg_ref, kg_ref, vg_ref, gains_ref,
    dot_all, ld_all, dk, dv, dq_own, dq_in, turn, xall, yall, dq_low, part, pair_in, far_in,
    gain_out, gain_in, med_bufs, lat_bufs,
    g_sems, l_sems, x_sems, y_sems, z_sems, n_sems, t_sems,
):
    place = Place(nb)
    lat_rows = lat_ref.shape[0]
    med_rows, model = med_ref.shape
    heads = kh_ref.shape[0]
    inner = heads * HEAD_DIM
    images_here = lat_rows // LATENTS
    dot_all[place.me] = dot_in[...]
    ld_all[place.me] = ld_in[...]
    greet(place.greeting() + TensorSum.greeting())
    gather = Gather(place, dot_all, g_sems)
    gather_ld = Gather(place, ld_all, l_sems)
    gather_ld.start()
    gather.start()

    row_image = lax.broadcasted_iota(jnp.int32, (lat_rows, lat_rows), 0) // LATENTS
    col_image = lax.broadcasted_iota(jnp.int32, (lat_rows, lat_rows), 1) // LATENTS
    same = row_image == col_image

    def turned(h, value, rows):
        turn[h * HEAD_DIM : (h + 1) * HEAD_DIM, 0:rows] = value

    def grads_of(h, keys, values, queries, grads, lse, delta, allowed):
        scores = jnp.where(allowed, dot_nn(keys, queries), NEG_FILL)
        probs = jnp.exp(scores - lse)
        score_grad = (probs * (dot_nn(values, grads) - delta)).astype(BF)
        return probs.astype(BF), score_grad

    for h in range(heads):
        queries, grads = q_all[place.me, h], dot_in[h]
        probs, score_grad = grads_of(
            h, lkh_ref[h], lvh_ref[h], queries, grads,
            ld_in[h : h + 1, :], ld_in[heads + h : heads + h + 1, :], same,
        )
        dk[h, :, 0:lat_rows] = dot_nt(queries, score_grad)
        dv[h, :, 0:lat_rows] = dot_nt(grads, probs)
        dq_own[h] = dot_nn(lkt_ref[h], score_grad)

    def put_rows(first, rows):
        for acc, column in ((dk, 0), (dv, inner)):
            for h in range(heads):
                turned(h, acc[h, :, 0:rows], rows)
            yall[first : first + rows, column : column + inner] = turn[:, 0:rows].T.astype(BF)

    put_rows(med_rows, lat_rows)
    xall[0:med_rows, :] = mn_ref[...]
    xall[med_rows:, :] = ln_ref[...]
    gather_ld.relay()
    gather.relay()
    gather_ld.finish()
    gather.finish()

    exchange = Exchange(place, dot_all, dq_in, x_sems, place.far)
    image = image_ref[...]
    order = list(range(1, nb)) + [0]
    for g in range(nb // 2):
        pair = order[2 * g : 2 * g + 2]
        sources = [place.far(d) for d in pair]
        lanes = jnp.concatenate([lane_image(s, images_here, lat_rows) for s in sources], axis=1)
        allowed = image == lanes
        for h in range(heads):
            queries = jnp.concatenate([q_all[s, h] for s in sources], axis=1)
            grads = jnp.concatenate([dot_all[s, h] for s in sources], axis=1)
            lse = jnp.concatenate([ld_all[s, h : h + 1, :] for s in sources], axis=1)
            delta = jnp.concatenate(
                [ld_all[s, heads + h : heads + h + 1, :] for s in sources], axis=1
            )
            probs, score_grad = grads_of(
                h, kh_ref[h], vh_ref[h], queries, grads, lse, delta, allowed
            )
            key_part = dot_nt(queries, score_grad)
            value_part = dot_nt(grads, probs)
            dk[h] = key_part if g == 0 else dk[h] + key_part
            dv[h] = value_part if g == 0 else dv[h] + value_part
            dq = dot_nn(kt_ref[h], score_grad)
            for n, d in enumerate(pair):
                piece = dq[:, n * lat_rows : (n + 1) * lat_rows]
                if d:
                    dot_all[place.far(d), h] = piece.astype(BF)
                else:
                    dq_own[h] = dq_own[h] + piece
        for d in pair:
            if d:
                exchange.start(d)
    put_rows(0, med_rows)

    med_tile, lat_tile = med_bufs.shape[-1], lat_bufs.shape[-1]

    def back_rows(first, rows, tile):
        def tile_of(column):
            cols = pl.ds(column, tile)
            values = yall[first : first + rows, :]
            return dot_nt(values[:, 0:inner], wk_ref[cols, :]) + dot_nt(
                values[:, inner:], wv_ref[cols, :]
            )

        return tile_of

    med_sum = TensorSum(med_bufs, t_sems.at[0], back_rows(0, med_rows, med_tile))
    med_sum.give()
    med_sum.cross()

    for d in range(1, nb):
        exchange.wait_recv(d)
    for h in range(heads):
        value = dq_own[h]
        for d in range(1, nb):
            value = value + dq_in[d, h].astype(F32)
        turned(h, value, lat_rows)
    dq_low[...] = turn[:, 0:lat_rows].T.astype(BF)

    own_rows = model // nb
    chunk = 2 * own_rows * max(1, 128 // math.gcd(128, 2 * own_rows))
    per_chunk = chunk // own_rows

    def pair_copy(o):
        return remote(
            part.at[2 * o + 1 - place.inner], pair_in.at[o], y_sems.at[0, o], y_sems.at[1, o],
            {"blk": place.partner},
        )

    def far_copy(o, d):
        return remote(
            part.at[2 * o + place.inner], far_in.at[d], z_sems.at[0, d], z_sems.at[1, d],
            {"blk": 2 * o + place.inner},
        )

    for c in range(model // chunk):
        cols = slice(c * chunk, (c + 1) * chunk)
        lnx = xall[med_rows:, cols]
        query_part = dot_tn(lnx, dq_low[...]) * SCALE
        other_part = dot_tn(xall[:, cols], yall[...])
        for n in range(per_chunk):
            owner = c * per_chunk + n
            rows = slice(n * own_rows, (n + 1) * own_rows)
            part[owner, 0:own_rows, 0:inner] = query_part[rows].astype(BF)
            part[owner, 0:own_rows, inner:] = other_part[rows].astype(BF)
        for o in range(c * per_chunk // 2, (c + 1) * per_chunk // 2):
            pair_copy(o).start()

    def lat_tile_of(column):
        cols = pl.ds(column, lat_tile)
        return (
            back_rows(med_rows, lat_rows, lat_tile)(column)
            + dot_nt(dq_low[...], wq_ref[cols, :]) * SCALE
        )

    lat_sum = TensorSum(lat_bufs, t_sems.at[1], lat_tile_of)
    lat_sum.give()
    lat_sum.cross()

    def own_part(o):
        return part[2 * o + place.inner].astype(F32) + pair_in[o].astype(F32)

    for d in range(1, place.no):
        o = place.outer_to(d)
        pair_copy(o).wait_recv()
        part[2 * o + place.inner] = own_part(o).astype(BF)
        far_copy(o, d).start()
    med_sum.back()

    def put(column, tile):
        xall[0 : tile.shape[0], pl.ds(column, tile.shape[1])] = tile

    med_sum.finish(put)
    gain_rows = [fgain_ref[0:1, :], fgain_ref[1:2, :]]

    def norm_rows(i, carry):
        rows = pl.ds(pl.multiple_of(i * 128, 128), 128)
        xhat, rstd = normalised(med_ref[rows, :].astype(F32))
        q = xall[rows, :].astype(F32)
        mgrad_ref[rows, :] = norm_back(q, mg_ref[...], xhat, rstd)
        return (
            carry[0] + jnp.sum(q * xhat, axis=0, keepdims=True),
            carry[1] + jnp.sum(q, axis=0, keepdims=True),
        )

    zero = jnp.zeros((1, model), F32)
    med_gain = lax.fori_loop(0, med_rows // 128, norm_rows, (zero, zero))
    lat_sum.back()
    lat_sum.finish(put)
    xhat, rstd = normalised(lat_ref[...].astype(F32))
    q = xall[0:lat_rows, :].astype(F32)
    lgrad_ref[...] = mid_grad_ref[...] + norm_back(q, lg_ref[...], xhat, rstd)
    all_rows = [
        *med_gain,
        jnp.sum(q * xhat, axis=0, keepdims=True),
        jnp.sum(q, axis=0, keepdims=True),
        *gain_rows,
    ]
    for o in range(nb):
        for n, row in enumerate(all_rows):
            gain_out[o, n : n + 1, :] = row[:, o * own_rows : (o + 1) * own_rows]

    def gain_copy(d):
        return remote(
            gain_out.at[place.far(d)], gain_in.at[d], n_sems.at[0, d], n_sems.at[1, d],
            {"blk": place.far(d)},
        )

    for d in range(1, nb):
        gain_copy(d).start()
    pair_copy(place.outer).wait_recv()
    total = own_part(place.outer)
    for d in range(1, place.no):
        far_copy(place.outer_to(d), d).wait_recv()
        total = total + far_in[d].astype(F32)
    qg_ref[...] = total[0:own_rows, 0:inner]
    kg_ref[...] = total[0:own_rows, inner : 2 * inner]
    vg_ref[...] = total[0:own_rows, 2 * inner :]
    gains = gain_out[place.me]
    for d in range(1, nb):
        gain_copy(d).wait_recv()
        gains = gains + gain_in[d]
    gains_ref[...] = gains
    exchange.finish_sends()
    for d in range(1, nb):
        gain_copy(d).wait_send()
    for o in range(place.no):
        pair_copy(o).wait_send()
    for d in range(1, place.no):
        far_copy(place.outer_to(d), d).wait_send()


def call(kernel, out_shapes, scratch, collective_id, any_args=(), args=()):
    vmem = pl.BlockSpec(memory_space=pltpu.VMEM)
    return pl.pallas_call(
        kernel,
        out_shape=[jax.ShapeDtypeStruct(s, d) for s, d in out_shapes],
        in_specs=[vmem] * len(args) + [pl.BlockSpec(memory_space=pl.ANY)] * len(any_args),
        out_specs=[vmem] * len(out_shapes),
        scratch_shapes=scratch,
        compiler_params=pltpu.CompilerParams(
            collective_id=collective_id, has_side_effects=True, vmem_limit_bytes=VMEM_LIMIT
        ),
    )(*args, *any_args)


def gelu_pair(pre):
    bell = 0.5 * (1.0 + lax.erf(pre * math.sqrt(0.5)))
    slope = bell + pre * jnp.exp(-0.5 * pre * pre) * (1.0 / math.sqrt(2.0 * math.pi))
    return pre * bell, slope


def per_device_many(
    latents, media, query_weight, key_weight, value_weight, out_weight, up_weight, down_weight,
    media_gain, media_shift, latent_gain, latent_shift, feed_gain, feed_shift, cotangent, media_image,
):
    nb = lax.axis_size("blk")
    me = lax.axis_index("blk")
    lat_rows, model = latents.shape
    med_rows = media.shape[0]
    inner = query_weight.shape[1]
    heads = inner // HEAD_DIM
    ff_here = up_weight.shape[1]
    no = nb // 2
    own_rows = model // nb
    own_pad = -(-own_rows // 16) * 16
    dma = pltpu.SemaphoreType.DMA
    vm = pltpu.VMEM
    row = lambda v: v.reshape(1, -1)
    image = media_image.reshape(-1, 1)
    hd = HEAD_DIM
    cot_all = lax.all_gather(cotangent, "blk", axis=0, tiled=True)

    (ln, mn, q_all, kh, kt, vh, lkh, lkt, lvh, att, lse) = call(
        functools.partial(attend_kernel, nb),
        [
            ((lat_rows, model), BF), ((med_rows, model), BF), ((nb, heads, hd, lat_rows), BF),
            ((heads, med_rows, hd), BF), ((heads, hd, med_rows), BF), ((heads, med_rows, hd), BF),
            ((heads, lat_rows, hd), BF), ((heads, hd, lat_rows), BF), ((heads, lat_rows, hd), BF),
            ((heads, hd, lat_rows), F32), ((2 * heads, lat_rows), F32),
        ],
        [
            vm((heads, hd, med_rows), BF), vm((heads, hd, lat_rows), BF),
            vm((nb, heads, hd, lat_rows), BF), vm((nb, heads, hd, lat_rows), BF),
            vm((nb, 2 * heads, lat_rows), F32), vm((nb, 2 * heads, lat_rows), F32),
            dma((2, 2, no)), dma((2, nb)), dma((2, nb)),
        ],
        0,
        args=(
            latents, media, query_weight, key_weight, value_weight, row(latent_gain),
            row(latent_shift), row(media_gain), row(media_shift), image,
        ),
    )

    tile = 256
    tiles = model // 2 // tile
    (resampled, mid_grad, branch, dot, ld, fn, low, feed_gains) = call(
        feed_kernel,
        [
            ((lat_rows, model), BF), ((lat_rows, model), F32), ((lat_rows, model), BF),
            ((heads, hd, lat_rows), BF), ((2 * heads, lat_rows), F32), ((lat_rows, model), BF),
            ((lat_rows, inner), BF), ((8, model), F32),
        ],
        [
            vm((model, ff_here), BF), vm((ff_here, model), BF), vm((lat_rows, ff_here), F32),
            vm((lat_rows, model), F32), vm((lat_rows, ff_here), BF), vm((lat_rows, ff_here), BF),
            vm((inner, lat_rows), F32), vm((lat_rows, model), F32),
            vm((3, 6, tiles, lat_rows, tile), BF), dma((3, 3, 2, tiles)), dma((2,)),
        ],
        1,
        any_args=(up_weight, down_weight),
        args=(att, lse, latents, cotangent, out_weight, row(feed_gain), row(feed_shift)),
    )
    fn_all = lax.all_gather(fn, "blk", axis=0, tiled=True)
    low_all = lax.all_gather(low, "blk", axis=0, tiled=True)
    branch_all = lax.all_gather(branch, "blk", axis=0, tiled=True)

    (media_grad, latent_grad, query_grad, key_grad, value_grad, gains) = call(
        functools.partial(back_kernel, nb),
        [
            ((med_rows, model), F32), ((lat_rows, model), F32), ((own_rows, inner), F32),
            ((own_rows, inner), F32), ((own_rows, inner), F32), ((8, own_rows), F32),
        ],
        [
            vm((nb, heads, hd, lat_rows), BF), vm((nb, 2 * heads, lat_rows), F32),
            vm((heads, hd, med_rows), F32), vm((heads, hd, med_rows), F32),
            vm((heads, hd, lat_rows), F32),
            vm((nb, heads, hd, lat_rows), BF),
            vm((inner, med_rows), F32), vm((med_rows + lat_rows, model), BF),
            vm((med_rows + lat_rows, 2 * inner), BF), vm((lat_rows, inner), BF),
            vm((nb, own_pad, 3 * inner), BF), vm((no, own_pad, 3 * inner), BF),
            vm((no, own_pad, 3 * inner), BF),
            vm((nb, 8, own_rows), F32), vm((nb, 8, own_rows), F32),
            vm((6, tiles, med_rows, tile), BF), vm((6, tiles, lat_rows, tile), BF),
            dma((2, 2, no)), dma((2, 2, no)), dma((2, nb)), dma((2, no)), dma((2, no)),
            dma((2, nb)), dma((2, 3, 2, tiles)),
        ],
        2,
        args=(
            q_all, dot, ld, kh, kt, vh, lkh, lkt, lvh, ln, mn, query_weight, key_weight,
            value_weight, mid_grad, latents, media, row(latent_gain), row(media_gain), feed_gains,
            image,
        ),
    )

    def own_columns(rows):
        return lax.dynamic_slice_in_dim(rows, me * own_rows, own_rows, axis=1)

    group = math.gcd(nb, 8)
    group_rows = group * lat_rows

    def feed_step(carry, rows):
        up_acc, down_acc, out_acc = carry
        fn_rows, cot_rows, low_rows, branch_rows = rows
        hidden, slope = gelu_pair(dot_nn(fn_rows, up_weight))
        grad = (dot_nt(cot_rows, down_weight) * slope).astype(BF)
        return (
            up_acc + dot_tn(own_columns(fn_rows), grad),
            down_acc + dot_tn(hidden.astype(BF), own_columns(cot_rows)),
            out_acc + dot_tn(low_rows, own_columns(branch_rows)),
        ), None

    whole = (fn_all, cot_all, low_all, branch_all)
    start = (
        jnp.zeros((own_rows, ff_here), F32),
        jnp.zeros((ff_here, own_rows), F32),
        jnp.zeros((inner, own_rows), F32),
    )
    if group == nb:
        (up_grad, down_grad, out_grad), _ = feed_step(start, whole)
    else:
        (up_grad, down_grad, out_grad), _ = lax.scan(
            feed_step, start, tuple(v.reshape(nb // group, group_rows, -1) for v in whole)
        )
    return (
        resampled, media_grad, latent_grad, query_grad, key_grad, value_grad, out_grad, up_grad,
        down_grad, gains[0], gains[1], gains[2], gains[3], gains[4], gains[5],
    )


class Spread:
    def __init__(self, place, slots, sems):
        self.place, self.slots, self.sems = place, slots, sems
        self.t = lax.axis_index("tp")

    def source(self, kind, d):
        pc = self.place
        return 2 * pc.outer_from(d) + (1 - pc.inner if kind else pc.inner)

    def copy_z(self, d):
        pc = self.place
        slot = self.slots.at[pc.me, self.t]
        return remote(
            slot, slot, self.sems.at[0, 0, d], self.sems.at[0, 1, d],
            {"blk": 2 * pc.outer_to(d) + pc.inner},
        )

    def copy_y(self, d):
        slot = self.slots.at[self.source(0, d), self.t]
        return remote(
            slot, slot, self.sems.at[1, 0, d], self.sems.at[1, 1, d], {"blk": self.place.partner}
        )

    def arrived(self, kind, d):
        slot = self.slots.at[self.source(kind, d), self.t]
        remote(
            slot, slot, self.sems.at[kind, 0, d], self.sems.at[kind, 1, d], {"blk": self.place.partner}
        ).wait_recv()

    def start(self):
        for d in range(1, self.place.no):
            self.copy_z(d).start()
        self.copy_y(0).start()

    def relay(self):
        for d in range(1, self.place.no):
            self.arrived(0, d)
            self.copy_y(d).start()

    def finish(self):
        for d in range(self.place.no):
            self.arrived(1, d)
        for d in range(1, self.place.no):
            self.copy_z(d).wait_send()
        for d in range(self.place.no):
            self.copy_y(d).wait_send()


class Share:
    def __init__(self, place, slots, sems):
        self.place, self.slots, self.sems = place, slots, sems
        t = lax.axis_index("tp")
        self.t = t
        core, chip = t % 2, t // 2
        self.sibling_t = 2 * chip + 1 - core
        self.across_t = 2 * (1 - chip) + core
        self.diagonal_t = 2 * (1 - chip) + 1 - core

    def blocks(self, step):
        pc = self.place
        base = 2 * pc.outer_from(step)
        partner = (pc.no + step, base + 1 - pc.inner)
        return [partner] if step == 0 else [(step, base + pc.inner), partner]

    def copy(self, stage, n, s):
        slot = self.slots.at[s, self.across_t if stage == 2 else self.t]
        return remote(
            slot, slot, self.sems.at[stage, 0, n], self.sems.at[stage, 1, n],
            {"tp": self.sibling_t if stage else self.across_t},
        )

    def arrived(self, stage, n, s, t):
        slot = self.slots.at[s, t]
        remote(
            slot, slot, self.sems.at[stage, 0, n], self.sems.at[stage, 1, n], {"tp": self.sibling_t}
        ).wait_recv()

    def start(self, step):
        for n, s in self.blocks(step):
            self.copy(0, n, s).start()
            self.copy(1, n, s).start()

    def forward(self, step):
        for n, s in self.blocks(step):
            self.arrived(0, n, s, self.across_t)
            self.copy(2, n, s).start()

    def ready(self, step):
        for n, s in self.blocks(step):
            self.arrived(1, n, s, self.sibling_t)
            self.arrived(2, n, s, self.diagonal_t)

    def finish(self):
        for step in range(self.place.no):
            for n, s in self.blocks(step):
                for stage in range(3):
                    self.copy(stage, n, s).wait_send()


class Slices:
    def __init__(self, place, out, into, sems):
        self.place, self.out, self.into, self.sems = place, out, into, sems
        t = lax.axis_index("tp")
        self.core = t % 2
        self.sibling = {"tp": 2 * (t // 2) + 1 - self.core}

    def copy(self, d):
        pc = self.place
        return remote(
            self.out.at[pc.far(d), self.core], self.into.at[pc.me, self.core],
            self.sems.at[0, 0, d], self.sems.at[0, 1, d], {"blk": pc.far(d)},
        )

    def share(self, d):
        slot = self.into.at[self.place.near(d), self.core]
        return remote(slot, slot, self.sems.at[1, 0, d], self.sems.at[1, 1, d], self.sibling)

    def arrived(self, stage, d, core):
        slot = self.into.at[self.place.near(d), core]
        remote(
            slot, slot, self.sems.at[stage, 0, d], self.sems.at[stage, 1, d], self.sibling
        ).wait_recv()

    def start(self):
        for d in range(1, self.place.nb):
            self.copy(d).start()

    def relay(self):
        for d in range(1, self.place.nb):
            self.arrived(0, d, self.core)
            self.share(d).start()

    def finish(self):
        for d in range(1, self.place.nb):
            self.arrived(1, d, 1 - self.core)
        for d in range(1, self.place.nb):
            self.copy(d).wait_send()
            self.share(d).wait_send()

    def cut(self, rows):
        nb, _, half, width = self.out.shape
        for o in range(nb):
            piece = rows[:, o * width : (o + 1) * width]
            self.out[o, 0] = piece[0:half]
            self.out[o, 1] = piece[half:]
        for c in range(2):
            self.into[self.place.me, c] = self.out[self.place.me, c]


class Fold:
    def __init__(self, place, give, got, send, into, sems):
        self.place, self.give, self.got, self.send, self.into = place, give, got, send, into
        self.sems = sems

    def pair(self, o):
        return remote(
            self.give(o), self.got.at[o], self.sems.at[0, 0, o], self.sems.at[0, 1, o],
            {"blk": self.place.partner},
        )

    def far(self, d):
        o = self.place.outer_to(d)
        return remote(
            self.send(o), self.into.at[d], self.sems.at[1, 0, d], self.sems.at[1, 1, d],
            {"blk": 2 * o + self.place.inner},
        )

    def finish(self):
        for o in range(self.place.no):
            self.pair(o).wait_send()
        for d in range(1, self.place.no):
            self.far(d).wait_send()


def image_columns(image_ref, rows, lanes):
    line = image_ref[...].astype(F32).reshape(1, rows)
    return jnp.broadcast_to(line, (lanes, rows)).T


def pair_lanes(place, sources, images_here, lat_rows):
    return jnp.concatenate(
        [lane_image(s, images_here, lat_rows).astype(F32) for s in sources], axis=1
    )


def line_of(ref):
    return ref[...].reshape(1, -1)


def whole_greeting(place):
    return place.greeting() + TensorSum.greeting()


def near_layer(
    nb,
    lat_ref, cot_ref, image_ref, lg_ref, ls_ref, mg_ref, ms_ref, fg_ref, fs_ref,
    med_hbm, wq_hbm, wk_hbm, wv_hbm, wo_hbm, up_hbm, down_hbm,
    x_ref, out_ref, lgrad_ref, qg_ref, kg_ref, vg_ref, og_ref, ug_ref, down_t, gains_ref,
    med_ref, wq, wk, wv, wo, up, down, q_all, dot_all, ld_all, low_all, dq_all, fn_all, cot_all,
    kh_ref, kt_ref, vh_ref, vt, lkh_ref, lkt_ref, lvh_ref, lvt, att_ref, lse_ref,
    mine, give, got, send, into, mstat, gstat, rstat, sstat, istat,
    hg, mid, hidden, pre_grad, low_t, sum_buf, branch_ref, ln_out, lns_ref, br_out, br_in,
    dk, dv, dq_own, turn, yall, own_cols, part, pair_in, far_in, gain_out, gain_in, bufs, med_bufs,
    g_sems, a_sems, s_sems, f_sems, h_sems, n_sems, p_sems, t_sems, e_sems, w_sems,
):
    place = Place(nb)
    lat_rows = lat_ref.shape[0]
    med_rows, model = med_ref.shape
    heads = kh_ref.shape[0]
    inner = heads * HEAD_DIM
    images_here = lat_rows // LATENTS
    own_rows = model // nb
    quarter = lat_rows // 4
    ff_here = up.shape[1]
    ff_tile = math.gcd(ff_here, 512)
    sources = {
        "q": (wq_hbm, wq), "k": (wk_hbm, wk), "m": (med_hbm, med_ref), "v": (wv_hbm, wv),
        "down": (down_hbm, down), "wo": (wo_hbm, wo), "up": (up_hbm, up),
    }
    loads = {
        name: pltpu.make_async_copy(*ends, w_sems.at[n]) for n, (name, ends) in enumerate(sources.items())
    }
    for load in loads.values():
        load.start()
    greet(whole_greeting(place))
    for q in range(4):
        cot_all[place.me, q] = cot_ref[q * quarter : (q + 1) * quarter]
    spread_cot = Spread(place, cot_all, f_sems.at[0])
    spread_cot.start()
    row_image = lax.broadcasted_iota(jnp.int32, (lat_rows, lat_rows), 0) // LATENTS
    col_image = lax.broadcasted_iota(jnp.int32, (lat_rows, lat_rows), 1) // LATENTS
    same = row_image == col_image
    image = image_columns(image_ref, med_rows, lat_rows)
    image = jnp.concatenate([image, image], axis=1)
    order = [*range(1, place.no), 0]

    xhat, _ = normalised(lat_ref[...].astype(F32))
    ln = (xhat * line_of(lg_ref) + line_of(ls_ref)).astype(BF)
    x_ref[med_rows:, :] = ln

    def heads_t(rows, ref):
        turned = rows.T
        for h in range(heads):
            ref[h] = turned[h * HEAD_DIM : (h + 1) * HEAD_DIM].astype(BF)

    def heads_n(rows, ref):
        for h in range(heads):
            ref[h] = rows[:, h * HEAD_DIM : (h + 1) * HEAD_DIM].astype(BF)

    loads["q"].wait()
    heads_t(dot_nn(ln, wq[...]) * SCALE, q_all.at[place.me])
    gather = Gather(place, q_all, g_sems.at[0])
    gather.start()
    loads["k"].wait()
    lk = dot_nn(ln, wk[...])
    heads_n(lk, lkh_ref)
    heads_t(lk, lkt_ref)
    loads["m"].wait()

    med_gain, med_shift = line_of(mg_ref), line_of(ms_ref)

    def norm_rows(i, carry):
        rows = pl.ds(pl.multiple_of(i * 128, 128), 128)
        hat, _ = normalised(med_ref[rows, :].astype(F32))
        x_ref[rows, :] = (hat * med_gain + med_shift).astype(BF)
        return carry

    lax.fori_loop(0, med_rows // 128, norm_rows, 0)
    mk = dot_nn(x_ref[0:med_rows, :], wk[...])
    heads_n(mk, kh_ref)
    heads_t(mk, kt_ref)
    spread_cot.relay()
    loads["v"].wait()
    mv = dot_nn(x_ref[0:med_rows, :], wv[...])
    heads_n(mv, vh_ref)
    heads_t(mv, vt)
    gather.relay()
    lv = dot_nn(ln, wv[...])
    heads_n(lv, lvh_ref)
    heads_t(lv, lvt)
    own = []
    for h in range(heads):
        scores = jnp.where(same, dot_nn(lkh_ref[h], q_all[place.me, h]), NEG_FILL)
        top = jnp.max(scores, axis=0, keepdims=True)
        weights = jnp.exp(scores - top)
        total = jnp.sum(weights, axis=0, keepdims=True)
        own.append((top, total, dot_nn(lvt[h], weights.astype(BF))))
    loads["down"].wait()

    def back_hidden(i, carry):
        cols = pl.ds(pl.multiple_of(i * ff_tile, ff_tile), ff_tile)
        hg[:, cols] = dot_nt(cot_ref[...], down[cols, :])
        return carry

    lax.fori_loop(0, ff_here // ff_tile, back_hidden, 0)
    ln_slices = Slices(place, ln_out, lns_ref, n_sems.at[0])
    ln_slices.cut(ln)
    gather.finish()
    spread_cot.finish()
    share_cot = Share(place, cot_all, h_sems.at[0])
    for step in range(place.no):
        share_cot.start(step)

    fold = Fold(place, lambda o: give.at[o], got, lambda o: send.at[o], into, a_sems.at[0])
    stats = Fold(place, lambda o: gstat.at[o], rstat, lambda o: sstat.at[o], istat, s_sems)

    def piece(acc_ref, stat_ref, at):
        return [
            (
                stat_ref[at, h : h + 1, :],
                stat_ref[at, heads + h : heads + h + 1, :],
                acc_ref[at, h].astype(F32),
            )
            for h in range(heads)
        ]

    def merged(left, right):
        both = []
        for (lt, ll, la), (rt, rl, ra) in zip(left, right):
            top = jnp.maximum(lt, rt)
            lf, rf = jnp.exp(lt - top), jnp.exp(rt - top)
            both.append((top, ll * lf + rl * rf, la * lf + ra * rf))
        return both

    def pass_attention(d):
        o = place.outer_to(d)
        stats.pair(o).wait_recv()
        fold.pair(o).wait_recv()
        both = merged(piece(mine, mstat, o), piece(got, rstat, o))
        if d == 0:
            return both
        for h, (top, total, acc) in enumerate(both):
            sstat[o, h : h + 1, :] = top
            sstat[o, heads + h : heads + h + 1, :] = total
            send[o, h] = acc.astype(BF)
        stats.far(d).start()
        fold.far(d).start()
        return None

    for step, d in enumerate(order):
        o = place.outer_to(d)
        sources = [2 * o + place.inner, 2 * o + 1 - place.inner]
        allowed = image == pair_lanes(place, sources, images_here, lat_rows)
        for h in range(heads):
            queries = jnp.concatenate([q_all[s, h] for s in sources], axis=1)
            scores = jnp.where(allowed, dot_nn(kh_ref[h], queries), NEG_FILL)
            top = jnp.max(scores, axis=0, keepdims=True)
            weights = jnp.exp(scores - top)
            total = jnp.sum(weights, axis=0, keepdims=True)
            acc = dot_nn(vt[h], weights.astype(BF))
            mine[o, h] = acc[:, 0:lat_rows]
            give[o, h] = acc[:, lat_rows:].astype(BF)
            for ref, lanes in ((mstat, slice(0, lat_rows)), (gstat, slice(lat_rows, 2 * lat_rows))):
                ref[o, h : h + 1, :] = top[:, lanes]
                ref[o, heads + h : heads + h + 1, :] = total[:, lanes]
        stats.pair(o).start()
        fold.pair(o).start()
        if step:
            pass_attention(order[step - 1])
    result = merged(own, pass_attention(0))
    for d in range(1, place.no):
        stats.far(d).wait_recv()
        fold.far(d).wait_recv()
        result = merged(result, piece(into, istat, d))
    lse_ref[...] = jnp.zeros_like(lse_ref)
    for h, (top, total, acc) in enumerate(result):
        att_ref[h] = acc / total
        lse_ref[h : h + 1, :] = top + jnp.log(total)

    for h in range(heads):
        low_t[h * HEAD_DIM : (h + 1) * HEAD_DIM, :] = att_ref[h]
    low_all[place.me] = low_t[...].T.astype(BF)
    low_gather = Gather(place, low_all, g_sems.at[1])
    low_gather.start()
    ln_slices.start()
    low = low_all[place.me]

    def put_sum(column, tile):
        sum_buf[:, pl.ds(column, tile.shape[1])] = tile

    def tile_sum(n, tile_of):
        return TensorSum(bufs.at[n], t_sems.at[n], tile_of)

    width = bufs.shape[-1]
    branch = tile_sum(0, lambda c: dot_nn(low, wo[:, pl.ds(c, width)]))
    loads["wo"].wait()
    branch.give()
    branch.cross()
    for step in range(place.no // 2):
        share_cot.forward(step)
    branch.back()
    branch.finish(put_sum)
    mid[...] = lat_ref[...].astype(F32) + sum_buf[...].astype(F32)
    xhat, rstd = normalised(mid[...])
    normed = (xhat * line_of(fg_ref) + line_of(fs_ref)).astype(BF)
    for q in range(4):
        fn_all[place.me, q] = normed[q * quarter : (q + 1) * quarter]
    spread_fn = Spread(place, fn_all, f_sems.at[1])
    spread_fn.start()
    for step in range(place.no // 2, place.no):
        share_cot.forward(step)
    loads["up"].wait()

    def feed_forward(i, carry):
        cols = pl.ds(pl.multiple_of(i * ff_tile, ff_tile), ff_tile)
        pre = dot_nn(normed, up[:, cols])
        value, slope = gelu_pair(pre)
        hidden[:, cols] = value.astype(BF)
        pre_grad[:, cols] = (hg[:, cols] * slope).astype(BF)
        return carry

    lax.fori_loop(0, ff_here // ff_tile, feed_forward, 0)
    low_gather.relay()
    grads = tile_sum(1, lambda c: dot_nt(pre_grad[...], up[pl.ds(c, width), :]))
    feed = tile_sum(2, lambda c: dot_nn(hidden[...], down[:, pl.ds(c, width)]))
    grads.give()
    grads.cross()
    feed.give()
    grads.back()
    ln_slices.relay()
    spread_fn.relay()
    grads.finish(put_sum)
    fng = sum_buf[...].astype(F32)
    xhat, rstd = normalised(mid[...])
    mid_grad = cot_ref[...].astype(F32) + norm_back(fng, line_of(fg_ref), xhat, rstd)
    lgrad_ref[...] = mid_grad
    branch_ref[...] = mid_grad.astype(BF)
    feed_gains = [
        jnp.sum(fng * xhat, axis=0, keepdims=True), jnp.sum(fng, axis=0, keepdims=True)
    ]
    back = dot_nt(wo[...], branch_ref[...])
    ld_all[place.me] = lse_ref[...]
    for h in range(heads):
        piece_grad = back[h * HEAD_DIM : (h + 1) * HEAD_DIM, :].astype(BF)
        dot_all[place.me, h] = piece_grad
        ld_all[place.me, heads + h : heads + h + 1, :] = jnp.sum(
            piece_grad.astype(F32) * att_ref[h], axis=0, keepdims=True
        )

    gather = Gather(place, dot_all, g_sems.at[2])
    gather_ld = Gather(place, ld_all, g_sems.at[3])
    gather_ld.start()
    gather.start()
    feed.cross()
    spread_fn.finish()
    share_fn = Share(place, fn_all, h_sems.at[1])
    for step in range(place.no):
        share_fn.start(step)

    shares = [share_cot, share_fn]

    def grads_of(keys, values, queries, grads, lse, delta, allowed):
        scores = jnp.where(allowed, dot_nn(keys, queries), NEG_FILL)
        probs = jnp.exp(scores - lse)
        score_grad = (probs * (dot_nn(values, grads) - delta)).astype(BF)
        return probs.astype(BF), score_grad

    for h in range(heads):
        queries, grads = q_all[place.me, h], dot_all[place.me, h]
        probs, score_grad = grads_of(
            lkh_ref[h], lvh_ref[h], queries, grads,
            ld_all[place.me, h : h + 1, :], ld_all[place.me, heads + h : heads + h + 1, :], same,
        )
        dk[h, :, 0:lat_rows] = dot_nt(queries, score_grad)
        dv[h, :, 0:lat_rows] = dot_nt(grads, probs)
        dq_own[h] = dot_nn(lkt_ref[h], score_grad)

    def put_rows(first, rows):
        for k, acc in enumerate((dk, dv)):
            for h in range(heads):
                turn[h * HEAD_DIM : (h + 1) * HEAD_DIM, 0:rows] = acc[h, :, 0:rows]
            yall[k, first : first + rows, :] = turn[:, 0:rows].T.astype(BF)

    put_rows(med_rows, lat_rows)
    slices = Slices(place, br_out, br_in, n_sems.at[1])
    slices.cut(branch_ref[...])
    slices.start()

    pick = (
        lax.broadcasted_iota(jnp.int32, (own_rows, model), 1)
        == lax.broadcasted_iota(jnp.int32, (own_rows, model), 0) + place.me * own_rows
    )
    pick = jnp.where(pick, 1.0, 0.0).astype(BF)
    ff_tiles = ff_here // ff_tile

    def step_rows(j, rows):
        base = 2 * place.outer_from(j)
        blocks = base + place.inner, base + 1 - place.inner
        return jnp.concatenate([rows[b].reshape(lat_rows, model) for b in blocks], axis=0)

    def feed_tile(j, i):
        fn_rows, cot_rows = step_rows(j, fn_all), step_rows(j, cot_all)
        if i == 0:
            own_cols[0] = dot_nt(pick, fn_rows).astype(BF)
            own_cols[1] = dot_nt(pick, cot_rows).astype(BF)
        cols = slice(i * ff_tile, (i + 1) * ff_tile)
        value, slope = gelu_pair(dot_nn(fn_rows, up[:, cols]))
        grad = (dot_nt(cot_rows, down[cols, :]) * slope).astype(BF)
        up_part = dot_nn(own_cols[0], grad)
        down_part = dot_nn(own_cols[1], value.astype(BF))
        if j == 0:
            ug_ref[:, cols] = up_part
            down_t[:, cols] = down_part
        else:
            ug_ref[:, cols] += up_part
            down_t[:, cols] += down_part

    fed = [0]

    def feed_on(count):
        for n in range(fed[0], min(fed[0] + count, place.no * ff_tiles)):
            j, i = divmod(n, ff_tiles)
            if i == 0:
                for share in shares:
                    share.ready(j)
            feed_tile(j, i)
        fed[0] += count

    feed.back()
    gather_ld.relay()
    gather.relay()
    feed.finish(put_sum)
    out_ref[...] = (mid[...] + sum_buf[...].astype(F32)).astype(BF)
    gather_ld.finish()
    gather.finish()
    fold.finish()
    stats.finish()
    low_gather.finish()
    ln_slices.finish()

    dq_fold = Fold(place, lambda o: give.at[o], got, lambda o: send.at[o], into, a_sems.at[1])
    folds = [
        Fold(
            place, lambda o, f=f: part.at[f, 2 * o + 1 - place.inner], pair_in.at[f],
            lambda o, f=f: part.at[f, 2 * o + place.inner], far_in.at[f], p_sems.at[f],
        )
        for f in range(2)
    ]

    def pass_queries(d):
        o = place.outer_to(d)
        dq_fold.pair(o).wait_recv()
        for h in range(heads):
            send[o, h] = (mine[o, h] + got[o, h].astype(F32)).astype(BF)
        dq_fold.far(d).start()

    for step, d in enumerate(order):
        o = place.outer_to(d)
        sources = [2 * o + place.inner, 2 * o + 1 - place.inner]
        allowed = image == pair_lanes(place, sources, images_here, lat_rows)
        for h in range(heads):
            queries = jnp.concatenate([q_all[s, h] for s in sources], axis=1)
            grads = jnp.concatenate([dot_all[s, h] for s in sources], axis=1)
            lse = jnp.concatenate([ld_all[s, h : h + 1, :] for s in sources], axis=1)
            delta = jnp.concatenate(
                [ld_all[s, heads + h : heads + h + 1, :] for s in sources], axis=1
            )
            probs, score_grad = grads_of(kh_ref[h], vh_ref[h], queries, grads, lse, delta, allowed)
            key_part = dot_nt(queries, score_grad)
            value_part = dot_nt(grads, probs)
            dk[h] = key_part if step == 0 else dk[h] + key_part
            dv[h] = value_part if step == 0 else dv[h] + value_part
            dq = dot_nn(kt_ref[h], score_grad)
            mine[o, h] = dq[:, 0:lat_rows]
            give[o, h] = dq[:, lat_rows:].astype(BF)
        dq_fold.pair(o).start()
        if step:
            pass_queries(order[step - 1])
        share_fn.forward(step)

    put_rows(0, med_rows)

    chunk = 2 * own_rows

    def weigh(d, k):
        o = place.outer_to(d)
        cols = pl.ds(pl.multiple_of(o * chunk, 128), chunk)
        value = dot_tn(x_ref[:, cols], yall[k])
        part[k, 2 * o] = value[0:own_rows].astype(BF)
        part[k, 2 * o + 1] = value[own_rows:].astype(BF)
        folds[k].pair(o).start()

    def both(d, k):
        o = place.outer_to(d)
        return part[k, 2 * o + place.inner].astype(F32) + pair_in[k, o].astype(F32)

    def pass_on(d, k):
        o = place.outer_to(d)
        folds[k].pair(o).wait_recv()
        if d:
            part[k, 2 * o + place.inner] = both(d, k).astype(BF)
            folds[k].far(d).start()

    med_tile, lat_tile = med_bufs.shape[-1], bufs.shape[-1]

    def back_rows(first, rows, tile):
        def tile_of(column):
            cols = pl.ds(column, tile)
            return dot_nt(yall[0, first : first + rows, :], wk[cols, :]) + dot_nt(
                yall[1, first : first + rows, :], wv[cols, :]
            )

        return tile_of

    med_sum = TensorSum(med_bufs, t_sems.at[4], back_rows(0, med_rows, med_tile))
    tasks = [(d, k) for d in order for k in range(2)]
    ahead = 4
    weigh(*tasks[0])
    weigh(*tasks[1])
    med_sum.give()
    for task in tasks[2:ahead]:
        weigh(*task)
    med_sum.cross()

    def lat_tile_of(column):
        cols = pl.ds(column, lat_tile)
        return (
            back_rows(med_rows, lat_rows, lat_tile)(column)
            + dot_nt(dq_all[place.me], wq[cols, :]) * SCALE
        )

    lat_sum = TensorSum(bufs.at[0], t_sems.at[3], lat_tile_of)
    dq_gather = Gather(place, dq_all, g_sems.at[4])

    def query_sums():
        o = place.outer
        dq_fold.pair(o).wait_recv()
        for h in range(heads):
            dq_own[h] = dq_own[h] + mine[o, h] + got[o, h].astype(F32)
        for d in range(1, place.no):
            dq_fold.far(d).wait_recv()
            for h in range(heads):
                dq_own[h] = dq_own[h] + into[d, h].astype(F32)
        for h in range(heads):
            turn[h * HEAD_DIM : (h + 1) * HEAD_DIM, 0:lat_rows] = dq_own[h]
        dq_all[place.me] = turn[:, 0:lat_rows].T.astype(BF)
        dq_gather.start()
        lat_sum.give()

    def put(column, tile):
        x_ref[0:med_rows, pl.ds(column, tile.shape[1])] = tile

    def put_lat(column, tile):
        x_ref[med_rows:, pl.ds(column, tile.shape[1])] = tile

    def norm_rows(i, carry):
        rows = pl.ds(pl.multiple_of(i * 128, 128), 128)
        xhat, _ = normalised(med_ref[rows, :].astype(F32))
        q = x_ref[rows, :].astype(F32)
        return (
            carry[0] + jnp.sum(q * xhat, axis=0, keepdims=True),
            carry[1] + jnp.sum(q, axis=0, keepdims=True),
        )

    def gain_copy(d):
        return remote(
            gain_out.at[place.far(d)], gain_in.at[d], e_sems.at[0, d], e_sems.at[1, d],
            {"blk": place.far(d)},
        )

    def norm_grads():
        med_sum.finish(put)
        zero = jnp.zeros((1, model), F32)
        med_gain = lax.fori_loop(0, med_rows // 128, norm_rows, (zero, zero))
        lat_sum.finish(put_lat)
        xhat, rstd = normalised(lat_ref[...].astype(F32))
        q = x_ref[med_rows:, :].astype(F32)
        lgrad_ref[...] += norm_back(q, line_of(lg_ref), xhat, rstd)
        all_rows = [
            *med_gain,
            jnp.sum(q * xhat, axis=0, keepdims=True),
            jnp.sum(q, axis=0, keepdims=True),
            *feed_gains,
        ]
        for o in range(nb):
            for n, line in enumerate(all_rows):
                gain_out[o, n : n + 1, :] = line[:, o * own_rows : (o + 1) * own_rows]
        for d in range(1, nb):
            gain_copy(d).start()

    between = {
        1: query_sums,
        3: slices.relay,
        4: lambda: (lat_sum.cross(), dq_gather.relay()),
        5: med_sum.back,
        6: lat_sum.back,
    }
    pace = -(-place.no * ff_tiles // len(tasks))
    for n in range(len(tasks)):
        if n + ahead < len(tasks):
            weigh(*tasks[n + ahead])
        feed_on(pace)
        if n in between:
            between.pop(n)()
        pass_on(*tasks[n])
    for late in between.values():
        late()
    norm_grads()
    feed_on(place.no * ff_tiles - fed[0])
    for share in shares:
        share.finish()
    slices.finish()
    dq_gather.finish()
    all_rows_of = lambda ref: ref[...].reshape(nb * lat_rows, -1)
    og_ref[...] = dot_tn(all_rows_of(br_in), all_rows_of(low_all))
    qg_ref[...] = dot_tn(all_rows_of(lns_ref), all_rows_of(dq_all)) * SCALE
    for k, ref in enumerate((kg_ref, vg_ref)):
        total = both(0, k)
        for d in range(1, place.no):
            folds[k].far(d).wait_recv()
            total = total + far_in[k, d].astype(F32)
        ref[...] = total
    gains = gain_out[place.me]
    for d in range(1, nb):
        gain_copy(d).wait_recv()
        gains = gains + gain_in[d]
    gains_ref[...] = gains
    for d in range(1, nb):
        gain_copy(d).wait_send()
    dq_fold.finish()
    for fold in folds:
        fold.finish()


def near_call(kernel, out_shapes, scratch, collective_id, args, any_args, any_outs=()):
    vmem = pl.BlockSpec(memory_space=pltpu.VMEM)
    anywhere = pl.BlockSpec(memory_space=pl.ANY)
    return pl.pallas_call(
        kernel,
        out_shape=[jax.ShapeDtypeStruct(s, d) for s, d in (*out_shapes, *any_outs)],
        in_specs=[vmem] * len(args) + [anywhere] * len(any_args),
        out_specs=[vmem] * len(out_shapes) + [anywhere] * len(any_outs),
        scratch_shapes=scratch,
        compiler_params=pltpu.CompilerParams(
            collective_id=collective_id, has_side_effects=True, vmem_limit_bytes=VMEM_LIMIT
        ),
    )(*args, *any_args)


def per_device(
    latents, media, query_weight, key_weight, value_weight, out_weight, up_weight, down_weight,
    media_gain, media_shift, latent_gain, latent_shift, feed_gain, feed_shift, cotangent, media_image,
):
    nb = lax.axis_size("blk")
    lat_rows, model = latents.shape
    med_rows = media.shape[0]
    inner = query_weight.shape[1]
    heads = inner // HEAD_DIM
    ff_here = up_weight.shape[1]
    no = nb // 2
    own_rows = model // nb
    dma = pltpu.SemaphoreType.DMA
    vm = pltpu.VMEM
    hd = HEAD_DIM
    half, quarter = lat_rows // 2, lat_rows // 4
    tile = 256
    tiles = model // 2 // tile
    every = med_rows + lat_rows
    block_t = (nb, heads, hd, lat_rows)
    pair_t = (no, heads, hd, lat_rows)
    rows_t = (nb, 4, quarter, model)
    slice_t = (nb, 2, half, own_rows)
    media_sum, *results = near_call(
        functools.partial(near_layer, nb),
        [
            ((every, model), BF), ((lat_rows, model), BF), ((lat_rows, model), F32),
            *[((own_rows, inner), F32)] * 4, *[((own_rows, ff_here), F32)] * 2, ((8, own_rows), F32),
        ],
        [
            vm((med_rows, model), BF), *[vm((model, inner), BF)] * 3, vm((inner, model), BF),
            vm((model, ff_here), BF), vm((ff_here, model), BF), vm(block_t, BF), vm(block_t, BF),
            vm((nb, 2 * heads, lat_rows), F32), vm((nb, lat_rows, inner), BF), vm((nb, lat_rows, inner), BF),
            vm(rows_t, BF), vm(rows_t, BF),
            vm((heads, med_rows, hd), BF), vm((heads, hd, med_rows), BF), vm((heads, med_rows, hd), BF),
            vm((heads, hd, med_rows), BF), vm((heads, lat_rows, hd), BF), vm((heads, hd, lat_rows), BF),
            vm((heads, lat_rows, hd), BF), vm((heads, hd, lat_rows), BF), vm((heads, hd, lat_rows), F32),
            vm((2 * heads, lat_rows), F32),
            vm(pair_t, F32), *[vm(pair_t, BF)] * 4, *[vm((no, 2 * heads, lat_rows), F32)] * 5,
            vm((lat_rows, ff_here), F32), vm((lat_rows, model), F32), vm((lat_rows, ff_here), BF),
            vm((lat_rows, ff_here), BF), vm((inner, lat_rows), F32), vm((lat_rows, model), BF),
            vm((lat_rows, model), BF), *[vm(slice_t, BF)] * 4,
            vm((heads, hd, med_rows), F32), vm((heads, hd, med_rows), F32), vm((heads, hd, lat_rows), F32),
            vm((inner, med_rows), F32), vm((2, every, inner), BF), vm((2, own_rows, 2 * lat_rows), BF),
            vm((2, nb, own_rows, inner), BF), vm((2, no, own_rows, inner), BF), vm((2, no, own_rows, inner), BF),
            vm((nb, 8, own_rows), F32), vm((nb, 8, own_rows), F32), vm((3, 6, tiles, lat_rows, tile), BF),
            vm((6, tiles, med_rows, tile), BF),
            dma((5, 2, 2, no)), dma((2, 2, 2, no)), dma((2, 2, no)), dma((2, 2, 2, no)),
            dma((2, 3, 2, 2 * no)), dma((2, 2, 2, nb)), dma((2, 2, 2, no)), dma((5, 3, 2, tiles)),
            dma((2, nb)), dma((7,)),
        ],
        0,
        (
            latents, cotangent, media_image, latent_gain, latent_shift, media_gain, media_shift, feed_gain,
            feed_shift,
        ),
        (media, query_weight, key_weight, value_weight, out_weight, up_weight, down_weight),
    )
    return last_step(media, media_gain, *results[:1], media_sum, *results[1:])


def last_kernel(media_ref, sum_ref, gain_ref, gains_ref, *refs):
    count = (len(refs) - 7) // 2
    moved, grad_ref = refs[0:count], refs[count]
    placed, gain_refs = refs[count + 1 : 2 * count + 1], refs[2 * count + 1 :]
    for source, target in zip(moved, placed, strict=True):
        target[...] = source[...]

    @pl.when(pl.program_id(0) == 0)
    def _():
        for n, ref in enumerate(gain_refs):
            ref[...] = gains_ref[n, :]

    xhat, rstd = normalised(media_ref[...].astype(F32))
    grad_ref[...] = norm_back(sum_ref[...].astype(F32), line_of(gain_ref), xhat, rstd)


def last_step(media, media_gain, resampled, media_sum, *rest):
    *moved, gains = (resampled, *rest)
    own_rows = gains.shape[1]
    steps = 2
    blocked = lambda v: pl.BlockSpec((v.shape[0] // steps, v.shape[1]), lambda i: (i, 0))
    gain_spec = pl.BlockSpec((own_rows,), lambda i: (0,))
    outs = pl.pallas_call(
        last_kernel,
        grid=(steps,),
        out_shape=[
            jax.ShapeDtypeStruct(media.shape, F32),
            *[jax.ShapeDtypeStruct(v.shape, v.dtype) for v in moved],
            *[jax.ShapeDtypeStruct((own_rows,), F32)] * 6,
        ],
        in_specs=[
            blocked(media), blocked(media), pl.BlockSpec(media_gain.shape, lambda i: (0,)),
            pl.BlockSpec(gains.shape, lambda i: (0, 0)), *[blocked(v) for v in moved],
        ],
        out_specs=[blocked(media), *[blocked(v) for v in moved], *[gain_spec] * 6],
        compiler_params=pltpu.CompilerParams(vmem_limit_bytes=VMEM_LIMIT),
    )(media, media_sum, media_gain, gains, *moved)
    (
        media_grad, resampled, latent_grad, query_grad, key_grad, value_grad, out_turned, up_grad,
        down_turned, *gain_grads,
    ) = outs
    return (
        resampled, media_grad, latent_grad, query_grad, key_grad, value_grad, out_turned.T, up_grad,
        down_turned.T, *gain_grads,
    )


def solution(mesh):
    in_specs = (
        P("blk", None), P("blk", None), P(None, "tp"), P(None, "tp"), P(None, "tp"), P("tp", None),
        P(None, "tp"), P("tp", None), P(), P(), P(), P(), P(), P(), P("blk", None), P("blk"),
    )
    out_specs = (
        P("blk", None), P("blk", None), P("blk", None), P("blk", "tp"), P("blk", "tp"),
        P("blk", "tp"), P("tp", "blk"), P("blk", "tp"), P("tp", "blk"), P("blk"), P("blk"),
        P("blk"), P("blk"), P("blk"), P("blk"),
    )
    body = per_device if mesh.shape["blk"] <= 16 else per_device_many
    return jax.shard_map(
        body, mesh=mesh, in_specs=in_specs, out_specs=out_specs, check_vma=False
    )
```

```python
import functools
import math

import jax
import jax.numpy as jnp
from jax import lax
from jax.experimental import pallas as pl
from jax.experimental.pallas import tpu as pltpu
from jax.sharding import PartitionSpec as P

HEAD_DIM = 96
LATENTS = 64
NEG_FILL = -1e30
NORM_EPS = 1e-05
BF = jnp.bfloat16
F32 = jnp.float32
MESH = pl.DeviceIdType.MESH
VMEM_LIMIT = 60 * 1024 * 1024
SCALE = 1.0 / math.sqrt(HEAD_DIM)


def dot_nn(a, b):
    return jnp.dot(a, b, preferred_element_type=F32)


def dot_nt(a, b):
    return lax.dot_general(a, b, (((1,), (1,)), ((), ())), preferred_element_type=F32)


def dot_tn(a, b):
    return lax.dot_general(a, b, (((0,), (0,)), ((), ())), preferred_element_type=F32)


def normalised(x):
    centred = x - jnp.mean(x, axis=-1, keepdims=True)
    rstd = lax.rsqrt(jnp.mean(centred * centred, axis=-1, keepdims=True) + NORM_EPS)
    return centred * rstd, rstd


def norm_back(q, gain, xhat, rstd):
    qg = q * gain
    inner = jnp.mean(qg * xhat, axis=-1, keepdims=True)
    return (qg - jnp.mean(qg, axis=-1, keepdims=True) - xhat * inner) * rstd


def greet(devices):
    barrier = pltpu.get_barrier_semaphore()
    for device in devices:
        pl.semaphore_signal(barrier, inc=1, device_id=device, device_id_type=MESH)
    pl.semaphore_wait(barrier, len(devices))


def remote(src, dst, send_sem, recv_sem, device):
    return pltpu.make_async_remote_copy(
        src_ref=src,
        dst_ref=dst,
        send_sem=send_sem,
        recv_sem=recv_sem,
        device_id=device,
        device_id_type=MESH,
    )


class Place:
    def __init__(self, nb):
        self.nb = nb
        self.no = nb // 2
        self.me = lax.axis_index("blk")
        self.outer = self.me // 2
        self.inner = self.me % 2
        self.partner = 2 * self.outer + 1 - self.inner

    def far(self, d):
        return (self.me + d) % self.nb

    def near(self, d):
        return (self.me - d + self.nb) % self.nb

    def outer_to(self, d):
        return (self.outer + d) % self.no

    def outer_from(self, d):
        return (self.outer - d + self.no) % self.no

    def greeting(self):
        return [{"blk": self.far(d)} for d in range(1, self.nb)]


class Gather:
    def __init__(self, place, slots, sems):
        self.place, self.slots, self.sems = place, slots, sems

    def copy_z(self, d):
        pc = self.place
        slot = self.slots.at[pc.me]
        return remote(
            slot, slot, self.sems.at[0, 0, d], self.sems.at[0, 1, d],
            {"blk": 2 * pc.outer_to(d) + pc.inner},
        )

    def copy_y(self, d):
        pc = self.place
        slot = self.slots.at[2 * pc.outer_from(d) + pc.inner]
        return remote(
            slot, slot, self.sems.at[1, 0, d], self.sems.at[1, 1, d], {"blk": pc.partner}
        )

    def start(self):
        for d in range(1, self.place.no):
            self.copy_z(d).start()
        self.copy_y(0).start()

    def relay(self):
        pc = self.place
        for d in range(1, pc.no):
            arrived = self.slots.at[2 * pc.outer_from(d) + pc.inner]
            remote(
                arrived, arrived, self.sems.at[0, 0, d], self.sems.at[0, 1, d], {"blk": pc.partner}
            ).wait_recv()
            self.copy_y(d).start()

    def finish(self):
        pc = self.place
        for d in range(pc.no):
            slot = self.slots.at[2 * pc.outer_from(d) + 1 - pc.inner]
            remote(
                slot, slot, self.sems.at[1, 0, d], self.sems.at[1, 1, d], {"blk": pc.partner}
            ).wait_recv()
        for d in range(1, pc.no):
            self.copy_z(d).wait_send()
        for d in range(pc.no):
            self.copy_y(d).wait_send()


class Exchange:
    def __init__(self, place, out, into, sems, slot=lambda d: d):
        self.place, self.out, self.into, self.sems, self.slot = place, out, into, sems, slot

    def copy(self, d):
        return remote(
            self.out.at[self.slot(d)], self.into.at[d], self.sems.at[0, d], self.sems.at[1, d],
            {"blk": self.place.far(d)},
        )

    def start(self, d):
        self.copy(d).start()

    def wait_recv(self, d):
        self.copy(d).wait_recv()

    def finish_sends(self):
        for d in range(1, self.place.nb):
            self.copy(d).wait_send()


def lane_image(source, images_here, width):
    lane = lax.broadcasted_iota(jnp.int32, (1, width), 1)
    return source * images_here + lane // LATENTS


def attend_kernel(
    nb,
    lat_ref, med_ref, wq_ref, wk_ref, wv_ref, lg_ref, ls_ref, mg_ref, ms_ref, image_ref,
    ln_ref, mn_ref, q_all, kh_ref, kt_ref, vh_ref, lkh_ref, lkt_ref, lvh_ref, att_ref, lse_ref,
    vt, lvt, acc_out, acc_in, stat_out, stat_in, g_sems, a_sems, s_sems,
):
    place = Place(nb)
    lat_rows = lat_ref.shape[0]
    med_rows = med_ref.shape[0]
    heads = kh_ref.shape[0]
    images_here = lat_rows // LATENTS
    greet(place.greeting())

    xhat, _ = normalised(lat_ref[...].astype(F32))
    ln_ref[...] = (xhat * lg_ref[...] + ls_ref[...]).astype(BF)
    ln = ln_ref[...]

    def heads_t(rows, ref):
        turned = rows.T
        for h in range(heads):
            ref[h] = turned[h * HEAD_DIM : (h + 1) * HEAD_DIM].astype(BF)

    def heads_n(rows, ref):
        for h in range(heads):
            ref[h] = rows[:, h * HEAD_DIM : (h + 1) * HEAD_DIM].astype(BF)

    heads_t(dot_nn(ln, wq_ref[...]) * SCALE, q_all.at[place.me])
    gather = Gather(place, q_all, g_sems)
    gather.start()
    lk = dot_nn(ln, wk_ref[...])
    heads_n(lk, lkh_ref)
    heads_t(lk, lkt_ref)
    lv = dot_nn(ln, wv_ref[...])
    heads_n(lv, lvh_ref)
    heads_t(lv, lvt)

    def norm_rows(i, carry):
        rows = pl.ds(pl.multiple_of(i * 128, 128), 128)
        hat, _ = normalised(med_ref[rows, :].astype(F32))
        mn_ref[rows, :] = (hat * mg_ref[...] + ms_ref[...]).astype(BF)
        return carry

    lax.fori_loop(0, med_rows // 128, norm_rows, 0)
    mk = dot_nn(mn_ref[...], wk_ref[...])
    heads_n(mk, kh_ref)
    heads_t(mk, kt_ref)
    gather.relay()
    mv = dot_nn(mn_ref[...], wv_ref[...])
    heads_n(mv, vh_ref)
    heads_t(mv, vt)
    gather.finish()

    exchange = Exchange(place, acc_out, acc_in, a_sems)
    stats = Exchange(place, stat_out, stat_in, s_sems)
    image = image_ref[...]
    order = list(range(1, nb)) + [0]
    for g in range(nb // 2):
        pair = order[2 * g : 2 * g + 2]
        sources = [place.far(d) for d in pair]
        lanes = jnp.concatenate([lane_image(s, images_here, lat_rows) for s in sources], axis=1)
        allowed = image == lanes
        for h in range(heads):
            queries = jnp.concatenate([q_all[s, h] for s in sources], axis=1)
            scores = jnp.where(allowed, dot_nn(kh_ref[h], queries), NEG_FILL)
            top = jnp.max(scores, axis=0, keepdims=True)
            weights = jnp.exp(scores - top)
            total = jnp.sum(weights, axis=0, keepdims=True)
            acc = dot_nn(vt[h], weights.astype(BF)).astype(BF)
            for n, d in enumerate(pair):
                part = slice(n * lat_rows, (n + 1) * lat_rows)
                acc_out[d, h] = acc[:, part]
                stat_out[d, h : h + 1, :] = top[:, part]
                stat_out[d, heads + h : heads + h + 1, :] = total[:, part]
        for d in pair:
            if d:
                exchange.start(d)
                stats.start(d)

    row_image = lax.broadcasted_iota(jnp.int32, (lat_rows, lat_rows), 0) // LATENTS
    col_image = lax.broadcasted_iota(jnp.int32, (lat_rows, lat_rows), 1) // LATENTS
    same = row_image == col_image
    own = []
    for h in range(heads):
        scores = jnp.where(same, dot_nn(lkh_ref[h], q_all[place.me, h]), NEG_FILL)
        top = jnp.max(scores, axis=0, keepdims=True)
        weights = jnp.exp(scores - top)
        total = jnp.sum(weights, axis=0, keepdims=True)
        own.append((top, total, dot_nn(lvt[h], weights.astype(BF))))
    for d in range(1, nb):
        stats.wait_recv(d)
        exchange.wait_recv(d)
    lse_ref[...] = jnp.zeros_like(lse_ref)
    for h in range(heads):
        own_top, own_total, own_acc = own[h]
        tops = [
            (stat_out if d == 0 else stat_in)[d, h : h + 1, :] for d in range(nb)
        ]
        best = functools.reduce(jnp.maximum, tops, own_top)
        factor = jnp.exp(own_top - best)
        total = own_total * factor
        acc = own_acc * factor
        for d in range(nb):
            factor = jnp.exp(tops[d] - best)
            stat = stat_out if d == 0 else stat_in
            piece = acc_out if d == 0 else acc_in
            total = total + stat[d, heads + h : heads + h + 1, :] * factor
            acc = acc + piece[d, h].astype(F32) * factor
        att_ref[h] = acc / total
        lse_ref[h : h + 1, :] = best + jnp.log(total)
    exchange.finish_sends()
    stats.finish_sends()


class TensorSum:
    def __init__(self, bufs, sems, tile_of):
        self.bufs, self.sems, self.tile_of = bufs, sems, tile_of
        self.tiles, self.rows, self.tile = bufs.shape[1:]
        t = lax.axis_index("tp")
        self.core = t % 2
        self.chip = t // 2
        self.sibling = {"tp": 2 * self.chip + 1 - self.core}
        self.across = {"tp": 2 * (1 - self.chip) + self.core}

    @staticmethod
    def greeting():
        t = lax.axis_index("tp")
        core, chip = t % 2, t // 2
        return [{"tp": 2 * chip + 1 - core}, {"tp": 2 * (1 - chip) + core}]

    def column(self, half, j):
        return pl.multiple_of((half * self.tiles + j) * self.tile, 128)

    def copy(self, stage, j):
        return remote(
            self.bufs.at[2 * stage, j], self.bufs.at[2 * stage + 1, j],
            self.sems.at[stage, 0, j], self.sems.at[stage, 1, j],
            self.across if stage == 1 else self.sibling,
        )

    def give(self):
        for j in range(self.tiles):
            self.bufs[0, j] = self.tile_of(self.column(1 - self.core, j)).astype(BF)
            self.copy(0, j).start()

    def cross(self):
        for j in range(self.tiles):
            mine = self.tile_of(self.column(self.core, j))
            self.copy(0, j).wait_recv()
            self.bufs[2, j] = (mine + self.bufs[1, j].astype(F32)).astype(BF)
            self.copy(1, j).start()

    def back(self):
        for j in range(self.tiles):
            self.copy(1, j).wait_recv()
            self.bufs[4, j] = (self.bufs[2, j].astype(F32) + self.bufs[3, j].astype(F32)).astype(BF)
            self.copy(2, j).start()

    def finish(self, put):
        for j in range(self.tiles):
            put(self.column(self.core, j), self.bufs[4, j])
        for j in range(self.tiles):
            self.copy(2, j).wait_recv()
            put(self.column(1 - self.core, j), self.bufs[5, j])
        for stage in range(3):
            for j in range(self.tiles):
                self.copy(stage, j).wait_send()


def feed_kernel(
    att_ref, lse_ref, lat_ref, cot_ref, wo_ref, fg_ref, fs_ref, up_hbm, down_hbm,
    out_ref, mid_grad_ref, branch_ref, dot_ref, ld_ref, fn_ref, low_ref, gain_ref,
    up, down, hg, mid, hidden, pre_grad, low_t, sum_buf, bufs, sems, w_sems,
):
    loads = [
        pltpu.make_async_copy(up_hbm, up, w_sems.at[0]),
        pltpu.make_async_copy(down_hbm, down, w_sems.at[1]),
    ]
    for load in loads:
        load.start()
    heads = att_ref.shape[0]
    ff_here = up.shape[1]
    ff_tile = math.gcd(ff_here, 512)
    greet(TensorSum.greeting())
    for h in range(heads):
        low_t[h * HEAD_DIM : (h + 1) * HEAD_DIM, :] = att_ref[h]
    low_ref[...] = low_t[...].T.astype(BF)
    low = low_ref[...]

    def put(column, tile):
        sum_buf[:, pl.ds(column, tile.shape[1])] = tile.astype(F32)

    def tile_sum(n, tile_of):
        return TensorSum(bufs.at[n], sems.at[n], tile_of)

    width = bufs.shape[-1]
    branch = tile_sum(0, lambda c: dot_nn(low, wo_ref[:, pl.ds(c, width)]))
    branch.give()
    branch.cross()
    loads[1].wait()
    cot = cot_ref[...]

    def back_hidden(i, carry):
        cols = pl.ds(pl.multiple_of(i * ff_tile, ff_tile), ff_tile)
        hg[:, cols] = dot_nt(cot, down[cols, :])
        return carry

    lax.fori_loop(0, ff_here // ff_tile, back_hidden, 0)
    branch.back()
    branch.finish(put)
    mid[...] = lat_ref[...].astype(F32) + sum_buf[...]
    xhat, rstd = normalised(mid[...])
    fn_ref[...] = (xhat * fg_ref[...] + fs_ref[...]).astype(BF)
    fn = fn_ref[...]
    loads[0].wait()

    def inner(i, carry):
        cols = pl.ds(pl.multiple_of(i * ff_tile, ff_tile), ff_tile)
        pre = dot_nn(fn, up[:, cols])
        bell = 0.5 * (1.0 + lax.erf(pre * math.sqrt(0.5)))
        hidden[:, cols] = (pre * bell).astype(BF)
        slope = bell + pre * jnp.exp(-0.5 * pre * pre) * (1.0 / math.sqrt(2.0 * math.pi))
        pre_grad[:, cols] = (hg[:, cols] * slope).astype(BF)
        return carry

    lax.fori_loop(0, ff_here // ff_tile, inner, 0)
    grads = tile_sum(1, lambda c: dot_nt(pre_grad[...], up[pl.ds(c, width), :]))
    feed = tile_sum(2, lambda c: dot_nn(hidden[...], down[:, pl.ds(c, width)]))
    grads.give()
    grads.cross()
    feed.give()
    feed.cross()
    grads.back()
    feed.back()
    grads.finish(put)
    fng = sum_buf[...]
    xhat, rstd = normalised(mid[...])
    mid_grad = cot_ref[...].astype(F32) + norm_back(fng, fg_ref[...], xhat, rstd)
    mid_grad_ref[...] = mid_grad
    branch_ref[...] = mid_grad.astype(BF)
    gain_ref[...] = jnp.zeros_like(gain_ref)
    gain_ref[0:1, :] = jnp.sum(fng * xhat, axis=0, keepdims=True)
    gain_ref[1:2, :] = jnp.sum(fng, axis=0, keepdims=True)
    back = dot_nt(wo_ref[...], branch_ref[...])
    ld_ref[...] = lse_ref[...]
    for h in range(heads):
        piece = back[h * HEAD_DIM : (h + 1) * HEAD_DIM, :].astype(BF)
        dot_ref[h] = piece
        ld_ref[heads + h : heads + h + 1, :] = jnp.sum(
            piece.astype(F32) * att_ref[h], axis=0, keepdims=True
        )
    feed.finish(put)
    out_ref[...] = (mid[...] + sum_buf[...]).astype(BF)


def back_kernel(
    nb,
    q_all, dot_in, ld_in, kh_ref, kt_ref, vh_ref, lkh_ref, lkt_ref, lvh_ref, ln_ref, mn_ref,
    wq_ref, wk_ref, wv_ref, mid_grad_ref, lat_ref, med_ref, lg_ref, mg_ref, fgain_ref, image_ref,
    mgrad_ref, lgrad_ref, qg_ref, kg_ref, vg_ref, gains_ref,
    dot_all, ld_all, dk, dv, dq_own, dq_in, turn, xall, yall, dq_low, part, pair_in, far_in,
    gain_out, gain_in, med_bufs, lat_bufs,
    g_sems, l_sems, x_sems, y_sems, z_sems, n_sems, t_sems,
):
    place = Place(nb)
    lat_rows = lat_ref.shape[0]
    med_rows, model = med_ref.shape
    heads = kh_ref.shape[0]
    inner = heads * HEAD_DIM
    images_here = lat_rows // LATENTS
    dot_all[place.me] = dot_in[...]
    ld_all[place.me] = ld_in[...]
    greet(place.greeting() + TensorSum.greeting())
    gather = Gather(place, dot_all, g_sems)
    gather_ld = Gather(place, ld_all, l_sems)
    gather_ld.start()
    gather.start()

    row_image = lax.broadcasted_iota(jnp.int32, (lat_rows, lat_rows), 0) // LATENTS
    col_image = lax.broadcasted_iota(jnp.int32, (lat_rows, lat_rows), 1) // LATENTS
    same = row_image == col_image

    def turned(h, value, rows):
        turn[h * HEAD_DIM : (h + 1) * HEAD_DIM, 0:rows] = value

    def grads_of(h, keys, values, queries, grads, lse, delta, allowed):
        scores = jnp.where(allowed, dot_nn(keys, queries), NEG_FILL)
        probs = jnp.exp(scores - lse)
        score_grad = (probs * (dot_nn(values, grads) - delta)).astype(BF)
        return probs.astype(BF), score_grad

    for h in range(heads):
        queries, grads = q_all[place.me, h], dot_in[h]
        probs, score_grad = grads_of(
            h, lkh_ref[h], lvh_ref[h], queries, grads,
            ld_in[h : h + 1, :], ld_in[heads + h : heads + h + 1, :], same,
        )
        dk[h, :, 0:lat_rows] = dot_nt(queries, score_grad)
        dv[h, :, 0:lat_rows] = dot_nt(grads, probs)
        dq_own[h] = dot_nn(lkt_ref[h], score_grad)

    def put_rows(first, rows):
        for acc, column in ((dk, 0), (dv, inner)):
            for h in range(heads):
                turned(h, acc[h, :, 0:rows], rows)
            yall[first : first + rows, column : column + inner] = turn[:, 0:rows].T.astype(BF)

    put_rows(med_rows, lat_rows)
    xall[0:med_rows, :] = mn_ref[...]
    xall[med_rows:, :] = ln_ref[...]
    gather_ld.relay()
    gather.relay()
    gather_ld.finish()
    gather.finish()

    exchange = Exchange(place, dot_all, dq_in, x_sems, place.far)
    image = image_ref[...]
    order = list(range(1, nb)) + [0]
    for g in range(nb // 2):
        pair = order[2 * g : 2 * g + 2]
        sources = [place.far(d) for d in pair]
        lanes = jnp.concatenate([lane_image(s, images_here, lat_rows) for s in sources], axis=1)
        allowed = image == lanes
        for h in range(heads):
            queries = jnp.concatenate([q_all[s, h] for s in sources], axis=1)
            grads = jnp.concatenate([dot_all[s, h] for s in sources], axis=1)
            lse = jnp.concatenate([ld_all[s, h : h + 1, :] for s in sources], axis=1)
            delta = jnp.concatenate(
                [ld_all[s, heads + h : heads + h + 1, :] for s in sources], axis=1
            )
            probs, score_grad = grads_of(
                h, kh_ref[h], vh_ref[h], queries, grads, lse, delta, allowed
            )
            key_part = dot_nt(queries, score_grad)
            value_part = dot_nt(grads, probs)
            dk[h] = key_part if g == 0 else dk[h] + key_part
            dv[h] = value_part if g == 0 else dv[h] + value_part
            dq = dot_nn(kt_ref[h], score_grad)
            for n, d in enumerate(pair):
                piece = dq[:, n * lat_rows : (n + 1) * lat_rows]
                if d:
                    dot_all[place.far(d), h] = piece.astype(BF)
                else:
                    dq_own[h] = dq_own[h] + piece
        for d in pair:
            if d:
                exchange.start(d)
    put_rows(0, med_rows)

    med_tile, lat_tile = med_bufs.shape[-1], lat_bufs.shape[-1]

    def back_rows(first, rows, tile):
        def tile_of(column):
            cols = pl.ds(column, tile)
            values = yall[first : first + rows, :]
            return dot_nt(values[:, 0:inner], wk_ref[cols, :]) + dot_nt(
                values[:, inner:], wv_ref[cols, :]
            )

        return tile_of

    med_sum = TensorSum(med_bufs, t_sems.at[0], back_rows(0, med_rows, med_tile))
    med_sum.give()
    med_sum.cross()

    for d in range(1, nb):
        exchange.wait_recv(d)
    for h in range(heads):
        value = dq_own[h]
        for d in range(1, nb):
            value = value + dq_in[d, h].astype(F32)
        turned(h, value, lat_rows)
    dq_low[...] = turn[:, 0:lat_rows].T.astype(BF)

    own_rows = model // nb
    chunk = 2 * own_rows * max(1, 128 // math.gcd(128, 2 * own_rows))
    per_chunk = chunk // own_rows

    def pair_copy(o):
        return remote(
            part.at[2 * o + 1 - place.inner], pair_in.at[o], y_sems.at[0, o], y_sems.at[1, o],
            {"blk": place.partner},
        )

    def far_copy(o, d):
        return remote(
            part.at[2 * o + place.inner], far_in.at[d], z_sems.at[0, d], z_sems.at[1, d],
            {"blk": 2 * o + place.inner},
        )

    for c in range(model // chunk):
        cols = slice(c * chunk, (c + 1) * chunk)
        lnx = xall[med_rows:, cols]
        query_part = dot_tn(lnx, dq_low[...]) * SCALE
        other_part = dot_tn(xall[:, cols], yall[...])
        for n in range(per_chunk):
            owner = c * per_chunk + n
            rows = slice(n * own_rows, (n + 1) * own_rows)
            part[owner, 0:own_rows, 0:inner] = query_part[rows].astype(BF)
            part[owner, 0:own_rows, inner:] = other_part[rows].astype(BF)
        for o in range(c * per_chunk // 2, (c + 1) * per_chunk // 2):
            pair_copy(o).start()

    def lat_tile_of(column):
        cols = pl.ds(column, lat_tile)
        return (
            back_rows(med_rows, lat_rows, lat_tile)(column)
            + dot_nt(dq_low[...], wq_ref[cols, :]) * SCALE
        )

    lat_sum = TensorSum(lat_bufs, t_sems.at[1], lat_tile_of)
    lat_sum.give()
    lat_sum.cross()

    def own_part(o):
        return part[2 * o + place.inner].astype(F32) + pair_in[o].astype(F32)

    for d in range(1, place.no):
        o = place.outer_to(d)
        pair_copy(o).wait_recv()
        part[2 * o + place.inner] = own_part(o).astype(BF)
        far_copy(o, d).start()
    med_sum.back()

    def put(column, tile):
        xall[0 : tile.shape[0], pl.ds(column, tile.shape[1])] = tile

    med_sum.finish(put)
    gain_rows = [fgain_ref[0:1, :], fgain_ref[1:2, :]]

    def norm_rows(i, carry):
        rows = pl.ds(pl.multiple_of(i * 128, 128), 128)
        xhat, rstd = normalised(med_ref[rows, :].astype(F32))
        q = xall[rows, :].astype(F32)
        mgrad_ref[rows, :] = norm_back(q, mg_ref[...], xhat, rstd)
        return (
            carry[0] + jnp.sum(q * xhat, axis=0, keepdims=True),
            carry[1] + jnp.sum(q, axis=0, keepdims=True),
        )

    zero = jnp.zeros((1, model), F32)
    med_gain = lax.fori_loop(0, med_rows // 128, norm_rows, (zero, zero))
    lat_sum.back()
    lat_sum.finish(put)
    xhat, rstd = normalised(lat_ref[...].astype(F32))
    q = xall[0:lat_rows, :].astype(F32)
    lgrad_ref[...] = mid_grad_ref[...] + norm_back(q, lg_ref[...], xhat, rstd)
    all_rows = [
        *med_gain,
        jnp.sum(q * xhat, axis=0, keepdims=True),
        jnp.sum(q, axis=0, keepdims=True),
        *gain_rows,
    ]
    for o in range(nb):
        for n, row in enumerate(all_rows):
            gain_out[o, n : n + 1, :] = row[:, o * own_rows : (o + 1) * own_rows]

    def gain_copy(d):
        return remote(
            gain_out.at[place.far(d)], gain_in.at[d], n_sems.at[0, d], n_sems.at[1, d],
            {"blk": place.far(d)},
        )

    for d in range(1, nb):
        gain_copy(d).start()
    pair_copy(place.outer).wait_recv()
    total = own_part(place.outer)
    for d in range(1, place.no):
        far_copy(place.outer_to(d), d).wait_recv()
        total = total + far_in[d].astype(F32)
    qg_ref[...] = total[0:own_rows, 0:inner]
    kg_ref[...] = total[0:own_rows, inner : 2 * inner]
    vg_ref[...] = total[0:own_rows, 2 * inner :]
    gains = gain_out[place.me]
    for d in range(1, nb):
        gain_copy(d).wait_recv()
        gains = gains + gain_in[d]
    gains_ref[...] = gains
    exchange.finish_sends()
    for d in range(1, nb):
        gain_copy(d).wait_send()
    for o in range(place.no):
        pair_copy(o).wait_send()
    for d in range(1, place.no):
        far_copy(place.outer_to(d), d).wait_send()


def call(kernel, out_shapes, scratch, collective_id, any_args=(), args=()):
    vmem = pl.BlockSpec(memory_space=pltpu.VMEM)
    return pl.pallas_call(
        kernel,
        out_shape=[jax.ShapeDtypeStruct(s, d) for s, d in out_shapes],
        in_specs=[vmem] * len(args) + [pl.BlockSpec(memory_space=pl.ANY)] * len(any_args),
        out_specs=[vmem] * len(out_shapes),
        scratch_shapes=scratch,
        compiler_params=pltpu.CompilerParams(
            collective_id=collective_id, has_side_effects=True, vmem_limit_bytes=VMEM_LIMIT
        ),
    )(*args, *any_args)


def gelu_pair(pre):
    bell = 0.5 * (1.0 + lax.erf(pre * math.sqrt(0.5)))
    slope = bell + pre * jnp.exp(-0.5 * pre * pre) * (1.0 / math.sqrt(2.0 * math.pi))
    return pre * bell, slope


def per_device_many(
    latents, media, query_weight, key_weight, value_weight, out_weight, up_weight, down_weight,
    media_gain, media_shift, latent_gain, latent_shift, feed_gain, feed_shift, cotangent, media_image,
):
    nb = lax.axis_size("blk")
    me = lax.axis_index("blk")
    lat_rows, model = latents.shape
    med_rows = media.shape[0]
    inner = query_weight.shape[1]
    heads = inner // HEAD_DIM
    ff_here = up_weight.shape[1]
    no = nb // 2
    own_rows = model // nb
    own_pad = -(-own_rows // 16) * 16
    dma = pltpu.SemaphoreType.DMA
    vm = pltpu.VMEM
    row = lambda v: v.reshape(1, -1)
    image = media_image.reshape(-1, 1)
    hd = HEAD_DIM
    cot_all = lax.all_gather(cotangent, "blk", axis=0, tiled=True)

    (ln, mn, q_all, kh, kt, vh, lkh, lkt, lvh, att, lse) = call(
        functools.partial(attend_kernel, nb),
        [
            ((lat_rows, model), BF), ((med_rows, model), BF), ((nb, heads, hd, lat_rows), BF),
            ((heads, med_rows, hd), BF), ((heads, hd, med_rows), BF), ((heads, med_rows, hd), BF),
            ((heads, lat_rows, hd), BF), ((heads, hd, lat_rows), BF), ((heads, lat_rows, hd), BF),
            ((heads, hd, lat_rows), F32), ((2 * heads, lat_rows), F32),
        ],
        [
            vm((heads, hd, med_rows), BF), vm((heads, hd, lat_rows), BF),
            vm((nb, heads, hd, lat_rows), BF), vm((nb, heads, hd, lat_rows), BF),
            vm((nb, 2 * heads, lat_rows), F32), vm((nb, 2 * heads, lat_rows), F32),
            dma((2, 2, no)), dma((2, nb)), dma((2, nb)),
        ],
        0,
        args=(
            latents, media, query_weight, key_weight, value_weight, row(latent_gain),
            row(latent_shift), row(media_gain), row(media_shift), image,
        ),
    )

    tile = 256
    tiles = model // 2 // tile
    (resampled, mid_grad, branch, dot, ld, fn, low, feed_gains) = call(
        feed_kernel,
        [
            ((lat_rows, model), BF), ((lat_rows, model), F32), ((lat_rows, model), BF),
            ((heads, hd, lat_rows), BF), ((2 * heads, lat_rows), F32), ((lat_rows, model), BF),
            ((lat_rows, inner), BF), ((8, model), F32),
        ],
        [
            vm((model, ff_here), BF), vm((ff_here, model), BF), vm((lat_rows, ff_here), F32),
            vm((lat_rows, model), F32), vm((lat_rows, ff_here), BF), vm((lat_rows, ff_here), BF),
            vm((inner, lat_rows), F32), vm((lat_rows, model), F32),
            vm((3, 6, tiles, lat_rows, tile), BF), dma((3, 3, 2, tiles)), dma((2,)),
        ],
        1,
        any_args=(up_weight, down_weight),
        args=(att, lse, latents, cotangent, out_weight, row(feed_gain), row(feed_shift)),
    )
    fn_all = lax.all_gather(fn, "blk", axis=0, tiled=True)
    low_all = lax.all_gather(low, "blk", axis=0, tiled=True)
    branch_all = lax.all_gather(branch, "blk", axis=0, tiled=True)

    (media_grad, latent_grad, query_grad, key_grad, value_grad, gains) = call(
        functools.partial(back_kernel, nb),
        [
            ((med_rows, model), F32), ((lat_rows, model), F32), ((own_rows, inner), F32),
            ((own_rows, inner), F32), ((own_rows, inner), F32), ((8, own_rows), F32),
        ],
        [
            vm((nb, heads, hd, lat_rows), BF), vm((nb, 2 * heads, lat_rows), F32),
            vm((heads, hd, med_rows), F32), vm((heads, hd, med_rows), F32),
            vm((heads, hd, lat_rows), F32),
            vm((nb, heads, hd, lat_rows), BF),
            vm((inner, med_rows), F32), vm((med_rows + lat_rows, model), BF),
            vm((med_rows + lat_rows, 2 * inner), BF), vm((lat_rows, inner), BF),
            vm((nb, own_pad, 3 * inner), BF), vm((no, own_pad, 3 * inner), BF),
            vm((no, own_pad, 3 * inner), BF),
            vm((nb, 8, own_rows), F32), vm((nb, 8, own_rows), F32),
            vm((6, tiles, med_rows, tile), BF), vm((6, tiles, lat_rows, tile), BF),
            dma((2, 2, no)), dma((2, 2, no)), dma((2, nb)), dma((2, no)), dma((2, no)),
            dma((2, nb)), dma((2, 3, 2, tiles)),
        ],
        2,
        args=(
            q_all, dot, ld, kh, kt, vh, lkh, lkt, lvh, ln, mn, query_weight, key_weight,
            value_weight, mid_grad, latents, media, row(latent_gain), row(media_gain), feed_gains,
            image,
        ),
    )

    def own_columns(rows):
        return lax.dynamic_slice_in_dim(rows, me * own_rows, own_rows, axis=1)

    group = math.gcd(nb, 8)
    group_rows = group * lat_rows

    def feed_step(carry, rows):
        up_acc, down_acc, out_acc = carry
        fn_rows, cot_rows, low_rows, branch_rows = rows
        hidden, slope = gelu_pair(dot_nn(fn_rows, up_weight))
        grad = (dot_nt(cot_rows, down_weight) * slope).astype(BF)
        return (
            up_acc + dot_tn(own_columns(fn_rows), grad),
            down_acc + dot_tn(hidden.astype(BF), own_columns(cot_rows)),
            out_acc + dot_tn(low_rows, own_columns(branch_rows)),
        ), None

    whole = (fn_all, cot_all, low_all, branch_all)
    start = (
        jnp.zeros((own_rows, ff_here), F32),
        jnp.zeros((ff_here, own_rows), F32),
        jnp.zeros((inner, own_rows), F32),
    )
    if group == nb:
        (up_grad, down_grad, out_grad), _ = feed_step(start, whole)
    else:
        (up_grad, down_grad, out_grad), _ = lax.scan(
            feed_step, start, tuple(v.reshape(nb // group, group_rows, -1) for v in whole)
        )
    return (
        resampled, media_grad, latent_grad, query_grad, key_grad, value_grad, out_grad, up_grad,
        down_grad, gains[0], gains[1], gains[2], gains[3], gains[4], gains[5],
    )


class Spread:
    def __init__(self, place, slots, sems):
        self.place, self.slots, self.sems = place, slots, sems
        self.t = lax.axis_index("tp")

    def source(self, kind, d):
        pc = self.place
        return 2 * pc.outer_from(d) + (1 - pc.inner if kind else pc.inner)

    def copy_z(self, d):
        pc = self.place
        slot = self.slots.at[pc.me, self.t]
        return remote(
            slot, slot, self.sems.at[0, 0, d], self.sems.at[0, 1, d],
            {"blk": 2 * pc.outer_to(d) + pc.inner},
        )

    def copy_y(self, d):
        slot = self.slots.at[self.source(0, d), self.t]
        return remote(
            slot, slot, self.sems.at[1, 0, d], self.sems.at[1, 1, d], {"blk": self.place.partner}
        )

    def arrived(self, kind, d):
        slot = self.slots.at[self.source(kind, d), self.t]
        remote(
            slot, slot, self.sems.at[kind, 0, d], self.sems.at[kind, 1, d], {"blk": self.place.partner}
        ).wait_recv()

    def start(self):
        for d in range(1, self.place.no):
            self.copy_z(d).start()
        self.copy_y(0).start()

    def relay(self):
        for d in range(1, self.place.no):
            self.arrived(0, d)
            self.copy_y(d).start()

    def finish(self):
        for d in range(self.place.no):
            self.arrived(1, d)
        for d in range(1, self.place.no):
            self.copy_z(d).wait_send()
        for d in range(self.place.no):
            self.copy_y(d).wait_send()


class Share:
    def __init__(self, place, slots, sems):
        self.place, self.slots, self.sems = place, slots, sems
        t = lax.axis_index("tp")
        self.t = t
        core, chip = t % 2, t // 2
        self.sibling_t = 2 * chip + 1 - core
        self.across_t = 2 * (1 - chip) + core
        self.diagonal_t = 2 * (1 - chip) + 1 - core

    def blocks(self, step):
        pc = self.place
        base = 2 * pc.outer_from(step)
        partner = (pc.no + step, base + 1 - pc.inner)
        return [partner] if step == 0 else [(step, base + pc.inner), partner]

    def copy(self, stage, n, s):
        slot = self.slots.at[s, self.across_t if stage == 2 else self.t]
        return remote(
            slot, slot, self.sems.at[stage, 0, n], self.sems.at[stage, 1, n],
            {"tp": self.sibling_t if stage else self.across_t},
        )

    def arrived(self, stage, n, s, t):
        slot = self.slots.at[s, t]
        remote(
            slot, slot, self.sems.at[stage, 0, n], self.sems.at[stage, 1, n], {"tp": self.sibling_t}
        ).wait_recv()

    def start(self, step):
        for n, s in self.blocks(step):
            self.copy(0, n, s).start()
            self.copy(1, n, s).start()

    def forward(self, step):
        for n, s in self.blocks(step):
            self.arrived(0, n, s, self.across_t)
            self.copy(2, n, s).start()

    def ready(self, step):
        for n, s in self.blocks(step):
            self.arrived(1, n, s, self.sibling_t)
            self.arrived(2, n, s, self.diagonal_t)

    def finish(self):
        for step in range(self.place.no):
            for n, s in self.blocks(step):
                for stage in range(3):
                    self.copy(stage, n, s).wait_send()


class Slices:
    def __init__(self, place, out, into, sems):
        self.place, self.out, self.into, self.sems = place, out, into, sems
        t = lax.axis_index("tp")
        self.core = t % 2
        self.sibling = {"tp": 2 * (t // 2) + 1 - self.core}

    def copy(self, d):
        pc = self.place
        return remote(
            self.out.at[pc.far(d), self.core], self.into.at[pc.me, self.core],
            self.sems.at[0, 0, d], self.sems.at[0, 1, d], {"blk": pc.far(d)},
        )

    def share(self, d):
        slot = self.into.at[self.place.near(d), self.core]
        return remote(slot, slot, self.sems.at[1, 0, d], self.sems.at[1, 1, d], self.sibling)

    def arrived(self, stage, d, core):
        slot = self.into.at[self.place.near(d), core]
        remote(
            slot, slot, self.sems.at[stage, 0, d], self.sems.at[stage, 1, d], self.sibling
        ).wait_recv()

    def start(self):
        for d in range(1, self.place.nb):
            self.copy(d).start()

    def relay(self):
        for d in range(1, self.place.nb):
            self.arrived(0, d, self.core)
            self.share(d).start()

    def finish(self):
        for d in range(1, self.place.nb):
            self.arrived(1, d, 1 - self.core)
        for d in range(1, self.place.nb):
            self.copy(d).wait_send()
            self.share(d).wait_send()

    def cut(self, rows):
        nb, _, half, width = self.out.shape
        for o in range(nb):
            piece = rows[:, o * width : (o + 1) * width]
            self.out[o, 0] = piece[0:half]
            self.out[o, 1] = piece[half:]
        for c in range(2):
            self.into[self.place.me, c] = self.out[self.place.me, c]


class Fold:
    def __init__(self, place, give, got, send, into, sems):
        self.place, self.give, self.got, self.send, self.into = place, give, got, send, into
        self.sems = sems

    def pair(self, o):
        return remote(
            self.give(o), self.got.at[o], self.sems.at[0, 0, o], self.sems.at[0, 1, o],
            {"blk": self.place.partner},
        )

    def far(self, d):
        o = self.place.outer_to(d)
        return remote(
            self.send(o), self.into.at[d], self.sems.at[1, 0, d], self.sems.at[1, 1, d],
            {"blk": 2 * o + self.place.inner},
        )

    def finish(self):
        for o in range(self.place.no):
            self.pair(o).wait_send()
        for d in range(1, self.place.no):
            self.far(d).wait_send()


def image_columns(image_ref, rows, lanes):
    line = image_ref[...].astype(F32).reshape(1, rows)
    return jnp.broadcast_to(line, (lanes, rows)).T


def pair_lanes(place, sources, images_here, lat_rows):
    return jnp.concatenate(
        [lane_image(s, images_here, lat_rows).astype(F32) for s in sources], axis=1
    )


def line_of(ref):
    return ref[...].reshape(1, -1)


def whole_greeting(place):
    return place.greeting() + TensorSum.greeting()


def near_layer(
    nb,
    lat_ref, cot_ref, image_ref, lg_ref, ls_ref, mg_ref, ms_ref, fg_ref, fs_ref,
    med_hbm, wq_hbm, wk_hbm, wv_hbm, wo_hbm, up_hbm, down_hbm,
    x_ref, out_ref, lgrad_ref, qg_ref, kg_ref, vg_ref, og_ref, ug_ref, down_t, gains_ref,
    med_ref, wq, wk, wv, wo, up, down, q_all, dot_all, ld_all, low_all, dq_all, fn_all, cot_all,
    kh_ref, kt_ref, vh_ref, vt, lkh_ref, lkt_ref, lvh_ref, lvt, att_ref, lse_ref,
    mine, give, got, send, into, mstat, gstat, rstat, sstat, istat,
    hg, mid, hidden, pre_grad, low_t, sum_buf, branch_ref, ln_out, lns_ref, br_out, br_in,
    dk, dv, dq_own, turn, yall, own_cols, part, pair_in, far_in, gain_out, gain_in, bufs, med_bufs,
    g_sems, a_sems, s_sems, f_sems, h_sems, n_sems, p_sems, t_sems, e_sems, w_sems,
):
    place = Place(nb)
    lat_rows = lat_ref.shape[0]
    med_rows, model = med_ref.shape
    heads = kh_ref.shape[0]
    inner = heads * HEAD_DIM
    images_here = lat_rows // LATENTS
    own_rows = model // nb
    quarter = lat_rows // 4
    ff_here = up.shape[1]
    ff_tile = math.gcd(ff_here, 512)
    sources = {
        "q": (wq_hbm, wq), "k": (wk_hbm, wk), "m": (med_hbm, med_ref), "v": (wv_hbm, wv),
        "down": (down_hbm, down), "wo": (wo_hbm, wo), "up": (up_hbm, up),
    }
    loads = {
        name: pltpu.make_async_copy(*ends, w_sems.at[n]) for n, (name, ends) in enumerate(sources.items())
    }
    for load in loads.values():
        load.start()
    greet(whole_greeting(place))
    for q in range(4):
        cot_all[place.me, q] = cot_ref[q * quarter : (q + 1) * quarter]
    spread_cot = Spread(place, cot_all, f_sems.at[0])
    spread_cot.start()
    row_image = lax.broadcasted_iota(jnp.int32, (lat_rows, lat_rows), 0) // LATENTS
    col_image = lax.broadcasted_iota(jnp.int32, (lat_rows, lat_rows), 1) // LATENTS
    same = row_image == col_image
    image = image_columns(image_ref, med_rows, lat_rows)
    image = jnp.concatenate([image, image], axis=1)
    order = [*range(1, place.no), 0]

    xhat, _ = normalised(lat_ref[...].astype(F32))
    ln = (xhat * line_of(lg_ref) + line_of(ls_ref)).astype(BF)
    x_ref[med_rows:, :] = ln

    def heads_t(rows, ref):
        turned = rows.T
        for h in range(heads):
            ref[h] = turned[h * HEAD_DIM : (h + 1) * HEAD_DIM].astype(BF)

    def heads_n(rows, ref):
        for h in range(heads):
            ref[h] = rows[:, h * HEAD_DIM : (h + 1) * HEAD_DIM].astype(BF)

    loads["q"].wait()
    heads_t(dot_nn(ln, wq[...]) * SCALE, q_all.at[place.me])
    gather = Gather(place, q_all, g_sems.at[0])
    gather.start()
    loads["k"].wait()
    lk = dot_nn(ln, wk[...])
    heads_n(lk, lkh_ref)
    heads_t(lk, lkt_ref)
    loads["m"].wait()

    med_gain, med_shift = line_of(mg_ref), line_of(ms_ref)

    def norm_rows(i, carry):
        rows = pl.ds(pl.multiple_of(i * 128, 128), 128)
        hat, _ = normalised(med_ref[rows, :].astype(F32))
        x_ref[rows, :] = (hat * med_gain + med_shift).astype(BF)
        return carry

    lax.fori_loop(0, med_rows // 128, norm_rows, 0)
    mk = dot_nn(x_ref[0:med_rows, :], wk[...])
    heads_n(mk, kh_ref)
    heads_t(mk, kt_ref)
    spread_cot.relay()
    loads["v"].wait()
    mv = dot_nn(x_ref[0:med_rows, :], wv[...])
    heads_n(mv, vh_ref)
    heads_t(mv, vt)
    gather.relay()
    lv = dot_nn(ln, wv[...])
    heads_n(lv, lvh_ref)
    heads_t(lv, lvt)
    own = []
    for h in range(heads):
        scores = jnp.where(same, dot_nn(lkh_ref[h], q_all[place.me, h]), NEG_FILL)
        top = jnp.max(scores, axis=0, keepdims=True)
        weights = jnp.exp(scores - top)
        total = jnp.sum(weights, axis=0, keepdims=True)
        own.append((top, total, dot_nn(lvt[h], weights.astype(BF))))
    loads["down"].wait()

    def back_hidden(i, carry):
        cols = pl.ds(pl.multiple_of(i * ff_tile, ff_tile), ff_tile)
        hg[:, cols] = dot_nt(cot_ref[...], down[cols, :])
        return carry

    lax.fori_loop(0, ff_here // ff_tile, back_hidden, 0)
    ln_slices = Slices(place, ln_out, lns_ref, n_sems.at[0])
    ln_slices.cut(ln)
    gather.finish()
    spread_cot.finish()
    share_cot = Share(place, cot_all, h_sems.at[0])
    for step in range(place.no):
        share_cot.start(step)

    fold = Fold(place, lambda o: give.at[o], got, lambda o: send.at[o], into, a_sems.at[0])
    stats = Fold(place, lambda o: gstat.at[o], rstat, lambda o: sstat.at[o], istat, s_sems)

    def piece(acc_ref, stat_ref, at):
        return [
            (
                stat_ref[at, h : h + 1, :],
                stat_ref[at, heads + h : heads + h + 1, :],
                acc_ref[at, h].astype(F32),
            )
            for h in range(heads)
        ]

    def merged(left, right):
        both = []
        for (lt, ll, la), (rt, rl, ra) in zip(left, right):
            top = jnp.maximum(lt, rt)
            lf, rf = jnp.exp(lt - top), jnp.exp(rt - top)
            both.append((top, ll * lf + rl * rf, la * lf + ra * rf))
        return both

    def pass_attention(d):
        o = place.outer_to(d)
        stats.pair(o).wait_recv()
        fold.pair(o).wait_recv()
        both = merged(piece(mine, mstat, o), piece(got, rstat, o))
        if d == 0:
            return both
        for h, (top, total, acc) in enumerate(both):
            sstat[o, h : h + 1, :] = top
            sstat[o, heads + h : heads + h + 1, :] = total
            send[o, h] = acc.astype(BF)
        stats.far(d).start()
        fold.far(d).start()
        return None

    for step, d in enumerate(order):
        o = place.outer_to(d)
        sources = [2 * o + place.inner, 2 * o + 1 - place.inner]
        allowed = image == pair_lanes(place, sources, images_here, lat_rows)
        for h in range(heads):
            queries = jnp.concatenate([q_all[s, h] for s in sources], axis=1)
            scores = jnp.where(allowed, dot_nn(kh_ref[h], queries), NEG_FILL)
            top = jnp.max(scores, axis=0, keepdims=True)
            weights = jnp.exp(scores - top)
            total = jnp.sum(weights, axis=0, keepdims=True)
            acc = dot_nn(vt[h], weights.astype(BF))
            mine[o, h] = acc[:, 0:lat_rows]
            give[o, h] = acc[:, lat_rows:].astype(BF)
            for ref, lanes in ((mstat, slice(0, lat_rows)), (gstat, slice(lat_rows, 2 * lat_rows))):
                ref[o, h : h + 1, :] = top[:, lanes]
                ref[o, heads + h : heads + h + 1, :] = total[:, lanes]
        stats.pair(o).start()
        fold.pair(o).start()
        if step:
            pass_attention(order[step - 1])
    result = merged(own, pass_attention(0))
    for d in range(1, place.no):
        stats.far(d).wait_recv()
        fold.far(d).wait_recv()
        result = merged(result, piece(into, istat, d))
    lse_ref[...] = jnp.zeros_like(lse_ref)
    for h, (top, total, acc) in enumerate(result):
        att_ref[h] = acc / total
        lse_ref[h : h + 1, :] = top + jnp.log(total)

    for h in range(heads):
        low_t[h * HEAD_DIM : (h + 1) * HEAD_DIM, :] = att_ref[h]
    low_all[place.me] = low_t[...].T.astype(BF)
    low_gather = Gather(place, low_all, g_sems.at[1])
    low_gather.start()
    ln_slices.start()
    low = low_all[place.me]

    def put_sum(column, tile):
        sum_buf[:, pl.ds(column, tile.shape[1])] = tile

    def tile_sum(n, tile_of):
        return TensorSum(bufs.at[n], t_sems.at[n], tile_of)

    width = bufs.shape[-1]
    branch = tile_sum(0, lambda c: dot_nn(low, wo[:, pl.ds(c, width)]))
    loads["wo"].wait()
    branch.give()
    branch.cross()
    for step in range(place.no // 2):
        share_cot.forward(step)
    branch.back()
    branch.finish(put_sum)
    mid[...] = lat_ref[...].astype(F32) + sum_buf[...].astype(F32)
    xhat, rstd = normalised(mid[...])
    normed = (xhat * line_of(fg_ref) + line_of(fs_ref)).astype(BF)
    for q in range(4):
        fn_all[place.me, q] = normed[q * quarter : (q + 1) * quarter]
    spread_fn = Spread(place, fn_all, f_sems.at[1])
    spread_fn.start()
    for step in range(place.no // 2, place.no):
        share_cot.forward(step)
    loads["up"].wait()

    def feed_forward(i, carry):
        cols = pl.ds(pl.multiple_of(i * ff_tile, ff_tile), ff_tile)
        pre = dot_nn(normed, up[:, cols])
        value, slope = gelu_pair(pre)
        hidden[:, cols] = value.astype(BF)
        pre_grad[:, cols] = (hg[:, cols] * slope).astype(BF)
        return carry

    lax.fori_loop(0, ff_here // ff_tile, feed_forward, 0)
    grads = tile_sum(1, lambda c: dot_nt(pre_grad[...], up[pl.ds(c, width), :]))
    feed = tile_sum(2, lambda c: dot_nn(hidden[...], down[:, pl.ds(c, width)]))
    grads.give()
    grads.cross()
    feed.give()
    low_gather.relay()
    grads.back()
    spread_fn.relay()
    grads.finish(put_sum)
    fng = sum_buf[...].astype(F32)
    xhat, rstd = normalised(mid[...])
    mid_grad = cot_ref[...].astype(F32) + norm_back(fng, line_of(fg_ref), xhat, rstd)
    lgrad_ref[...] = mid_grad
    branch_ref[...] = mid_grad.astype(BF)
    feed_gains = [
        jnp.sum(fng * xhat, axis=0, keepdims=True), jnp.sum(fng, axis=0, keepdims=True)
    ]
    back = dot_nt(wo[...], branch_ref[...])
    ld_all[place.me] = lse_ref[...]
    for h in range(heads):
        piece_grad = back[h * HEAD_DIM : (h + 1) * HEAD_DIM, :].astype(BF)
        dot_all[place.me, h] = piece_grad
        ld_all[place.me, heads + h : heads + h + 1, :] = jnp.sum(
            piece_grad.astype(F32) * att_ref[h], axis=0, keepdims=True
        )

    gather = Gather(place, dot_all, g_sems.at[2])
    gather_ld = Gather(place, ld_all, g_sems.at[3])
    gather_ld.start()
    gather.start()
    feed.cross()
    spread_fn.finish()
    share_fn = Share(place, fn_all, h_sems.at[1])
    for step in range(place.no):
        share_fn.start(step)

    shares = [share_cot, share_fn]

    def grads_of(keys, values, queries, grads, lse, delta, allowed):
        scores = jnp.where(allowed, dot_nn(keys, queries), NEG_FILL)
        probs = jnp.exp(scores - lse)
        score_grad = (probs * (dot_nn(values, grads) - delta)).astype(BF)
        return probs.astype(BF), score_grad

    for h in range(heads):
        queries, grads = q_all[place.me, h], dot_all[place.me, h]
        probs, score_grad = grads_of(
            lkh_ref[h], lvh_ref[h], queries, grads,
            ld_all[place.me, h : h + 1, :], ld_all[place.me, heads + h : heads + h + 1, :], same,
        )
        dk[h, :, 0:lat_rows] = dot_nt(queries, score_grad)
        dv[h, :, 0:lat_rows] = dot_nt(grads, probs)
        dq_own[h] = dot_nn(lkt_ref[h], score_grad)

    def put_rows(first, rows):
        for k, acc in enumerate((dk, dv)):
            for h in range(heads):
                turn[h * HEAD_DIM : (h + 1) * HEAD_DIM, 0:rows] = acc[h, :, 0:rows]
            yall[k, first : first + rows, :] = turn[:, 0:rows].T.astype(BF)

    put_rows(med_rows, lat_rows)
    slices = Slices(place, br_out, br_in, n_sems.at[1])
    slices.cut(branch_ref[...])
    slices.start()

    pick = (
        lax.broadcasted_iota(jnp.int32, (own_rows, model), 1)
        == lax.broadcasted_iota(jnp.int32, (own_rows, model), 0) + place.me * own_rows
    )
    pick = jnp.where(pick, 1.0, 0.0).astype(BF)
    ff_tiles = ff_here // ff_tile

    def step_rows(j, rows):
        base = 2 * place.outer_from(j)
        blocks = base + place.inner, base + 1 - place.inner
        return jnp.concatenate([rows[b].reshape(lat_rows, model) for b in blocks], axis=0)

    def feed_tile(j, i):
        fn_rows, cot_rows = step_rows(j, fn_all), step_rows(j, cot_all)
        if i == 0:
            own_cols[0] = dot_nt(pick, fn_rows).astype(BF)
            own_cols[1] = dot_nt(pick, cot_rows).astype(BF)
        cols = slice(i * ff_tile, (i + 1) * ff_tile)
        value, slope = gelu_pair(dot_nn(fn_rows, up[:, cols]))
        grad = (dot_nt(cot_rows, down[cols, :]) * slope).astype(BF)
        up_part = dot_nn(own_cols[0], grad)
        down_part = dot_nn(own_cols[1], value.astype(BF))
        if j == 0:
            ug_ref[:, cols] = up_part
            down_t[:, cols] = down_part
        else:
            ug_ref[:, cols] += up_part
            down_t[:, cols] += down_part

    fed = [0]

    def feed_on(count):
        for n in range(fed[0], min(fed[0] + count, place.no * ff_tiles)):
            j, i = divmod(n, ff_tiles)
            if i == 0:
                for share in shares:
                    share.ready(j)
            feed_tile(j, i)
        fed[0] += count

    feed.back()
    gather_ld.relay()
    gather.relay()
    ln_slices.relay()
    feed.finish(put_sum)
    out_ref[...] = (mid[...] + sum_buf[...].astype(F32)).astype(BF)
    gather_ld.finish()
    gather.finish()
    fold.finish()
    stats.finish()
    low_gather.finish()
    ln_slices.finish()

    dq_fold = Fold(place, lambda o: give.at[o], got, lambda o: send.at[o], into, a_sems.at[1])
    folds = [
        Fold(
            place, lambda o, f=f: part.at[f, 2 * o + 1 - place.inner], pair_in.at[f],
            lambda o, f=f: part.at[f, 2 * o + place.inner], far_in.at[f], p_sems.at[f],
        )
        for f in range(2)
    ]

    def pass_queries(d):
        o = place.outer_to(d)
        dq_fold.pair(o).wait_recv()
        for h in range(heads):
            send[o, h] = (mine[o, h] + got[o, h].astype(F32)).astype(BF)
        dq_fold.far(d).start()

    for step, d in enumerate(order):
        o = place.outer_to(d)
        sources = [2 * o + place.inner, 2 * o + 1 - place.inner]
        allowed = image == pair_lanes(place, sources, images_here, lat_rows)
        for h in range(heads):
            queries = jnp.concatenate([q_all[s, h] for s in sources], axis=1)
            grads = jnp.concatenate([dot_all[s, h] for s in sources], axis=1)
            lse = jnp.concatenate([ld_all[s, h : h + 1, :] for s in sources], axis=1)
            delta = jnp.concatenate(
                [ld_all[s, heads + h : heads + h + 1, :] for s in sources], axis=1
            )
            probs, score_grad = grads_of(kh_ref[h], vh_ref[h], queries, grads, lse, delta, allowed)
            key_part = dot_nt(queries, score_grad)
            value_part = dot_nt(grads, probs)
            dk[h] = key_part if step == 0 else dk[h] + key_part
            dv[h] = value_part if step == 0 else dv[h] + value_part
            dq = dot_nn(kt_ref[h], score_grad)
            mine[o, h] = dq[:, 0:lat_rows]
            give[o, h] = dq[:, lat_rows:].astype(BF)
        dq_fold.pair(o).start()
        if step:
            pass_queries(order[step - 1])
        share_fn.forward(step)

    put_rows(0, med_rows)

    chunk = 2 * own_rows

    def weigh(d, k):
        o = place.outer_to(d)
        cols = pl.ds(pl.multiple_of(o * chunk, 128), chunk)
        value = dot_tn(x_ref[:, cols], yall[k])
        part[k, 2 * o] = value[0:own_rows].astype(BF)
        part[k, 2 * o + 1] = value[own_rows:].astype(BF)
        folds[k].pair(o).start()

    def both(d, k):
        o = place.outer_to(d)
        return part[k, 2 * o + place.inner].astype(F32) + pair_in[k, o].astype(F32)

    def pass_on(d, k):
        o = place.outer_to(d)
        folds[k].pair(o).wait_recv()
        if d:
            part[k, 2 * o + place.inner] = both(d, k).astype(BF)
            folds[k].far(d).start()

    med_tile, lat_tile = med_bufs.shape[-1], bufs.shape[-1]

    def back_rows(first, rows, tile):
        def tile_of(column):
            cols = pl.ds(column, tile)
            return dot_nt(yall[0, first : first + rows, :], wk[cols, :]) + dot_nt(
                yall[1, first : first + rows, :], wv[cols, :]
            )

        return tile_of

    med_sum = TensorSum(med_bufs, t_sems.at[4], back_rows(0, med_rows, med_tile))
    tasks = [(d, k) for d in order for k in range(2)]
    ahead = 3
    weigh(*tasks[0])
    weigh(*tasks[1])
    med_sum.give()
    for task in tasks[2:ahead]:
        weigh(*task)
    med_sum.cross()

    def lat_tile_of(column):
        cols = pl.ds(column, lat_tile)
        return (
            back_rows(med_rows, lat_rows, lat_tile)(column)
            + dot_nt(dq_all[place.me], wq[cols, :]) * SCALE
        )

    lat_sum = TensorSum(bufs.at[0], t_sems.at[3], lat_tile_of)
    dq_gather = Gather(place, dq_all, g_sems.at[4])

    def query_sums():
        o = place.outer
        dq_fold.pair(o).wait_recv()
        for h in range(heads):
            dq_own[h] = dq_own[h] + mine[o, h] + got[o, h].astype(F32)
        for d in range(1, place.no):
            dq_fold.far(d).wait_recv()
            for h in range(heads):
                dq_own[h] = dq_own[h] + into[d, h].astype(F32)
        for h in range(heads):
            turn[h * HEAD_DIM : (h + 1) * HEAD_DIM, 0:lat_rows] = dq_own[h]
        dq_all[place.me] = turn[:, 0:lat_rows].T.astype(BF)
        dq_gather.start()
        lat_sum.give()

    def put(column, tile):
        x_ref[0:med_rows, pl.ds(column, tile.shape[1])] = tile

    def put_lat(column, tile):
        x_ref[med_rows:, pl.ds(column, tile.shape[1])] = tile

    def norm_rows(i, carry):
        rows = pl.ds(pl.multiple_of(i * 128, 128), 128)
        xhat, _ = normalised(med_ref[rows, :].astype(F32))
        q = x_ref[rows, :].astype(F32)
        return (
            carry[0] + jnp.sum(q * xhat, axis=0, keepdims=True),
            carry[1] + jnp.sum(q, axis=0, keepdims=True),
        )

    def gain_copy(d):
        return remote(
            gain_out.at[place.far(d)], gain_in.at[d], e_sems.at[0, d], e_sems.at[1, d],
            {"blk": place.far(d)},
        )

    def norm_grads():
        med_sum.finish(put)
        zero = jnp.zeros((1, model), F32)
        med_gain = lax.fori_loop(0, med_rows // 128, norm_rows, (zero, zero))
        lat_sum.finish(put_lat)
        xhat, rstd = normalised(lat_ref[...].astype(F32))
        q = x_ref[med_rows:, :].astype(F32)
        lgrad_ref[...] += norm_back(q, line_of(lg_ref), xhat, rstd)
        all_rows = [
            *med_gain,
            jnp.sum(q * xhat, axis=0, keepdims=True),
            jnp.sum(q, axis=0, keepdims=True),
            *feed_gains,
        ]
        for o in range(nb):
            for n, line in enumerate(all_rows):
                gain_out[o, n : n + 1, :] = line[:, o * own_rows : (o + 1) * own_rows]
        for d in range(1, nb):
            gain_copy(d).start()

    all_rows_of = lambda ref: ref[...].reshape(nb * lat_rows, -1)

    def out_weights():
        slices.finish()
        og_ref[...] = dot_tn(all_rows_of(br_in), all_rows_of(low_all))

    between = {
        0: query_sums,
        3: lambda: (slices.relay(), lat_sum.cross(), dq_gather.relay()),
        5: med_sum.back,
        6: lat_sum.back,
        7: out_weights,
    }
    pace = -(-place.no * ff_tiles // len(tasks))
    for n in range(len(tasks)):
        if n + ahead < len(tasks):
            weigh(*tasks[n + ahead])
        feed_on(pace)
        if n in between:
            between.pop(n)()
        pass_on(*tasks[n])
    for late in between.values():
        late()
    norm_grads()
    feed_on(place.no * ff_tiles - fed[0])
    for share in shares:
        share.finish()
    dq_gather.finish()
    qg_ref[...] = dot_tn(all_rows_of(lns_ref), all_rows_of(dq_all)) * SCALE
    for k, ref in enumerate((kg_ref, vg_ref)):
        total = both(0, k)
        for d in range(1, place.no):
            folds[k].far(d).wait_recv()
            total = total + far_in[k, d].astype(F32)
        ref[...] = total
    gains = gain_out[place.me]
    for d in range(1, nb):
        gain_copy(d).wait_recv()
        gains = gains + gain_in[d]
    gains_ref[...] = gains
    for d in range(1, nb):
        gain_copy(d).wait_send()
    dq_fold.finish()
    for fold in folds:
        fold.finish()


def near_call(kernel, out_shapes, scratch, collective_id, args, any_args, any_outs=()):
    vmem = pl.BlockSpec(memory_space=pltpu.VMEM)
    anywhere = pl.BlockSpec(memory_space=pl.ANY)
    return pl.pallas_call(
        kernel,
        out_shape=[jax.ShapeDtypeStruct(s, d) for s, d in (*out_shapes, *any_outs)],
        in_specs=[vmem] * len(args) + [anywhere] * len(any_args),
        out_specs=[vmem] * len(out_shapes) + [anywhere] * len(any_outs),
        scratch_shapes=scratch,
        compiler_params=pltpu.CompilerParams(
            collective_id=collective_id, has_side_effects=True, vmem_limit_bytes=VMEM_LIMIT
        ),
    )(*args, *any_args)


def per_device(
    latents, media, query_weight, key_weight, value_weight, out_weight, up_weight, down_weight,
    media_gain, media_shift, latent_gain, latent_shift, feed_gain, feed_shift, cotangent, media_image,
):
    nb = lax.axis_size("blk")
    lat_rows, model = latents.shape
    med_rows = media.shape[0]
    inner = query_weight.shape[1]
    heads = inner // HEAD_DIM
    ff_here = up_weight.shape[1]
    no = nb // 2
    own_rows = model // nb
    dma = pltpu.SemaphoreType.DMA
    vm = pltpu.VMEM
    hd = HEAD_DIM
    half, quarter = lat_rows // 2, lat_rows // 4
    tile = 256
    tiles = model // 2 // tile
    every = med_rows + lat_rows
    block_t = (nb, heads, hd, lat_rows)
    pair_t = (no, heads, hd, lat_rows)
    rows_t = (nb, 4, quarter, model)
    slice_t = (nb, 2, half, own_rows)
    media_sum, *results = near_call(
        functools.partial(near_layer, nb),
        [
            ((every, model), BF), ((lat_rows, model), BF), ((lat_rows, model), F32),
            *[((own_rows, inner), F32)] * 4, *[((own_rows, ff_here), F32)] * 2, ((8, own_rows), F32),
        ],
        [
            vm((med_rows, model), BF), *[vm((model, inner), BF)] * 3, vm((inner, model), BF),
            vm((model, ff_here), BF), vm((ff_here, model), BF), vm(block_t, BF), vm(block_t, BF),
            vm((nb, 2 * heads, lat_rows), F32), vm((nb, lat_rows, inner), BF), vm((nb, lat_rows, inner), BF),
            vm(rows_t, BF), vm(rows_t, BF),
            vm((heads, med_rows, hd), BF), vm((heads, hd, med_rows), BF), vm((heads, med_rows, hd), BF),
            vm((heads, hd, med_rows), BF), vm((heads, lat_rows, hd), BF), vm((heads, hd, lat_rows), BF),
            vm((heads, lat_rows, hd), BF), vm((heads, hd, lat_rows), BF), vm((heads, hd, lat_rows), F32),
            vm((2 * heads, lat_rows), F32),
            vm(pair_t, F32), *[vm(pair_t, BF)] * 4, *[vm((no, 2 * heads, lat_rows), F32)] * 5,
            vm((lat_rows, ff_here), F32), vm((lat_rows, model), F32), vm((lat_rows, ff_here), BF),
            vm((lat_rows, ff_here), BF), vm((inner, lat_rows), F32), vm((lat_rows, model), BF),
            vm((lat_rows, model), BF), *[vm(slice_t, BF)] * 4,
            vm((heads, hd, med_rows), F32), vm((heads, hd, med_rows), F32), vm((heads, hd, lat_rows), F32),
            vm((inner, med_rows), F32), vm((2, every, inner), BF), vm((2, own_rows, 2 * lat_rows), BF),
            vm((2, nb, own_rows, inner), BF), vm((2, no, own_rows, inner), BF), vm((2, no, own_rows, inner), BF),
            vm((nb, 8, own_rows), F32), vm((nb, 8, own_rows), F32), vm((3, 6, tiles, lat_rows, tile), BF),
            vm((6, tiles, med_rows, tile), BF),
            dma((5, 2, 2, no)), dma((2, 2, 2, no)), dma((2, 2, no)), dma((2, 2, 2, no)),
            dma((2, 3, 2, 2 * no)), dma((2, 2, 2, nb)), dma((2, 2, 2, no)), dma((5, 3, 2, tiles)),
            dma((2, nb)), dma((7,)),
        ],
        0,
        (
            latents, cotangent, media_image, latent_gain, latent_shift, media_gain, media_shift, feed_gain,
            feed_shift,
        ),
        (media, query_weight, key_weight, value_weight, out_weight, up_weight, down_weight),
    )
    return last_step(media, media_gain, *results[:1], media_sum, *results[1:])


def last_kernel(media_ref, sum_ref, gain_ref, gains_ref, *refs):
    count = (len(refs) - 7) // 2
    moved, grad_ref = refs[0:count], refs[count]
    placed, gain_refs = refs[count + 1 : 2 * count + 1], refs[2 * count + 1 :]
    for source, target in zip(moved, placed, strict=True):
        target[...] = source[...]

    @pl.when(pl.program_id(0) == 0)
    def _():
        for n, ref in enumerate(gain_refs):
            ref[...] = gains_ref[n, :]

    xhat, rstd = normalised(media_ref[...].astype(F32))
    grad_ref[...] = norm_back(sum_ref[...].astype(F32), line_of(gain_ref), xhat, rstd)


def last_step(media, media_gain, resampled, media_sum, *rest):
    *moved, gains = (resampled, *rest)
    own_rows = gains.shape[1]
    steps = 2
    blocked = lambda v: pl.BlockSpec((v.shape[0] // steps, v.shape[1]), lambda i: (i, 0))
    gain_spec = pl.BlockSpec((own_rows,), lambda i: (0,))
    outs = pl.pallas_call(
        last_kernel,
        grid=(steps,),
        out_shape=[
            jax.ShapeDtypeStruct(media.shape, F32),
            *[jax.ShapeDtypeStruct(v.shape, v.dtype) for v in moved],
            *[jax.ShapeDtypeStruct((own_rows,), F32)] * 6,
        ],
        in_specs=[
            blocked(media), blocked(media), pl.BlockSpec(media_gain.shape, lambda i: (0,)),
            pl.BlockSpec(gains.shape, lambda i: (0, 0)), *[blocked(v) for v in moved],
        ],
        out_specs=[blocked(media), *[blocked(v) for v in moved], *[gain_spec] * 6],
        compiler_params=pltpu.CompilerParams(vmem_limit_bytes=VMEM_LIMIT),
    )(media, media_sum, media_gain, gains, *moved)
    (
        media_grad, resampled, latent_grad, query_grad, key_grad, value_grad, out_turned, up_grad,
        down_turned, *gain_grads,
    ) = outs
    return (
        resampled, media_grad, latent_grad, query_grad, key_grad, value_grad, out_turned.T, up_grad,
        down_turned.T, *gain_grads,
    )


def solution(mesh):
    in_specs = (
        P("blk", None), P("blk", None), P(None, "tp"), P(None, "tp"), P(None, "tp"), P("tp", None),
        P(None, "tp"), P("tp", None), P(), P(), P(), P(), P(), P(), P("blk", None), P("blk"),
    )
    out_specs = (
        P("blk", None), P("blk", None), P("blk", None), P("blk", "tp"), P("blk", "tp"),
        P("blk", "tp"), P("tp", "blk"), P("blk", "tp"), P("tp", "blk"), P("blk"), P("blk"),
        P("blk"), P("blk"), P("blk"), P("blk"),
    )
    body = per_device if mesh.shape["blk"] <= 16 else per_device_many
    return jax.shard_map(
        body, mesh=mesh, in_specs=in_specs, out_specs=out_specs, check_vma=False
    )
```

```python
import functools
import math

import jax
import jax.numpy as jnp
from jax import lax
from jax.experimental import pallas as pl
from jax.experimental.pallas import tpu as pltpu
from jax.sharding import PartitionSpec as P

HEAD_DIM = 96
LATENTS = 64
NEG_FILL = -1e30
NORM_EPS = 1e-05
BF = jnp.bfloat16
F32 = jnp.float32
MESH = pl.DeviceIdType.MESH
VMEM_LIMIT = 60 * 1024 * 1024
SCALE = 1.0 / math.sqrt(HEAD_DIM)


def dot_nn(a, b):
    return jnp.dot(a, b, preferred_element_type=F32)


def dot_nt(a, b):
    return lax.dot_general(a, b, (((1,), (1,)), ((), ())), preferred_element_type=F32)


def dot_tn(a, b):
    return lax.dot_general(a, b, (((0,), (0,)), ((), ())), preferred_element_type=F32)


def normalised(x):
    centred = x - jnp.mean(x, axis=-1, keepdims=True)
    rstd = lax.rsqrt(jnp.mean(centred * centred, axis=-1, keepdims=True) + NORM_EPS)
    return centred * rstd, rstd


def norm_back(q, gain, xhat, rstd):
    qg = q * gain
    inner = jnp.mean(qg * xhat, axis=-1, keepdims=True)
    return (qg - jnp.mean(qg, axis=-1, keepdims=True) - xhat * inner) * rstd


def greet(devices):
    barrier = pltpu.get_barrier_semaphore()
    for device in devices:
        pl.semaphore_signal(barrier, inc=1, device_id=device, device_id_type=MESH)
    pl.semaphore_wait(barrier, len(devices))


def remote(src, dst, send_sem, recv_sem, device):
    return pltpu.make_async_remote_copy(
        src_ref=src,
        dst_ref=dst,
        send_sem=send_sem,
        recv_sem=recv_sem,
        device_id=device,
        device_id_type=MESH,
    )


class Place:
    def __init__(self, nb):
        self.nb = nb
        self.no = nb // 2
        self.me = lax.axis_index("blk")
        self.outer = self.me // 2
        self.inner = self.me % 2
        self.partner = 2 * self.outer + 1 - self.inner

    def far(self, d):
        return (self.me + d) % self.nb

    def near(self, d):
        return (self.me - d + self.nb) % self.nb

    def outer_to(self, d):
        return (self.outer + d) % self.no

    def outer_from(self, d):
        return (self.outer - d + self.no) % self.no

    def greeting(self):
        return [{"blk": self.far(d)} for d in range(1, self.nb)]


class Gather:
    def __init__(self, place, slots, sems):
        self.place, self.slots, self.sems = place, slots, sems

    def copy_z(self, d):
        pc = self.place
        slot = self.slots.at[pc.me]
        return remote(
            slot, slot, self.sems.at[0, 0, d], self.sems.at[0, 1, d],
            {"blk": 2 * pc.outer_to(d) + pc.inner},
        )

    def copy_y(self, d):
        pc = self.place
        slot = self.slots.at[2 * pc.outer_from(d) + pc.inner]
        return remote(
            slot, slot, self.sems.at[1, 0, d], self.sems.at[1, 1, d], {"blk": pc.partner}
        )

    def start(self):
        for d in range(1, self.place.no):
            self.copy_z(d).start()
        self.copy_y(0).start()

    def relay(self):
        pc = self.place
        for d in range(1, pc.no):
            arrived = self.slots.at[2 * pc.outer_from(d) + pc.inner]
            remote(
                arrived, arrived, self.sems.at[0, 0, d], self.sems.at[0, 1, d], {"blk": pc.partner}
            ).wait_recv()
            self.copy_y(d).start()

    def finish(self):
        pc = self.place
        for d in range(pc.no):
            slot = self.slots.at[2 * pc.outer_from(d) + 1 - pc.inner]
            remote(
                slot, slot, self.sems.at[1, 0, d], self.sems.at[1, 1, d], {"blk": pc.partner}
            ).wait_recv()
        for d in range(1, pc.no):
            self.copy_z(d).wait_send()
        for d in range(pc.no):
            self.copy_y(d).wait_send()


class Exchange:
    def __init__(self, place, out, into, sems, slot=lambda d: d):
        self.place, self.out, self.into, self.sems, self.slot = place, out, into, sems, slot

    def copy(self, d):
        return remote(
            self.out.at[self.slot(d)], self.into.at[d], self.sems.at[0, d], self.sems.at[1, d],
            {"blk": self.place.far(d)},
        )

    def start(self, d):
        self.copy(d).start()

    def wait_recv(self, d):
        self.copy(d).wait_recv()

    def finish_sends(self):
        for d in range(1, self.place.nb):
            self.copy(d).wait_send()


def lane_image(source, images_here, width):
    lane = lax.broadcasted_iota(jnp.int32, (1, width), 1)
    return source * images_here + lane // LATENTS


def attend_kernel(
    nb,
    lat_ref, med_ref, wq_ref, wk_ref, wv_ref, lg_ref, ls_ref, mg_ref, ms_ref, image_ref,
    ln_ref, mn_ref, q_all, kh_ref, kt_ref, vh_ref, lkh_ref, lkt_ref, lvh_ref, att_ref, lse_ref,
    vt, lvt, acc_out, acc_in, stat_out, stat_in, g_sems, a_sems, s_sems,
):
    place = Place(nb)
    lat_rows = lat_ref.shape[0]
    med_rows = med_ref.shape[0]
    heads = kh_ref.shape[0]
    images_here = lat_rows // LATENTS
    greet(place.greeting())

    xhat, _ = normalised(lat_ref[...].astype(F32))
    ln_ref[...] = (xhat * lg_ref[...] + ls_ref[...]).astype(BF)
    ln = ln_ref[...]

    def heads_t(rows, ref):
        turned = rows.T
        for h in range(heads):
            ref[h] = turned[h * HEAD_DIM : (h + 1) * HEAD_DIM].astype(BF)

    def heads_n(rows, ref):
        for h in range(heads):
            ref[h] = rows[:, h * HEAD_DIM : (h + 1) * HEAD_DIM].astype(BF)

    heads_t(dot_nn(ln, wq_ref[...]) * SCALE, q_all.at[place.me])
    gather = Gather(place, q_all, g_sems)
    gather.start()
    lk = dot_nn(ln, wk_ref[...])
    heads_n(lk, lkh_ref)
    heads_t(lk, lkt_ref)
    lv = dot_nn(ln, wv_ref[...])
    heads_n(lv, lvh_ref)
    heads_t(lv, lvt)

    def norm_rows(i, carry):
        rows = pl.ds(pl.multiple_of(i * 128, 128), 128)
        hat, _ = normalised(med_ref[rows, :].astype(F32))
        mn_ref[rows, :] = (hat * mg_ref[...] + ms_ref[...]).astype(BF)
        return carry

    lax.fori_loop(0, med_rows // 128, norm_rows, 0)
    mk = dot_nn(mn_ref[...], wk_ref[...])
    heads_n(mk, kh_ref)
    heads_t(mk, kt_ref)
    gather.relay()
    mv = dot_nn(mn_ref[...], wv_ref[...])
    heads_n(mv, vh_ref)
    heads_t(mv, vt)
    gather.finish()

    exchange = Exchange(place, acc_out, acc_in, a_sems)
    stats = Exchange(place, stat_out, stat_in, s_sems)
    image = image_ref[...]
    order = list(range(1, nb)) + [0]
    for g in range(nb // 2):
        pair = order[2 * g : 2 * g + 2]
        sources = [place.far(d) for d in pair]
        lanes = jnp.concatenate([lane_image(s, images_here, lat_rows) for s in sources], axis=1)
        allowed = image == lanes
        for h in range(heads):
            queries = jnp.concatenate([q_all[s, h] for s in sources], axis=1)
            scores = jnp.where(allowed, dot_nn(kh_ref[h], queries), NEG_FILL)
            top = jnp.max(scores, axis=0, keepdims=True)
            weights = jnp.exp(scores - top)
            total = jnp.sum(weights, axis=0, keepdims=True)
            acc = dot_nn(vt[h], weights.astype(BF)).astype(BF)
            for n, d in enumerate(pair):
                part = slice(n * lat_rows, (n + 1) * lat_rows)
                acc_out[d, h] = acc[:, part]
                stat_out[d, h : h + 1, :] = top[:, part]
                stat_out[d, heads + h : heads + h + 1, :] = total[:, part]
        for d in pair:
            if d:
                exchange.start(d)
                stats.start(d)

    row_image = lax.broadcasted_iota(jnp.int32, (lat_rows, lat_rows), 0) // LATENTS
    col_image = lax.broadcasted_iota(jnp.int32, (lat_rows, lat_rows), 1) // LATENTS
    same = row_image == col_image
    own = []
    for h in range(heads):
        scores = jnp.where(same, dot_nn(lkh_ref[h], q_all[place.me, h]), NEG_FILL)
        top = jnp.max(scores, axis=0, keepdims=True)
        weights = jnp.exp(scores - top)
        total = jnp.sum(weights, axis=0, keepdims=True)
        own.append((top, total, dot_nn(lvt[h], weights.astype(BF))))
    for d in range(1, nb):
        stats.wait_recv(d)
        exchange.wait_recv(d)
    lse_ref[...] = jnp.zeros_like(lse_ref)
    for h in range(heads):
        own_top, own_total, own_acc = own[h]
        tops = [
            (stat_out if d == 0 else stat_in)[d, h : h + 1, :] for d in range(nb)
        ]
        best = functools.reduce(jnp.maximum, tops, own_top)
        factor = jnp.exp(own_top - best)
        total = own_total * factor
        acc = own_acc * factor
        for d in range(nb):
            factor = jnp.exp(tops[d] - best)
            stat = stat_out if d == 0 else stat_in
            piece = acc_out if d == 0 else acc_in
            total = total + stat[d, heads + h : heads + h + 1, :] * factor
            acc = acc + piece[d, h].astype(F32) * factor
        att_ref[h] = acc / total
        lse_ref[h : h + 1, :] = best + jnp.log(total)
    exchange.finish_sends()
    stats.finish_sends()


class TensorSum:
    def __init__(self, bufs, sems, tile_of):
        self.bufs, self.sems, self.tile_of = bufs, sems, tile_of
        self.tiles, self.rows, self.tile = bufs.shape[1:]
        t = lax.axis_index("tp")
        self.core = t % 2
        self.chip = t // 2
        self.sibling = {"tp": 2 * self.chip + 1 - self.core}
        self.across = {"tp": 2 * (1 - self.chip) + self.core}

    @staticmethod
    def greeting():
        t = lax.axis_index("tp")
        core, chip = t % 2, t // 2
        return [{"tp": 2 * chip + 1 - core}, {"tp": 2 * (1 - chip) + core}]

    def column(self, half, j):
        return pl.multiple_of((half * self.tiles + j) * self.tile, 128)

    def copy(self, stage, j):
        return remote(
            self.bufs.at[2 * stage, j], self.bufs.at[2 * stage + 1, j],
            self.sems.at[stage, 0, j], self.sems.at[stage, 1, j],
            self.across if stage == 1 else self.sibling,
        )

    def give(self):
        for j in range(self.tiles):
            self.bufs[0, j] = self.tile_of(self.column(1 - self.core, j)).astype(BF)
            self.copy(0, j).start()

    def cross(self):
        for j in range(self.tiles):
            mine = self.tile_of(self.column(self.core, j))
            self.copy(0, j).wait_recv()
            self.bufs[2, j] = (mine + self.bufs[1, j].astype(F32)).astype(BF)
            self.copy(1, j).start()

    def back(self):
        for j in range(self.tiles):
            self.copy(1, j).wait_recv()
            self.bufs[4, j] = (self.bufs[2, j].astype(F32) + self.bufs[3, j].astype(F32)).astype(BF)
            self.copy(2, j).start()

    def finish(self, put):
        for j in range(self.tiles):
            put(self.column(self.core, j), self.bufs[4, j])
        for j in range(self.tiles):
            self.copy(2, j).wait_recv()
            put(self.column(1 - self.core, j), self.bufs[5, j])
        for stage in range(3):
            for j in range(self.tiles):
                self.copy(stage, j).wait_send()


def feed_kernel(
    att_ref, lse_ref, lat_ref, cot_ref, wo_ref, fg_ref, fs_ref, up_hbm, down_hbm,
    out_ref, mid_grad_ref, branch_ref, dot_ref, ld_ref, fn_ref, low_ref, gain_ref,
    up, down, hg, mid, hidden, pre_grad, low_t, sum_buf, bufs, sems, w_sems,
):
    loads = [
        pltpu.make_async_copy(up_hbm, up, w_sems.at[0]),
        pltpu.make_async_copy(down_hbm, down, w_sems.at[1]),
    ]
    for load in loads:
        load.start()
    heads = att_ref.shape[0]
    ff_here = up.shape[1]
    ff_tile = math.gcd(ff_here, 512)
    greet(TensorSum.greeting())
    for h in range(heads):
        low_t[h * HEAD_DIM : (h + 1) * HEAD_DIM, :] = att_ref[h]
    low_ref[...] = low_t[...].T.astype(BF)
    low = low_ref[...]

    def put(column, tile):
        sum_buf[:, pl.ds(column, tile.shape[1])] = tile.astype(F32)

    def tile_sum(n, tile_of):
        return TensorSum(bufs.at[n], sems.at[n], tile_of)

    width = bufs.shape[-1]
    branch = tile_sum(0, lambda c: dot_nn(low, wo_ref[:, pl.ds(c, width)]))
    branch.give()
    branch.cross()
    loads[1].wait()
    cot = cot_ref[...]

    def back_hidden(i, carry):
        cols = pl.ds(pl.multiple_of(i * ff_tile, ff_tile), ff_tile)
        hg[:, cols] = dot_nt(cot, down[cols, :])
        return carry

    lax.fori_loop(0, ff_here // ff_tile, back_hidden, 0)
    branch.back()
    branch.finish(put)
    mid[...] = lat_ref[...].astype(F32) + sum_buf[...]
    xhat, rstd = normalised(mid[...])
    fn_ref[...] = (xhat * fg_ref[...] + fs_ref[...]).astype(BF)
    fn = fn_ref[...]
    loads[0].wait()

    def inner(i, carry):
        cols = pl.ds(pl.multiple_of(i * ff_tile, ff_tile), ff_tile)
        pre = dot_nn(fn, up[:, cols])
        bell = 0.5 * (1.0 + lax.erf(pre * math.sqrt(0.5)))
        hidden[:, cols] = (pre * bell).astype(BF)
        slope = bell + pre * jnp.exp(-0.5 * pre * pre) * (1.0 / math.sqrt(2.0 * math.pi))
        pre_grad[:, cols] = (hg[:, cols] * slope).astype(BF)
        return carry

    lax.fori_loop(0, ff_here // ff_tile, inner, 0)
    grads = tile_sum(1, lambda c: dot_nt(pre_grad[...], up[pl.ds(c, width), :]))
    feed = tile_sum(2, lambda c: dot_nn(hidden[...], down[:, pl.ds(c, width)]))
    grads.give()
    grads.cross()
    feed.give()
    feed.cross()
    grads.back()
    feed.back()
    grads.finish(put)
    fng = sum_buf[...]
    xhat, rstd = normalised(mid[...])
    mid_grad = cot_ref[...].astype(F32) + norm_back(fng, fg_ref[...], xhat, rstd)
    mid_grad_ref[...] = mid_grad
    branch_ref[...] = mid_grad.astype(BF)
    gain_ref[...] = jnp.zeros_like(gain_ref)
    gain_ref[0:1, :] = jnp.sum(fng * xhat, axis=0, keepdims=True)
    gain_ref[1:2, :] = jnp.sum(fng, axis=0, keepdims=True)
    back = dot_nt(wo_ref[...], branch_ref[...])
    ld_ref[...] = lse_ref[...]
    for h in range(heads):
        piece = back[h * HEAD_DIM : (h + 1) * HEAD_DIM, :].astype(BF)
        dot_ref[h] = piece
        ld_ref[heads + h : heads + h + 1, :] = jnp.sum(
            piece.astype(F32) * att_ref[h], axis=0, keepdims=True
        )
    feed.finish(put)
    out_ref[...] = (mid[...] + sum_buf[...]).astype(BF)


def back_kernel(
    nb,
    q_all, dot_in, ld_in, kh_ref, kt_ref, vh_ref, lkh_ref, lkt_ref, lvh_ref, ln_ref, mn_ref,
    wq_ref, wk_ref, wv_ref, mid_grad_ref, lat_ref, med_ref, lg_ref, mg_ref, fgain_ref, image_ref,
    mgrad_ref, lgrad_ref, qg_ref, kg_ref, vg_ref, gains_ref,
    dot_all, ld_all, dk, dv, dq_own, dq_in, turn, xall, yall, dq_low, part, pair_in, far_in,
    gain_out, gain_in, med_bufs, lat_bufs,
    g_sems, l_sems, x_sems, y_sems, z_sems, n_sems, t_sems,
):
    place = Place(nb)
    lat_rows = lat_ref.shape[0]
    med_rows, model = med_ref.shape
    heads = kh_ref.shape[0]
    inner = heads * HEAD_DIM
    images_here = lat_rows // LATENTS
    dot_all[place.me] = dot_in[...]
    ld_all[place.me] = ld_in[...]
    greet(place.greeting() + TensorSum.greeting())
    gather = Gather(place, dot_all, g_sems)
    gather_ld = Gather(place, ld_all, l_sems)
    gather_ld.start()
    gather.start()

    row_image = lax.broadcasted_iota(jnp.int32, (lat_rows, lat_rows), 0) // LATENTS
    col_image = lax.broadcasted_iota(jnp.int32, (lat_rows, lat_rows), 1) // LATENTS
    same = row_image == col_image

    def turned(h, value, rows):
        turn[h * HEAD_DIM : (h + 1) * HEAD_DIM, 0:rows] = value

    def grads_of(h, keys, values, queries, grads, lse, delta, allowed):
        scores = jnp.where(allowed, dot_nn(keys, queries), NEG_FILL)
        probs = jnp.exp(scores - lse)
        score_grad = (probs * (dot_nn(values, grads) - delta)).astype(BF)
        return probs.astype(BF), score_grad

    for h in range(heads):
        queries, grads = q_all[place.me, h], dot_in[h]
        probs, score_grad = grads_of(
            h, lkh_ref[h], lvh_ref[h], queries, grads,
            ld_in[h : h + 1, :], ld_in[heads + h : heads + h + 1, :], same,
        )
        dk[h, :, 0:lat_rows] = dot_nt(queries, score_grad)
        dv[h, :, 0:lat_rows] = dot_nt(grads, probs)
        dq_own[h] = dot_nn(lkt_ref[h], score_grad)

    def put_rows(first, rows):
        for acc, column in ((dk, 0), (dv, inner)):
            for h in range(heads):
                turned(h, acc[h, :, 0:rows], rows)
            yall[first : first + rows, column : column + inner] = turn[:, 0:rows].T.astype(BF)

    put_rows(med_rows, lat_rows)
    xall[0:med_rows, :] = mn_ref[...]
    xall[med_rows:, :] = ln_ref[...]
    gather_ld.relay()
    gather.relay()
    gather_ld.finish()
    gather.finish()

    exchange = Exchange(place, dot_all, dq_in, x_sems, place.far)
    image = image_ref[...]
    order = list(range(1, nb)) + [0]
    for g in range(nb // 2):
        pair = order[2 * g : 2 * g + 2]
        sources = [place.far(d) for d in pair]
        lanes = jnp.concatenate([lane_image(s, images_here, lat_rows) for s in sources], axis=1)
        allowed = image == lanes
        for h in range(heads):
            queries = jnp.concatenate([q_all[s, h] for s in sources], axis=1)
            grads = jnp.concatenate([dot_all[s, h] for s in sources], axis=1)
            lse = jnp.concatenate([ld_all[s, h : h + 1, :] for s in sources], axis=1)
            delta = jnp.concatenate(
                [ld_all[s, heads + h : heads + h + 1, :] for s in sources], axis=1
            )
            probs, score_grad = grads_of(
                h, kh_ref[h], vh_ref[h], queries, grads, lse, delta, allowed
            )
            key_part = dot_nt(queries, score_grad)
            value_part = dot_nt(grads, probs)
            dk[h] = key_part if g == 0 else dk[h] + key_part
            dv[h] = value_part if g == 0 else dv[h] + value_part
            dq = dot_nn(kt_ref[h], score_grad)
            for n, d in enumerate(pair):
                piece = dq[:, n * lat_rows : (n + 1) * lat_rows]
                if d:
                    dot_all[place.far(d), h] = piece.astype(BF)
                else:
                    dq_own[h] = dq_own[h] + piece
        for d in pair:
            if d:
                exchange.start(d)
    put_rows(0, med_rows)

    med_tile, lat_tile = med_bufs.shape[-1], lat_bufs.shape[-1]

    def back_rows(first, rows, tile):
        def tile_of(column):
            cols = pl.ds(column, tile)
            values = yall[first : first + rows, :]
            return dot_nt(values[:, 0:inner], wk_ref[cols, :]) + dot_nt(
                values[:, inner:], wv_ref[cols, :]
            )

        return tile_of

    med_sum = TensorSum(med_bufs, t_sems.at[0], back_rows(0, med_rows, med_tile))
    med_sum.give()
    med_sum.cross()

    for d in range(1, nb):
        exchange.wait_recv(d)
    for h in range(heads):
        value = dq_own[h]
        for d in range(1, nb):
            value = value + dq_in[d, h].astype(F32)
        turned(h, value, lat_rows)
    dq_low[...] = turn[:, 0:lat_rows].T.astype(BF)

    own_rows = model // nb
    chunk = 2 * own_rows * max(1, 128 // math.gcd(128, 2 * own_rows))
    per_chunk = chunk // own_rows

    def pair_copy(o):
        return remote(
            part.at[2 * o + 1 - place.inner], pair_in.at[o], y_sems.at[0, o], y_sems.at[1, o],
            {"blk": place.partner},
        )

    def far_copy(o, d):
        return remote(
            part.at[2 * o + place.inner], far_in.at[d], z_sems.at[0, d], z_sems.at[1, d],
            {"blk": 2 * o + place.inner},
        )

    for c in range(model // chunk):
        cols = slice(c * chunk, (c + 1) * chunk)
        lnx = xall[med_rows:, cols]
        query_part = dot_tn(lnx, dq_low[...]) * SCALE
        other_part = dot_tn(xall[:, cols], yall[...])
        for n in range(per_chunk):
            owner = c * per_chunk + n
            rows = slice(n * own_rows, (n + 1) * own_rows)
            part[owner, 0:own_rows, 0:inner] = query_part[rows].astype(BF)
            part[owner, 0:own_rows, inner:] = other_part[rows].astype(BF)
        for o in range(c * per_chunk // 2, (c + 1) * per_chunk // 2):
            pair_copy(o).start()

    def lat_tile_of(column):
        cols = pl.ds(column, lat_tile)
        return (
            back_rows(med_rows, lat_rows, lat_tile)(column)
            + dot_nt(dq_low[...], wq_ref[cols, :]) * SCALE
        )

    lat_sum = TensorSum(lat_bufs, t_sems.at[1], lat_tile_of)
    lat_sum.give()
    lat_sum.cross()

    def own_part(o):
        return part[2 * o + place.inner].astype(F32) + pair_in[o].astype(F32)

    for d in range(1, place.no):
        o = place.outer_to(d)
        pair_copy(o).wait_recv()
        part[2 * o + place.inner] = own_part(o).astype(BF)
        far_copy(o, d).start()
    med_sum.back()

    def put(column, tile):
        xall[0 : tile.shape[0], pl.ds(column, tile.shape[1])] = tile

    med_sum.finish(put)
    gain_rows = [fgain_ref[0:1, :], fgain_ref[1:2, :]]

    def norm_rows(i, carry):
        rows = pl.ds(pl.multiple_of(i * 128, 128), 128)
        xhat, rstd = normalised(med_ref[rows, :].astype(F32))
        q = xall[rows, :].astype(F32)
        mgrad_ref[rows, :] = norm_back(q, mg_ref[...], xhat, rstd)
        return (
            carry[0] + jnp.sum(q * xhat, axis=0, keepdims=True),
            carry[1] + jnp.sum(q, axis=0, keepdims=True),
        )

    zero = jnp.zeros((1, model), F32)
    med_gain = lax.fori_loop(0, med_rows // 128, norm_rows, (zero, zero))
    lat_sum.back()
    lat_sum.finish(put)
    xhat, rstd = normalised(lat_ref[...].astype(F32))
    q = xall[0:lat_rows, :].astype(F32)
    lgrad_ref[...] = mid_grad_ref[...] + norm_back(q, lg_ref[...], xhat, rstd)
    all_rows = [
        *med_gain,
        jnp.sum(q * xhat, axis=0, keepdims=True),
        jnp.sum(q, axis=0, keepdims=True),
        *gain_rows,
    ]
    for o in range(nb):
        for n, row in enumerate(all_rows):
            gain_out[o, n : n + 1, :] = row[:, o * own_rows : (o + 1) * own_rows]

    def gain_copy(d):
        return remote(
            gain_out.at[place.far(d)], gain_in.at[d], n_sems.at[0, d], n_sems.at[1, d],
            {"blk": place.far(d)},
        )

    for d in range(1, nb):
        gain_copy(d).start()
    pair_copy(place.outer).wait_recv()
    total = own_part(place.outer)
    for d in range(1, place.no):
        far_copy(place.outer_to(d), d).wait_recv()
        total = total + far_in[d].astype(F32)
    qg_ref[...] = total[0:own_rows, 0:inner]
    kg_ref[...] = total[0:own_rows, inner : 2 * inner]
    vg_ref[...] = total[0:own_rows, 2 * inner :]
    gains = gain_out[place.me]
    for d in range(1, nb):
        gain_copy(d).wait_recv()
        gains = gains + gain_in[d]
    gains_ref[...] = gains
    exchange.finish_sends()
    for d in range(1, nb):
        gain_copy(d).wait_send()
    for o in range(place.no):
        pair_copy(o).wait_send()
    for d in range(1, place.no):
        far_copy(place.outer_to(d), d).wait_send()


def call(kernel, out_shapes, scratch, collective_id, any_args=(), args=()):
    vmem = pl.BlockSpec(memory_space=pltpu.VMEM)
    return pl.pallas_call(
        kernel,
        out_shape=[jax.ShapeDtypeStruct(s, d) for s, d in out_shapes],
        in_specs=[vmem] * len(args) + [pl.BlockSpec(memory_space=pl.ANY)] * len(any_args),
        out_specs=[vmem] * len(out_shapes),
        scratch_shapes=scratch,
        compiler_params=pltpu.CompilerParams(
            collective_id=collective_id, has_side_effects=True, vmem_limit_bytes=VMEM_LIMIT
        ),
    )(*args, *any_args)


def gelu_pair(pre):
    bell = 0.5 * (1.0 + lax.erf(pre * math.sqrt(0.5)))
    slope = bell + pre * jnp.exp(-0.5 * pre * pre) * (1.0 / math.sqrt(2.0 * math.pi))
    return pre * bell, slope


def per_device_many(
    latents, media, query_weight, key_weight, value_weight, out_weight, up_weight, down_weight,
    media_gain, media_shift, latent_gain, latent_shift, feed_gain, feed_shift, cotangent, media_image,
):
    nb = lax.axis_size("blk")
    me = lax.axis_index("blk")
    lat_rows, model = latents.shape
    med_rows = media.shape[0]
    inner = query_weight.shape[1]
    heads = inner // HEAD_DIM
    ff_here = up_weight.shape[1]
    no = nb // 2
    own_rows = model // nb
    own_pad = -(-own_rows // 16) * 16
    dma = pltpu.SemaphoreType.DMA
    vm = pltpu.VMEM
    row = lambda v: v.reshape(1, -1)
    image = media_image.reshape(-1, 1)
    hd = HEAD_DIM
    cot_all = lax.all_gather(cotangent, "blk", axis=0, tiled=True)

    (ln, mn, q_all, kh, kt, vh, lkh, lkt, lvh, att, lse) = call(
        functools.partial(attend_kernel, nb),
        [
            ((lat_rows, model), BF), ((med_rows, model), BF), ((nb, heads, hd, lat_rows), BF),
            ((heads, med_rows, hd), BF), ((heads, hd, med_rows), BF), ((heads, med_rows, hd), BF),
            ((heads, lat_rows, hd), BF), ((heads, hd, lat_rows), BF), ((heads, lat_rows, hd), BF),
            ((heads, hd, lat_rows), F32), ((2 * heads, lat_rows), F32),
        ],
        [
            vm((heads, hd, med_rows), BF), vm((heads, hd, lat_rows), BF),
            vm((nb, heads, hd, lat_rows), BF), vm((nb, heads, hd, lat_rows), BF),
            vm((nb, 2 * heads, lat_rows), F32), vm((nb, 2 * heads, lat_rows), F32),
            dma((2, 2, no)), dma((2, nb)), dma((2, nb)),
        ],
        0,
        args=(
            latents, media, query_weight, key_weight, value_weight, row(latent_gain),
            row(latent_shift), row(media_gain), row(media_shift), image,
        ),
    )

    tile = 256
    tiles = model // 2 // tile
    (resampled, mid_grad, branch, dot, ld, fn, low, feed_gains) = call(
        feed_kernel,
        [
            ((lat_rows, model), BF), ((lat_rows, model), F32), ((lat_rows, model), BF),
            ((heads, hd, lat_rows), BF), ((2 * heads, lat_rows), F32), ((lat_rows, model), BF),
            ((lat_rows, inner), BF), ((8, model), F32),
        ],
        [
            vm((model, ff_here), BF), vm((ff_here, model), BF), vm((lat_rows, ff_here), F32),
            vm((lat_rows, model), F32), vm((lat_rows, ff_here), BF), vm((lat_rows, ff_here), BF),
            vm((inner, lat_rows), F32), vm((lat_rows, model), F32),
            vm((3, 6, tiles, lat_rows, tile), BF), dma((3, 3, 2, tiles)), dma((2,)),
        ],
        1,
        any_args=(up_weight, down_weight),
        args=(att, lse, latents, cotangent, out_weight, row(feed_gain), row(feed_shift)),
    )
    fn_all = lax.all_gather(fn, "blk", axis=0, tiled=True)
    low_all = lax.all_gather(low, "blk", axis=0, tiled=True)
    branch_all = lax.all_gather(branch, "blk", axis=0, tiled=True)

    (media_grad, latent_grad, query_grad, key_grad, value_grad, gains) = call(
        functools.partial(back_kernel, nb),
        [
            ((med_rows, model), F32), ((lat_rows, model), F32), ((own_rows, inner), F32),
            ((own_rows, inner), F32), ((own_rows, inner), F32), ((8, own_rows), F32),
        ],
        [
            vm((nb, heads, hd, lat_rows), BF), vm((nb, 2 * heads, lat_rows), F32),
            vm((heads, hd, med_rows), F32), vm((heads, hd, med_rows), F32),
            vm((heads, hd, lat_rows), F32),
            vm((nb, heads, hd, lat_rows), BF),
            vm((inner, med_rows), F32), vm((med_rows + lat_rows, model), BF),
            vm((med_rows + lat_rows, 2 * inner), BF), vm((lat_rows, inner), BF),
            vm((nb, own_pad, 3 * inner), BF), vm((no, own_pad, 3 * inner), BF),
            vm((no, own_pad, 3 * inner), BF),
            vm((nb, 8, own_rows), F32), vm((nb, 8, own_rows), F32),
            vm((6, tiles, med_rows, tile), BF), vm((6, tiles, lat_rows, tile), BF),
            dma((2, 2, no)), dma((2, 2, no)), dma((2, nb)), dma((2, no)), dma((2, no)),
            dma((2, nb)), dma((2, 3, 2, tiles)),
        ],
        2,
        args=(
            q_all, dot, ld, kh, kt, vh, lkh, lkt, lvh, ln, mn, query_weight, key_weight,
            value_weight, mid_grad, latents, media, row(latent_gain), row(media_gain), feed_gains,
            image,
        ),
    )

    def own_columns(rows):
        return lax.dynamic_slice_in_dim(rows, me * own_rows, own_rows, axis=1)

    group = math.gcd(nb, 8)
    group_rows = group * lat_rows

    def feed_step(carry, rows):
        up_acc, down_acc, out_acc = carry
        fn_rows, cot_rows, low_rows, branch_rows = rows
        hidden, slope = gelu_pair(dot_nn(fn_rows, up_weight))
        grad = (dot_nt(cot_rows, down_weight) * slope).astype(BF)
        return (
            up_acc + dot_tn(own_columns(fn_rows), grad),
            down_acc + dot_tn(hidden.astype(BF), own_columns(cot_rows)),
            out_acc + dot_tn(low_rows, own_columns(branch_rows)),
        ), None

    whole = (fn_all, cot_all, low_all, branch_all)
    start = (
        jnp.zeros((own_rows, ff_here), F32),
        jnp.zeros((ff_here, own_rows), F32),
        jnp.zeros((inner, own_rows), F32),
    )
    if group == nb:
        (up_grad, down_grad, out_grad), _ = feed_step(start, whole)
    else:
        (up_grad, down_grad, out_grad), _ = lax.scan(
            feed_step, start, tuple(v.reshape(nb // group, group_rows, -1) for v in whole)
        )
    return (
        resampled, media_grad, latent_grad, query_grad, key_grad, value_grad, out_grad, up_grad,
        down_grad, gains[0], gains[1], gains[2], gains[3], gains[4], gains[5],
    )


class Spread:
    def __init__(self, place, slots, sems):
        self.place, self.slots, self.sems = place, slots, sems
        self.t = lax.axis_index("tp")

    def source(self, kind, d):
        pc = self.place
        return 2 * pc.outer_from(d) + (1 - pc.inner if kind else pc.inner)

    def copy_z(self, d):
        pc = self.place
        slot = self.slots.at[pc.me, self.t]
        return remote(
            slot, slot, self.sems.at[0, 0, d], self.sems.at[0, 1, d],
            {"blk": 2 * pc.outer_to(d) + pc.inner},
        )

    def copy_y(self, d):
        slot = self.slots.at[self.source(0, d), self.t]
        return remote(
            slot, slot, self.sems.at[1, 0, d], self.sems.at[1, 1, d], {"blk": self.place.partner}
        )

    def arrived(self, kind, d):
        slot = self.slots.at[self.source(kind, d), self.t]
        remote(
            slot, slot, self.sems.at[kind, 0, d], self.sems.at[kind, 1, d], {"blk": self.place.partner}
        ).wait_recv()

    def start(self):
        for d in range(1, self.place.no):
            self.copy_z(d).start()
        self.copy_y(0).start()

    def relay(self):
        for d in range(1, self.place.no):
            self.arrived(0, d)
            self.copy_y(d).start()

    def finish(self):
        for d in range(self.place.no):
            self.arrived(1, d)
        for d in range(1, self.place.no):
            self.copy_z(d).wait_send()
        for d in range(self.place.no):
            self.copy_y(d).wait_send()


class Share:
    def __init__(self, place, slots, sems):
        self.place, self.slots, self.sems = place, slots, sems
        t = lax.axis_index("tp")
        self.t = t
        core, chip = t % 2, t // 2
        self.sibling_t = 2 * chip + 1 - core
        self.across_t = 2 * (1 - chip) + core
        self.diagonal_t = 2 * (1 - chip) + 1 - core

    def blocks(self, step):
        pc = self.place
        base = 2 * pc.outer_from(step)
        partner = (pc.no + step, base + 1 - pc.inner)
        return [partner] if step == 0 else [(step, base + pc.inner), partner]

    def copy(self, stage, n, s):
        slot = self.slots.at[s, self.across_t if stage == 2 else self.t]
        return remote(
            slot, slot, self.sems.at[stage, 0, n], self.sems.at[stage, 1, n],
            {"tp": self.sibling_t if stage else self.across_t},
        )

    def arrived(self, stage, n, s, t):
        slot = self.slots.at[s, t]
        remote(
            slot, slot, self.sems.at[stage, 0, n], self.sems.at[stage, 1, n], {"tp": self.sibling_t}
        ).wait_recv()

    def start(self, step):
        for n, s in self.blocks(step):
            self.copy(0, n, s).start()
            self.copy(1, n, s).start()

    def forward(self, step):
        for n, s in self.blocks(step):
            self.arrived(0, n, s, self.across_t)
            self.copy(2, n, s).start()

    def ready(self, step):
        for n, s in self.blocks(step):
            self.arrived(1, n, s, self.sibling_t)
            self.arrived(2, n, s, self.diagonal_t)

    def finish(self):
        for step in range(self.place.no):
            for n, s in self.blocks(step):
                for stage in range(3):
                    self.copy(stage, n, s).wait_send()


class Slices:
    def __init__(self, place, out, into, sems):
        self.place, self.out, self.into, self.sems = place, out, into, sems
        t = lax.axis_index("tp")
        self.core = t % 2
        self.sibling = {"tp": 2 * (t // 2) + 1 - self.core}

    def copy(self, d):
        pc = self.place
        return remote(
            self.out.at[pc.far(d), self.core], self.into.at[pc.me, self.core],
            self.sems.at[0, 0, d], self.sems.at[0, 1, d], {"blk": pc.far(d)},
        )

    def share(self, d):
        slot = self.into.at[self.place.near(d), self.core]
        return remote(slot, slot, self.sems.at[1, 0, d], self.sems.at[1, 1, d], self.sibling)

    def arrived(self, stage, d, core):
        slot = self.into.at[self.place.near(d), core]
        remote(
            slot, slot, self.sems.at[stage, 0, d], self.sems.at[stage, 1, d], self.sibling
        ).wait_recv()

    def start(self):
        for d in range(1, self.place.nb):
            self.copy(d).start()

    def relay(self):
        for d in range(1, self.place.nb):
            self.arrived(0, d, self.core)
            self.share(d).start()

    def finish(self):
        for d in range(1, self.place.nb):
            self.arrived(1, d, 1 - self.core)
        for d in range(1, self.place.nb):
            self.copy(d).wait_send()
            self.share(d).wait_send()

    def cut(self, rows):
        nb, _, half, width = self.out.shape
        for o in range(nb):
            piece = rows[:, o * width : (o + 1) * width]
            self.out[o, 0] = piece[0:half]
            self.out[o, 1] = piece[half:]
        for c in range(2):
            self.into[self.place.me, c] = self.out[self.place.me, c]


class Fold:
    def __init__(self, place, give, got, send, into, sems):
        self.place, self.give, self.got, self.send, self.into = place, give, got, send, into
        self.sems = sems

    def pair(self, o):
        return remote(
            self.give(o), self.got.at[o], self.sems.at[0, 0, o], self.sems.at[0, 1, o],
            {"blk": self.place.partner},
        )

    def far(self, d):
        o = self.place.outer_to(d)
        return remote(
            self.send(o), self.into.at[d], self.sems.at[1, 0, d], self.sems.at[1, 1, d],
            {"blk": 2 * o + self.place.inner},
        )

    def finish(self):
        for o in range(self.place.no):
            self.pair(o).wait_send()
        for d in range(1, self.place.no):
            self.far(d).wait_send()


def image_columns(image_ref, rows, lanes):
    line = image_ref[...].astype(F32).reshape(1, rows)
    return jnp.broadcast_to(line, (lanes, rows)).T


def pair_lanes(place, sources, images_here, lat_rows):
    return jnp.concatenate(
        [lane_image(s, images_here, lat_rows).astype(F32) for s in sources], axis=1
    )


def line_of(ref):
    return ref[...].reshape(1, -1)


def whole_greeting(place):
    return place.greeting() + TensorSum.greeting()


def near_layer(
    nb,
    lat_ref, cot_ref, image_ref, lg_ref, ls_ref, mg_ref, ms_ref, fg_ref, fs_ref,
    med_hbm, wq_hbm, wk_hbm, wv_hbm, wo_hbm, up_hbm, down_hbm,
    x_ref, out_ref, lgrad_ref, qg_ref, kg_ref, vg_ref, og_ref, ug_ref, down_t, gains_ref,
    med_ref, wq, wk, wv, wo, up, down, q_all, dot_all, ld_all, low_all, dq_all, fn_all, cot_all,
    kh_ref, kt_ref, vh_ref, vt, lkh_ref, lkt_ref, lvh_ref, lvt, att_ref, lse_ref,
    mine, give, got, send, into, mstat, gstat, rstat, sstat, istat,
    hg, mid, hidden, pre_grad, low_t, sum_buf, branch_ref, ln_out, lns_ref, br_out, br_in,
    dk, dv, dq_own, turn, yall, own_cols, part, pair_in, far_in, gain_out, gain_in, bufs, med_bufs,
    g_sems, a_sems, s_sems, f_sems, h_sems, n_sems, p_sems, t_sems, e_sems, w_sems,
):
    place = Place(nb)
    lat_rows = lat_ref.shape[0]
    med_rows, model = med_ref.shape
    heads = kh_ref.shape[0]
    inner = heads * HEAD_DIM
    images_here = lat_rows // LATENTS
    own_rows = model // nb
    quarter = lat_rows // 4
    ff_here = up.shape[1]
    ff_tile = math.gcd(ff_here, 512)
    sources = {
        "q": (wq_hbm, wq), "k": (wk_hbm, wk), "m": (med_hbm, med_ref), "v": (wv_hbm, wv),
        "down": (down_hbm, down), "wo": (wo_hbm, wo), "up": (up_hbm, up),
    }
    loads = {
        name: pltpu.make_async_copy(*ends, w_sems.at[n]) for n, (name, ends) in enumerate(sources.items())
    }
    for load in loads.values():
        load.start()
    greet(whole_greeting(place))
    for q in range(4):
        cot_all[place.me, q] = cot_ref[q * quarter : (q + 1) * quarter]
    spread_cot = Spread(place, cot_all, f_sems.at[0])
    spread_cot.start()
    row_image = lax.broadcasted_iota(jnp.int32, (lat_rows, lat_rows), 0) // LATENTS
    col_image = lax.broadcasted_iota(jnp.int32, (lat_rows, lat_rows), 1) // LATENTS
    same = row_image == col_image
    image = image_columns(image_ref, med_rows, lat_rows)
    image = jnp.concatenate([image, image], axis=1)
    order = [*range(1, place.no), 0]

    xhat, _ = normalised(lat_ref[...].astype(F32))
    ln = (xhat * line_of(lg_ref) + line_of(ls_ref)).astype(BF)
    x_ref[med_rows:, :] = ln

    def heads_t(rows, ref):
        turned = rows.T
        for h in range(heads):
            ref[h] = turned[h * HEAD_DIM : (h + 1) * HEAD_DIM].astype(BF)

    def heads_n(rows, ref):
        for h in range(heads):
            ref[h] = rows[:, h * HEAD_DIM : (h + 1) * HEAD_DIM].astype(BF)

    loads["q"].wait()
    heads_t(dot_nn(ln, wq[...]) * SCALE, q_all.at[place.me])
    gather = Gather(place, q_all, g_sems.at[0])
    gather.start()
    loads["k"].wait()
    lk = dot_nn(ln, wk[...])
    heads_n(lk, lkh_ref)
    heads_t(lk, lkt_ref)
    loads["m"].wait()

    med_gain, med_shift = line_of(mg_ref), line_of(ms_ref)

    def norm_rows(i, carry):
        rows = pl.ds(pl.multiple_of(i * 128, 128), 128)
        hat, _ = normalised(med_ref[rows, :].astype(F32))
        x_ref[rows, :] = (hat * med_gain + med_shift).astype(BF)
        return carry

    lax.fori_loop(0, med_rows // 128, norm_rows, 0)
    mk = dot_nn(x_ref[0:med_rows, :], wk[...])
    heads_n(mk, kh_ref)
    heads_t(mk, kt_ref)
    spread_cot.relay()
    loads["v"].wait()
    mv = dot_nn(x_ref[0:med_rows, :], wv[...])
    heads_n(mv, vh_ref)
    heads_t(mv, vt)
    gather.relay()
    lv = dot_nn(ln, wv[...])
    heads_n(lv, lvh_ref)
    heads_t(lv, lvt)
    own = []
    for h in range(heads):
        scores = jnp.where(same, dot_nn(lkh_ref[h], q_all[place.me, h]), NEG_FILL)
        top = jnp.max(scores, axis=0, keepdims=True)
        weights = jnp.exp(scores - top)
        total = jnp.sum(weights, axis=0, keepdims=True)
        own.append((top, total, dot_nn(lvt[h], weights.astype(BF))))
    loads["down"].wait()

    def back_hidden(i, carry):
        cols = pl.ds(pl.multiple_of(i * ff_tile, ff_tile), ff_tile)
        hg[:, cols] = dot_nt(cot_ref[...], down[cols, :])
        return carry

    lax.fori_loop(0, ff_here // ff_tile, back_hidden, 0)
    ln_slices = Slices(place, ln_out, lns_ref, n_sems.at[0])
    ln_slices.cut(ln)
    gather.finish()
    spread_cot.finish()
    share_cot = Share(place, cot_all, h_sems.at[0])
    for step in range(place.no):
        share_cot.start(step)

    fold = Fold(place, lambda o: give.at[o], got, lambda o: send.at[o], into, a_sems.at[0])
    stats = Fold(place, lambda o: gstat.at[o], rstat, lambda o: sstat.at[o], istat, s_sems)

    def piece(acc_ref, stat_ref, at):
        return [
            (
                stat_ref[at, h : h + 1, :],
                stat_ref[at, heads + h : heads + h + 1, :],
                acc_ref[at, h].astype(F32),
            )
            for h in range(heads)
        ]

    def merged(left, right):
        both = []
        for (lt, ll, la), (rt, rl, ra) in zip(left, right):
            top = jnp.maximum(lt, rt)
            lf, rf = jnp.exp(lt - top), jnp.exp(rt - top)
            both.append((top, ll * lf + rl * rf, la * lf + ra * rf))
        return both

    def pass_attention(d):
        o = place.outer_to(d)
        stats.pair(o).wait_recv()
        fold.pair(o).wait_recv()
        both = merged(piece(mine, mstat, o), piece(got, rstat, o))
        if d == 0:
            return both
        for h, (top, total, acc) in enumerate(both):
            sstat[o, h : h + 1, :] = top
            sstat[o, heads + h : heads + h + 1, :] = total
            send[o, h] = acc.astype(BF)
        stats.far(d).start()
        fold.far(d).start()
        return None

    for step, d in enumerate(order):
        o = place.outer_to(d)
        sources = [2 * o + place.inner, 2 * o + 1 - place.inner]
        allowed = image == pair_lanes(place, sources, images_here, lat_rows)
        for h in range(heads):
            queries = jnp.concatenate([q_all[s, h] for s in sources], axis=1)
            scores = jnp.where(allowed, dot_nn(kh_ref[h], queries), NEG_FILL)
            top = jnp.max(scores, axis=0, keepdims=True)
            weights = jnp.exp(scores - top)
            total = jnp.sum(weights, axis=0, keepdims=True)
            acc = dot_nn(vt[h], weights.astype(BF))
            mine[o, h] = acc[:, 0:lat_rows]
            give[o, h] = acc[:, lat_rows:].astype(BF)
            for ref, lanes in ((mstat, slice(0, lat_rows)), (gstat, slice(lat_rows, 2 * lat_rows))):
                ref[o, h : h + 1, :] = top[:, lanes]
                ref[o, heads + h : heads + h + 1, :] = total[:, lanes]
        stats.pair(o).start()
        fold.pair(o).start()
        if step:
            pass_attention(order[step - 1])
    result = merged(own, pass_attention(0))
    for d in range(1, place.no):
        stats.far(d).wait_recv()
        fold.far(d).wait_recv()
        result = merged(result, piece(into, istat, d))
    lse_ref[...] = jnp.zeros_like(lse_ref)
    for h, (top, total, acc) in enumerate(result):
        att_ref[h] = acc / total
        lse_ref[h : h + 1, :] = top + jnp.log(total)

    for h in range(heads):
        low_t[h * HEAD_DIM : (h + 1) * HEAD_DIM, :] = att_ref[h]
    low_all[place.me] = low_t[...].T.astype(BF)
    low_gather = Gather(place, low_all, g_sems.at[1])
    low_gather.start()
    ln_slices.start()
    low = low_all[place.me]

    def put_sum(column, tile):
        sum_buf[:, pl.ds(column, tile.shape[1])] = tile

    def tile_sum(n, tile_of):
        return TensorSum(bufs.at[n], t_sems.at[n], tile_of)

    width = bufs.shape[-1]
    branch = tile_sum(0, lambda c: dot_nn(low, wo[:, pl.ds(c, width)]))
    loads["wo"].wait()
    branch.give()
    branch.cross()
    for step in range(place.no // 2):
        share_cot.forward(step)
    branch.back()
    branch.finish(put_sum)
    mid[...] = lat_ref[...].astype(F32) + sum_buf[...].astype(F32)
    xhat, rstd = normalised(mid[...])
    normed = (xhat * line_of(fg_ref) + line_of(fs_ref)).astype(BF)
    for q in range(4):
        fn_all[place.me, q] = normed[q * quarter : (q + 1) * quarter]
    spread_fn = Spread(place, fn_all, f_sems.at[1])
    spread_fn.start()
    for step in range(place.no // 2, place.no):
        share_cot.forward(step)
    loads["up"].wait()

    def feed_forward(i, carry):
        cols = pl.ds(pl.multiple_of(i * ff_tile, ff_tile), ff_tile)
        pre = dot_nn(normed, up[:, cols])
        value, slope = gelu_pair(pre)
        hidden[:, cols] = value.astype(BF)
        pre_grad[:, cols] = (hg[:, cols] * slope).astype(BF)
        return carry

    lax.fori_loop(0, ff_here // ff_tile, feed_forward, 0)
    grads = tile_sum(1, lambda c: dot_nt(pre_grad[...], up[pl.ds(c, width), :]))
    feed = tile_sum(2, lambda c: dot_nn(hidden[...], down[:, pl.ds(c, width)]))
    grads.give()
    grads.cross()
    feed.give()
    low_gather.relay()
    grads.back()
    spread_fn.relay()
    grads.finish(put_sum)
    fng = sum_buf[...].astype(F32)
    xhat, rstd = normalised(mid[...])
    mid_grad = cot_ref[...].astype(F32) + norm_back(fng, line_of(fg_ref), xhat, rstd)
    lgrad_ref[...] = mid_grad
    branch_ref[...] = mid_grad.astype(BF)
    feed_gains = [
        jnp.sum(fng * xhat, axis=0, keepdims=True), jnp.sum(fng, axis=0, keepdims=True)
    ]
    back = dot_nt(wo[...], branch_ref[...])
    ld_all[place.me] = lse_ref[...]
    for h in range(heads):
        piece_grad = back[h * HEAD_DIM : (h + 1) * HEAD_DIM, :].astype(BF)
        dot_all[place.me, h] = piece_grad
        ld_all[place.me, heads + h : heads + h + 1, :] = jnp.sum(
            piece_grad.astype(F32) * att_ref[h], axis=0, keepdims=True
        )

    gather = Gather(place, dot_all, g_sems.at[2])
    gather_ld = Gather(place, ld_all, g_sems.at[3])
    gather_ld.start()
    gather.start()
    feed.cross()
    spread_fn.finish()
    share_fn = Share(place, fn_all, h_sems.at[1])
    for step in range(place.no):
        share_fn.start(step)

    shares = [share_cot, share_fn]

    def grads_of(keys, values, queries, grads, lse, delta, allowed):
        scores = jnp.where(allowed, dot_nn(keys, queries), NEG_FILL)
        probs = jnp.exp(scores - lse)
        score_grad = (probs * (dot_nn(values, grads) - delta)).astype(BF)
        return probs.astype(BF), score_grad

    for h in range(heads):
        queries, grads = q_all[place.me, h], dot_all[place.me, h]
        probs, score_grad = grads_of(
            lkh_ref[h], lvh_ref[h], queries, grads,
            ld_all[place.me, h : h + 1, :], ld_all[place.me, heads + h : heads + h + 1, :], same,
        )
        dk[h, :, 0:lat_rows] = dot_nt(queries, score_grad)
        dv[h, :, 0:lat_rows] = dot_nt(grads, probs)
        dq_own[h] = dot_nn(lkt_ref[h], score_grad)

    def put_rows(first, rows):
        for k, acc in enumerate((dk, dv)):
            for h in range(heads):
                turn[h * HEAD_DIM : (h + 1) * HEAD_DIM, 0:rows] = acc[h, :, 0:rows]
            yall[k, first : first + rows, :] = turn[:, 0:rows].T.astype(BF)

    put_rows(med_rows, lat_rows)
    slices = Slices(place, br_out, br_in, n_sems.at[1])
    slices.cut(branch_ref[...])
    slices.start()

    pick = (
        lax.broadcasted_iota(jnp.int32, (own_rows, model), 1)
        == lax.broadcasted_iota(jnp.int32, (own_rows, model), 0) + place.me * own_rows
    )
    pick = jnp.where(pick, 1.0, 0.0).astype(BF)
    ff_tiles = ff_here // ff_tile

    def step_rows(j, rows):
        base = 2 * place.outer_from(j)
        blocks = base + place.inner, base + 1 - place.inner
        return jnp.concatenate([rows[b].reshape(lat_rows, model) for b in blocks], axis=0)

    def feed_tile(j, i):
        fn_rows, cot_rows = step_rows(j, fn_all), step_rows(j, cot_all)
        if i == 0:
            own_cols[0] = dot_nt(pick, fn_rows).astype(BF)
            own_cols[1] = dot_nt(pick, cot_rows).astype(BF)
        cols = slice(i * ff_tile, (i + 1) * ff_tile)
        value, slope = gelu_pair(dot_nn(fn_rows, up[:, cols]))
        grad = (dot_nt(cot_rows, down[cols, :]) * slope).astype(BF)
        up_part = dot_nn(own_cols[0], grad)
        down_part = dot_nn(own_cols[1], value.astype(BF))
        if j == 0:
            ug_ref[:, cols] = up_part
            down_t[:, cols] = down_part
        else:
            ug_ref[:, cols] += up_part
            down_t[:, cols] += down_part

    fed = [0]

    def feed_on(count):
        for n in range(fed[0], min(fed[0] + count, place.no * ff_tiles)):
            j, i = divmod(n, ff_tiles)
            if i == 0:
                for share in shares:
                    share.ready(j)
            feed_tile(j, i)
        fed[0] += count

    feed.back()
    gather_ld.relay()
    gather.relay()
    ln_slices.relay()
    feed.finish(put_sum)
    out_ref[...] = (mid[...] + sum_buf[...].astype(F32)).astype(BF)
    gather_ld.finish()
    gather.finish()
    fold.finish()
    stats.finish()
    low_gather.finish()
    ln_slices.finish()

    dq_fold = Fold(place, lambda o: give.at[o], got, lambda o: send.at[o], into, a_sems.at[1])
    folds = [
        Fold(
            place, lambda o, f=f: part.at[f, 2 * o + 1 - place.inner], pair_in.at[f],
            lambda o, f=f: part.at[f, 2 * o + place.inner], far_in.at[f], p_sems.at[f],
        )
        for f in range(2)
    ]

    def pass_queries(d):
        o = place.outer_to(d)
        dq_fold.pair(o).wait_recv()
        for h in range(heads):
            send[o, h] = (mine[o, h] + got[o, h].astype(F32)).astype(BF)
        dq_fold.far(d).start()

    for step, d in enumerate(order):
        o = place.outer_to(d)
        sources = [2 * o + place.inner, 2 * o + 1 - place.inner]
        allowed = image == pair_lanes(place, sources, images_here, lat_rows)
        for h in range(heads):
            queries = jnp.concatenate([q_all[s, h] for s in sources], axis=1)
            grads = jnp.concatenate([dot_all[s, h] for s in sources], axis=1)
            lse = jnp.concatenate([ld_all[s, h : h + 1, :] for s in sources], axis=1)
            delta = jnp.concatenate(
                [ld_all[s, heads + h : heads + h + 1, :] for s in sources], axis=1
            )
            probs, score_grad = grads_of(kh_ref[h], vh_ref[h], queries, grads, lse, delta, allowed)
            key_part = dot_nt(queries, score_grad)
            value_part = dot_nt(grads, probs)
            dk[h] = key_part if step == 0 else dk[h] + key_part
            dv[h] = value_part if step == 0 else dv[h] + value_part
            dq = dot_nn(kt_ref[h], score_grad)
            mine[o, h] = dq[:, 0:lat_rows]
            give[o, h] = dq[:, lat_rows:].astype(BF)
        dq_fold.pair(o).start()
        if step:
            pass_queries(order[step - 1])
        share_fn.forward(step)

    put_rows(0, med_rows)

    chunk = 2 * own_rows

    def weigh(d, k):
        o = place.outer_to(d)
        cols = pl.ds(pl.multiple_of(o * chunk, 128), chunk)
        value = dot_tn(x_ref[:, cols], yall[k])
        part[k, 2 * o] = value[0:own_rows].astype(BF)
        part[k, 2 * o + 1] = value[own_rows:].astype(BF)
        folds[k].pair(o).start()

    def both(d, k):
        o = place.outer_to(d)
        return part[k, 2 * o + place.inner].astype(F32) + pair_in[k, o].astype(F32)

    def pass_on(d, k):
        o = place.outer_to(d)
        folds[k].pair(o).wait_recv()
        if d:
            part[k, 2 * o + place.inner] = both(d, k).astype(BF)
            folds[k].far(d).start()

    med_tile, lat_tile = med_bufs.shape[-1], bufs.shape[-1]

    def back_rows(first, rows, tile):
        def tile_of(column):
            cols = pl.ds(column, tile)
            return dot_nt(yall[0, first : first + rows, :], wk[cols, :]) + dot_nt(
                yall[1, first : first + rows, :], wv[cols, :]
            )

        return tile_of

    med_sum = TensorSum(med_bufs, t_sems.at[4], back_rows(0, med_rows, med_tile))
    tasks = [(d, k) for d in order for k in range(2)]
    ahead = 3
    weigh(*tasks[0])
    weigh(*tasks[1])
    med_sum.give()
    for task in tasks[2:ahead]:
        weigh(*task)
    med_sum.cross()

    def lat_tile_of(column):
        cols = pl.ds(column, lat_tile)
        return (
            back_rows(med_rows, lat_rows, lat_tile)(column)
            + dot_nt(dq_all[place.me], wq[cols, :]) * SCALE
        )

    lat_sum = TensorSum(bufs.at[0], t_sems.at[3], lat_tile_of)
    dq_gather = Gather(place, dq_all, g_sems.at[4])

    def query_sums():
        o = place.outer
        dq_fold.pair(o).wait_recv()
        for h in range(heads):
            dq_own[h] = dq_own[h] + mine[o, h] + got[o, h].astype(F32)
        for d in range(1, place.no):
            dq_fold.far(d).wait_recv()
            for h in range(heads):
                dq_own[h] = dq_own[h] + into[d, h].astype(F32)
        for h in range(heads):
            turn[h * HEAD_DIM : (h + 1) * HEAD_DIM, 0:lat_rows] = dq_own[h]
        dq_all[place.me] = turn[:, 0:lat_rows].T.astype(BF)
        dq_gather.start()
        lat_sum.give()

    def put(column, tile):
        x_ref[0:med_rows, pl.ds(column, tile.shape[1])] = tile

    def put_lat(column, tile):
        x_ref[med_rows:, pl.ds(column, tile.shape[1])] = tile

    def norm_rows(i, carry):
        rows = pl.ds(pl.multiple_of(i * 128, 128), 128)
        xhat, _ = normalised(med_ref[rows, :].astype(F32))
        q = x_ref[rows, :].astype(F32)
        return (
            carry[0] + jnp.sum(q * xhat, axis=0, keepdims=True),
            carry[1] + jnp.sum(q, axis=0, keepdims=True),
        )

    def gain_copy(d):
        return remote(
            gain_out.at[place.far(d)], gain_in.at[d], e_sems.at[0, d], e_sems.at[1, d],
            {"blk": place.far(d)},
        )

    def norm_grads():
        med_sum.finish(put)
        zero = jnp.zeros((1, model), F32)
        med_gain = lax.fori_loop(0, med_rows // 128, norm_rows, (zero, zero))
        lat_sum.finish(put_lat)
        xhat, rstd = normalised(lat_ref[...].astype(F32))
        q = x_ref[med_rows:, :].astype(F32)
        lgrad_ref[...] += norm_back(q, line_of(lg_ref), xhat, rstd)
        all_rows = [
            *med_gain,
            jnp.sum(q * xhat, axis=0, keepdims=True),
            jnp.sum(q, axis=0, keepdims=True),
            *feed_gains,
        ]
        for o in range(nb):
            for n, line in enumerate(all_rows):
                gain_out[o, n : n + 1, :] = line[:, o * own_rows : (o + 1) * own_rows]
        for d in range(1, nb):
            gain_copy(d).start()

    all_rows_of = lambda ref: ref[...].reshape(nb * lat_rows, -1)

    def out_weights():
        slices.finish()
        og_ref[...] = dot_tn(all_rows_of(br_in), all_rows_of(low_all))

    between = {
        0: query_sums,
        3: lambda: (slices.relay(), lat_sum.cross(), dq_gather.relay()),
        5: med_sum.back,
        6: lat_sum.back,
        7: out_weights,
    }
    pace = -(-place.no * ff_tiles // len(tasks))
    for n in range(len(tasks)):
        if n + ahead < len(tasks):
            weigh(*tasks[n + ahead])
        feed_on(pace)
        if n in between:
            between.pop(n)()
        pass_on(*tasks[n])
    for late in between.values():
        late()
    norm_grads()
    feed_on(place.no * ff_tiles - fed[0])
    for share in shares:
        share.finish()
    dq_gather.finish()
    qg_ref[...] = dot_tn(all_rows_of(lns_ref), all_rows_of(dq_all)) * SCALE
    for k, ref in enumerate((kg_ref, vg_ref)):
        total = both(0, k)
        for d in range(1, place.no):
            folds[k].far(d).wait_recv()
            total = total + far_in[k, d].astype(F32)
        ref[...] = total
    gains = gain_out[place.me]
    for d in range(1, nb):
        gain_copy(d).wait_recv()
        gains = gains + gain_in[d]
    gains_ref[...] = gains
    for d in range(1, nb):
        gain_copy(d).wait_send()
    dq_fold.finish()
    for fold in folds:
        fold.finish()


def near_call(kernel, out_shapes, scratch, collective_id, args, any_args, any_outs=()):
    vmem = pl.BlockSpec(memory_space=pltpu.VMEM)
    anywhere = pl.BlockSpec(memory_space=pl.ANY)
    return pl.pallas_call(
        kernel,
        out_shape=[jax.ShapeDtypeStruct(s, d) for s, d in (*out_shapes, *any_outs)],
        in_specs=[vmem] * len(args) + [anywhere] * len(any_args),
        out_specs=[vmem] * len(out_shapes) + [anywhere] * len(any_outs),
        scratch_shapes=scratch,
        compiler_params=pltpu.CompilerParams(
            collective_id=collective_id, has_side_effects=True, vmem_limit_bytes=VMEM_LIMIT
        ),
    )(*args, *any_args)


def per_device(
    latents, media, query_weight, key_weight, value_weight, out_weight, up_weight, down_weight,
    media_gain, media_shift, latent_gain, latent_shift, feed_gain, feed_shift, cotangent, media_image,
):
    nb = lax.axis_size("blk")
    lat_rows, model = latents.shape
    med_rows = media.shape[0]
    inner = query_weight.shape[1]
    heads = inner // HEAD_DIM
    ff_here = up_weight.shape[1]
    no = nb // 2
    own_rows = model // nb
    dma = pltpu.SemaphoreType.DMA
    vm = pltpu.VMEM
    hd = HEAD_DIM
    half, quarter = lat_rows // 2, lat_rows // 4
    tile = 384
    tiles = model // 2 // tile
    every = med_rows + lat_rows
    block_t = (nb, heads, hd, lat_rows)
    pair_t = (no, heads, hd, lat_rows)
    rows_t = (nb, 4, quarter, model)
    slice_t = (nb, 2, half, own_rows)
    media_sum, *results = near_call(
        functools.partial(near_layer, nb),
        [
            ((every, model), BF), ((lat_rows, model), BF), ((lat_rows, model), F32),
            *[((own_rows, inner), F32)] * 4, *[((own_rows, ff_here), F32)] * 2, ((8, own_rows), F32),
        ],
        [
            vm((med_rows, model), BF), *[vm((model, inner), BF)] * 3, vm((inner, model), BF),
            vm((model, ff_here), BF), vm((ff_here, model), BF), vm(block_t, BF), vm(block_t, BF),
            vm((nb, 2 * heads, lat_rows), F32), vm((nb, lat_rows, inner), BF), vm((nb, lat_rows, inner), BF),
            vm(rows_t, BF), vm(rows_t, BF),
            vm((heads, med_rows, hd), BF), vm((heads, hd, med_rows), BF), vm((heads, med_rows, hd), BF),
            vm((heads, hd, med_rows), BF), vm((heads, lat_rows, hd), BF), vm((heads, hd, lat_rows), BF),
            vm((heads, lat_rows, hd), BF), vm((heads, hd, lat_rows), BF), vm((heads, hd, lat_rows), F32),
            vm((2 * heads, lat_rows), F32),
            vm(pair_t, F32), *[vm(pair_t, BF)] * 4, *[vm((no, 2 * heads, lat_rows), F32)] * 5,
            vm((lat_rows, ff_here), F32), vm((lat_rows, model), F32), vm((lat_rows, ff_here), BF),
            vm((lat_rows, ff_here), BF), vm((inner, lat_rows), F32), vm((lat_rows, model), BF),
            vm((lat_rows, model), BF), *[vm(slice_t, BF)] * 4,
            vm((heads, hd, med_rows), F32), vm((heads, hd, med_rows), F32), vm((heads, hd, lat_rows), F32),
            vm((inner, med_rows), F32), vm((2, every, inner), BF), vm((2, own_rows, 2 * lat_rows), BF),
            vm((2, nb, own_rows, inner), BF), vm((2, no, own_rows, inner), BF), vm((2, no, own_rows, inner), BF),
            vm((nb, 8, own_rows), F32), vm((nb, 8, own_rows), F32), vm((3, 6, tiles, lat_rows, tile), BF),
            vm((6, tiles, med_rows, tile), BF),
            dma((5, 2, 2, no)), dma((2, 2, 2, no)), dma((2, 2, no)), dma((2, 2, 2, no)),
            dma((2, 3, 2, 2 * no)), dma((2, 2, 2, nb)), dma((2, 2, 2, no)), dma((5, 3, 2, tiles)),
            dma((2, nb)), dma((7,)),
        ],
        0,
        (
            latents, cotangent, media_image, latent_gain, latent_shift, media_gain, media_shift, feed_gain,
            feed_shift,
        ),
        (media, query_weight, key_weight, value_weight, out_weight, up_weight, down_weight),
    )
    return last_step(media, media_gain, *results[:1], media_sum, *results[1:])


def last_kernel(media_ref, sum_ref, gain_ref, gains_ref, *refs):
    count = (len(refs) - 7) // 2
    moved, grad_ref = refs[0:count], refs[count]
    placed, gain_refs = refs[count + 1 : 2 * count + 1], refs[2 * count + 1 :]
    for source, target in zip(moved, placed, strict=True):
        target[...] = source[...]

    @pl.when(pl.program_id(0) == 0)
    def _():
        for n, ref in enumerate(gain_refs):
            ref[...] = gains_ref[n, :]

    xhat, rstd = normalised(media_ref[...].astype(F32))
    grad_ref[...] = norm_back(sum_ref[...].astype(F32), line_of(gain_ref), xhat, rstd)


def last_step(media, media_gain, resampled, media_sum, *rest):
    *moved, gains = (resampled, *rest)
    own_rows = gains.shape[1]
    steps = 2
    blocked = lambda v: pl.BlockSpec((v.shape[0] // steps, v.shape[1]), lambda i: (i, 0))
    gain_spec = pl.BlockSpec((own_rows,), lambda i: (0,))
    outs = pl.pallas_call(
        last_kernel,
        grid=(steps,),
        out_shape=[
            jax.ShapeDtypeStruct(media.shape, F32),
            *[jax.ShapeDtypeStruct(v.shape, v.dtype) for v in moved],
            *[jax.ShapeDtypeStruct((own_rows,), F32)] * 6,
        ],
        in_specs=[
            blocked(media), blocked(media), pl.BlockSpec(media_gain.shape, lambda i: (0,)),
            pl.BlockSpec(gains.shape, lambda i: (0, 0)), *[blocked(v) for v in moved],
        ],
        out_specs=[blocked(media), *[blocked(v) for v in moved], *[gain_spec] * 6],
        compiler_params=pltpu.CompilerParams(vmem_limit_bytes=VMEM_LIMIT),
    )(media, media_sum, media_gain, gains, *moved)
    (
        media_grad, resampled, latent_grad, query_grad, key_grad, value_grad, out_turned, up_grad,
        down_turned, *gain_grads,
    ) = outs
    return (
        resampled, media_grad, latent_grad, query_grad, key_grad, value_grad, out_turned.T, up_grad,
        down_turned.T, *gain_grads,
    )


def solution(mesh):
    in_specs = (
        P("blk", None), P("blk", None), P(None, "tp"), P(None, "tp"), P(None, "tp"), P("tp", None),
        P(None, "tp"), P("tp", None), P(), P(), P(), P(), P(), P(), P("blk", None), P("blk"),
    )
    out_specs = (
        P("blk", None), P("blk", None), P("blk", None), P("blk", "tp"), P("blk", "tp"),
        P("blk", "tp"), P("tp", "blk"), P("blk", "tp"), P("tp", "blk"), P("blk"), P("blk"),
        P("blk"), P("blk"), P("blk"), P("blk"),
    )
    body = per_device if mesh.shape["blk"] <= 16 else per_device_many
    return jax.shard_map(
        body, mesh=mesh, in_specs=in_specs, out_specs=out_specs, check_vma=False
    )
```
